128 devices in a mesh: dp: 16 (over z_hi, y, core), mp: 8 (over z_lo, x).
Axes of the slice: x: 4, y: 4, z: 4 (z_hi: 2, z_lo: 2; z = z_hi * 2 + z_lo), core: 2. Of those that a mesh axis runs over, the one named last changes fastest.
Arguments:
- prefix_input: bfloat16 [16, 1536, 1152], P('dp', 'mp'), may hold values from -6 to 6
- action_input: bfloat16 [16, 96, 1024], P('dp', 'mp'), may hold values from -6 to 6
- prefix_cotangent: bfloat16 [16, 1536, 1152], P('dp', 'mp'), may hold values from -6 to 6
- action_cotangent: bfloat16 [16, 96, 1024], P('dp', 'mp'), may hold values from -6 to 6
- prefix_lengths: int32 [16, 2], P('dp'), may hold values from 1 to 1152, as said below
- mixture: int32 [16, 2], P('dp'), may hold values from 8 to 64
- cut_points: int32 [9], replicated, may hold values from 0 to 4096, as said below
- prefix_query: bfloat16 [1152, 1024], P(('dp', 'mp')), may hold values from -0.1875 to 0.1875
- prefix_key: bfloat16 [1152, 256], P(('dp', 'mp')), may hold values from -0.1875 to 0.1875
- prefix_value: bfloat16 [1152, 256], P(('dp', 'mp')), may hold values from -0.1875 to 0.1875
- prefix_out: bfloat16 [1024, 1152], P(('dp', 'mp')), may hold values from -3 to 3
- prefix_first_gain: bfloat16 [1152], P(('dp', 'mp')), may hold values from 0.099609375 to 1.8984375
- prefix_second_gain: bfloat16 [1152], P(('dp', 'mp')), may hold values from 0.099609375 to 1.8984375
- action_query: bfloat16 [1024, 1024], P(('dp', 'mp')), may hold values from -0.1875 to 0.1875
- action_key: bfloat16 [1024, 256], P(('dp', 'mp')), may hold values from -0.1875 to 0.1875
- action_value: bfloat16 [1024, 256], P(('dp', 'mp')), may hold values from -0.1875 to 0.1875
- action_out: bfloat16 [1024, 1024], P(('dp', 'mp')), may hold values from -3 to 3
- action_first_gain: bfloat16 [1024], P(('dp', 'mp')), may hold values from 0.099609375 to 1.8984375
- action_second_gain: bfloat16 [1024], P(('dp', 'mp')), may hold values from 0.099609375 to 1.8984375
- prefix_gate: bfloat16 [1152, 6912], P(None, 'mp'), may hold values from -0.1875 to 0.1875
- prefix_up: bfloat16 [1152, 6912], P(None, 'mp'), may hold values from -0.1875 to 0.1875
- prefix_down: bfloat16 [6912, 1152], P('mp'), may hold values from -0.078125 to 0.078125
- action_gate: bfloat16 [8, 1024, 1024], P('mp'), may hold values from -0.1875 to 0.1875
- action_up: bfloat16 [8, 1024, 1024], P('mp'), may hold values from -0.1875 to 0.1875
- action_down: bfloat16 [8, 1024, 1024], P('mp'), may hold values from -0.25 to 0.25
Outputs:
- prefix_output: bfloat16 [16, 1536, 1152], P('dp', 'mp')
- action_output: bfloat16 [16, 96, 1024], P('dp', 'mp')
- prefix_input_gradient: bfloat16 [16, 1536, 1152], P('dp', 'mp')
- action_input_gradient: bfloat16 [16, 96, 1024], P('dp', 'mp')
- prefix_query_gradient: float32 [1152, 1024], P(('dp', 'mp'))
- prefix_key_gradient: float32 [1152, 256], P(('dp', 'mp'))
- prefix_value_gradient: float32 [1152, 256], P(('dp', 'mp'))
- prefix_out_gradient: float32 [1024, 1152], P(('dp', 'mp'))
- prefix_first_gradient: float32 [1152], P(('dp', 'mp'))
- prefix_second_gradient: float32 [1152], P(('dp', 'mp'))
- action_query_gradient: float32 [1024, 1024], P(('dp', 'mp'))
- action_key_gradient: float32 [1024, 256], P(('dp', 'mp'))
- action_value_gradient: float32 [1024, 256], P(('dp', 'mp'))
- action_out_gradient: float32 [1024, 1024], P(('dp', 'mp'))
- action_first_gradient: float32 [1024], P(('dp', 'mp'))
- action_second_gradient: float32 [1024], P(('dp', 'mp'))
- prefix_gate_gradient: float32 [1152, 6912], P(None, 'mp')
- prefix_up_gradient: float32 [1152, 6912], P(None, 'mp')
- prefix_down_gradient: float32 [6912, 1152], P('mp')
- action_gate_gradient: float32 [8, 1024, 1024], P('mp')
- action_up_gradient: float32 [8, 1024, 1024], P('mp')
- action_down_gradient: float32 [8, 1024, 1024], P('mp')
The draws below stay inside these ranges and needn't reach their ends.
Inputs may be any that keep to these rules, and one draw needn't show every extreme that they name: `prefix_lengths`: each row sums to 1536; exactly one entry of each row is 1152. cut_points[0] = 0, cut_points[8] = 4096, rising, multiples of 128; each difference cut_points[j+1] - cut_points[j] is at most 1024, reached by exactly one j in every draw.
All inputs are finite; a program needn't handle non-finite values.
Results may differ from the reference program's by a relative error of at most 0.024.
Values may be sent and summed in bfloat16 or wider, within the bound.
No kernel may reach another device: no remote copies, remote signals or barrier semaphores. Data moves between devices by JAX's collectives and lax.ppermute only.
A program may use at most 256 MiB of HBM per device.

```python
import jax
import jax.numpy as jnp
from jax import lax

D = 1152
HEADS = 4
HD = 256
FF = 6912
DA = 1024
FFA = 4096
CUT_UNIT = 128
ACT_LEN = 48
ITEMS_GRP = 2
GROUPS = 16
PREF_GRP = 1536
ACT_GRP = 96
CUT_MOST = 1024
LEN_MOST = 1152
N_MP = 8


def draw_cut_points(key, part):
    key = jax.random.fold_in(key, 7)
    pick_key, order_key = jax.random.split(key)
    unit_share = FFA // CUT_UNIT // N_MP
    others = N_MP - 1
    per_other = 2 * unit_share - 2
    slot_total = others * per_other
    extra_units = (N_MP - 2) * unit_share - others
    widest = jax.random.randint(pick_key, (), 0, N_MP)
    order_rank = jax.random.permutation(order_key, slot_total)
    taken = (order_rank < extra_units).astype(jnp.int32)
    slot_owner = jnp.arange(slot_total, dtype=jnp.int32) // per_other
    owner_ids = jnp.arange(others, dtype=jnp.int32)
    added = jnp.sum(jnp.where(slot_owner[None, :] == owner_ids[:, None], taken[None, :], 0), axis=1).astype(jnp.int32)
    other_widths = 1 + added
    device_ids = jnp.arange(N_MP, dtype=jnp.int32)
    other_slot = jnp.clip(device_ids - (device_ids > widest).astype(jnp.int32), 0, others - 1)
    widths = jnp.where(device_ids == widest, 2 * unit_share, other_widths[other_slot]).astype(jnp.int32)
    edge_list = jnp.concatenate([jnp.zeros((1,), jnp.int32), jnp.cumsum(widths).astype(jnp.int32)])
    return (edge_list * CUT_UNIT).astype(jnp.int32)


def group_lengths(key):
    pick_key, shift_key = jax.random.split(key)
    others = ITEMS_GRP - 1
    rest = PREF_GRP - LEN_MOST
    base_share = rest // others
    spread_half = base_share // 4
    offsets = jax.random.randint(shift_key, (others,), -spread_half, spread_half + 1).astype(jnp.int32)
    other_lengths = base_share + offsets - jnp.roll(offsets, 1)
    other_lengths = other_lengths + (jnp.arange(others, dtype=jnp.int32) == 0).astype(jnp.int32) * (rest % others)
    longest = jax.random.randint(pick_key, (), 0, ITEMS_GRP).astype(jnp.int32)
    item_ids = jnp.arange(ITEMS_GRP, dtype=jnp.int32)
    other_slot = jnp.clip(item_ids - (item_ids > longest).astype(jnp.int32), 0, others - 1)
    return jnp.where(item_ids == longest, LEN_MOST, other_lengths[other_slot]).astype(jnp.int32)


def draw_prefix_lengths(key, part):
    key = jax.random.fold_in(key, 11)
    group_keys = jax.random.split(key, GROUPS)
    return jax.vmap(group_lengths)(group_keys).astype(jnp.int32)


def plant(array, rng, smallest, largest):
    longest = array.shape.index(max(array.shape))
    spots = []
    for shift in (0, 1):
        where = [jax.random.randint(jax.random.fold_in(rng, axis), (), 0, length) for axis, length in enumerate(array.shape)]
        where[longest] = (where[longest] + shift) % array.shape[longest]
        spots.append(tuple(where))
    return array.at[spots[0]].set(smallest).at[spots[1]].set(largest)


def shard_levels(rng, shape, pieces, least, top_value):
    gain = 1.0
    for dim, parts in pieces:
        draws = jax.random.uniform(jax.random.fold_in(jax.random.fold_in(rng, 6), dim), (parts,), jnp.float32, least / len(pieces), top_value / len(pieces))
        gain = gain * jnp.repeat(jnp.exp(draws), shape[dim] // parts).reshape((-1,) + (1,) * (len(shape) - 1 - dim))
    return gain


def noise(rng, extent, width, limit, pieces=(), held_as=jnp.bfloat16):
    values = jax.random.normal(rng, extent, jnp.float32) * width
    if len(pieces) > 0:
        values = shard_levels(rng, extent, pieces, -0.22, 0.18) * values
    return jnp.clip(values, min=-limit, max=limit).astype(held_as)


def setup_inputs(seed: int = 0) -> dict:
    seeds = jax.random.split(jax.random.key(seed), 26)
    return {
        "prefix_input": noise(seeds[0], (GROUPS, PREF_GRP, D), 1.0, 6.0, ((0, 16), (1, 8))),
        "action_input": noise(seeds[1], (GROUPS, ACT_GRP, DA), 1.0, 6.0, ((0, 16), (1, 8))),
        "prefix_cotangent": noise(seeds[2], (GROUPS, PREF_GRP, D), 1.0, 6.0, ((0, 16), (1, 8))),
        "action_cotangent": noise(seeds[3], (GROUPS, ACT_GRP, DA), 1.0, 6.0, ((0, 16), (1, 8))),
        "prefix_lengths": draw_prefix_lengths(jax.random.fold_in(seeds[25], 71), 0),
        "mixture": plant(jax.random.randint(seeds[5], (GROUPS, ITEMS_GRP), 8, 65), jax.random.fold_in(seeds[5], 1), 8, 64).astype(jnp.int32),
        "cut_points": draw_cut_points(jax.random.fold_in(seeds[25], 71), 0),
        "prefix_query": noise(seeds[7], (D, HEADS * HD), D ** -0.5, 0.1875, ((0, 128),)),
        "prefix_key": noise(seeds[8], (D, HD), D ** -0.5, 0.1875, ((0, 128),)),
        "prefix_value": noise(seeds[9], (D, HD), D ** -0.5, 0.1875, ((0, 128),)),
        "prefix_out": noise(seeds[10], (HEADS * HD, D), (max(1, HEADS * HD // 256)) ** -0.5, 3.0, ((0, 128),)),
        "prefix_first_gain": jnp.clip(1.0 + 0.18 * jax.random.normal(seeds[11], (D,), jnp.float32), 0.099609375, 1.8984375).astype(jnp.bfloat16),
        "prefix_second_gain": jnp.clip(1.0 + 0.18 * jax.random.normal(seeds[12], (D,), jnp.float32), 0.099609375, 1.8984375).astype(jnp.bfloat16),
        "action_query": noise(seeds[13], (DA, HEADS * HD), DA ** -0.5, 0.1875, ((0, 128),)),
        "action_key": noise(seeds[14], (DA, HD), DA ** -0.5, 0.1875, ((0, 128),)),
        "action_value": noise(seeds[15], (DA, HD), DA ** -0.5, 0.1875, ((0, 128),)),
        "action_out": noise(seeds[16], (HEADS * HD, DA), (max(1, HEADS * HD // 256)) ** -0.5, 3.0, ((0, 128),)),
        "action_first_gain": jnp.clip(1.0 + 0.18 * jax.random.normal(seeds[17], (DA,), jnp.float32), 0.099609375, 1.8984375).astype(jnp.bfloat16),
        "action_second_gain": jnp.clip(1.0 + 0.18 * jax.random.normal(seeds[18], (DA,), jnp.float32), 0.099609375, 1.8984375).astype(jnp.bfloat16),
        "prefix_gate": noise(seeds[19], (D, FF), D ** -0.5, 0.1875, ((1, 8),)),
        "prefix_up": noise(seeds[20], (D, FF), D ** -0.5, 0.1875, ((1, 8),)),
        "prefix_down": noise(seeds[21], (FF, D), FF ** -0.5, 0.078125, ((0, 8),)),
        "action_gate": noise(seeds[22], (N_MP, DA, CUT_MOST), DA ** -0.5, 0.1875, ((0, 8),)),
        "action_up": noise(seeds[23], (N_MP, DA, CUT_MOST), DA ** -0.5, 0.1875, ((0, 8),)),
        "action_down": noise(seeds[24], (N_MP, CUT_MOST, DA), (FFA // N_MP) ** -0.5, 0.25, ((0, 8),)),
    }


epsilon = 1e-06
mix_denominator = 32.0
rope_base = 10000.0
highest = lax.Precision.HIGHEST

@jax.custom_vjp
def low(v):
    return lax.optimization_barrier(v.astype(jnp.bfloat16)).astype(jnp.float32)

@jax.custom_vjp
def low_back(v):
    return v

def low_keep(v):
    return (low(v), None)

def low_pass(kept, grad):
    return (grad,)

def back_keep(v):
    return (v, None)

def back_low(kept, grad):
    return (low(grad),)
low.defvjp(low_keep, low_pass)
low_back.defvjp(back_keep, back_low)

def matmul(operand, factor):
    return jnp.dot(operand, factor, precision=highest)

def normalize(inputs, gain_vector):
    return inputs * lax.rsqrt(lax.optimization_barrier(jnp.mean(inputs * inputs, axis=-1, keepdims=True)) + epsilon) * gain_vector

def rotate(inputs, position):
    half_size = inputs.shape[-1] // 2
    frequency = rope_base ** (-jnp.arange(half_size, dtype=jnp.float32) / half_size)
    angles = position.astype(jnp.float32)[:, None] * frequency[None, :]
    cosine = jnp.cos(angles)[:, None, :]
    sine_table = jnp.sin(angles)[:, None, :]
    first_half = inputs[..., :half_size]
    second_half = inputs[..., half_size:]
    return jnp.concatenate([first_half * cosine - second_half * sine_table, second_half * cosine + first_half * sine_table], axis=-1)

def item_tables(lengths, prefix_total, action_total, item_count, action_length):
    ends_at = jnp.cumsum(lengths).astype(jnp.int32)
    starts_at = (ends_at - lengths).astype(jnp.int32)
    prefix_rows = jnp.arange(prefix_total, dtype=jnp.int32)
    prefix_item = lax.optimization_barrier(jnp.sum((prefix_rows[:, None] >= ends_at[None, :]).astype(jnp.int32), axis=1)).astype(jnp.int32)
    item_ids = jnp.arange(item_count, dtype=jnp.int32)
    prefix_pick = prefix_item[:, None] == item_ids[None, :]
    prefix_place = prefix_rows - lax.optimization_barrier(jnp.sum(jnp.where(prefix_pick, starts_at[None, :], 0), axis=1)).astype(jnp.int32)
    action_rows = jnp.arange(action_total, dtype=jnp.int32)
    action_item = action_rows // action_length
    action_pick = action_item[:, None] == item_ids[None, :]
    action_place = lax.optimization_barrier(jnp.sum(jnp.where(action_pick, lengths[None, :], 0), axis=1)).astype(jnp.int32) + action_rows % action_length
    return (prefix_item, prefix_place, prefix_pick, action_item, action_place, action_pick)

def stream_inputs(inputs, gain_vector, query_weight, key_weight, value_weight, place):
    row_count = inputs.shape[0]
    normed = low(normalize(inputs, gain_vector))
    queries = low_back(matmul(normed, query_weight)).reshape(row_count, HEADS, HD)
    key_rows = low_back(matmul(normed, key_weight)).reshape(row_count, 1, HD)
    value_rows = low(low_back(matmul(normed, value_weight)))
    queries = low(rotate(queries, place) * HD ** (-0.5))
    key_rows = low(rotate(key_rows, place)[:, 0, :])
    return (queries, key_rows, value_rows)

def mixed_attention(queries, key_rows, value_rows, visible):
    scores = low_back(jnp.einsum('qhd,kd->hqk', queries, key_rows, precision=highest))
    scores = jnp.where(visible[None], scores, -1e+30)
    probs = jax.nn.softmax(scores, axis=-1)
    context = jnp.einsum('hqk,kd->qhd', low(probs), value_rows, precision=highest)
    return low(low_back(context)).reshape(queries.shape[0], HEADS * HD)

def stream_tail(inputs, context, out_weight, gain_vector, gate_weight, up_weight, down_weight, valid):
    hidden_state = inputs + low_back(matmul(context, out_weight))
    normed = low(normalize(hidden_state, gain_vector))
    gate_values = low_back(matmul(normed, gate_weight))
    up_values = low_back(matmul(normed, up_weight))
    product = low(jax.nn.gelu(gate_values, approximate=True) * up_values * valid)
    return hidden_state + low_back(matmul(product, down_weight))

def group_forward(weight_set, prefix_x, action_x, lengths, valid):
    prefix_query, prefix_key, prefix_value, prefix_out, prefix_first_gain, prefix_second_gain, action_query, action_key, action_value, action_out, action_first_gain, action_second_gain, prefix_gate, prefix_up, prefix_down, action_gate, action_up, action_down = weight_set
    tables = item_tables(lengths, PREF_GRP, ACT_GRP, ITEMS_GRP, ACT_LEN)
    prefix_queries, prefix_keys, prefix_values = stream_inputs(prefix_x, prefix_first_gain, prefix_query, prefix_key, prefix_value, tables[1])
    action_queries, action_keys, action_values = stream_inputs(action_x, action_first_gain, action_query, action_key, action_value, tables[4])
    queries = jnp.concatenate([prefix_queries, action_queries], axis=0)
    key_rows = jnp.concatenate([prefix_keys, action_keys], axis=0)
    value_rows = jnp.concatenate([prefix_values, action_values], axis=0)
    row_item = jnp.concatenate([tables[0], tables[3]], axis=0)
    is_action = jnp.concatenate([jnp.zeros((PREF_GRP,), jnp.bool_), jnp.ones((ACT_GRP,), jnp.bool_)], axis=0)
    visible = (row_item[:, None] == row_item[None, :]) & (is_action[:, None] | ~is_action[None, :])
    context = mixed_attention(queries, key_rows, value_rows, visible)
    prefix_result = stream_tail(prefix_x, context[:PREF_GRP], prefix_out, prefix_second_gain, prefix_gate, prefix_up, prefix_down, 1.0)
    gate_matrix = jnp.transpose(action_gate, (1, 0, 2)).reshape(DA, N_MP * CUT_MOST)
    up_matrix = jnp.transpose(action_up, (1, 0, 2)).reshape(DA, N_MP * CUT_MOST)
    down_matrix = action_down.reshape(N_MP * CUT_MOST, DA)
    action_result = stream_tail(action_x, context[PREF_GRP:], action_out, action_second_gain, gate_matrix, up_matrix, down_matrix, valid)
    return (prefix_result, action_result)

def reference(prefix_input, action_input, prefix_cotangent, action_cotangent, prefix_lengths, mixture, cut_points, prefix_query, prefix_key, prefix_value, prefix_out, prefix_first_gain, prefix_second_gain, action_query, action_key, action_value, action_out, action_first_gain, action_second_gain, prefix_gate, prefix_up, prefix_down, action_gate, action_up, action_down):
    widths = (cut_points[1:] - cut_points[:-1]).astype(jnp.int32)
    valid = (jnp.arange(CUT_MOST, dtype=jnp.int32)[None, :] < widths[:, None]).astype(jnp.float32).reshape(N_MP * CUT_MOST)
    weight_set = tuple((entry.astype(jnp.float32) for entry in (prefix_query, prefix_key, prefix_value, prefix_out, prefix_first_gain, prefix_second_gain, action_query, action_key, action_value, action_out, action_first_gain, action_second_gain, prefix_gate, prefix_up, prefix_down, action_gate, action_up, action_down)))

    def group_step(totals, group):
        prefix_x, action_x, prefix_seed, action_seed, lengths, numerators = group
        tables = item_tables(lengths, PREF_GRP, ACT_GRP, ITEMS_GRP, ACT_LEN)
        share_value = numerators.astype(jnp.float32) / mix_denominator
        prefix_scale = lax.optimization_barrier(jnp.sum(jnp.where(tables[2], share_value[None, :], 0.0), axis=1))
        action_scale = lax.optimization_barrier(jnp.sum(jnp.where(tables[5], share_value[None, :], 0.0), axis=1))

        def inner(weights_in, prefix_rows, action_rows):
            return group_forward(weights_in, prefix_rows, action_rows, lengths, valid)
        results, pullback = jax.vjp(inner, weight_set, prefix_x, action_x)
        deltas = pullback((prefix_seed * prefix_scale[:, None], action_seed * action_scale[:, None]))
        totals = jax.tree.map(jnp.add, totals, deltas[0])
        return (totals, (results[0].astype(jnp.bfloat16), results[1].astype(jnp.bfloat16), deltas[1].astype(jnp.bfloat16), deltas[2].astype(jnp.bfloat16)))
    zero_set = jax.tree.map(jnp.zeros_like, weight_set)
    sequence = (prefix_input.astype(jnp.float32), action_input.astype(jnp.float32), prefix_cotangent.astype(jnp.float32), action_cotangent.astype(jnp.float32), prefix_lengths, mixture)
    totals, stacked = lax.scan(group_step, zero_set, sequence)
    return (stacked[0], stacked[1], stacked[2], stacked[3], totals[0], totals[1], totals[2], totals[3], totals[4], totals[5], totals[6], totals[7], totals[8], totals[9], totals[10], totals[11], totals[12], totals[13], totals[14], totals[15], totals[16], totals[17])
```

```python
import jax
import jax.numpy as jnp
from jax import lax
from jax.sharding import PartitionSpec as P

ACT_LEN = 48
EPSILON = 1e-06
ROPE_BASE = 10000.0
HEADS = 4
HD = 256
PREF = 192
ACT = 12
ACT_PAD = 16
BLOCK = PREF + ACT_PAD
N_MP = 8
bf16 = jnp.bfloat16
f32 = jnp.float32


def mp_swap(array, step):
    return lax.ppermute(array, "mp", [(i, i ^ step) for i in range(N_MP)])


def dp_swap(array, step):
    return lax.ppermute(array, "dp", [(i, i ^ step) for i in range(16)])


def yz_swap(array, step):
    return dp_swap(array, (step >> 2) * 8 + (step & 3) * 2)


def core_swap(array):
    return dp_swap(array, 1)


ORDER = (4, 1, 3, 6, 2, 5, 7)


def dot(a, b):
    return jnp.dot(a, b, preferred_element_type=f32)


def dot_t(a, b):
    return lax.dot_general(a, b, (((1,), (1,)), ((), ())), preferred_element_type=f32)


def t_dot(a, b):
    return lax.dot_general(a, b, (((0,), (0,)), ((), ())), preferred_element_type=f32)


def inverse_rms(rows):
    return lax.rsqrt(jnp.mean(rows * rows, axis=-1, keepdims=True) + EPSILON)


def normalize_back(rows, scale, gain, delta):
    a = delta * gain
    return scale * (a - rows * (scale * scale) * jnp.mean(a * rows, axis=-1, keepdims=True))


def rotate(rows, cosine, sine):
    half = HD // 2
    first, second = rows[:, :half], rows[:, half:]
    return jnp.concatenate(
        [first * cosine - second * sine, second * cosine + first * sine], axis=1
    )


def unrotate(rows, cosine, sine):
    return rotate(rows, cosine, -sine)


def angle_tables(place):
    half = HD // 2
    frequency = ROPE_BASE ** (-jnp.arange(half, dtype=f32) / half)
    angles = place.astype(f32)[:, None] * frequency[None, :]
    return jnp.cos(angles), jnp.sin(angles)


def gather_mp(array, index, order=ORDER):
    out = jnp.zeros((N_MP,) + array.shape, array.dtype)
    out = lax.dynamic_update_index_in_dim(out, array, index, 0)
    for step in order:
        out = lax.dynamic_update_index_in_dim(out, mp_swap(array, step), index ^ step, 0)
    return out


def gather_yz(array, index, order=ORDER):
    out = jnp.zeros((8,) + array.shape, array.dtype)
    out = lax.dynamic_update_index_in_dim(out, array, index, 0)
    for step in order:
        out = lax.dynamic_update_index_in_dim(out, yz_swap(array, step), index ^ step, 0)
    return out


def gather_core(array, core):
    other = core_swap(array)
    low = jnp.where(core == 0, array, other)
    high = jnp.where(core == 0, other, array)
    return jnp.stack([low, high], axis=1)


def scatter_sum(pieces, index, swap, order=ORDER):
    total = lax.dynamic_index_in_dim(pieces, index, 0, keepdims=False).astype(f32)
    for step in order:
        piece = lax.dynamic_index_in_dim(pieces, index ^ step, 0, keepdims=False)
        total = total + swap(piece, step).astype(f32)
    return total


def gelu_parts(gate):
    c0 = 0.7978845608028654
    c1 = 0.044715
    square = gate * gate
    tanh = jnp.tanh(c0 * gate * (1.0 + c1 * square))
    half = 0.5 * (1.0 + tanh)
    slope = half + 0.5 * gate * (1.0 - tanh * tanh) * c0 * (1.0 + 3.0 * c1 * square)
    return gate * half, slope


def feed_chunk(rows, seed, gate_weight, up_weight, down_weight, valid):
    gate = dot(rows, gate_weight)
    up = dot(rows, up_weight)
    active, slope = gelu_parts(gate)
    product_delta = dot_t(seed, down_weight)
    if valid is not None:
        active = active * valid
        product_delta = product_delta * valid
    product = (active * up).astype(bf16)
    gate_delta = (product_delta * up * slope).astype(bf16)
    up_delta = (product_delta * active).astype(bf16)
    rows_delta = dot_t(gate_delta, gate_weight) + dot_t(up_delta, up_weight)
    partial = dot(product, down_weight)
    return product, gate_delta, up_delta, rows_delta.astype(bf16), partial.astype(bf16)


def pad_action(rows):
    return jnp.pad(rows, ((0, ACT_PAD - ACT), (0, 0)))


def block_of(prefix_rows, action_rows):
    width = prefix_rows.shape[1] - action_rows.shape[1]
    return jnp.concatenate([prefix_rows, jnp.pad(action_rows, ((0, 0), (0, width)))], axis=0)


def on_device(
    prefix_input,
    action_input,
    prefix_cotangent,
    action_cotangent,
    prefix_lengths,
    mixture,
    cut_points,
    prefix_query,
    prefix_key,
    prefix_value,
    prefix_out,
    prefix_first_gain,
    prefix_second_gain,
    action_query,
    action_key,
    action_value,
    action_out,
    action_first_gain,
    action_second_gain,
    prefix_gate,
    prefix_up,
    prefix_down,
    action_gate,
    action_up,
    action_down,
):
    mp = lax.axis_index("mp")
    dp = lax.axis_index("dp")
    core = dp & 1
    yz = (dp >> 3) * 4 + ((dp >> 1) & 3)
    D = prefix_input.shape[2]
    DA = action_input.shape[2]

    lengths = prefix_lengths[0]
    first_length = lengths[0]
    prefix_rows = jnp.arange(N_MP * PREF, dtype=jnp.int32)
    prefix_item = (prefix_rows >= first_length).astype(jnp.int32)
    prefix_place = prefix_rows - jnp.where(prefix_item == 1, first_length, 0)
    slot = jnp.arange(N_MP * ACT_PAD, dtype=jnp.int32)
    slot_real = (slot % ACT_PAD) < ACT
    action_rows = (slot // ACT_PAD) * ACT + slot % ACT_PAD
    action_item = (action_rows >= ACT_LEN).astype(jnp.int32)
    action_place = jnp.where(action_item == 1, lengths[1], first_length) + action_rows % ACT_LEN
    action_item = jnp.where(slot_real, action_item, 2)
    key_item = jnp.concatenate([prefix_item, action_item])
    key_is_action = jnp.concatenate(
        [jnp.zeros((N_MP * PREF,), jnp.bool_), jnp.ones((N_MP * ACT_PAD,), jnp.bool_)]
    )
    own_prefix_item = lax.dynamic_slice_in_dim(prefix_item, mp * PREF, PREF)
    own_action_item = lax.dynamic_slice_in_dim(action_item, mp * ACT_PAD, ACT_PAD)
    own_item = jnp.concatenate([own_prefix_item, own_action_item])
    own_is_action = jnp.concatenate(
        [jnp.zeros((PREF,), jnp.bool_), jnp.ones((ACT_PAD,), jnp.bool_)]
    )
    visible = (own_item[:, None] == key_item[None, :]) & (
        own_is_action[:, None] | ~key_is_action[None, :]
    )
    all_place = jnp.concatenate([prefix_place, action_place])
    key_cos, key_sin = angle_tables(all_place)
    own_place = jnp.concatenate(
        [
            lax.dynamic_slice_in_dim(prefix_place, mp * PREF, PREF),
            lax.dynamic_slice_in_dim(action_place, mp * ACT_PAD, ACT_PAD),
        ]
    )
    own_cos, own_sin = angle_tables(own_place)

    own_action = pad_action(action_input[0])
    own_block = block_of(prefix_input[0], own_action)
    x_all = lax.all_gather(own_block, "mp", axis=0, tiled=False)

    share = mixture[0].astype(f32) / 32.0
    prefix_seed = prefix_cotangent[0].astype(f32) * jnp.where(
        own_prefix_item == 1, share[1], share[0]
    )[:, None]
    action_seed = pad_action(action_cotangent[0]).astype(f32) * jnp.where(
        own_action_item == 1, share[1], share[0]
    )[:, None]
    seed_block = block_of(prefix_seed.astype(bf16), action_seed.astype(bf16))
    seed_block, _ = lax.optimization_barrier((seed_block, x_all[0, :8, :128]))
    seed_all = lax.all_gather(seed_block, "mp", axis=0, tiled=False)

    def column_block(first, second):
        return jnp.pad(jnp.stack([first, second], axis=1), ((0, 0), (0, 126)))

    pack_d = jnp.concatenate(
        [
            prefix_key,
            prefix_value,
            column_block(prefix_first_gain, prefix_second_gain),
            prefix_query,
        ],
        axis=1,
    )
    pack_a = jnp.concatenate(
        [
            action_key,
            action_value,
            column_block(action_first_gain, action_second_gain),
            action_query,
            prefix_out,
            action_out,
        ],
        axis=1,
    )
    pack = jnp.concatenate([pack_d, jnp.pad(pack_a, ((0, 1), (0, 0)))], axis=1)
    wide = pack_d.shape[1]
    near = gather_mp(pack, mp)
    near_d = near[:, :, :wide].reshape(72, wide)
    near_a = near[:, :8, wide:].reshape(64, pack_a.shape[1])
    kv_pack = jnp.concatenate([near_d[:, :640], near_a[:, :640]], axis=0)
    q_pack = jnp.concatenate([near_d[:, 640:], near_a[:, 640:1664]], axis=0)
    o_pack = near_a[:, 1664:]
    kv_full = gather_core(gather_yz(kv_pack, yz), core)
    q_full = gather_core(gather_yz(q_pack, yz), core)
    o_full = gather_core(gather_yz(o_pack, yz), core)
    kv_d = kv_full[:, :, :72].reshape(D, 640)
    kv_a = kv_full[:, :, 72:].reshape(DA, 640)
    wkv_d, wkv_a = kv_d[:, :512], kv_a[:, :512]
    wq_d = q_full[:, :, :72].reshape(D, 1024)
    wq_a = q_full[:, :, 72:].reshape(DA, 1024)
    wo_d = o_full[..., :D].reshape(1024, D)
    wo_a = o_full[..., D:].reshape(1024, DA)
    gains_d = kv_d[:, 512:].T.astype(f32)
    gains_a = kv_a[:, 512:].T.astype(f32)
    first_gain_d, second_gain_d = gains_d[0:1], gains_d[1:2]
    first_gain_a, second_gain_a = gains_a[0:1], gains_a[1:2]

    all_x_d = x_all[:, :PREF].reshape(N_MP * PREF, D).astype(f32)
    all_x_a = x_all[:, PREF:, :DA].reshape(N_MP * ACT_PAD, DA).astype(f32)
    all_normed_d = (all_x_d * inverse_rms(all_x_d) * first_gain_d).astype(bf16)
    all_normed_a = (all_x_a * inverse_rms(all_x_a) * first_gain_a).astype(bf16)
    kv_raw = jnp.concatenate([dot(all_normed_d, wkv_d), dot(all_normed_a, wkv_a)], axis=0)
    keys = rotate(kv_raw[:, :HD], key_cos, key_sin).astype(bf16)
    values = kv_raw[:, HD:].astype(bf16)

    x_d = prefix_input[0].astype(f32)
    x_a = own_action.astype(f32)
    rms_d, rms_a = inverse_rms(x_d), inverse_rms(x_a)
    normed_d = (x_d * rms_d * first_gain_d).astype(bf16)
    normed_a = (x_a * rms_a * first_gain_a).astype(bf16)
    query_raw = jnp.concatenate([dot(normed_d, wq_d), dot(normed_a, wq_a)], axis=0)
    queries = jnp.concatenate(
        [
            (rotate(query_raw[:, h * HD : (h + 1) * HD], own_cos, own_sin) * HD**-0.5)
            for h in range(HEADS)
        ],
        axis=0,
    ).astype(bf16)

    mask = visible[None]
    scores = dot_t(queries, keys).reshape(HEADS, BLOCK, -1)
    scores = jnp.where(mask, scores, -1e30)
    top = jnp.max(scores, axis=-1, keepdims=True)
    shifted = jnp.exp(scores - top)
    probs = shifted / jnp.sum(shifted, axis=-1, keepdims=True)
    probs_low = probs.astype(bf16).reshape(HEADS * BLOCK, -1)
    context_rows = dot(probs_low, values).astype(bf16)
    context = jnp.concatenate(
        [context_rows[h * BLOCK : (h + 1) * BLOCK] for h in range(HEADS)], axis=1
    )
    context_d, context_a = context[:PREF], context[PREF:]

    hidden_d = x_d + dot(context_d, wo_d)
    real = (jnp.arange(ACT_PAD) < ACT)[:, None]
    hidden_a = jnp.where(real, x_a + dot(context_a, wo_a), 0.0)
    scale_d, scale_a = inverse_rms(hidden_d), inverse_rms(hidden_a)
    second_d = (hidden_d * scale_d * second_gain_d).astype(bf16)
    second_a = (hidden_a * scale_a * second_gain_a).astype(bf16)

    second_block = block_of(second_d, second_a)
    cut_pair = lax.dynamic_slice_in_dim(cut_points, mp, 2)
    valid = (jnp.arange(action_gate.shape[2], dtype=jnp.int32) < cut_pair[1] - cut_pair[0]).astype(
        f32
    )[None, :]
    steps = (0,) + ORDER
    blocks = {0: second_block}
    for k in ORDER:
        blocks[k] = mp_swap(second_block, k)
    seeds = {k: lax.dynamic_index_in_dim(seed_all, mp ^ k, 0, keepdims=False) for k in steps}
    done = {}
    for k in steps:
        done[k] = feed_chunk(
            blocks[k][:PREF], seeds[k][:PREF], prefix_gate, prefix_up, prefix_down, None
        )
    rows_a = jnp.concatenate([blocks[k][PREF:, :DA] for k in steps], axis=0)
    seeds_a = jnp.concatenate([seeds[k][PREF:, :DA] for k in steps], axis=0)
    done_a = feed_chunk(rows_a, seeds_a, action_gate[0], action_up[0], action_down[0], valid)

    def rows_for(item, which):
        k = steps[item]
        return block_of(done[k][which], done_a[which][item * ACT_PAD : (item + 1) * ACT_PAD])

    delta_total = rows_for(0, 3).astype(f32)
    for item in range(1, N_MP):
        delta_total = delta_total + mp_swap(rows_for(item, 3), steps[item]).astype(f32)
    out_total = rows_for(0, 4).astype(f32)
    for item in range(1, N_MP):
        out_total = out_total + mp_swap(rows_for(item, 4), steps[item]).astype(f32)
    prefix_output = (hidden_d + out_total[:PREF]).astype(bf16)[None]
    action_output = (hidden_a + out_total[PREF:, :DA])[:ACT].astype(bf16)[None]

    rows_d = jnp.concatenate([blocks[k][:PREF] for k in steps], axis=0)
    seeds_d = jnp.concatenate([seeds[k][:PREF] for k in steps], axis=0)
    product_d, gate_delta_d, up_delta_d = (
        jnp.concatenate([done[k][i] for k in steps], axis=0) for i in range(3)
    )
    mlp = (
        t_dot(rows_d, gate_delta_d),
        t_dot(rows_d, up_delta_d),
        t_dot(product_d, seeds_d),
        t_dot(rows_a, done_a[1]),
        t_dot(rows_a, done_a[2]),
        t_dot(done_a[0], seeds_a),
    )
    mlp = tuple(lax.psum(g.astype(bf16), "dp").astype(f32) for g in mlp)

    delta_d, delta_a = delta_total[:PREF], delta_total[PREF:, :DA]
    hidden_delta_d = prefix_seed + normalize_back(hidden_d, scale_d, second_gain_d, delta_d)
    hidden_delta_a = action_seed + normalize_back(hidden_a, scale_a, second_gain_a, delta_a)
    ones_d = jnp.ones((PREF, 128), bf16)
    ones_a = jnp.ones((ACT_PAD, 128), bf16)
    second_term_d = t_dot((delta_d * hidden_d * scale_d).astype(bf16), ones_d)
    second_term_a = t_dot((delta_a * hidden_a * scale_a).astype(bf16), ones_a)
    low_d, low_a = hidden_delta_d.astype(bf16), hidden_delta_a.astype(bf16)
    out_grad_d = t_dot(context_d, low_d)
    out_grad_a = t_dot(context_a, low_a)
    context_delta = jnp.concatenate([dot_t(low_d, wo_d), dot_t(low_a, wo_a)], axis=0).astype(bf16)
    context_delta = jnp.concatenate(
        [context_delta[:, h * HD : (h + 1) * HD] for h in range(HEADS)], axis=0
    )

    probs_delta = dot_t(context_delta, values).reshape(HEADS, BLOCK, -1)
    row_dot = jnp.sum(probs * probs_delta, axis=-1, keepdims=True)
    score_delta = (probs * (probs_delta - row_dot)).astype(bf16).reshape(HEADS * BLOCK, -1)
    queries_delta = dot(score_delta, keys)
    keys_delta = t_dot(score_delta, queries)
    values_delta = t_dot(probs_low, context_delta)
    query_raw_delta = jnp.concatenate(
        [
            unrotate(queries_delta[h * BLOCK : (h + 1) * BLOCK], own_cos, own_sin) * HD**-0.5
            for h in range(HEADS)
        ],
        axis=1,
    ).astype(bf16)
    key_raw_delta = unrotate(keys_delta, key_cos, key_sin)
    kv_delta = jnp.concatenate([key_raw_delta, values_delta], axis=1).astype(bf16)
    kv_pieces = jnp.concatenate(
        [
            kv_delta[: N_MP * PREF].reshape(N_MP, PREF, 512),
            kv_delta[N_MP * PREF :].reshape(N_MP, ACT_PAD, 512),
        ],
        axis=1,
    )
    kv_own = scatter_sum(kv_pieces, mp, mp_swap).astype(bf16)

    q_grad_d = t_dot(normed_d, query_raw_delta[:PREF])
    q_grad_a = t_dot(normed_a, query_raw_delta[PREF:])
    kv_grad_d = t_dot(all_normed_d, kv_delta[: N_MP * PREF])
    kv_grad_a = t_dot(all_normed_a, kv_delta[N_MP * PREF :])

    def split(array):
        return array.astype(bf16).reshape(8, 2, -1, array.shape[1])

    o_grads = split(jnp.concatenate([out_grad_d, out_grad_a], axis=1))
    q_grads = jnp.concatenate(
        [
            split(jnp.concatenate([q_grad_d, second_term_d], axis=1)),
            split(jnp.concatenate([q_grad_a, second_term_a], axis=1)),
        ],
        axis=2,
    )
    kv_grads = jnp.concatenate([split(kv_grad_d), split(kv_grad_a)], axis=2)

    def reduce_far(pieces):
        mine = lax.dynamic_index_in_dim(pieces, core, 1, keepdims=False)
        theirs = lax.dynamic_index_in_dim(pieces, 1 - core, 1, keepdims=False)
        summed = (mine.astype(f32) + core_swap(theirs).astype(f32)).astype(bf16)
        return scatter_sum(summed, yz, yz_swap)

    o_near = reduce_far(o_grads)
    q_near = reduce_far(q_grads)
    kv_near = reduce_far(kv_grads)
    last_d = jnp.concatenate([q_near[:72], kv_near[:72]], axis=1).astype(bf16)
    last_a = jnp.concatenate([q_near[72:], kv_near[72:], o_near], axis=1).astype(bf16)
    last = jnp.concatenate(
        [
            last_d.reshape(N_MP, 9, -1),
            jnp.pad(last_a.reshape(N_MP, 8, -1), ((0, 0), (0, 1), (0, 0))),
        ],
        axis=2,
    )
    last = scatter_sum(last, mp, mp_swap)
    w_d = last_d.shape[1]
    grads_d, grads_a = last[:, :w_d], last[:8, w_d:]

    def split_grads(grads, query, key, value, gain):
        query_grad = grads[:, :1024]
        second = grads[:, 1024]
        key_grad = grads[:, 1152:1408]
        value_grad = grads[:, 1408:1664]
        first = (
            jnp.sum(query_grad * query.astype(f32), axis=1)
            + jnp.sum(key_grad * key.astype(f32), axis=1)
            + jnp.sum(value_grad * value.astype(f32), axis=1)
        ) / gain.astype(f32)
        return query_grad, key_grad, value_grad, first, second

    gd = split_grads(grads_d, prefix_query, prefix_key, prefix_value, prefix_first_gain)
    ga = split_grads(grads_a, action_query, action_key, action_value, action_first_gain)
    prefix_out_grad = grads_a[:, 1664 : 1664 + D]
    action_out_grad = grads_a[:, 1664 + D :]

    first_delta_d = dot_t(query_raw_delta[:PREF], wq_d) + dot_t(kv_own[:PREF], wkv_d)
    first_delta_a = dot_t(query_raw_delta[PREF:], wq_a) + dot_t(kv_own[PREF:], wkv_a)
    input_d = hidden_delta_d + normalize_back(x_d, rms_d, first_gain_d, first_delta_d)
    input_a = hidden_delta_a + normalize_back(x_a, rms_a, first_gain_a, first_delta_a)

    return (
        prefix_output,
        action_output,
        input_d.astype(bf16)[None],
        input_a[:ACT].astype(bf16)[None],
        gd[0],
        gd[1],
        gd[2],
        prefix_out_grad,
        gd[3],
        gd[4],
        ga[0],
        ga[1],
        ga[2],
        action_out_grad,
        ga[3],
        ga[4],
        mlp[0],
        mlp[1],
        mlp[2],
        mlp[3][None],
        mlp[4][None],
        mlp[5][None],
    )


def solution(mesh):
    rows = P("dp", "mp", None)
    both = P(("dp", "mp"), None)
    vector = P(("dp", "mp"))
    slots = P("mp", None, None)
    return jax.shard_map(
        on_device,
        mesh=mesh,
        in_specs=(rows,) * 4
        + (P("dp", None), P("dp", None), P())
        + (both,) * 4
        + (vector,) * 2
        + (both,) * 4
        + (vector,) * 2
        + (P(None, "mp"), P(None, "mp"), P("mp", None))
        + (slots,) * 3,
        out_specs=(rows,) * 4
        + (both,) * 4
        + (vector,) * 2
        + (both,) * 4
        + (vector,) * 2
        + (P(None, "mp"), P(None, "mp"), P("mp", None))
        + (slots,) * 3,
        check_vma=False,
    )
```

```python
import functools

import jax
import jax.numpy as jnp
import numpy as np
from jax import lax
from jax.experimental import pallas as pl
from jax.experimental.pallas import tpu as pltpu
from jax.sharding import PartitionSpec as P

ACT_LEN = 48
EPSILON = 1e-06
ROPE_BASE = 10000.0
HEADS = 4
HD = 256
PREF = 192
ACT = 12
ACT_PAD = 16
BLOCK = PREF + ACT_PAD
N_MP = 8
HALF_A = 96
HALF_B = BLOCK - HALF_A
HIDDEN_PAD = 896
VMEM_FEED = 50
bf16 = jnp.bfloat16
f32 = jnp.float32
ANY = pl.BlockSpec(memory_space=pl.ANY)
SMEM = pl.BlockSpec(memory_space=pltpu.SMEM)
VMEM = pl.BlockSpec(memory_space=pltpu.VMEM)
ARRIVALS = (
    ((0, 0), (0, 1)),
    ((1, 0), (1, 1)),
    ((3, 0), (3, 1)),
    ((4, 0), (4, 1)),
    ((5, 0), (7, 0)),
    ((2, 0), (5, 1)),
    ((2, 1), (7, 1)),
    ((6, 0),),
    ((6, 1),),
)
PARTS = tuple(part for parts in ARRIVALS for part in parts)
ROW_BLOCK = np.concatenate([np.full((HALF_A, HALF_B)[h], k) for k, h in PARTS]).astype(np.int32)
ROW_ID = np.concatenate(
    [np.arange(HALF_A) if h == 0 else np.arange(HALF_A, BLOCK) for _, h in PARTS]
).astype(np.int32)


def mp_swap(array, step):
    return lax.ppermute(array, "mp", [(i, i ^ step) for i in range(N_MP)])


def dp_swap(array, step):
    return lax.ppermute(array, "dp", [(i, i ^ step) for i in range(16)])


def yz_swap(array, step):
    return dp_swap(array, (step >> 2) * 8 + (step & 3) * 2)


def core_swap(array):
    return dp_swap(array, 1)


def where_parts(first, arrays, sizes):
    where = {}
    for i in range(arrays):
        at = 0
        for k, h in ARRIVALS[first + i]:
            where[k, h] = (i, at)
            at += sizes[h]
    return where


def fence_kernel(*refs):
    pass


def fence(array, *after):
    return pl.pallas_call(
        fence_kernel,
        in_specs=[pl.BlockSpec(memory_space=pl.ANY)] * (1 + len(after)),
        out_specs=pl.BlockSpec(memory_space=pl.ANY),
        out_shape=jax.ShapeDtypeStruct(array.shape, array.dtype),
        input_output_aliases={0: 0},
        cost_estimate=pl.CostEstimate(flops=0, bytes_accessed=0, transcendentals=0),
        name="fence",
    )(array, *after)


def join(*parts):
    return jnp.concatenate(parts, axis=0)


def add_low(*parts):
    total = parts[0].astype(f32)
    for part in parts[1:]:
        total = total + part.astype(f32)
    return total.astype(bf16)


def held(array, after):
    return fence(array, *after) if after else array


def relay_gather(a, b, swap, during=None, hold=None):
    na, nb = a.shape[0], b.shape[0]
    during = during or (lambda stage, arrived, sends: ())
    hold = hold or {}
    own = held(join(a, b), hold.get(1, ()))
    s1, s3, s4 = swap(own, 1), swap(own, 3), swap(own, 4)
    after = during(1, (own,), (own,)) + hold.get(2, ())
    sends = (join(s1[:na], s3[:na]), join(s3[:na], s4[na:]), join(s1[na:], s4[na:]))
    sends = tuple(held(x, after) for x in sends)
    zz, v1, v3 = swap(sends[0], 4), swap(sends[1], 1), swap(sends[2], 3)
    after = during(2, (s1, s3, s4), sends) + hold.get(3, ())
    sends = (held(zz[na:], after), held(v1[na:], after))
    z2a, z2b = swap(sends[0], 1), swap(sends[1], 3)
    during(3, (zz, v1, v3), sends)
    return own, s1, s3, s4, zz, v1, v3, z2a, z2b


def relay_scatter(pa, pb, swap, hold=None, sent=None):
    na, nb = pa[0].shape[0], pb[0].shape[0]
    hold = hold or {}
    sent = {} if sent is None else sent
    get = lambda stage: hold[stage]() if stage in hold else ()
    after = get(1)
    sent[1] = (held(pa[6], after), held(pb[6], after))
    r1, r3 = swap(sent[1][0], 1), swap(sent[1][1], 3)
    p7a = add_low(pa[7], r1)
    p5b = add_low(pb[5], r3)
    after = get(2)
    sends = (join(pa[5], p7a), join(pa[2], p5b), join(pb[2], pb[7]))
    sent[2] = tuple(held(x, after) for x in sends)
    zz, v1, v3 = swap(sent[2][0], 4), swap(sent[2][1], 1), swap(sent[2][2], 3)
    p1 = join(add_low(pa[1], zz[:na]), add_low(pb[1], v3[:nb]))
    p3 = join(add_low(pa[3], zz[na:], v1[:na]), pb[3])
    p4 = join(pa[4], add_low(pb[4], v1[na:], v3[nb:]))
    after = get(3)
    sent[3] = tuple(held(x, after) for x in (p1, p3, p4))
    s1, s3, s4 = swap(sent[3][0], 1), swap(sent[3][1], 3), swap(sent[3][2], 4)
    return pa[0], pb[0], s1, s3, s4


def total_of(pieces):
    pa, pb, s1, s3, s4 = pieces
    na = pa.shape[0]
    total_a = pa.astype(f32) + s1[:na].astype(f32) + s3[:na].astype(f32) + s4[:na].astype(f32)
    total_b = pb.astype(f32) + s1[na:].astype(f32) + s3[na:].astype(f32) + s4[na:].astype(f32)
    return total_a, total_b


def ring_scatter(pieces, swap, hold=None, sent=None):
    n = pieces[0].shape[0]
    hold = hold or {}
    near = [join(pieces[j], pieces[j ^ 4]) for j in range(4)]
    near[1:] = [held(x, hold.get(1, ())) for x in near[1:]]
    if sent is not None:
        sent += near[1:]
    total = near[0].astype(f32)
    for j in (1, 3, 2):
        total = total + swap(near[j], j).astype(f32)
    return total[:n] + swap(held(total[n:].astype(bf16), hold.get(2, ())), 4).astype(f32)


def gather_direct(array, index, swap):
    pair = index & 4
    high = (index >> 2) & 1
    two = jnp.zeros((2,) + array.shape, array.dtype)
    two = lax.dynamic_update_index_in_dim(two, array, high, 0)
    two = lax.dynamic_update_index_in_dim(two, swap(array, 4), 1 - high, 0)
    ring = index & 3
    out = jnp.zeros((2, 4) + array.shape, array.dtype)
    out = lax.dynamic_update_index_in_dim(out, two, ring, 1)
    for step in (1, 3, 2):
        out = lax.dynamic_update_index_in_dim(out, swap(two, step), ring ^ step, 1)
    return out.reshape((8,) + array.shape)


def scatter_direct(pieces, index, swap):
    high = (index >> 2) & 1
    ring = index & 3
    quads = pieces.reshape((2, 4) + pieces.shape[1:])
    total = lax.dynamic_index_in_dim(quads, ring, 1, keepdims=False).astype(f32)
    for step in (1, 3, 2):
        piece = lax.dynamic_index_in_dim(quads, ring ^ step, 1, keepdims=False)
        total = total + swap(piece, step).astype(f32)
    mine = lax.dynamic_index_in_dim(total, high, 0, keepdims=False)
    theirs = lax.dynamic_index_in_dim(total, 1 - high, 0, keepdims=False)
    return mine + swap(theirs.astype(bf16), 4).astype(f32)


def place_kernel(sizes, index_ref, *refs):
    arrays, outs = refs[:9], refs[9:]
    for (k, h), (i, at) in where_parts(0, 9, sizes).items():
        outs[h][index_ref[0] ^ k] = arrays[i][at : at + sizes[h]]


def place(arrays, na, index):
    rows, columns = arrays[0].shape
    eights = [x.reshape(x.shape[0] // 8, 8, columns) for x in arrays]
    sizes = (na // 8, (rows - na) // 8)
    return pl.pallas_call(
        functools.partial(place_kernel, sizes),
        in_specs=[SMEM] + [VMEM] * 9,
        out_specs=[VMEM] * 2,
        out_shape=[jax.ShapeDtypeStruct((8, n, 8, columns), bf16) for n in sizes],
        compiler_params=pltpu.CompilerParams(vmem_limit_bytes=20 * 1024 * 1024),
        name="place",
    )(index.reshape(1), *eights)


def interleave_kernel(cuts, core_ref, *refs):
    mine, theirs, outs = refs[:2], refs[2:4], refs[4:]
    core = core_ref[0]
    for out, (which, first, n) in zip(outs, cuts):
        for i in range(8):
            out[i, core] = mine[which][i, first : first + n]
            out[i, 1 - core] = theirs[which][i, first : first + n]


def interleave(halves_of, cuts, core):
    theirs = [core_swap(x) for x in halves_of]
    columns = halves_of[0].shape[-1]
    outs = pl.pallas_call(
        functools.partial(interleave_kernel, cuts),
        in_specs=[SMEM] + [VMEM] * 4,
        out_specs=[VMEM] * len(cuts),
        out_shape=[jax.ShapeDtypeStruct((8, 2, n, 8, columns), bf16) for _, _, n in cuts],
        compiler_params=pltpu.CompilerParams(vmem_limit_bytes=40 * 1024 * 1024),
        name="interleave",
    )(core.reshape(1), *halves_of, *theirs)
    return [x.reshape(-1, columns) for x in outs]


def gelu_parts(gate):
    c0 = 0.7978845608028654
    c1 = 0.044715
    square = gate * gate
    tanh = jnp.tanh(c0 * gate * (1.0 + c1 * square))
    half = 0.5 * (1.0 + tanh)
    slope = half + 0.5 * gate * (1.0 - tanh * tanh) * c0 * (1.0 + 3.0 * c1 * square)
    return gate * half, slope


def feed_block(rows, seed, gate_weight, up_weight, down_weight, valid):
    into, out_of = (dot_t, dot) if valid is None else (dot, dot_t)
    gate = into(rows, gate_weight)
    up = into(rows, up_weight)
    active, slope = gelu_parts(gate)
    product_delta = dot_t(seed, down_weight)
    if valid is not None:
        active = active * valid
        product_delta = product_delta * valid
    product = (active * up).astype(bf16)
    gate_delta = (product_delta * up * slope).astype(bf16)
    up_delta = (product_delta * active).astype(bf16)
    rows_delta = out_of(gate_delta, gate_weight) + out_of(up_delta, up_weight)
    return product, gate_delta, up_delta, rows_delta.astype(bf16)


def feed_kernel(layout, *refs):
    arrays = 1 + max(i for parts in layout for i, _ in parts)
    rows_refs, seed_refs, refs = refs[:arrays], refs[arrays : 2 * arrays], refs[2 * arrays :]
    gate_ref, up_ref, down_ref = refs[:3]
    action_gate_ref, action_up_ref, action_down_ref, valid_ref = refs[3:7]
    count = len(layout)
    outs = refs[-(2 * count + 8) :]
    products, deltas, kept_rows, kept_seeds = outs[:4]
    action_products, action_deltas, action_rows, action_seeds = outs[4:8]
    width = action_gate_ref.shape[0]
    rest = PREF - HALF_A

    def prefix_of(blocks):
        parts = []
        for (ia, a), (ib, b) in layout:
            parts += [blocks[ia][a : a + HALF_A], blocks[ib][b : b + rest]]
        return join(*parts)

    def action_of(blocks):
        parts = []
        for _, (ib, b) in layout:
            parts.append(blocks[ib][b + rest : b + HALF_B, :width])
        return join(*parts) if count > 1 else parts[0]

    rows, seed = prefix_of(rows_refs), prefix_of(seed_refs)
    product, gate_delta, up_delta, rows_delta = feed_block(
        rows, seed, gate_ref[...], up_ref[...], down_ref[...], None
    )
    hidden = product.shape[1]
    spare = jnp.zeros((count * PREF, HIDDEN_PAD - hidden), bf16)
    products[:, :hidden] = product
    products[:, hidden:] = spare
    deltas[:, :hidden] = gate_delta
    deltas[:, hidden:HIDDEN_PAD] = spare
    deltas[:, HIDDEN_PAD : HIDDEN_PAD + hidden] = up_delta
    deltas[:, HIDDEN_PAD + hidden :] = spare
    kept_rows[...] = rows
    kept_seeds[...] = seed
    rows, seed = action_of(rows_refs), action_of(seed_refs)
    product, gate_delta, up_delta, action_rows_delta = feed_block(
        rows,
        seed,
        action_gate_ref[...],
        action_up_ref[...],
        action_down_ref[...],
        valid_ref[...],
    )
    slots = gate_delta.shape[1]
    action_products[...] = product
    action_deltas[:, :slots] = gate_delta
    action_deltas[:, slots:] = up_delta
    action_rows[...] = rows
    action_seeds[...] = seed
    blank = jnp.zeros((ACT_PAD, rows_delta.shape[1] - width), bf16)
    for i in range(count):
        a, b, c = i * PREF, i * PREF + HALF_A, (i + 1) * PREF
        extra = slice(i * ACT_PAD, (i + 1) * ACT_PAD)
        ref_a, ref_b = outs[8 + 2 * i : 10 + 2 * i]
        ref_a[...] = rows_delta[a:b]
        ref_b[:rest] = rows_delta[b:c]
        ref_b[rest:, :width] = action_rows_delta[extra]
        ref_b[rest:, width:] = blank


def feed(arrays, seeds, weights, layout, base, kept, after):
    count = len(layout)
    width = arrays[0].shape[1]
    hidden = weights[0].shape[0]
    action_width, slots = weights[3].shape
    once = pl.Buffered(1)
    at = base // count

    def whole(array):
        return pl.BlockSpec(array.shape, lambda i: (0, 0), pipeline_mode=once)

    def part(size, columns):
        return (
            jax.ShapeDtypeStruct((N_MP * size, columns), bf16),
            pl.BlockSpec((count * size, columns), lambda i: (at, 0), pipeline_mode=once),
        )

    def own(size):
        return (
            jax.ShapeDtypeStruct((size, width), bf16),
            pl.BlockSpec((size, width), lambda i: (0, 0), pipeline_mode=once),
        )

    outs = [
        part(PREF, HIDDEN_PAD),
        part(PREF, 2 * HIDDEN_PAD),
        part(PREF, width),
        part(PREF, width),
        part(ACT_PAD, slots),
        part(ACT_PAD, 2 * slots),
        part(ACT_PAD, action_width),
        part(ACT_PAD, action_width),
    ] + [own(HALF_A), own(HALF_B)] * count
    reused = [] if kept is None else list(kept)
    given = [*arrays, *seeds]
    placed = len(given) + len(weights)
    results = pl.pallas_call(
        functools.partial(feed_kernel, layout),
        grid=(1,),
        in_specs=[whole(x) for x in given]
        + [VMEM] * len(weights)
        + [ANY] * (len(reused) + len(after)),
        out_shape=[shape for shape, _ in outs],
        out_specs=[spec for _, spec in outs],
        input_output_aliases={placed + i: i for i in range(len(reused))},
        compiler_params=pltpu.CompilerParams(
            dimension_semantics=("arbitrary",), vmem_limit_bytes=VMEM_FEED * 1024 * 1024
        ),
        cost_estimate=pl.CostEstimate(
            flops=10 * count * (PREF * width * hidden + ACT_PAD * action_width * slots),
            bytes_accessed=6 * (width * hidden + action_width * slots),
            transcendentals=count * PREF * hidden,
        ),
        name="feed",
    )(*given, *weights, *reused, *after)
    blocks = [results[8 + 2 * i : 10 + 2 * i] for i in range(count)]
    return blocks, results[:8]


def see(own_ref, key_ref):
    own, key = own_ref[...], key_ref[...]
    return (own[:, 0:1] == key[0:1]) | (own[:, 1:2] == key[1:2])


def attend_kernel(*refs):
    (normed_d, normed_a, x_d, x_a, wq_d, wq_a, wo_m, wo_e, wo_a) = refs[:9]
    (gain_d, gain_a, cosine, sine, own_codes, key_codes) = refs[9:15]
    kv = refs[15:24]
    (queries, context, tops, totals, hidden_d, hidden_a, block) = refs[24:]
    raw = join(dot(normed_d[...], wq_d[...]), dot(normed_a[...], wq_a[...]))
    keys = join(*[ref[:, :HD] for ref in kv])
    values = join(*[ref[:, HD:] for ref in kv])
    visible = see(own_codes, key_codes)
    cos, sin = cosine[...], sine[...]
    heads = []
    for h in range(HEADS):
        rows = slice(h * BLOCK, (h + 1) * BLOCK)
        query = (rotate(raw[:, h * HD : (h + 1) * HD], cos, sin) * HD**-0.5).astype(bf16)
        queries[rows] = query
        scores = jnp.where(visible, dot_t(query, keys), -1e30)
        top = jnp.max(scores, axis=1, keepdims=True)
        shifted = jnp.exp(scores - top)
        total = jnp.sum(shifted, axis=1, keepdims=True)
        tops[rows] = top
        totals[rows] = total
        heads.append(dot((shifted / total).astype(bf16), values).astype(bf16))
    mixed = jnp.concatenate(heads, axis=1)
    context[...] = mixed
    main, width_d, width_a = wo_m.shape[1], x_d.shape[1], x_a.shape[1]
    low_d, low_a = mixed[:PREF], mixed[PREF:]
    state = x_d[...].astype(f32) + jnp.concatenate(
        [dot(low_d, wo_m[...]), dot(low_d, wo_e[...])], axis=1
    )
    hidden_d[...] = state
    second_d = (state * inverse_rms(state) * gain_d[...]).astype(bf16)
    real = lax.broadcasted_iota(jnp.int32, (ACT_PAD, width_a), 0) < ACT
    state = jnp.where(real, x_a[...].astype(f32) + dot(low_a, wo_a[...]), 0.0)
    hidden_a[...] = state
    second_a = (state * inverse_rms(state) * gain_a[...]).astype(bf16)
    block[:PREF] = second_d
    block[PREF:, :width_a] = second_a
    block[PREF:, width_a:] = jnp.zeros((ACT_PAD, width_d - width_a), bf16)


def attend(*given):
    x_d, x_a = given[2:4]
    width_d, width_a = x_d.shape[1], x_a.shape[1]
    shape = jax.ShapeDtypeStruct
    stacked = HEADS * BLOCK
    return pl.pallas_call(
        attend_kernel,
        out_shape=[
            shape((stacked, HD), bf16),
            shape((BLOCK, HEADS * HD), bf16),
            shape((stacked, 1), f32),
            shape((stacked, 1), f32),
            shape((PREF, width_d), f32),
            shape((ACT_PAD, width_a), f32),
            shape((BLOCK, width_d), bf16),
        ],
        compiler_params=pltpu.CompilerParams(vmem_limit_bytes=50 * 1024 * 1024),
        cost_estimate=pl.CostEstimate(
            flops=4 * BLOCK * HEADS * HD * (N_MP * BLOCK + width_d),
            bytes_accessed=4 * 1024 * 1024 * 5,
            transcendentals=stacked * N_MP * BLOCK,
        ),
        name="attend",
    )(*given)


def attend_back_kernel(*refs):
    pieces = refs[:5]
    (hidden_d, hidden_a, cotangent_d, cotangent_a, share, gain_d, gain_a) = refs[5:12]
    (wo_m, wo_e, wo_a, queries, tops, totals, cosine, sine, own_codes, key_codes) = refs[12:22]
    kv = refs[22:31]
    outs = refs[-(6 + len(PARTS)) :]
    (hidden_delta_d, hidden_delta_a, low, terms_d, terms_a, query_delta) = outs[:6]
    kv_deltas = outs[6:]
    delta = join(*total_of([piece[...] for piece in pieces]))
    width_d, width_a = hidden_d.shape[1], hidden_a.shape[1]
    lows = []
    for rows, state_ref, cotangent, gain, out, terms in (
        (slice(0, PREF), hidden_d, cotangent_d, gain_d, hidden_delta_d, terms_d),
        (slice(PREF, BLOCK), hidden_a, cotangent_a, gain_a, hidden_delta_a, terms_a),
    ):
        state = state_ref[...]
        change = delta[rows, : state.shape[1]]
        scale = inverse_rms(state)
        seed = cotangent[...].astype(f32) * share[rows]
        back = seed + normalize_back(state, scale, gain[...], change)
        out[...] = back
        terms[...] = (change * state * scale).astype(bf16)
        lows.append(back.astype(bf16))
    low_d, low_a = lows
    low[:PREF] = low_d
    low[PREF:, :width_a] = low_a
    low[PREF:, width_a:] = jnp.zeros((ACT_PAD, width_d - width_a), bf16)
    main = wo_m.shape[1]
    context_delta = join(
        dot_t(low_d[:, :main], wo_m[...]) + dot_t(low_d[:, main:], wo_e[...]),
        dot_t(low_a, wo_a[...]),
    ).astype(bf16)
    keys = join(*[ref[:, :HD] for ref in kv])
    values = join(*[ref[:, HD:] for ref in kv])
    visible = see(own_codes, key_codes)
    cos, sin = cosine[...], sine[...]
    keys_delta, values_delta = None, None
    for h in range(HEADS):
        rows = slice(h * BLOCK, (h + 1) * BLOCK)
        query = queries[rows]
        change = context_delta[:, h * HD : (h + 1) * HD]
        scores = jnp.where(visible, dot_t(query, keys), -1e30)
        probs = jnp.exp(scores - tops[rows]) / totals[rows]
        probs_delta = dot_t(change, values)
        row_dot = jnp.sum(probs * probs_delta, axis=1, keepdims=True)
        score_delta = (probs * (probs_delta - row_dot)).astype(bf16)
        turned = unrotate(dot(score_delta, keys), cos, sin) * HD**-0.5
        query_delta[:, h * HD : (h + 1) * HD] = turned.astype(bf16)
        key_part = t_dot(score_delta, query)
        value_part = t_dot(probs.astype(bf16), change)
        keys_delta = key_part if h == 0 else keys_delta + key_part
        values_delta = value_part if h == 0 else values_delta + value_part
    at = 0
    for (_, half), out in zip(PARTS, kv_deltas):
        n = (HALF_A, HALF_B)[half]
        out[:, :HD] = keys_delta[at : at + n].astype(bf16)
        out[:, HD:] = values_delta[at : at + n].astype(bf16)
        at += n


def attend_back(*given):
    hidden_d, hidden_a = given[5:7]
    width_d, width_a = hidden_d.shape[1], hidden_a.shape[1]
    shape = jax.ShapeDtypeStruct
    stacked = HEADS * BLOCK
    outs = pl.pallas_call(
        attend_back_kernel,
        out_shape=[
            shape((PREF, width_d), f32),
            shape((ACT_PAD, width_a), f32),
            shape((BLOCK, width_d), bf16),
            shape((PREF, width_d), bf16),
            shape((ACT_PAD, width_a), bf16),
            shape((BLOCK, HEADS * HD), bf16),
        ]
        + [shape(((HALF_A, HALF_B)[half], 2 * HD), bf16) for _, half in PARTS],
        compiler_params=pltpu.CompilerParams(vmem_limit_bytes=50 * 1024 * 1024),
        cost_estimate=pl.CostEstimate(
            flops=2 * BLOCK * HEADS * HD, bytes_accessed=4 * BLOCK, transcendentals=stacked
        ),
        name="attend_back",
    )(*given)
    kv_deltas = dict(zip(PARTS, outs[6:]))
    pa = {k: kv_deltas[k, 0] for k in range(8)}
    pb = {k: kv_deltas[k, 1] for k in range(8)}
    return outs[:6], pa, pb


def pad_action(rows):
    return jnp.pad(rows, ((0, ACT_PAD - ACT), (0, 0)))


def widen(rows, width):
    return jnp.pad(rows, ((0, 0), (0, width - rows.shape[1])))


def block_of(prefix_rows, action_rows):
    return join(prefix_rows, widen(action_rows, prefix_rows.shape[1]))


def order_matrix(size, rows):
    d = jnp.arange(size, dtype=jnp.int32)
    r = d % rows
    mp = (d // rows) % 8
    dp = d // (8 * rows)
    place = (dp % 2) * (size // 2) + mp * (8 * rows) + (dp // 2) * rows + r
    return (place[:, None] == jnp.arange(size, dtype=jnp.int32)[None, :]).astype(bf16)


def dot(a, b):
    return jnp.dot(a, b, preferred_element_type=f32)


def dot_t(a, b):
    return lax.dot_general(a, b, (((1,), (1,)), ((), ())), preferred_element_type=f32)


def t_dot(a, b):
    return lax.dot_general(a, b, (((0,), (0,)), ((), ())), preferred_element_type=f32)


def inverse_rms(rows):
    return lax.rsqrt(jnp.mean(rows * rows, axis=-1, keepdims=True) + EPSILON)


def normalize_back(rows, scale, gain, delta):
    a = delta * gain
    return scale * (a - rows * (scale * scale) * jnp.mean(a * rows, axis=-1, keepdims=True))


def rotate(rows, cosine, sine):
    half = HD // 2
    first, second = rows[:, :half], rows[:, half:]
    return jnp.concatenate(
        [first * cosine - second * sine, second * cosine + first * sine], axis=1
    )


def unrotate(rows, cosine, sine):
    return rotate(rows, cosine, -sine)


def angle_tables(place):
    half = HD // 2
    frequency = ROPE_BASE ** (-jnp.arange(half, dtype=f32) / half)
    angles = place.astype(f32)[:, None] * frequency[None, :]
    return jnp.cos(angles), jnp.sin(angles)


def on_device(
    prefix_input,
    action_input,
    prefix_cotangent,
    action_cotangent,
    prefix_lengths,
    mixture,
    cut_points,
    prefix_query,
    prefix_key,
    prefix_value,
    prefix_out,
    prefix_first_gain,
    prefix_second_gain,
    action_query,
    action_key,
    action_value,
    action_out,
    action_first_gain,
    action_second_gain,
    prefix_gate,
    prefix_up,
    prefix_down,
    action_gate,
    action_up,
    action_down,
):
    mp = lax.axis_index("mp")
    dp = lax.axis_index("dp")
    core = dp & 1
    yz = (dp >> 3) * 4 + ((dp >> 1) & 3)
    D = prefix_input.shape[2]
    DA = action_input.shape[2]

    def column_block(first, second):
        return jnp.pad(jnp.stack([first, second], axis=1), ((0, 0), (0, 126)))

    pack_d = jnp.concatenate(
        [
            prefix_key,
            prefix_value,
            column_block(prefix_first_gain, prefix_second_gain),
            prefix_query,
        ],
        axis=1,
    )
    wide = pack_d.shape[1]
    pack = jnp.concatenate(
        [
            pack_d[:8],
            action_key,
            action_value,
            column_block(action_first_gain, action_second_gain),
            action_query,
            action_out,
            prefix_out,
            jnp.pad(pack_d[8:].reshape(8, wide // 8), ((0, 0), (0, 48))),
        ],
        axis=1,
    )
    lengths = prefix_lengths[0]
    first_length = lengths[0]

    def tables(source, row):
        is_action = row >= PREF
        prefix_row = source * PREF + row
        prefix_item = (prefix_row >= first_length).astype(jnp.int32)
        prefix_place = prefix_row - jnp.where(prefix_item == 1, first_length, 0)
        action_row = source * ACT + row - PREF
        action_item = (action_row >= ACT_LEN).astype(jnp.int32)
        action_place = jnp.where(action_item == 1, lengths[1], first_length) + action_row % ACT_LEN
        action_item = jnp.where(row - PREF < ACT, action_item, 2)
        item = jnp.where(is_action, action_item, prefix_item)
        place = jnp.where(is_action, action_place, prefix_place)
        return item, place, is_action

    own_item, own_place, own_is_action = tables(mp, jnp.arange(BLOCK, dtype=jnp.int32))
    key_item, _, key_is_action = tables(jnp.asarray(ROW_BLOCK) ^ mp, jnp.asarray(ROW_ID))
    own_codes = jnp.stack([own_item, jnp.where(own_is_action, own_item, -2)], axis=1)
    key_codes = jnp.stack(
        [jnp.where(key_is_action, -1, key_item), jnp.where(key_is_action, key_item, -1)], axis=0
    )
    own_cos, own_sin = angle_tables(own_place)

    share = mixture[0].astype(f32) / 32.0
    row_share = jnp.where(own_item == 1, share[1], share[0])[:, None]
    cotangent_a = pad_action(action_cotangent[0])
    prefix_seed = prefix_cotangent[0].astype(f32) * row_share[:PREF]
    action_seed = cotangent_a.astype(f32) * row_share[PREF:]
    seed_block = block_of(prefix_seed.astype(bf16), action_seed.astype(bf16))

    near = gather_direct(pack, mp, mp_swap)
    last_row = near[:, :, pack.shape[1] - 256 : pack.shape[1] - 48].reshape(8, 1, wide)
    near_d = jnp.concatenate([near[:, :, :wide], last_row], axis=1).reshape(72, wide)
    near_a = near[:, :, wide : pack.shape[1] - 256].reshape(64, -1)
    kv_a = jnp.concatenate([near_a[:, :640], near_a[:, 2688 + 1024 :]], axis=1)
    kv_d = widen(near_d[:, :640], 768)
    qo_a = join(near_a[:, 640:1664], near_a[:, 1664:2688])
    qo_b = join(near_d[:, 640:], near_a[:, 2688 : 2688 + 1024])

    seed_block = fence(seed_block, near)
    seeds = relay_gather(seed_block[:HALF_A], seed_block[HALF_A:], mp_swap)
    arrived = {}

    def note(name):
        def during(stage, blocks, sends):
            arrived[name, stage] = blocks
            return ()

        return during

    kv_halves = place(relay_gather(kv_a, kv_d, yz_swap, note("kv"), {3: seeds[1:4]}), 64, yz)
    kv_a, kv_d = interleave(kv_halves, ((0, 0, 8), (1, 0, 9)), core)
    wkv_d, wkv_a, wo_e = kv_d[:, :512], kv_a[:, :512], kv_a[:, 640:]
    gains_d = kv_d[:, 512:640].T.astype(f32)
    gains_a = kv_a[:, 512:640].T.astype(f32)
    first_gain_d, second_gain_d = gains_d[0:1], gains_d[1:2]
    first_gain_a, second_gain_a = gains_a[0:1], gains_a[1:2]

    own_action = pad_action(action_input[0])
    x_d, x_a = prefix_input[0].astype(f32), own_action.astype(f32)
    rms_d, rms_a = inverse_rms(x_d), inverse_rms(x_a)
    normed_d = (x_d * rms_d * first_gain_d).astype(bf16)
    normed_a = (x_a * rms_a * first_gain_a).astype(bf16)
    kv_raw = join(dot(normed_d, wkv_d), dot(normed_a, wkv_a))
    kv_own = jnp.concatenate(
        [rotate(kv_raw[:, :HD], own_cos, own_sin).astype(bf16), kv_raw[:, HD:].astype(bf16)],
        axis=1,
    )
    kv_rows = relay_gather(kv_own[:HALF_A], kv_own[HALF_A:], mp_swap, note("rows"))
    qo_a = fence(qo_a, arrived["kv", 2][0])
    qo_hold = {2: (kv_own, *seeds[4:7]), 3: (*arrived["rows", 2], *seeds[7:9])}
    qo_halves = place(relay_gather(qo_a, qo_b, yz_swap, note("qo"), qo_hold), 128, yz)
    cuts = ((0, 0, 8), (0, 8, 8), (1, 0, 9), (1, 9, 8))
    wq_a, wo_a, wq_d, wo_m = interleave(qo_halves, cuts, core)
    queries, context, tops, totals, hidden_d, hidden_a, second_block = attend(
        normed_d,
        normed_a,
        prefix_input[0],
        own_action,
        wq_d,
        wq_a,
        wo_m,
        wo_e,
        wo_a,
        second_gain_d,
        second_gain_a,
        own_cos,
        own_sin,
        own_codes,
        key_codes,
        *kv_rows,
    )

    slots = action_gate.shape[2]
    cut_pair = lax.dynamic_slice_in_dim(cut_points, mp, 2)
    valid = (jnp.arange(slots, dtype=jnp.int32) < cut_pair[1] - cut_pair[0]).astype(f32)[None, :]
    weights = (prefix_gate.T, prefix_up.T, prefix_down)
    weights += (action_gate[0], action_up[0], action_down[0], valid)
    kept = None
    results = {}

    def run(arrays, first, blocks, base, after):
        nonlocal kept
        where = where_parts(first, len(arrays), (HALF_A, HALF_B))
        layout = tuple((where[k, 0], where[k, 1]) for k in blocks)
        some = seeds[first : first + len(arrays)]
        done, kept = feed(arrays, some, weights, layout, base, kept, after)
        results.update(zip(blocks, done))
        return (done[0][0],)

    def feed_during(stage, arrays, sends):
        first, blocks, base = {1: (0, (0,), 6), 2: (1, (1, 3, 4), 0), 3: (4, (2, 5, 7), 3)}[stage]
        return run(arrays, first, blocks, base, sends)

    second_block = fence(second_block, seeds[8])
    arrays = relay_gather(
        second_block[:HALF_A], second_block[HALF_A:], mp_swap, feed_during
    )
    run(arrays[7:], 7, (6,), 7, ())
    product_d, deltas_d, rows_d, seeds_d, product_a, deltas_a, rows_a, seeds_a = kept

    grads = (
        t_dot(deltas_d, rows_d),
        t_dot(product_d, seeds_d),
        t_dot(rows_a, deltas_a),
        t_dot(product_a, seeds_a),
    )
    hidden = prefix_down.shape[0]
    grads = tuple(g.astype(bf16) for g in grads)
    after_grads = tuple(grads)
    one = lax.psum(grads[0], "dp")
    grads = (one,) + tuple(lax.psum(fence(g, one), "dp") for g in grads[1:])
    finished = (
        grads[0][:hidden].astype(f32),
        grads[0][HIDDEN_PAD : HIDDEN_PAD + hidden].astype(f32),
        grads[1][:hidden].astype(f32),
        grads[2][:, :slots].astype(f32),
        grads[2][:, slots:].astype(f32),
        grads[3].astype(f32),
    )

    pa = {k: v[0] for k, v in results.items()}
    pb = {k: v[1] for k, v in results.items()}
    delta_pieces = relay_scatter(pa, pb, mp_swap, {3: lambda: after_grads})
    (hidden_delta_d, hidden_delta_a, low, terms_d, terms_a, query_delta), pa, pb = attend_back(
        *delta_pieces,
        hidden_d,
        hidden_a,
        prefix_cotangent[0],
        cotangent_a,
        row_share,
        second_gain_d,
        second_gain_a,
        wo_m,
        wo_e,
        wo_a,
        queries,
        tops,
        totals,
        own_cos,
        own_sin,
        own_codes,
        key_codes,
        *kv_rows,
    )
    low_d, low_a = low[:PREF], low[PREF:, :DA]

    order_d, order_a = order_matrix(D, 9), order_matrix(DA, 8)
    turned_d = dot(normed_d, order_d).astype(bf16)
    turned_a = dot(normed_a, order_a).astype(bf16)
    turned_context = dot(context, order_a).astype(bf16)
    second_term_d = t_dot(dot(terms_d, order_d).astype(bf16), jnp.ones((PREF, 128), bf16))
    second_term_a = t_dot(dot(terms_a, order_a).astype(bf16), jnp.ones((ACT_PAD, 128), bf16))
    out_grad_d = t_dot(turned_context[:PREF], low_d).astype(bf16)
    out_grad_a = t_dot(turned_context[PREF:], low_a).astype(bf16)
    q_grad_d = t_dot(turned_d, query_delta[:PREF]).astype(bf16)
    q_grad_a = t_dot(turned_a, query_delta[PREF:]).astype(bf16)

    def split(array):
        return array.reshape(2, 8, -1, array.shape[1])

    def sum_cores(pieces):
        mine = lax.dynamic_index_in_dim(pieces, core, 0, keepdims=False)
        theirs = lax.dynamic_index_in_dim(pieces, 1 - core, 0, keepdims=False)
        return add_low(mine, core_swap(theirs))

    def sum_mp(pack, sent=None):
        pack = sum_cores(pack)
        pieces = [lax.dynamic_index_in_dim(pack, mp ^ k, 0, keepdims=False) for k in range(8)]
        return ring_scatter(pieces, mp_swap, {}, sent).astype(bf16)

    qo = [q_grad_a, out_grad_a, q_grad_d, out_grad_d[:, :1024]]
    qo_sent, kv_sent = [], []
    qo = sum_mp(jnp.concatenate([split(g) for g in qo], axis=2), qo_sent)
    kv_sum = ring_scatter(
        [join(pa[k], pb[k]) for k in range(8)], mp_swap, {2: tuple(qo_sent)}
    )
    kv_raw_delta = jnp.concatenate(
        [unrotate(kv_sum[:, :HD], own_cos, own_sin), kv_sum[:, HD:]], axis=1
    ).astype(bf16)
    kv_grad_d = t_dot(turned_d, kv_raw_delta[:PREF])
    kv_grad_a = t_dot(turned_a, kv_raw_delta[PREF:])
    kv_grad_d = jnp.concatenate([kv_grad_d, second_term_d], axis=1).astype(bf16)
    kv_grad_a = jnp.concatenate(
        [kv_grad_a.astype(bf16), second_term_a.astype(bf16), out_grad_d[:, 1024:]], axis=1
    )
    kv = sum_mp(jnp.concatenate([split(kv_grad_a), split(widen(kv_grad_d, 768))], axis=2), kv_sent)
    kv_a, kv_d = kv[:64], kv[64:, :640]
    qo_a, qo_b = qo[:128], qo[128:]

    product_d = fence(product_d, qo_sent[0])
    partial_d = dot(product_d[:, :hidden], prefix_down).astype(bf16)
    partial_a = dot(product_a, action_down[0]).astype(bf16)
    out = []
    for k in range(8):
        i = (1, 3, 4, 2, 5, 7, 0, 6).index(k)
        mine = partial_a[i * ACT_PAD : (i + 1) * ACT_PAD]
        out.append(block_of(partial_d[i * PREF : (i + 1) * PREF], mine))
    out = ring_scatter(out, mp_swap, {1: tuple(qo_sent)})
    prefix_output = (hidden_d + out[:PREF]).astype(bf16)[None]
    action_output = (hidden_a + out[PREF:, :DA])[:ACT].astype(bf16)[None]

    last_d = jnp.concatenate([kv_d, qo_b[:72]], axis=1).reshape(8, 9, wide)
    last_a = jnp.concatenate(
        [kv_a[:, :640], qo_a[:64], qo_a[64:], qo_b[72:], kv_a[:, 640:]], axis=1
    ).reshape(8, 8, -1)
    last = jnp.concatenate(
        [
            last_d[:, :8],
            last_a,
            jnp.pad(last_d[:, 8:].reshape(8, 8, wide // 8), ((0, 0), (0, 0), (0, 48))),
        ],
        axis=2,
    )
    last = scatter_direct(last, yz, yz_swap)
    ninth = last[:, last.shape[1] - 256 : last.shape[1] - 48].reshape(1, wide)
    grads_d = join(last[:, :wide], ninth)
    grads_a = last[:, wide : last.shape[1] - 256]

    def split_grads(grads, query, key, value, gain):
        key_grad = grads[:, :256]
        value_grad = grads[:, 256:512]
        second = grads[:, 512]
        query_grad = grads[:, 640:1664]
        first = (
            jnp.sum(query_grad * query.astype(f32), axis=1)
            + jnp.sum(key_grad * key.astype(f32), axis=1)
            + jnp.sum(value_grad * value.astype(f32), axis=1)
        ) / gain.astype(f32)
        return query_grad, key_grad, value_grad, first, second

    gd = split_grads(grads_d, prefix_query, prefix_key, prefix_value, prefix_first_gain)
    ga = split_grads(grads_a, action_query, action_key, action_value, action_first_gain)
    action_out_grad = grads_a[:, 1664:2688]
    prefix_out_grad = grads_a[:, 2688:]

    first_delta_d = dot_t(query_delta[:PREF], wq_d) + dot_t(kv_raw_delta[:PREF], wkv_d)
    first_delta_a = dot_t(query_delta[PREF:], wq_a) + dot_t(kv_raw_delta[PREF:], wkv_a)
    input_d = hidden_delta_d + normalize_back(x_d, rms_d, first_gain_d, first_delta_d)
    input_a = hidden_delta_a + normalize_back(x_a, rms_a, first_gain_a, first_delta_a)

    return (
        prefix_output,
        action_output,
        input_d.astype(bf16)[None],
        input_a[:ACT].astype(bf16)[None],
        gd[0],
        gd[1],
        gd[2],
        prefix_out_grad,
        gd[3],
        gd[4],
        ga[0],
        ga[1],
        ga[2],
        action_out_grad,
        ga[3],
        ga[4],
        finished[0].T,
        finished[1].T,
        finished[2],
        finished[3][None],
        finished[4][None],
        finished[5][None],
    )


def solution(mesh):
    rows = P("dp", "mp", None)
    both = P(("dp", "mp"), None)
    vector = P(("dp", "mp"))
    slots = P("mp", None, None)
    return jax.shard_map(
        on_device,
        mesh=mesh,
        in_specs=(rows,) * 4
        + (P("dp", None), P("dp", None), P())
        + (both,) * 4
        + (vector,) * 2
        + (both,) * 4
        + (vector,) * 2
        + (P(None, "mp"), P(None, "mp"), P("mp", None))
        + (slots,) * 3,
        out_specs=(rows,) * 4
        + (both,) * 4
        + (vector,) * 2
        + (both,) * 4
        + (vector,) * 2
        + (P(None, "mp"), P(None, "mp"), P("mp", None))
        + (slots,) * 3,
        check_vma=False,
    )
```

```python
import functools

import jax
import jax.numpy as jnp
import numpy as np
from jax import lax
from jax.experimental import pallas as pl
from jax.experimental.pallas import tpu as pltpu
from jax.sharding import PartitionSpec as P

ACT_LEN = 48
EPSILON = 1e-06
ROPE_BASE = 10000.0
HEADS = 4
HD = 256
PREF = 192
ACT = 12
ACT_PAD = 16
BLOCK = PREF + ACT_PAD
N_MP = 8
HALF_A = 96
HALF_B = BLOCK - HALF_A
HIDDEN_PAD = 896
VMEM_FEED = 50
bf16 = jnp.bfloat16
f32 = jnp.float32
ANY = pl.BlockSpec(memory_space=pl.ANY)
SMEM = pl.BlockSpec(memory_space=pltpu.SMEM)
VMEM = pl.BlockSpec(memory_space=pltpu.VMEM)
ARRIVALS = (
    ((0, 0), (0, 1)),
    ((1, 0), (1, 1)),
    ((3, 0), (3, 1)),
    ((4, 0), (4, 1)),
    ((5, 0), (7, 0)),
    ((2, 0), (5, 1)),
    ((2, 1), (7, 1)),
    ((6, 0),),
    ((6, 1),),
)
PARTS = tuple(part for parts in ARRIVALS for part in parts)
KEY_BLOCK = np.concatenate(
    [np.full(HALF_A, k) for k, _ in PARTS] + [np.full(ACT_PAD, k) for k, h in PARTS if h]
).astype(np.int32)
KEY_ROW = np.concatenate(
    [np.arange(HALF_A) + h * HALF_A for _, h in PARTS]
    + [np.arange(PREF, BLOCK) for _, h in PARTS if h]
).astype(np.int32)


ROW_PAIR, ACT_PAIR = 3 * PREF, 3 * ACT_PAD


def mp_swap(array, step):
    return lax.ppermute(array, "mp", [(i, i ^ step) for i in range(N_MP)])


def dp_swap(array, step):
    return lax.ppermute(array, "dp", [(i, i ^ step) for i in range(16)])


def yz_swap(array, step):
    return dp_swap(array, (step >> 2) * 8 + (step & 3) * 2)


def core_swap(array):
    return dp_swap(array, 1)


def where_parts(first, arrays, sizes):
    where = {}
    for i in range(arrays):
        at = 0
        for k, h in ARRIVALS[first + i]:
            where[k, h] = (i, at)
            at += sizes[h]
    return where


def fence_kernel(*refs):
    pass


def fence(array, *after):
    return pl.pallas_call(
        fence_kernel,
        in_specs=[pl.BlockSpec(memory_space=pl.ANY)] * (1 + len(after)),
        out_specs=pl.BlockSpec(memory_space=pl.ANY),
        out_shape=jax.ShapeDtypeStruct(array.shape, array.dtype),
        input_output_aliases={0: 0},
        cost_estimate=pl.CostEstimate(flops=0, bytes_accessed=0, transcendentals=0),
        name="fence",
    )(array, *after)


def join(*parts):
    return jnp.concatenate(parts, axis=0)


def add_low(*parts):
    total = parts[0].astype(f32)
    for part in parts[1:]:
        total = total + part.astype(f32)
    return total.astype(bf16)


def held(array, after):
    return fence(array, *after) if after else array


def sends_kernel(count, layout, *refs):
    for out, parts in zip(refs[len(refs) - len(layout) :], layout):
        at = 0
        for which, first, n in parts:
            out[at : at + n] = refs[which][first : first + n]
            at += n


def make_sends(arrays, layout, after=()):
    width = arrays[0].shape[1]
    low = lambda parts: jax.ShapeDtypeStruct((sum(n for _, _, n in parts), width), arrays[0].dtype)
    return pl.pallas_call(
        functools.partial(sends_kernel, len(arrays), layout),
        in_specs=[VMEM] * len(arrays) + [ANY] * len(after),
        out_specs=[VMEM] * len(layout),
        out_shape=[low(parts) for parts in layout],
        compiler_params=pltpu.CompilerParams(vmem_limit_bytes=16 * 1024 * 1024),
        cost_estimate=pl.CostEstimate(flops=0, bytes_accessed=0, transcendentals=0),
        name="sends",
    )(*arrays, *after)


def relay_gather(own, na, swap, during=None, hold=None):
    nb = own.shape[0] - na
    during = during or (lambda stage, arrived, sends: ())
    hold = hold or {}
    own = held(own, hold.get(1, ()))
    s1, s3, s4 = swap(own, 1), swap(own, 3), swap(own, 4)
    after = during(1, (own,), (own,)) + hold.get(2, ())
    layout = (
        ((0, 0, na), (1, 0, na)),
        ((1, 0, na), (2, na, nb)),
        ((0, na, nb), (2, na, nb)),
    )
    sends = make_sends((s1, s3, s4), layout, after)
    zz, v1, v3 = swap(sends[0], 4), swap(sends[1], 1), swap(sends[2], 3)
    after = during(2, (s1, s3, s4), tuple(sends)) + hold.get(3, ())
    sends = make_sends((zz, v1), (((0, na, na),), ((1, na, nb),)), after)
    z2a, z2b = swap(sends[0], 1), swap(sends[1], 3)
    during(3, (zz, v1, v3), tuple(sends))
    return own, s1, s3, s4, zz, v1, v3, z2a, z2b


def relay_scatter(pa, pb, swap, hold=None, sent=None):
    na, nb = pa[0].shape[0], pb[0].shape[0]
    hold = hold or {}
    sent = {} if sent is None else sent
    get = lambda stage: hold[stage]() if stage in hold else ()
    after = get(1)
    sent[1] = (held(pa[6], after), held(pb[6], after))
    r1, r3 = swap(sent[1][0], 1), swap(sent[1][1], 3)
    p7a = add_low(pa[7], r1)
    p5b = add_low(pb[5], r3)
    after = get(2)
    sends = (join(pa[5], p7a), join(pa[2], p5b), join(pb[2], pb[7]))
    sent[2] = tuple(held(x, after) for x in sends)
    zz, v1, v3 = swap(sent[2][0], 4), swap(sent[2][1], 1), swap(sent[2][2], 3)
    p1 = join(add_low(pa[1], zz[:na]), add_low(pb[1], v3[:nb]))
    p3 = join(add_low(pa[3], zz[na:], v1[:na]), pb[3])
    p4 = join(pa[4], add_low(pb[4], v1[na:], v3[nb:]))
    after = get(3)
    sent[3] = tuple(held(x, after) for x in (p1, p3, p4))
    s1, s3, s4 = swap(sent[3][0], 1), swap(sent[3][1], 3), swap(sent[3][2], 4)
    return pa[0], pb[0], s1, s3, s4


def total_of(pieces):
    pa, pb, s1, s3, s4 = pieces
    na = pa.shape[0]
    total_a = pa.astype(f32) + s1[:na].astype(f32) + s3[:na].astype(f32) + s4[:na].astype(f32)
    total_b = pb.astype(f32) + s1[na:].astype(f32) + s3[na:].astype(f32) + s4[na:].astype(f32)
    return total_a, total_b


def ring_scatter(pieces, swap, hold=None, sent=None):
    n = pieces[0].shape[0]
    hold = hold or {}
    near = [join(pieces[j], pieces[j ^ 4]) for j in range(4)]
    near[1:] = [held(x, hold.get(1, ())) for x in near[1:]]
    if sent is not None:
        sent += near[1:]
    total = near[0].astype(f32)
    for j in (1, 3, 2):
        total = total + swap(near[j], j).astype(f32)
    return total[:n] + swap(held(total[n:].astype(bf16), hold.get(2, ())), 4).astype(f32)


def gather_direct(array, index, swap):
    pair = index & 4
    high = (index >> 2) & 1
    two = jnp.zeros((2,) + array.shape, array.dtype)
    two = lax.dynamic_update_index_in_dim(two, array, high, 0)
    two = lax.dynamic_update_index_in_dim(two, swap(array, 4), 1 - high, 0)
    ring = index & 3
    out = jnp.zeros((2, 4) + array.shape, array.dtype)
    out = lax.dynamic_update_index_in_dim(out, two, ring, 1)
    for step in (1, 3, 2):
        out = lax.dynamic_update_index_in_dim(out, swap(two, step), ring ^ step, 1)
    return out.reshape((8,) + array.shape)


def scatter_direct(pieces, index, swap):
    high = (index >> 2) & 1
    ring = index & 3
    quads = pieces.reshape((2, 4) + pieces.shape[1:])
    total = lax.dynamic_index_in_dim(quads, ring, 1, keepdims=False).astype(f32)
    for step in (1, 3, 2):
        piece = lax.dynamic_index_in_dim(quads, ring ^ step, 1, keepdims=False)
        total = total + swap(piece, step).astype(f32)
    mine = lax.dynamic_index_in_dim(total, high, 0, keepdims=False)
    theirs = lax.dynamic_index_in_dim(total, 1 - high, 0, keepdims=False)
    return mine + swap(theirs.astype(bf16), 4).astype(f32)


def assemble_kernel(cuts, sizes, place_ref, *refs):
    arrays, outs = refs[:18], refs[18:]
    index, core = place_ref[0], place_ref[1]
    for (k, h), (i, at) in where_parts(0, 9, sizes).items():
        for out, (which, first, n, column, width) in zip(outs, cuts):
            if which == h:
                rows, columns = slice(at + first, at + first + n), slice(column, column + width)
                out[index ^ k, core] = arrays[i][rows, :, columns]
                out[index ^ k, 1 - core] = arrays[9 + i][rows, :, columns]


def assemble(mine, theirs, na, cuts, index, core):
    rows, columns = mine[0].shape
    eights = [x.reshape(x.shape[0] // 8, 8, columns) for x in (*mine, *theirs)]
    sizes = (na // 8, (rows - na) // 8)
    outs = pl.pallas_call(
        functools.partial(assemble_kernel, cuts, sizes),
        in_specs=[SMEM] + [VMEM] * 18,
        out_specs=[VMEM] * len(cuts),
        out_shape=[jax.ShapeDtypeStruct((8, 2, n, 8, width), bf16) for _, _, n, _, width in cuts],
        compiler_params=pltpu.CompilerParams(vmem_limit_bytes=40 * 1024 * 1024),
        name="assemble",
    )(jnp.stack([index, core]), *eights)
    return [x.reshape(-1, x.shape[-1]) for x in outs]


def gain_rows(block):
    pick = lax.broadcasted_iota(jnp.int32, (ACT_PAD, 128), 0)
    pick = (pick == lax.broadcasted_iota(jnp.int32, (ACT_PAD, 128), 1)).astype(bf16)
    turned = dot_t(pick, block)
    return turned[0:1], turned[1:2]


def keys_kernel(*refs):
    rows, (gain_d, gain_a, weight_d, weight_a, cosine, sine) = refs[:9], refs[9:15]
    normed_d, normed_a, keys, values = refs[-4:]
    gain_d, gain_a = gain_rows(gain_d[...])[0], gain_rows(gain_a[...])[0]
    width = weight_a.shape[0]
    prefix, action = [], []
    for i, parts in enumerate(ARRIVALS):
        at = 0
        for _, h in parts:
            prefix.append(rows[i][at : at + HALF_A])
            at += HALF_A
            if h:
                action.append(rows[i][at : at + ACT_PAD, :width])
                at += ACT_PAD
    x = join(*prefix).astype(f32)
    low_d = (x * inverse_rms(x) * gain_d).astype(bf16)
    x = join(*action).astype(f32)
    low_a = (x * inverse_rms(x) * gain_a).astype(bf16)
    normed_d[:PREF] = low_d[:PREF]
    normed_a[:ACT_PAD] = low_a[:ACT_PAD]
    normed_d[PREF:] = low_d[ROW_PAIR : ROW_PAIR + PREF]
    normed_a[ACT_PAD:] = low_a[ACT_PAIR : ACT_PAIR + ACT_PAD]
    raw = join(dot(low_d, weight_d[...]), dot(low_a, weight_a[...]))
    keys[...] = rotate(raw[:, :HD], cosine[...], sine[...]).astype(bf16)
    values[...] = raw[:, HD:].astype(bf16)


def keys_of(rows, gain_d, gain_a, weight_d, weight_a, cosine, sine, after):
    width_d, width_a = gain_d.shape[0], gain_a.shape[0]
    count = cosine.shape[0]
    shape = lambda *dims: jax.ShapeDtypeStruct(dims, bf16)
    given = [*rows, gain_d, gain_a, weight_d, weight_a, cosine, sine]
    return pl.pallas_call(
        keys_kernel,
        in_specs=[VMEM] * len(given) + [ANY] * len(after),
        out_specs=[VMEM] * 4,
        out_shape=[
            shape(2 * PREF, width_d),
            shape(2 * ACT_PAD, width_a),
            shape(count, HD),
            shape(count, HD),
        ],
        compiler_params=pltpu.CompilerParams(vmem_limit_bytes=48 * 1024 * 1024),
        cost_estimate=pl.CostEstimate(
            flops=4 * count * width_d * HD, bytes_accessed=8 * 1024 * 1024, transcendentals=count
        ),
        name="keys_of",
    )(*given, *after)


def gelu_parts(gate):
    c0 = 0.7978845608028654
    c1 = 0.044715
    square = gate * gate
    tanh = jnp.tanh(c0 * gate * (1.0 + c1 * square))
    half = 0.5 * (1.0 + tanh)
    slope = half + 0.5 * gate * (1.0 - tanh * tanh) * c0 * (1.0 + 3.0 * c1 * square)
    return gate * half, slope


def feed_block(rows, seed, gate_weight, up_weight, down_weight, valid):
    into, out_of = (dot_t, dot) if valid is None else (dot, dot_t)
    gate = into(rows, gate_weight)
    up = into(rows, up_weight)
    active, slope = gelu_parts(gate)
    product_delta = dot_t(seed, down_weight)
    if valid is not None:
        active = active * valid
        product_delta = product_delta * valid
    product = (active * up).astype(bf16)
    gate_delta = (product_delta * up * slope).astype(bf16)
    up_delta = (product_delta * active).astype(bf16)
    rows_delta = out_of(gate_delta, gate_weight) + out_of(up_delta, up_weight)
    return product, gate_delta, up_delta, rows_delta.astype(bf16)


def feed_kernel(layout, *refs):
    arrays = 1 + max(i for parts in layout for i, _ in parts)
    rows_refs, seed_refs, refs = refs[:arrays], refs[arrays : 2 * arrays], refs[2 * arrays :]
    gate_ref, up_ref, down_ref = refs[:3]
    action_gate_ref, action_up_ref, action_down_ref, valid_ref = refs[3:7]
    count = len(layout)
    outs = refs[-(2 * count + 8) :]
    products, deltas, kept_rows, kept_seeds = outs[:4]
    action_products, action_deltas, action_rows, action_seeds = outs[4:8]
    width = action_gate_ref.shape[0]
    rest = PREF - HALF_A

    def prefix_of(blocks):
        parts = []
        for (ia, a), (ib, b) in layout:
            parts += [blocks[ia][a : a + HALF_A], blocks[ib][b : b + rest]]
        return join(*parts)

    def action_of(blocks):
        parts = []
        for _, (ib, b) in layout:
            parts.append(blocks[ib][b + rest : b + HALF_B, :width])
        return join(*parts) if count > 1 else parts[0]

    rows, seed = prefix_of(rows_refs), prefix_of(seed_refs)
    product, gate_delta, up_delta, rows_delta = feed_block(
        rows, seed, gate_ref[...], up_ref[...], down_ref[...], None
    )
    hidden = product.shape[1]
    spare = jnp.zeros((count * PREF, HIDDEN_PAD - hidden), bf16)
    products[:, :hidden] = product
    products[:, hidden:] = spare
    deltas[:, :hidden] = gate_delta
    deltas[:, hidden:HIDDEN_PAD] = spare
    deltas[:, HIDDEN_PAD : HIDDEN_PAD + hidden] = up_delta
    deltas[:, HIDDEN_PAD + hidden :] = spare
    kept_rows[...] = rows
    kept_seeds[...] = seed
    rows, seed = action_of(rows_refs), action_of(seed_refs)
    product, gate_delta, up_delta, action_rows_delta = feed_block(
        rows,
        seed,
        action_gate_ref[...],
        action_up_ref[...],
        action_down_ref[...],
        valid_ref[...],
    )
    slots = gate_delta.shape[1]
    action_products[...] = product
    action_deltas[:, :slots] = gate_delta
    action_deltas[:, slots:] = up_delta
    action_rows[...] = rows
    action_seeds[...] = seed
    blank = jnp.zeros((ACT_PAD, rows_delta.shape[1] - width), bf16)
    for i in range(count):
        a, b, c = i * PREF, i * PREF + HALF_A, (i + 1) * PREF
        extra = slice(i * ACT_PAD, (i + 1) * ACT_PAD)
        ref_a, ref_b = outs[8 + 2 * i : 10 + 2 * i]
        ref_a[...] = rows_delta[a:b]
        ref_b[:rest] = rows_delta[b:c]
        ref_b[rest:, :width] = action_rows_delta[extra]
        ref_b[rest:, width:] = blank


def feed(arrays, seeds, weights, layout, base, kept, after):
    count = len(layout)
    width = arrays[0].shape[1]
    hidden = weights[0].shape[0]
    action_width, slots = weights[3].shape
    once = pl.Buffered(1)
    at = base // count

    def whole(array):
        return pl.BlockSpec(array.shape, lambda i: (0, 0), pipeline_mode=once)

    def part(size, columns):
        return (
            jax.ShapeDtypeStruct((N_MP * size, columns), bf16),
            pl.BlockSpec((count * size, columns), lambda i: (at, 0), pipeline_mode=once),
        )

    def own(size):
        return (
            jax.ShapeDtypeStruct((size, width), bf16),
            pl.BlockSpec((size, width), lambda i: (0, 0), pipeline_mode=once),
        )

    outs = [
        part(PREF, HIDDEN_PAD),
        part(PREF, 2 * HIDDEN_PAD),
        part(PREF, width),
        part(PREF, width),
        part(ACT_PAD, slots),
        part(ACT_PAD, 2 * slots),
        part(ACT_PAD, action_width),
        part(ACT_PAD, action_width),
    ] + [own(HALF_A), own(HALF_B)] * count
    reused = [] if kept is None else list(kept)
    given = [*arrays, *seeds]
    placed = len(given) + len(weights)
    results = pl.pallas_call(
        functools.partial(feed_kernel, layout),
        grid=(1,),
        in_specs=[whole(x) for x in given]
        + [VMEM] * len(weights)
        + [ANY] * (len(reused) + len(after)),
        out_shape=[shape for shape, _ in outs],
        out_specs=[spec for _, spec in outs],
        input_output_aliases={placed + i: i for i in range(len(reused))},
        compiler_params=pltpu.CompilerParams(
            dimension_semantics=("arbitrary",), vmem_limit_bytes=VMEM_FEED * 1024 * 1024
        ),
        cost_estimate=pl.CostEstimate(
            flops=10 * count * (PREF * width * hidden + ACT_PAD * action_width * slots),
            bytes_accessed=6 * (width * hidden + action_width * slots),
            transcendentals=count * PREF * hidden,
        ),
        name="feed",
    )(*given, *weights, *reused, *after)
    blocks = [results[8 + 2 * i : 10 + 2 * i] for i in range(count)]
    return blocks, results[:8]


def see(own_ref, key_ref):
    own, key = own_ref[...], key_ref[...]
    return (own[:, 0:1] == key[0:1]) | (own[:, 1:2] == key[1:2])


def attend_kernel(*refs):
    (normed_d, normed_a, x_d, x_a, wq_d, wq_a, wo_m, wo_e, wo_a) = refs[:9]
    (gain_d, gain_a, cosine, sine, own_codes, key_codes) = refs[9:15]
    keys, values = refs[15][...], refs[16][...]
    (queries, context, tops, totals, hidden_d, hidden_a, block) = refs[-7:]
    gain_d, gain_a = gain_rows(gain_d[...])[1], gain_rows(gain_a[...])[1]
    raw = join(dot(normed_d[:PREF], wq_d[...]), dot(normed_a[:ACT_PAD], wq_a[...]))
    visible = see(own_codes, key_codes)
    cos, sin = cosine[...], sine[...]
    heads = []
    for h in range(HEADS):
        rows = slice(h * BLOCK, (h + 1) * BLOCK)
        query = (rotate(raw[:, h * HD : (h + 1) * HD], cos, sin) * HD**-0.5).astype(bf16)
        queries[rows] = query
        scores = jnp.where(visible, dot_t(query, keys), -1e30)
        top = jnp.max(scores, axis=1, keepdims=True)
        shifted = jnp.exp(scores - top)
        total = jnp.sum(shifted, axis=1, keepdims=True)
        tops[rows] = top
        totals[rows] = total
        heads.append(dot((shifted / total).astype(bf16), values).astype(bf16))
    mixed = jnp.concatenate(heads, axis=1)
    context[...] = mixed
    main, width_d, width_a = wo_m.shape[1], x_d.shape[1], x_a.shape[1]
    low_d, low_a = mixed[:PREF], mixed[PREF:]
    state = x_d[...].astype(f32) + jnp.concatenate(
        [dot(low_d, wo_m[...]), dot(low_d, wo_e[...])], axis=1
    )
    hidden_d[...] = state
    second_d = (state * inverse_rms(state) * gain_d).astype(bf16)
    real = lax.broadcasted_iota(jnp.int32, (ACT_PAD, width_a), 0) < ACT
    state = jnp.where(real, x_a[...].astype(f32) + dot(low_a, wo_a[...]), 0.0)
    hidden_a[...] = state
    second_a = (state * inverse_rms(state) * gain_a).astype(bf16)
    block[:PREF] = second_d
    block[PREF:, :width_a] = second_a
    block[PREF:, width_a:] = jnp.zeros((ACT_PAD, width_d - width_a), bf16)


def attend(*given, after):
    x_d, x_a = given[2:4]
    width_d, width_a = x_d.shape[1], x_a.shape[1]
    shape = jax.ShapeDtypeStruct
    stacked = HEADS * BLOCK
    return pl.pallas_call(
        attend_kernel,
        in_specs=[VMEM] * len(given) + [ANY] * len(after),
        out_specs=[VMEM] * 7,
        out_shape=[
            shape((stacked, HD), bf16),
            shape((BLOCK, HEADS * HD), bf16),
            shape((stacked, 1), f32),
            shape((stacked, 1), f32),
            shape((PREF, width_d), f32),
            shape((ACT_PAD, width_a), f32),
            shape((BLOCK, width_d), bf16),
        ],
        compiler_params=pltpu.CompilerParams(vmem_limit_bytes=50 * 1024 * 1024),
        cost_estimate=pl.CostEstimate(
            flops=4 * BLOCK * HEADS * HD * (N_MP * BLOCK + width_d),
            bytes_accessed=4 * 1024 * 1024 * 5,
            transcendentals=stacked * N_MP * BLOCK,
        ),
        name="attend",
    )(*given, *after)


def attend_back_kernel(*refs):
    pieces = refs[:5]
    (hidden_d, hidden_a, cotangent_d, cotangent_a, share, gain_d, gain_a) = refs[5:12]
    (wo_m, wo_e, wo_a, queries, tops, totals, cosine, sine, own_codes, key_codes) = refs[12:22]
    keys, values = refs[22][...], refs[23][...]
    outs = refs[-(6 + len(PARTS)) :]
    (hidden_delta_d, hidden_delta_a, low, terms_d, terms_a, query_delta) = outs[:6]
    kv_deltas = outs[6:]
    gain_d, gain_a = gain_rows(gain_d[...])[1], gain_rows(gain_a[...])[1]
    delta = join(*total_of([piece[...] for piece in pieces]))
    width_d, width_a = hidden_d.shape[1], hidden_a.shape[1]
    lows = []
    for rows, state_ref, cotangent, gain, out, terms in (
        (slice(0, PREF), hidden_d, cotangent_d, gain_d, hidden_delta_d, terms_d),
        (slice(PREF, BLOCK), hidden_a, cotangent_a, gain_a, hidden_delta_a, terms_a),
    ):
        state = state_ref[...]
        change = delta[rows, : state.shape[1]]
        scale = inverse_rms(state)
        seed = cotangent[...].astype(f32) * share[rows]
        back = seed + normalize_back(state, scale, gain, change)
        out[...] = back
        terms[...] = (change * state * scale).astype(bf16)
        lows.append(back.astype(bf16))
    low_d, low_a = lows
    low[:PREF] = low_d
    low[PREF:, :width_a] = low_a
    low[PREF:, width_a:] = jnp.zeros((ACT_PAD, width_d - width_a), bf16)
    main = wo_m.shape[1]
    context_delta = join(
        dot_t(low_d[:, :main], wo_m[...]) + dot_t(low_d[:, main:], wo_e[...]),
        dot_t(low_a, wo_a[...]),
    ).astype(bf16)
    visible = see(own_codes, key_codes)
    cos, sin = cosine[...], sine[...]
    keys_delta, values_delta = None, None
    for h in range(HEADS):
        rows = slice(h * BLOCK, (h + 1) * BLOCK)
        query = queries[rows]
        change = context_delta[:, h * HD : (h + 1) * HD]
        scores = jnp.where(visible, dot_t(query, keys), -1e30)
        probs = jnp.exp(scores - tops[rows]) / totals[rows]
        probs_delta = dot_t(change, values)
        row_dot = jnp.sum(probs * probs_delta, axis=1, keepdims=True)
        score_delta = (probs * (probs_delta - row_dot)).astype(bf16)
        turned = unrotate(dot(score_delta, keys), cos, sin) * HD**-0.5
        query_delta[:, h * HD : (h + 1) * HD] = turned.astype(bf16)
        key_part = t_dot(score_delta, query)
        value_part = t_dot(probs.astype(bf16), change)
        keys_delta = key_part if h == 0 else keys_delta + key_part
        values_delta = value_part if h == 0 else values_delta + value_part
    at, extra = 0, len(PARTS) * HALF_A
    for (_, half), out in zip(PARTS, kv_deltas):
        for columns, change in ((slice(0, HD), keys_delta), (slice(HD, 2 * HD), values_delta)):
            out[:HALF_A, columns] = change[at : at + HALF_A].astype(bf16)
            if half:
                out[HALF_A:, columns] = change[extra : extra + ACT_PAD].astype(bf16)
        at += HALF_A
        extra += half * ACT_PAD


def attend_back(*given):
    hidden_d, hidden_a = given[5:7]
    width_d, width_a = hidden_d.shape[1], hidden_a.shape[1]
    shape = jax.ShapeDtypeStruct
    stacked = HEADS * BLOCK
    outs = pl.pallas_call(
        attend_back_kernel,
        out_shape=[
            shape((PREF, width_d), f32),
            shape((ACT_PAD, width_a), f32),
            shape((BLOCK, width_d), bf16),
            shape((PREF, width_d), bf16),
            shape((ACT_PAD, width_a), bf16),
            shape((BLOCK, HEADS * HD), bf16),
        ]
        + [shape(((HALF_A, HALF_B)[half], 2 * HD), bf16) for _, half in PARTS],
        compiler_params=pltpu.CompilerParams(vmem_limit_bytes=50 * 1024 * 1024),
        cost_estimate=pl.CostEstimate(
            flops=2 * BLOCK * HEADS * HD, bytes_accessed=4 * BLOCK, transcendentals=stacked
        ),
        name="attend_back",
    )(*given)
    kv_deltas = dict(zip(PARTS, outs[6:]))
    pa = {k: kv_deltas[k, 0] for k in range(8)}
    pb = {k: kv_deltas[k, 1] for k in range(8)}
    return outs[:6], pa, pb


def theirs_kernel(cuts, place_ref, *refs):
    out = refs[-1]
    core = place_ref[1]
    for ref, (row, n, source, column, width) in zip(refs, cuts):
        out[:, row : row + n, :, column : column + width] = ref[
            1 - core, :, :, :, source : source + width
        ]


def near_kernel(cuts, place_ref, *refs):
    got, outs = refs[len(cuts)], refs[-4:]
    mp, core = place_ref[0], place_ref[1]
    for step, out in zip((0, 1, 3, 2), outs):
        for pair in range(2):
            block = mp ^ step ^ (4 * pair)
            base = pair * got.shape[1]
            for ref, (row, n, source, column, width) in zip(refs, cuts):
                columns = slice(column, column + width)
                mine = ref[core, block, :, :, source : source + width].astype(f32)
                total = mine + got[block, row : row + n, :, columns].astype(f32)
                out[base + row : base + row + n, :, columns] = total.astype(bf16)


def sum_weights(grads, cuts, columns, place, sent, got, after, before_last):
    views = [g.reshape(2, 8, -1, 8, g.shape[1]) for g in grads]
    eights = max(row + n for row, n, _, _, _ in cuts)
    params = pltpu.CompilerParams(vmem_limit_bytes=44 * 1024 * 1024)
    cost = pl.CostEstimate(flops=0, bytes_accessed=0, transcendentals=0)
    low = lambda *dims: jax.ShapeDtypeStruct(dims, bf16)
    theirs = pl.pallas_call(
        functools.partial(theirs_kernel, cuts),
        in_specs=[SMEM] + [VMEM] * len(views),
        out_specs=VMEM,
        out_shape=low(8, eights, 8, columns),
        compiler_params=params,
        cost_estimate=cost,
        name="theirs",
    )(place, *views)
    near = pl.pallas_call(
        functools.partial(near_kernel, cuts),
        in_specs=[SMEM] + [VMEM] * (len(views) + 1) + [ANY] * len(after),
        out_specs=[VMEM] * 4,
        out_shape=[low(2 * eights, 8, columns)] * 4,
        compiler_params=params,
        cost_estimate=cost,
        name="near",
    )(place, *views, core_swap(theirs), *after)
    near = [x.reshape(16 * eights, columns) for x in near]
    sent += near[1:]
    total = near[0].astype(f32)
    for step, x in zip((1, 3, 2), near[1:]):
        got.append(mp_swap(x, step))
        total = total + got[-1].astype(f32)
    half = 8 * eights
    last = held(total[half:].astype(bf16), before_last)
    return (total[:half] + mp_swap(last, 4).astype(f32)).astype(bf16)


def pad_action(rows):
    return jnp.pad(rows, ((0, ACT_PAD - ACT), (0, 0)))


def widen(rows, width):
    return jnp.pad(rows, ((0, 0), (0, width - rows.shape[1])))


def block_of(prefix_rows, action_rows):
    return join(prefix_rows, widen(action_rows, prefix_rows.shape[1]))


def order_matrix(size, rows):
    d = jnp.arange(size, dtype=jnp.int32)
    r = d % rows
    mp = (d // rows) % 8
    dp = d // (8 * rows)
    place = (dp % 2) * (size // 2) + mp * (8 * rows) + (dp // 2) * rows + r
    return (place[:, None] == jnp.arange(size, dtype=jnp.int32)[None, :]).astype(bf16)


def dot(a, b):
    return jnp.dot(a, b, preferred_element_type=f32)


def dot_t(a, b):
    return lax.dot_general(a, b, (((1,), (1,)), ((), ())), preferred_element_type=f32)


def t_dot(a, b):
    return lax.dot_general(a, b, (((0,), (0,)), ((), ())), preferred_element_type=f32)


def inverse_rms(rows):
    return lax.rsqrt(jnp.mean(rows * rows, axis=-1, keepdims=True) + EPSILON)


def normalize_back(rows, scale, gain, delta):
    a = delta * gain
    return scale * (a - rows * (scale * scale) * jnp.mean(a * rows, axis=-1, keepdims=True))


def rotate(rows, cosine, sine):
    half = HD // 2
    first, second = rows[:, :half], rows[:, half:]
    return jnp.concatenate(
        [first * cosine - second * sine, second * cosine + first * sine], axis=1
    )


def unrotate(rows, cosine, sine):
    return rotate(rows, cosine, -sine)


def angle_tables(place):
    half = HD // 2
    frequency = ROPE_BASE ** (-jnp.arange(half, dtype=f32) / half)
    angles = place.astype(f32)[:, None] * frequency[None, :]
    return jnp.cos(angles), jnp.sin(angles)


def on_device(
    prefix_input,
    action_input,
    prefix_cotangent,
    action_cotangent,
    prefix_lengths,
    mixture,
    cut_points,
    prefix_query,
    prefix_key,
    prefix_value,
    prefix_out,
    prefix_first_gain,
    prefix_second_gain,
    action_query,
    action_key,
    action_value,
    action_out,
    action_first_gain,
    action_second_gain,
    prefix_gate,
    prefix_up,
    prefix_down,
    action_gate,
    action_up,
    action_down,
):
    mp = lax.axis_index("mp")
    dp = lax.axis_index("dp")
    core = dp & 1
    yz = (dp >> 3) * 4 + ((dp >> 1) & 3)
    D = prefix_input.shape[2]
    DA = action_input.shape[2]

    def column_block(first, second):
        return jnp.pad(jnp.stack([first, second], axis=1), ((0, 0), (0, 126)))

    pack_d = jnp.concatenate(
        [
            prefix_key,
            prefix_value,
            column_block(prefix_first_gain, prefix_second_gain),
            prefix_query,
        ],
        axis=1,
    )
    wide = pack_d.shape[1]
    pack = jnp.concatenate(
        [
            pack_d[:8],
            action_key,
            action_value,
            column_block(action_first_gain, action_second_gain),
            action_query,
            action_out,
            prefix_out,
            jnp.pad(pack_d[8:].reshape(8, wide // 8), ((0, 0), (0, 48))),
        ],
        axis=1,
    )
    lengths = prefix_lengths[0]
    first_length = lengths[0]

    def tables(source, row):
        is_action = row >= PREF
        prefix_row = source * PREF + row
        prefix_item = (prefix_row >= first_length).astype(jnp.int32)
        prefix_place = prefix_row - jnp.where(prefix_item == 1, first_length, 0)
        action_row = source * ACT + row - PREF
        action_item = (action_row >= ACT_LEN).astype(jnp.int32)
        action_place = jnp.where(action_item == 1, lengths[1], first_length) + action_row % ACT_LEN
        action_item = jnp.where(row - PREF < ACT, action_item, 2)
        item = jnp.where(is_action, action_item, prefix_item)
        place = jnp.where(is_action, action_place, prefix_place)
        return item, place, is_action

    own_item, own_place, own_is_action = tables(mp, jnp.arange(BLOCK, dtype=jnp.int32))
    key_item, key_place, key_is_action = tables(jnp.asarray(KEY_BLOCK) ^ mp, jnp.asarray(KEY_ROW))
    key_cos, key_sin = angle_tables(key_place)
    own_codes = jnp.stack([own_item, jnp.where(own_is_action, own_item, -2)], axis=1)
    key_codes = jnp.stack(
        [jnp.where(key_is_action, -1, key_item), jnp.where(key_is_action, key_item, -1)], axis=0
    )
    own_cos, own_sin = angle_tables(own_place)

    share = mixture[0].astype(f32) / 32.0
    row_share = jnp.where(own_item == 1, share[1], share[0])[:, None]
    cotangent_a = pad_action(action_cotangent[0])
    prefix_seed = prefix_cotangent[0].astype(f32) * row_share[:PREF]
    action_seed = cotangent_a.astype(f32) * row_share[PREF:]
    seed_block = block_of(prefix_seed.astype(bf16), action_seed.astype(bf16))

    near = gather_direct(pack, mp, mp_swap)
    last_row = near[:, :, pack.shape[1] - 256 : pack.shape[1] - 48].reshape(8, 1, wide)
    near_d = jnp.concatenate([near[:, :, :wide], last_row], axis=1).reshape(72, wide)
    near_a = near[:, :, wide : pack.shape[1] - 256].reshape(64, -1)
    edge = near_a[:, 2688 + 1024 :]
    kv_a = widen(jnp.concatenate([near_a[:, :640], edge], axis=1), 1024)
    pack_a = join(near_a[:, 640:1664], near_a[:, 1664:2688], kv_a)
    pack_b = join(near_d[:, 640:], near_a[:, 2688 : 2688 + 1024], widen(near_d[:, :640], 1024))
    arrived = {}

    def note(name):
        def during(stage, blocks, sends):
            arrived[name, stage] = blocks
            arrived[name, "sends", stage] = sends
            return ()

        return during

    own_action = pad_action(action_input[0])
    own_block = block_of(prefix_input[0], own_action)
    own_block = fence(own_block, near)
    x_rows = relay_gather(own_block, HALF_A, mp_swap)
    hold = {2: x_rows[1:4], 3: x_rows[4:7]}
    mine = relay_gather(join(pack_a, pack_b), pack_a.shape[0], yz_swap, note("weights"), hold)
    theirs = [core_swap(x) for x in mine]
    cuts = (
        (0, 0, 8, 0, 1024),
        (0, 8, 8, 0, 1024),
        (0, 16, 8, 0, 512),
        (0, 16, 8, 512, 128),
        (0, 16, 8, 640, 128),
        (1, 0, 9, 0, 1024),
        (1, 9, 8, 0, 1024),
        (1, 17, 9, 0, 512),
        (1, 17, 9, 512, 128),
    )
    wq_a, wo_a, wkv_a, gains_a, wo_e, wq_d, wo_m, wkv_d, gains_d = assemble(
        mine, theirs, pack_a.shape[0], cuts, yz, core
    )
    seeds = relay_gather(
        seed_block,
        HALF_A,
        mp_swap,
        note("seeds"),
        {1: arrived["weights", "sends", 3][:1]},
    )

    normed_d, normed_a, keys, values = keys_of(
        x_rows,
        gains_d,
        gains_a,
        wkv_d,
        wkv_a,
        key_cos,
        key_sin,
        arrived["seeds", "sends", 2],
    )
    x_d, x_a = prefix_input[0].astype(f32), own_action.astype(f32)
    rms_d, rms_a = inverse_rms(x_d), inverse_rms(x_a)
    queries, context, tops, totals, hidden_d, hidden_a, second_block = attend(
        normed_d,
        normed_a,
        prefix_input[0],
        own_action,
        wq_d,
        wq_a,
        wo_m,
        wo_e,
        wo_a,
        gains_d,
        gains_a,
        own_cos,
        own_sin,
        own_codes,
        key_codes,
        keys,
        values,
        after=arrived["seeds", "sends", 3],
    )

    slots = action_gate.shape[2]
    cut_pair = lax.dynamic_slice_in_dim(cut_points, mp, 2)
    valid = (jnp.arange(slots, dtype=jnp.int32) < cut_pair[1] - cut_pair[0]).astype(f32)[None, :]
    weights = (prefix_gate.T, prefix_up.T, prefix_down)
    weights += (action_gate[0], action_up[0], action_down[0], valid)
    kept = None
    results = {}

    def run(arrays, first, blocks, base, after):
        nonlocal kept
        where = where_parts(first, len(arrays), (HALF_A, HALF_B))
        layout = tuple((where[k, 0], where[k, 1]) for k in blocks)
        some = seeds[first : first + len(arrays)]
        done, kept = feed(arrays, some, weights, layout, base, kept, after)
        results.update(zip(blocks, done))
        return (done[0][0],)

    def feed_during(stage, arrays, sends):
        if stage == 3:
            return ()
        first, blocks, base = {1: (0, (0,), 3), 2: (1, (1, 3, 4), 0)}[stage]
        return run(arrays, first, blocks, base, sends)

    second_block = fence(second_block, seeds[8])
    arrays = relay_gather(second_block, HALF_A, mp_swap, feed_during)
    run(arrays[4:], 4, (2, 5, 7, 6), 4, ())
    product_d, deltas_d, rows_d, seeds_d, product_a, deltas_a, rows_a, seeds_a = kept

    grads = (
        t_dot(deltas_d, rows_d),
        t_dot(product_d, seeds_d),
        t_dot(rows_a, deltas_a),
        t_dot(product_a, seeds_a),
    )
    hidden = prefix_down.shape[0]
    grads = tuple(g.astype(bf16) for g in grads)
    after_grads = tuple(grads)
    grads = tuple(lax.psum(g, "dp") for g in grads)
    finished = (
        grads[0][:hidden].astype(f32),
        grads[0][HIDDEN_PAD : HIDDEN_PAD + hidden].astype(f32),
        grads[1][:hidden].astype(f32),
        grads[2][:, :slots].astype(f32),
        grads[2][:, slots:].astype(f32),
        grads[3].astype(f32),
    )

    pa = {k: v[0] for k, v in results.items()}
    pb = {k: v[1] for k, v in results.items()}
    delta_pieces = relay_scatter(pa, pb, mp_swap)
    (hidden_delta_d, hidden_delta_a, low, terms_d, terms_a, query_delta), pa, pb = attend_back(
        *delta_pieces,
        hidden_d,
        hidden_a,
        prefix_cotangent[0],
        cotangent_a,
        row_share,
        gains_d,
        gains_a,
        wo_m,
        wo_e,
        wo_a,
        queries,
        tops,
        totals,
        own_cos,
        own_sin,
        own_codes,
        key_codes,
        keys,
        values,
    )
    low_d, low_a = low[:PREF], low[PREF:, :DA]

    kv_near = [join(pa[k], pb[k], pa[k ^ 4], pb[k ^ 4]) for k in range(4)]
    kv_part = kv_near[0].astype(f32)
    for k in (1, 3, 2):
        kv_part = kv_part + mp_swap(kv_near[k], k).astype(f32)
    pair = lambda table: join(
        own_cos if table is key_cos else own_sin,
        table[ROW_PAIR : ROW_PAIR + PREF],
        table[len(PARTS) * HALF_A + ACT_PAIR : len(PARTS) * HALF_A + ACT_PAIR + ACT_PAD],
    )
    kv_turned = jnp.concatenate(
        [unrotate(kv_part[:, :HD], pair(key_cos), pair(key_sin)), kv_part[:, HD:]], axis=1
    )
    kv_turned_low = kv_turned.astype(bf16)
    kv_rows_d = join(kv_turned_low[:PREF], kv_turned_low[BLOCK : BLOCK + PREF])
    kv_rows_a = join(kv_turned_low[PREF:BLOCK], kv_turned_low[BLOCK + PREF :])

    order_d, order_a = order_matrix(D, 9), order_matrix(DA, 8)
    turned_d = dot(normed_d, order_d).astype(bf16)
    turned_a = dot(normed_a, order_a).astype(bf16)
    turned_context = dot(context, order_a).astype(bf16)
    second_term_d = t_dot(dot(terms_d, order_d).astype(bf16), jnp.ones((PREF, 256), bf16))
    second_term_a = t_dot(dot(terms_a, order_a).astype(bf16), jnp.ones((ACT_PAD, 128), bf16))
    out_grad_d = t_dot(turned_context[:PREF], low_d).astype(bf16)
    out_grad_a = t_dot(turned_context[PREF:], low_a).astype(bf16)
    q_grad_d = t_dot(turned_d[:PREF], query_delta[:PREF]).astype(bf16)
    q_grad_a = t_dot(turned_a[:ACT_PAD], query_delta[PREF:]).astype(bf16)
    place = jnp.stack([mp, core])
    cuts = (
        (0, 8, 0, 0, 1024),
        (8, 8, 0, 0, 1024),
        (16, 9, 0, 0, 1024),
        (25, 8, 0, 0, 1024),
    )
    qo_sent, kv_sent, kv_got = [], [], []
    qo_grads = (q_grad_a, out_grad_a, q_grad_d, out_grad_d)
    qo = sum_weights(qo_grads, cuts, 1024, place, qo_sent, [], (), grads[:1])
    kv_grad_d = t_dot(turned_d, kv_rows_d).astype(bf16)
    kv_grad_a = t_dot(turned_a, kv_rows_a).astype(bf16)
    cuts = (
        (0, 8, 0, 0, 512),
        (0, 8, 0, 512, 128),
        (0, 8, 1024, 640, 128),
        (8, 9, 0, 0, 512),
        (8, 9, 0, 512, 256),
    )
    kv_grads = (
        kv_grad_a,
        second_term_a.astype(bf16),
        out_grad_d,
        kv_grad_d,
        second_term_d.astype(bf16),
    )
    kv = sum_weights(kv_grads, cuts, 768, place, kv_sent, kv_got, qo_sent, grads[:1])
    kv_a, kv_d = kv[:64], kv[64:, :640]
    qo_a, qo_b = qo[:128], qo[128:]
    kv_other = mp_swap(held(kv_part[BLOCK:].astype(bf16), tuple(kv_sent)), 4)
    kv_sum = kv_part[:BLOCK] + kv_other.astype(f32)
    kv_raw_delta = jnp.concatenate(
        [unrotate(kv_sum[:, :HD], own_cos, own_sin), kv_sum[:, HD:]], axis=1
    ).astype(bf16)

    product_d = fence(product_d, kv_sent[0])
    partial_d = dot(product_d[:, :hidden], prefix_down).astype(bf16)
    partial_a = dot(product_a, action_down[0]).astype(bf16)
    out = []
    for k in range(8):
        i = (1, 3, 4, 0, 2, 5, 7, 6).index(k)
        mine = partial_a[i * ACT_PAD : (i + 1) * ACT_PAD]
        out.append(block_of(partial_d[i * PREF : (i + 1) * PREF], mine))
    out = ring_scatter(out, mp_swap, {1: tuple(kv_got)})
    prefix_output = (hidden_d + out[:PREF]).astype(bf16)[None]
    action_output = (hidden_a + out[PREF:, :DA])[:ACT].astype(bf16)[None]

    last_d = jnp.concatenate([kv_d, qo_b[:72]], axis=1).reshape(8, 9, wide)
    last_a = jnp.concatenate(
        [kv_a[:, :640], qo_a[:64], qo_a[64:], qo_b[72:], kv_a[:, 640:]], axis=1
    ).reshape(8, 8, -1)
    last = jnp.concatenate(
        [
            last_d[:, :8],
            last_a,
            jnp.pad(last_d[:, 8:].reshape(8, 8, wide // 8), ((0, 0), (0, 0), (0, 48))),
        ],
        axis=2,
    )
    last = scatter_direct(fence(last, *finished), yz, yz_swap)
    ninth = last[:, last.shape[1] - 256 : last.shape[1] - 48].reshape(1, wide)
    grads_d = join(last[:, :wide], ninth)
    grads_a = last[:, wide : last.shape[1] - 256]

    def split_grads(grads, query, key, value, gain):
        key_grad = grads[:, :256]
        value_grad = grads[:, 256:512]
        second = grads[:, 512]
        query_grad = grads[:, 640:1664]
        first = (
            jnp.sum(query_grad * query.astype(f32), axis=1)
            + jnp.sum(key_grad * key.astype(f32), axis=1)
            + jnp.sum(value_grad * value.astype(f32), axis=1)
        ) / gain.astype(f32)
        return query_grad, key_grad, value_grad, first, second

    gd = split_grads(grads_d, prefix_query, prefix_key, prefix_value, prefix_first_gain)
    ga = split_grads(grads_a, action_query, action_key, action_value, action_first_gain)
    action_out_grad = grads_a[:, 1664:2688]
    prefix_out_grad = grads_a[:, 2688:]

    first_delta_d = dot_t(query_delta[:PREF], wq_d) + dot_t(kv_raw_delta[:PREF], wkv_d)
    first_delta_a = dot_t(query_delta[PREF:], wq_a) + dot_t(kv_raw_delta[PREF:], wkv_a)
    first_gain_d, first_gain_a = gain_rows(gains_d)[0], gain_rows(gains_a)[0]
    input_d = hidden_delta_d + normalize_back(x_d, rms_d, first_gain_d, first_delta_d)
    input_a = hidden_delta_a + normalize_back(x_a, rms_a, first_gain_a, first_delta_a)

    return (
        prefix_output,
        action_output,
        input_d.astype(bf16)[None],
        input_a[:ACT].astype(bf16)[None],
        gd[0],
        gd[1],
        gd[2],
        prefix_out_grad,
        gd[3],
        gd[4],
        ga[0],
        ga[1],
        ga[2],
        action_out_grad,
        ga[3],
        ga[4],
        finished[0].T,
        finished[1].T,
        finished[2],
        finished[3][None],
        finished[4][None],
        finished[5][None],
    )


def solution(mesh):
    rows = P("dp", "mp", None)
    both = P(("dp", "mp"), None)
    vector = P(("dp", "mp"))
    slots = P("mp", None, None)
    return jax.shard_map(
        on_device,
        mesh=mesh,
        in_specs=(rows,) * 4
        + (P("dp", None), P("dp", None), P())
        + (both,) * 4
        + (vector,) * 2
        + (both,) * 4
        + (vector,) * 2
        + (P(None, "mp"), P(None, "mp"), P("mp", None))
        + (slots,) * 3,
        out_specs=(rows,) * 4
        + (both,) * 4
        + (vector,) * 2
        + (both,) * 4
        + (vector,) * 2
        + (P(None, "mp"), P(None, "mp"), P("mp", None))
        + (slots,) * 3,
        check_vma=False,
    )
```

```python
import functools

import jax
import jax.numpy as jnp
import numpy as np
from jax import lax
from jax.experimental import pallas as pl
from jax.experimental.pallas import tpu as pltpu
from jax.sharding import PartitionSpec as P

ACT_LEN = 48
EPSILON = 1e-06
ROPE_BASE = 10000.0
HEADS = 4
HD = 256
PREF = 192
ACT = 12
ACT_PAD = 16
BLOCK = PREF + ACT_PAD
N_MP = 8
HALF_A = 96
HALF_B = BLOCK - HALF_A
HIDDEN_PAD = 896
VMEM_FEED = 50
bf16 = jnp.bfloat16
f32 = jnp.float32
ANY = pl.BlockSpec(memory_space=pl.ANY)
SMEM = pl.BlockSpec(memory_space=pltpu.SMEM)
VMEM = pl.BlockSpec(memory_space=pltpu.VMEM)
ARRIVALS = (
    ((0, 0), (0, 1)),
    ((1, 0), (1, 1)),
    ((3, 0), (3, 1)),
    ((4, 0), (4, 1)),
    ((5, 0), (7, 0)),
    ((2, 0), (5, 1)),
    ((2, 1), (7, 1)),
    ((6, 0),),
    ((6, 1),),
)
PARTS = tuple(part for parts in ARRIVALS for part in parts)
KEY_BLOCK = np.concatenate(
    [np.full(HALF_A, k) for k, _ in PARTS] + [np.full(ACT_PAD, k) for k, h in PARTS if h]
).astype(np.int32)
KEY_ROW = np.concatenate(
    [np.arange(HALF_A) + h * HALF_A for _, h in PARTS]
    + [np.arange(PREF, BLOCK) for _, h in PARTS if h]
).astype(np.int32)


ROW_PAIR, ACT_PAIR = 3 * PREF, 3 * ACT_PAD


def mp_swap(array, step):
    return lax.ppermute(array, "mp", [(i, i ^ step) for i in range(N_MP)])


def dp_swap(array, step):
    return lax.ppermute(array, "dp", [(i, i ^ step) for i in range(16)])


def yz_swap(array, step):
    return dp_swap(array, (step >> 2) * 8 + (step & 3) * 2)


def core_swap(array):
    return dp_swap(array, 1)


def where_parts(first, arrays, sizes):
    where = {}
    for i in range(arrays):
        at = 0
        for k, h in ARRIVALS[first + i]:
            where[k, h] = (i, at)
            at += sizes[h]
    return where


def fence_kernel(*refs):
    pass


def fence(array, *after):
    return pl.pallas_call(
        fence_kernel,
        in_specs=[pl.BlockSpec(memory_space=pl.ANY)] * (1 + len(after)),
        out_specs=pl.BlockSpec(memory_space=pl.ANY),
        out_shape=jax.ShapeDtypeStruct(array.shape, array.dtype),
        input_output_aliases={0: 0},
        cost_estimate=pl.CostEstimate(flops=0, bytes_accessed=0, transcendentals=0),
        name="fence",
    )(array, *after)


def join(*parts):
    return jnp.concatenate(parts, axis=0)


def add_low(*parts):
    total = parts[0].astype(f32)
    for part in parts[1:]:
        total = total + part.astype(f32)
    return total.astype(bf16)


def held(array, after):
    return fence(array, *after) if after else array


def sends_kernel(count, layout, *refs):
    for out, parts in zip(refs[len(refs) - len(layout) :], layout):
        at = 0
        for which, first, n in parts:
            out[at : at + n] = refs[which][first : first + n]
            at += n


def make_sends(arrays, layout, after=()):
    width = arrays[0].shape[1]
    low = lambda parts: jax.ShapeDtypeStruct((sum(n for _, _, n in parts), width), arrays[0].dtype)
    return pl.pallas_call(
        functools.partial(sends_kernel, len(arrays), layout),
        in_specs=[VMEM] * len(arrays) + [ANY] * len(after),
        out_specs=[VMEM] * len(layout),
        out_shape=[low(parts) for parts in layout],
        compiler_params=pltpu.CompilerParams(vmem_limit_bytes=16 * 1024 * 1024),
        cost_estimate=pl.CostEstimate(flops=0, bytes_accessed=0, transcendentals=0),
        name="sends",
    )(*arrays, *after)


def relay_gather(own, na, swap, during=None, hold=None):
    nb = own.shape[0] - na
    during = during or (lambda stage, arrived, sends: ())
    hold = hold or {}
    own = held(own, hold.get(1, ()))
    s1, s3, s4 = swap(own, 1), swap(own, 3), swap(own, 4)
    after = during(1, (own,), (own,)) + hold.get(2, ())
    layout = (
        ((0, 0, na), (1, 0, na)),
        ((1, 0, na), (2, na, nb)),
        ((0, na, nb), (2, na, nb)),
    )
    sends = make_sends((s1, s3, s4), layout, after)
    zz, v1, v3 = swap(sends[0], 4), swap(sends[1], 1), swap(sends[2], 3)
    after = during(2, (s1, s3, s4), tuple(sends)) + hold.get(3, ())
    sends = make_sends((zz, v1), (((0, na, na),), ((1, na, nb),)), after)
    z2a, z2b = swap(sends[0], 1), swap(sends[1], 3)
    during(3, (zz, v1, v3), tuple(sends))
    return own, s1, s3, s4, zz, v1, v3, z2a, z2b


def relay_scatter(pa, pb, swap, hold=None, sent=None):
    na, nb = pa[0].shape[0], pb[0].shape[0]
    hold = hold or {}
    sent = {} if sent is None else sent
    get = lambda stage: hold[stage]() if stage in hold else ()
    after = get(1)
    sent[1] = (held(pa[6], after), held(pb[6], after))
    r1, r3 = swap(sent[1][0], 1), swap(sent[1][1], 3)
    p7a = add_low(pa[7], r1)
    p5b = add_low(pb[5], r3)
    after = get(2)
    sends = (join(pa[5], p7a), join(pa[2], p5b), join(pb[2], pb[7]))
    sent[2] = tuple(held(x, after) for x in sends)
    zz, v1, v3 = swap(sent[2][0], 4), swap(sent[2][1], 1), swap(sent[2][2], 3)
    p1 = join(add_low(pa[1], zz[:na]), add_low(pb[1], v3[:nb]))
    p3 = join(add_low(pa[3], zz[na:], v1[:na]), pb[3])
    p4 = join(pa[4], add_low(pb[4], v1[na:], v3[nb:]))
    after = get(3)
    sent[3] = tuple(held(x, after) for x in (p1, p3, p4))
    s1, s3, s4 = swap(sent[3][0], 1), swap(sent[3][1], 3), swap(sent[3][2], 4)
    return pa[0], pb[0], s1, s3, s4


def total_of(pieces):
    pa, pb, s1, s3, s4 = pieces
    na = pa.shape[0]
    total_a = pa.astype(f32) + s1[:na].astype(f32) + s3[:na].astype(f32) + s4[:na].astype(f32)
    total_b = pb.astype(f32) + s1[na:].astype(f32) + s3[na:].astype(f32) + s4[na:].astype(f32)
    return total_a, total_b


def ring_scatter(pieces, swap, after, sent):
    near = [join(pieces[j], pieces[j ^ 4]) for j in range(4)]
    near[1:] = [held(x, after) for x in near[1:]]
    sent += near[1:]
    total = near[0].astype(f32)
    for j in (1, 3, 2):
        total = total + swap(near[j], j).astype(f32)
    return total


def pair_sum(total, swap, after=()):
    half = total.shape[0] // 2
    return total[:half] + swap(held(total[half:].astype(bf16), after), 4).astype(f32)


def gather_direct(array, index, swap):
    pair = index & 4
    high = (index >> 2) & 1
    two = jnp.zeros((2,) + array.shape, array.dtype)
    two = lax.dynamic_update_index_in_dim(two, array, high, 0)
    two = lax.dynamic_update_index_in_dim(two, swap(array, 4), 1 - high, 0)
    ring = index & 3
    out = jnp.zeros((2, 4) + array.shape, array.dtype)
    out = lax.dynamic_update_index_in_dim(out, two, ring, 1)
    for step in (1, 3, 2):
        out = lax.dynamic_update_index_in_dim(out, swap(two, step), ring ^ step, 1)
    return out.reshape((8,) + array.shape)


def scatter_direct(pieces, index, swap):
    high = (index >> 2) & 1
    ring = index & 3
    quads = pieces.reshape((2, 4) + pieces.shape[1:])
    total = lax.dynamic_index_in_dim(quads, ring, 1, keepdims=False).astype(f32)
    for step in (1, 3, 2):
        piece = lax.dynamic_index_in_dim(quads, ring ^ step, 1, keepdims=False)
        total = total + swap(piece, step).astype(f32)
    mine = lax.dynamic_index_in_dim(total, high, 0, keepdims=False)
    theirs = lax.dynamic_index_in_dim(total, 1 - high, 0, keepdims=False)
    return mine + swap(theirs.astype(bf16), 4).astype(f32)


def place_kernel(cuts, sizes, index_ref, *refs):
    arrays, outs = refs[:9], refs[len(refs) - len(cuts) :]
    for (k, h), (i, at) in where_parts(0, 9, sizes).items():
        for out, (which, first, n, width) in zip(outs, cuts):
            if which == h:
                rows = slice(at + first, at + first + n)
                out[index_ref[0] ^ k] = arrays[i][rows, :, :width]


def place(arrays, na, cuts, index, after):
    rows, columns = arrays[0].shape
    eights = [x.reshape(x.shape[0] // 8, 8, columns) for x in arrays]
    sizes = (na // 8, (rows - na) // 8)
    return pl.pallas_call(
        functools.partial(place_kernel, cuts, sizes),
        in_specs=[SMEM] + [VMEM] * 9 + [ANY] * len(after),
        out_specs=[VMEM] * len(cuts),
        out_shape=[jax.ShapeDtypeStruct((8, n, 8, width), bf16) for _, _, n, width in cuts],
        compiler_params=pltpu.CompilerParams(vmem_limit_bytes=24 * 1024 * 1024),
        name="place",
    )(index.reshape(1), *eights, *after)


def interleave_kernel(cuts, core_ref, *refs):
    count = (len(refs) - len(cuts)) // 2
    mine, theirs, outs = refs[:count], refs[count : 2 * count], refs[2 * count :]
    core = core_ref[0]
    for out, (which, first, n, column, width) in zip(outs, cuts):
        columns = slice(column, column + width)
        for i in range(8):
            out[i, core] = mine[which][i, first : first + n, :, columns]
            out[i, 1 - core] = theirs[which][i, first : first + n, :, columns]


def interleave(mine, theirs, cuts, core):
    outs = pl.pallas_call(
        functools.partial(interleave_kernel, cuts),
        in_specs=[SMEM] + [VMEM] * (2 * len(mine)),
        out_specs=[VMEM] * len(cuts),
        out_shape=[jax.ShapeDtypeStruct((8, 2, n, 8, width), bf16) for _, _, n, _, width in cuts],
        compiler_params=pltpu.CompilerParams(vmem_limit_bytes=40 * 1024 * 1024),
        name="interleave",
    )(core.reshape(1), *mine, *theirs)
    return [x.reshape(-1, x.shape[-1]) for x in outs]


def gain_rows(block):
    pick = lax.broadcasted_iota(jnp.int32, (ACT_PAD, 128), 0)
    pick = (pick == lax.broadcasted_iota(jnp.int32, (ACT_PAD, 128), 1)).astype(bf16)
    turned = dot_t(pick, block)
    return turned[0:1], turned[1:2]


def keys_kernel(*refs):
    rows, (gain_d, gain_a, weight_d, weight_a, cosine, sine) = refs[:9], refs[9:15]
    normed_d, normed_a, keys, values = refs[-4:]
    gain_d, gain_a = gain_rows(gain_d[...])[0], gain_rows(gain_a[...])[0]
    width = weight_a.shape[0]
    prefix, action = [], []
    for i, parts in enumerate(ARRIVALS):
        at = 0
        for _, h in parts:
            prefix.append(rows[i][at : at + HALF_A])
            at += HALF_A
            if h:
                action.append(rows[i][at : at + ACT_PAD, :width])
                at += ACT_PAD
    x = join(*prefix).astype(f32)
    low_d = (x * inverse_rms(x) * gain_d).astype(bf16)
    x = join(*action).astype(f32)
    low_a = (x * inverse_rms(x) * gain_a).astype(bf16)
    normed_d[:PREF] = low_d[:PREF]
    normed_a[:ACT_PAD] = low_a[:ACT_PAD]
    normed_d[PREF:] = low_d[ROW_PAIR : ROW_PAIR + PREF]
    normed_a[ACT_PAD:] = low_a[ACT_PAIR : ACT_PAIR + ACT_PAD]
    raw = join(dot(low_d, weight_d[...]), dot(low_a, weight_a[...]))
    keys[...] = rotate(raw[:, :HD], cosine[...], sine[...]).astype(bf16)
    values[...] = raw[:, HD:].astype(bf16)


def keys_of(rows, gain_d, gain_a, weight_d, weight_a, cosine, sine, after):
    width_d, width_a = gain_d.shape[0], gain_a.shape[0]
    count = cosine.shape[0]
    shape = lambda *dims: jax.ShapeDtypeStruct(dims, bf16)
    given = [*rows, gain_d, gain_a, weight_d, weight_a, cosine, sine]
    return pl.pallas_call(
        keys_kernel,
        in_specs=[VMEM] * len(given) + [ANY] * len(after),
        out_specs=[VMEM] * 4,
        out_shape=[
            shape(2 * PREF, width_d),
            shape(2 * ACT_PAD, width_a),
            shape(count, HD),
            shape(count, HD),
        ],
        compiler_params=pltpu.CompilerParams(vmem_limit_bytes=48 * 1024 * 1024),
        cost_estimate=pl.CostEstimate(
            flops=4 * count * width_d * HD, bytes_accessed=8 * 1024 * 1024, transcendentals=count
        ),
        name="keys_of",
    )(*given, *after)


def gelu_parts(gate):
    c0 = 0.7978845608028654
    c1 = 0.044715
    square = gate * gate
    tanh = jnp.tanh(c0 * gate * (1.0 + c1 * square))
    half = 0.5 * (1.0 + tanh)
    slope = half + 0.5 * gate * (1.0 - tanh * tanh) * c0 * (1.0 + 3.0 * c1 * square)
    return gate * half, slope


def feed_block(rows, seed, gate_weight, up_weight, down_weight, valid):
    into, out_of = (dot_t, dot) if valid is None else (dot, dot_t)
    gate = into(rows, gate_weight)
    up = into(rows, up_weight)
    active, slope = gelu_parts(gate)
    product_delta = dot_t(seed, down_weight)
    if valid is not None:
        active = active * valid
        product_delta = product_delta * valid
    product = (active * up).astype(bf16)
    gate_delta = (product_delta * up * slope).astype(bf16)
    up_delta = (product_delta * active).astype(bf16)
    rows_delta = out_of(gate_delta, gate_weight) + out_of(up_delta, up_weight)
    return product, gate_delta, up_delta, rows_delta.astype(bf16)


def feed_kernel(layout, *refs):
    arrays = 1 + max(i for parts in layout for i, _ in parts)
    rows_refs, seed_refs, refs = refs[:arrays], refs[arrays : 2 * arrays], refs[2 * arrays :]
    gate_ref, up_ref, down_ref = refs[:3]
    action_gate_ref, action_up_ref, action_down_ref, valid_ref = refs[3:7]
    count = len(layout)
    outs = refs[-(2 * count + 8) :]
    products, deltas, kept_rows, kept_seeds = outs[:4]
    action_products, action_deltas, action_rows, action_seeds = outs[4:8]
    width = action_gate_ref.shape[0]
    rest = PREF - HALF_A

    def prefix_of(blocks):
        parts = []
        for (ia, a), (ib, b) in layout:
            parts += [blocks[ia][a : a + HALF_A], blocks[ib][b : b + rest]]
        return join(*parts)

    def action_of(blocks):
        parts = []
        for _, (ib, b) in layout:
            parts.append(blocks[ib][b + rest : b + HALF_B, :width])
        return join(*parts) if count > 1 else parts[0]

    rows, seed = prefix_of(rows_refs), prefix_of(seed_refs)
    product, gate_delta, up_delta, rows_delta = feed_block(
        rows, seed, gate_ref[...], up_ref[...], down_ref[...], None
    )
    hidden = product.shape[1]
    spare = jnp.zeros((count * PREF, HIDDEN_PAD - hidden), bf16)
    products[:, :hidden] = product
    products[:, hidden:] = spare
    deltas[:, :hidden] = gate_delta
    deltas[:, hidden:HIDDEN_PAD] = spare
    deltas[:, HIDDEN_PAD : HIDDEN_PAD + hidden] = up_delta
    deltas[:, HIDDEN_PAD + hidden :] = spare
    kept_rows[...] = rows
    kept_seeds[...] = seed
    rows, seed = action_of(rows_refs), action_of(seed_refs)
    product, gate_delta, up_delta, action_rows_delta = feed_block(
        rows,
        seed,
        action_gate_ref[...],
        action_up_ref[...],
        action_down_ref[...],
        valid_ref[...],
    )
    slots = gate_delta.shape[1]
    action_products[...] = product
    action_deltas[:, :slots] = gate_delta
    action_deltas[:, slots:] = up_delta
    action_rows[...] = rows
    action_seeds[...] = seed
    blank = jnp.zeros((ACT_PAD, rows_delta.shape[1] - width), bf16)
    for i in range(count):
        a, b, c = i * PREF, i * PREF + HALF_A, (i + 1) * PREF
        extra = slice(i * ACT_PAD, (i + 1) * ACT_PAD)
        ref_a, ref_b = outs[8 + 2 * i : 10 + 2 * i]
        ref_a[...] = rows_delta[a:b]
        ref_b[:rest] = rows_delta[b:c]
        ref_b[rest:, :width] = action_rows_delta[extra]
        ref_b[rest:, width:] = blank


def feed(arrays, seeds, weights, layout, base, kept, after):
    count = len(layout)
    width = arrays[0].shape[1]
    hidden = weights[0].shape[0]
    action_width, slots = weights[3].shape
    once = pl.Buffered(1)
    at = base // count

    def whole(array):
        return pl.BlockSpec(array.shape, lambda i: (0, 0), pipeline_mode=once)

    def part(size, columns):
        return (
            jax.ShapeDtypeStruct((N_MP * size, columns), bf16),
            pl.BlockSpec((count * size, columns), lambda i: (at, 0), pipeline_mode=once),
        )

    def own(size):
        return (
            jax.ShapeDtypeStruct((size, width), bf16),
            pl.BlockSpec((size, width), lambda i: (0, 0), pipeline_mode=once),
        )

    outs = [
        part(PREF, HIDDEN_PAD),
        part(PREF, 2 * HIDDEN_PAD),
        part(PREF, width),
        part(PREF, width),
        part(ACT_PAD, slots),
        part(ACT_PAD, 2 * slots),
        part(ACT_PAD, action_width),
        part(ACT_PAD, action_width),
    ] + [own(HALF_A), own(HALF_B)] * count
    reused = [] if kept is None else list(kept)
    given = [*arrays, *seeds]
    placed = len(given) + len(weights)
    results = pl.pallas_call(
        functools.partial(feed_kernel, layout),
        grid=(1,),
        in_specs=[whole(x) for x in given]
        + [VMEM] * len(weights)
        + [ANY] * (len(reused) + len(after)),
        out_shape=[shape for shape, _ in outs],
        out_specs=[spec for _, spec in outs],
        input_output_aliases={placed + i: i for i in range(len(reused))},
        compiler_params=pltpu.CompilerParams(
            dimension_semantics=("arbitrary",), vmem_limit_bytes=VMEM_FEED * 1024 * 1024
        ),
        cost_estimate=pl.CostEstimate(
            flops=10 * count * (PREF * width * hidden + ACT_PAD * action_width * slots),
            bytes_accessed=6 * (width * hidden + action_width * slots),
            transcendentals=count * PREF * hidden,
        ),
        name="feed",
    )(*given, *weights, *reused, *after)
    blocks = [results[8 + 2 * i : 10 + 2 * i] for i in range(count)]
    return blocks, results[:8]


def see(own_ref, key_ref):
    own, key = own_ref[...], key_ref[...]
    return (own[:, 0:1] == key[0:1]) | (own[:, 1:2] == key[1:2])


def attend_kernel(*refs):
    (normed_d, normed_a, x_d, x_a, wq_d, wq_a, wo_m, wo_e, wo_a) = refs[:9]
    (gain_d, gain_a, cosine, sine, own_codes, key_codes) = refs[9:15]
    keys, values = refs[15][...], refs[16][...]
    (queries, context, tops, totals, hidden_d, hidden_a, block) = refs[-7:]
    gain_d, gain_a = gain_rows(gain_d[...])[1], gain_rows(gain_a[...])[1]
    raw = join(dot(normed_d[:PREF], wq_d[...]), dot(normed_a[:ACT_PAD], wq_a[...]))
    visible = see(own_codes, key_codes)
    cos, sin = cosine[...], sine[...]
    heads = []
    for h in range(HEADS):
        rows = slice(h * BLOCK, (h + 1) * BLOCK)
        query = (rotate(raw[:, h * HD : (h + 1) * HD], cos, sin) * HD**-0.5).astype(bf16)
        queries[rows] = query
        scores = jnp.where(visible, dot_t(query, keys), -1e30)
        top = jnp.max(scores, axis=1, keepdims=True)
        shifted = jnp.exp(scores - top)
        total = jnp.sum(shifted, axis=1, keepdims=True)
        tops[rows] = top
        totals[rows] = total
        heads.append(dot((shifted / total).astype(bf16), values).astype(bf16))
    mixed = jnp.concatenate(heads, axis=1)
    context[...] = mixed
    main, width_d, width_a = wo_m.shape[1], x_d.shape[1], x_a.shape[1]
    low_d, low_a = mixed[:PREF], mixed[PREF:]
    state = x_d[...].astype(f32) + jnp.concatenate(
        [dot(low_d, wo_m[...]), dot(low_d, wo_e[...])], axis=1
    )
    hidden_d[...] = state
    second_d = (state * inverse_rms(state) * gain_d).astype(bf16)
    real = lax.broadcasted_iota(jnp.int32, (ACT_PAD, width_a), 0) < ACT
    state = jnp.where(real, x_a[...].astype(f32) + dot(low_a, wo_a[...]), 0.0)
    hidden_a[...] = state
    second_a = (state * inverse_rms(state) * gain_a).astype(bf16)
    block[:PREF] = second_d
    block[PREF:, :width_a] = second_a
    block[PREF:, width_a:] = jnp.zeros((ACT_PAD, width_d - width_a), bf16)


def attend(*given, after):
    x_d, x_a = given[2:4]
    width_d, width_a = x_d.shape[1], x_a.shape[1]
    shape = jax.ShapeDtypeStruct
    stacked = HEADS * BLOCK
    return pl.pallas_call(
        attend_kernel,
        in_specs=[VMEM] * len(given) + [ANY] * len(after),
        out_specs=[VMEM] * 7,
        out_shape=[
            shape((stacked, HD), bf16),
            shape((BLOCK, HEADS * HD), bf16),
            shape((stacked, 1), f32),
            shape((stacked, 1), f32),
            shape((PREF, width_d), f32),
            shape((ACT_PAD, width_a), f32),
            shape((BLOCK, width_d), bf16),
        ],
        compiler_params=pltpu.CompilerParams(vmem_limit_bytes=50 * 1024 * 1024),
        cost_estimate=pl.CostEstimate(
            flops=4 * BLOCK * HEADS * HD * (N_MP * BLOCK + width_d),
            bytes_accessed=4 * 1024 * 1024 * 5,
            transcendentals=stacked * N_MP * BLOCK,
        ),
        name="attend",
    )(*given, *after)


def attend_back_kernel(*refs):
    pieces = refs[:5]
    (hidden_d, hidden_a, cotangent_d, cotangent_a, share, gain_d, gain_a) = refs[5:12]
    (wo_m, wo_e, wo_a, queries, tops, totals, cosine, sine, own_codes, key_codes) = refs[12:22]
    keys, values = refs[22][...], refs[23][...]
    outs = refs[-(6 + len(PARTS)) :]
    (hidden_delta_d, hidden_delta_a, low, terms_d, terms_a, query_delta) = outs[:6]
    kv_deltas = outs[6:]
    gain_d, gain_a = gain_rows(gain_d[...])[1], gain_rows(gain_a[...])[1]
    delta = join(*total_of([piece[...] for piece in pieces]))
    width_d, width_a = hidden_d.shape[1], hidden_a.shape[1]
    lows = []
    for rows, state_ref, cotangent, gain, out, terms in (
        (slice(0, PREF), hidden_d, cotangent_d, gain_d, hidden_delta_d, terms_d),
        (slice(PREF, BLOCK), hidden_a, cotangent_a, gain_a, hidden_delta_a, terms_a),
    ):
        state = state_ref[...]
        change = delta[rows, : state.shape[1]]
        scale = inverse_rms(state)
        seed = cotangent[...].astype(f32) * share[rows]
        back = seed + normalize_back(state, scale, gain, change)
        out[...] = back
        terms[...] = (change * state * scale).astype(bf16)
        lows.append(back.astype(bf16))
    low_d, low_a = lows
    low[:PREF] = low_d
    low[PREF:, :width_a] = low_a
    low[PREF:, width_a:] = jnp.zeros((ACT_PAD, width_d - width_a), bf16)
    main = wo_m.shape[1]
    context_delta = join(
        dot_t(low_d[:, :main], wo_m[...]) + dot_t(low_d[:, main:], wo_e[...]),
        dot_t(low_a, wo_a[...]),
    ).astype(bf16)
    visible = see(own_codes, key_codes)
    cos, sin = cosine[...], sine[...]
    keys_delta, values_delta = None, None
    for h in range(HEADS):
        rows = slice(h * BLOCK, (h + 1) * BLOCK)
        query = queries[rows]
        change = context_delta[:, h * HD : (h + 1) * HD]
        scores = jnp.where(visible, dot_t(query, keys), -1e30)
        probs = jnp.exp(scores - tops[rows]) / totals[rows]
        probs_delta = dot_t(change, values)
        row_dot = jnp.sum(probs * probs_delta, axis=1, keepdims=True)
        score_delta = (probs * (probs_delta - row_dot)).astype(bf16)
        turned = unrotate(dot(score_delta, keys), cos, sin) * HD**-0.5
        query_delta[:, h * HD : (h + 1) * HD] = turned.astype(bf16)
        key_part = t_dot(score_delta, query)
        value_part = t_dot(probs.astype(bf16), change)
        keys_delta = key_part if h == 0 else keys_delta + key_part
        values_delta = value_part if h == 0 else values_delta + value_part
    at, extra = 0, len(PARTS) * HALF_A
    for (_, half), out in zip(PARTS, kv_deltas):
        for columns, change in ((slice(0, HD), keys_delta), (slice(HD, 2 * HD), values_delta)):
            out[:HALF_A, columns] = change[at : at + HALF_A].astype(bf16)
            if half:
                out[HALF_A:, columns] = change[extra : extra + ACT_PAD].astype(bf16)
        at += HALF_A
        extra += half * ACT_PAD


def attend_back(*given, after):
    hidden_d, hidden_a = given[5:7]
    width_d, width_a = hidden_d.shape[1], hidden_a.shape[1]
    shape = jax.ShapeDtypeStruct
    stacked = HEADS * BLOCK
    outs = pl.pallas_call(
        attend_back_kernel,
        in_specs=[VMEM] * len(given) + [ANY] * len(after),
        out_specs=[VMEM] * (6 + len(PARTS)),
        out_shape=[
            shape((PREF, width_d), f32),
            shape((ACT_PAD, width_a), f32),
            shape((BLOCK, width_d), bf16),
            shape((PREF, width_d), bf16),
            shape((ACT_PAD, width_a), bf16),
            shape((BLOCK, HEADS * HD), bf16),
        ]
        + [shape(((HALF_A, HALF_B)[half], 2 * HD), bf16) for _, half in PARTS],
        compiler_params=pltpu.CompilerParams(vmem_limit_bytes=50 * 1024 * 1024),
        cost_estimate=pl.CostEstimate(
            flops=2 * BLOCK * HEADS * HD, bytes_accessed=4 * BLOCK, transcendentals=stacked
        ),
        name="attend_back",
    )(*given, *after)
    kv_deltas = dict(zip(PARTS, outs[6:]))
    pa = {k: kv_deltas[k, 0] for k in range(8)}
    pb = {k: kv_deltas[k, 1] for k in range(8)}
    return outs[:6], pa, pb


def theirs_kernel(cuts, place_ref, *refs):
    out = refs[-1]
    core = place_ref[1]
    for ref, (row, n, source, column, width) in zip(refs, cuts):
        out[:, row : row + n, :, column : column + width] = ref[
            1 - core, :, :, :, source : source + width
        ]


def near_kernel(cuts, place_ref, *refs):
    got, outs = refs[len(cuts)], refs[-4:]
    mp, core = place_ref[0], place_ref[1]
    for step, out in zip((0, 1, 3, 2), outs):
        for pair in range(2):
            block = mp ^ step ^ (4 * pair)
            base = pair * got.shape[1]
            for ref, (row, n, source, column, width) in zip(refs, cuts):
                columns = slice(column, column + width)
                mine = ref[core, block, :, :, source : source + width].astype(f32)
                total = mine + got[block, row : row + n, :, columns].astype(f32)
                out[base + row : base + row + n, :, columns] = total.astype(bf16)


def sum_weights(grads, cuts, columns, place, sent, after):
    views = [g.reshape(2, 8, -1, 8, g.shape[1]) for g in grads]
    eights = max(row + n for row, n, _, _, _ in cuts)
    params = pltpu.CompilerParams(vmem_limit_bytes=44 * 1024 * 1024)
    cost = pl.CostEstimate(flops=0, bytes_accessed=0, transcendentals=0)
    low = lambda *dims: jax.ShapeDtypeStruct(dims, bf16)
    theirs = pl.pallas_call(
        functools.partial(theirs_kernel, cuts),
        in_specs=[SMEM] + [VMEM] * len(views),
        out_specs=VMEM,
        out_shape=low(8, eights, 8, columns),
        compiler_params=params,
        cost_estimate=cost,
        name="theirs",
    )(place, *views)
    near = pl.pallas_call(
        functools.partial(near_kernel, cuts),
        in_specs=[SMEM] + [VMEM] * (len(views) + 1) + [ANY] * len(after),
        out_specs=[VMEM] * 4,
        out_shape=[low(2 * eights, 8, columns)] * 4,
        compiler_params=params,
        cost_estimate=cost,
        name="near",
    )(place, *views, core_swap(theirs), *after)
    near = [x.reshape(16 * eights, columns) for x in near]
    sent += near[1:]
    total = near[0].astype(f32)
    for step, x in zip((1, 3, 2), near[1:]):
        total = total + mp_swap(x, step).astype(f32)
    half = 8 * eights
    return (total[:half] + mp_swap(total[half:].astype(bf16), 4).astype(f32)).astype(bf16)


def pad_action(rows):
    return jnp.pad(rows, ((0, ACT_PAD - ACT), (0, 0)))


def widen(rows, width):
    return jnp.pad(rows, ((0, 0), (0, width - rows.shape[1])))


def block_of(prefix_rows, action_rows):
    return join(prefix_rows, widen(action_rows, prefix_rows.shape[1]))


def order_matrix(size, rows):
    d = jnp.arange(size, dtype=jnp.int32)
    r = d % rows
    mp = (d // rows) % 8
    dp = d // (8 * rows)
    place = (dp % 2) * (size // 2) + mp * (8 * rows) + (dp // 2) * rows + r
    return (place[:, None] == jnp.arange(size, dtype=jnp.int32)[None, :]).astype(bf16)


def dot(a, b):
    return jnp.dot(a, b, preferred_element_type=f32)


def dot_t(a, b):
    return lax.dot_general(a, b, (((1,), (1,)), ((), ())), preferred_element_type=f32)


def t_dot(a, b):
    return lax.dot_general(a, b, (((0,), (0,)), ((), ())), preferred_element_type=f32)


def inverse_rms(rows):
    return lax.rsqrt(jnp.mean(rows * rows, axis=-1, keepdims=True) + EPSILON)


def normalize_back(rows, scale, gain, delta):
    a = delta * gain
    return scale * (a - rows * (scale * scale) * jnp.mean(a * rows, axis=-1, keepdims=True))


def rotate(rows, cosine, sine):
    half = HD // 2
    first, second = rows[:, :half], rows[:, half:]
    return jnp.concatenate(
        [first * cosine - second * sine, second * cosine + first * sine], axis=1
    )


def unrotate(rows, cosine, sine):
    return rotate(rows, cosine, -sine)


def angle_tables(place):
    half = HD // 2
    frequency = ROPE_BASE ** (-jnp.arange(half, dtype=f32) / half)
    angles = place.astype(f32)[:, None] * frequency[None, :]
    return jnp.cos(angles), jnp.sin(angles)


def on_device(
    prefix_input,
    action_input,
    prefix_cotangent,
    action_cotangent,
    prefix_lengths,
    mixture,
    cut_points,
    prefix_query,
    prefix_key,
    prefix_value,
    prefix_out,
    prefix_first_gain,
    prefix_second_gain,
    action_query,
    action_key,
    action_value,
    action_out,
    action_first_gain,
    action_second_gain,
    prefix_gate,
    prefix_up,
    prefix_down,
    action_gate,
    action_up,
    action_down,
):
    mp = lax.axis_index("mp")
    dp = lax.axis_index("dp")
    core = dp & 1
    yz = (dp >> 3) * 4 + ((dp >> 1) & 3)
    D = prefix_input.shape[2]
    DA = action_input.shape[2]

    def column_block(first, second):
        return jnp.pad(jnp.stack([first, second], axis=1), ((0, 0), (0, 126)))

    pack_d = jnp.concatenate(
        [
            prefix_key,
            prefix_value,
            column_block(prefix_first_gain, prefix_second_gain),
            prefix_query,
        ],
        axis=1,
    )
    wide = pack_d.shape[1]
    pack = jnp.concatenate(
        [
            pack_d[:8],
            action_key,
            action_value,
            column_block(action_first_gain, action_second_gain),
            action_query,
            action_out,
            prefix_out,
            jnp.pad(pack_d[8:].reshape(8, wide // 8), ((0, 0), (0, 48))),
        ],
        axis=1,
    )
    lengths = prefix_lengths[0]
    first_length = lengths[0]

    def tables(source, row):
        is_action = row >= PREF
        prefix_row = source * PREF + row
        prefix_item = (prefix_row >= first_length).astype(jnp.int32)
        prefix_place = prefix_row - jnp.where(prefix_item == 1, first_length, 0)
        action_row = source * ACT + row - PREF
        action_item = (action_row >= ACT_LEN).astype(jnp.int32)
        action_place = jnp.where(action_item == 1, lengths[1], first_length) + action_row % ACT_LEN
        action_item = jnp.where(row - PREF < ACT, action_item, 2)
        item = jnp.where(is_action, action_item, prefix_item)
        place = jnp.where(is_action, action_place, prefix_place)
        return item, place, is_action

    own_item, own_place, own_is_action = tables(mp, jnp.arange(BLOCK, dtype=jnp.int32))
    key_item, key_place, key_is_action = tables(jnp.asarray(KEY_BLOCK) ^ mp, jnp.asarray(KEY_ROW))
    key_cos, key_sin = angle_tables(key_place)
    own_codes = jnp.stack([own_item, jnp.where(own_is_action, own_item, -2)], axis=1)
    key_codes = jnp.stack(
        [jnp.where(key_is_action, -1, key_item), jnp.where(key_is_action, key_item, -1)], axis=0
    )
    own_cos, own_sin = angle_tables(own_place)

    share = mixture[0].astype(f32) / 32.0
    row_share = jnp.where(own_item == 1, share[1], share[0])[:, None]
    cotangent_a = pad_action(action_cotangent[0])
    prefix_seed = prefix_cotangent[0].astype(f32) * row_share[:PREF]
    action_seed = cotangent_a.astype(f32) * row_share[PREF:]
    seed_block = block_of(prefix_seed.astype(bf16), action_seed.astype(bf16))

    near = gather_direct(pack, mp, mp_swap)
    last_row = near[:, :, pack.shape[1] - 256 : pack.shape[1] - 48].reshape(8, 1, wide)
    near_d = jnp.concatenate([near[:, :, :wide], last_row], axis=1).reshape(72, wide)
    near_a = near[:, :, wide : pack.shape[1] - 256].reshape(64, -1)
    edge = near_a[:, 2688 + 1024 :]
    kv_a = widen(jnp.concatenate([near_a[:, :640], edge], axis=1), 1024)
    pack_a = join(near_a[:, 640:1664], near_a[:, 1664:2688], kv_a)
    pack_b = join(near_d[:, 640:], near_a[:, 2688 : 2688 + 1024], widen(near_d[:, :640], 1024))
    arrived = {}

    def note(name):
        def during(stage, blocks, sends):
            arrived[name, stage] = blocks
            arrived[name, "sends", stage] = sends
            return ()

        return during

    own_action = pad_action(action_input[0])
    own_block = block_of(prefix_input[0], own_action)
    pack = join(pack_a, pack_b)
    x_hold = {2: (pack,)}
    x_rows = relay_gather(own_block, HALF_A, mp_swap, note("rows"), x_hold)
    hold = {1: x_rows[1:4], 3: x_rows[4:7]}
    pieces = relay_gather(pack, pack_a.shape[0], yz_swap, note("weights"), hold)
    cuts = ((0, 16, 8, 768), (1, 17, 9, 640), (0, 0, 16, 1024), (1, 0, 17, 1024))
    mine = place(pieces, pack_a.shape[0], cuts, yz, arrived["rows", "sends", 3])
    theirs = [core_swap(x) for x in mine]
    cuts = ((0, 0, 8, 0, 512), (0, 0, 8, 512, 128), (0, 0, 8, 640, 128))
    cuts += ((1, 0, 9, 0, 512), (1, 0, 9, 512, 128))
    wkv_a, gains_a, wo_e, wkv_d, gains_d = interleave(mine[:2], theirs[:2], cuts, core)
    cuts = ((0, 0, 8, 0, 1024), (0, 8, 8, 0, 1024), (1, 0, 9, 0, 1024), (1, 9, 8, 0, 1024))
    wq_a, wo_a, wq_d, wo_m = interleave(mine[2:], theirs[2:], cuts, core)
    seeds = relay_gather(
        seed_block,
        HALF_A,
        mp_swap,
        note("seeds"),
        {1: pieces[7:9]},
    )

    normed_d, normed_a, keys, values = keys_of(
        x_rows,
        gains_d,
        gains_a,
        wkv_d,
        wkv_a,
        key_cos,
        key_sin,
        arrived["seeds", "sends", 1],
    )
    x_d, x_a = prefix_input[0].astype(f32), own_action.astype(f32)
    rms_d, rms_a = inverse_rms(x_d), inverse_rms(x_a)
    queries, context, tops, totals, hidden_d, hidden_a, second_block = attend(
        normed_d,
        normed_a,
        prefix_input[0],
        own_action,
        wq_d,
        wq_a,
        wo_m,
        wo_e,
        wo_a,
        gains_d,
        gains_a,
        own_cos,
        own_sin,
        own_codes,
        key_codes,
        keys,
        values,
        after=arrived["seeds", "sends", 2],
    )

    slots = action_gate.shape[2]
    cut_pair = lax.dynamic_slice_in_dim(cut_points, mp, 2)
    valid = (jnp.arange(slots, dtype=jnp.int32) < cut_pair[1] - cut_pair[0]).astype(f32)[None, :]
    weights = (prefix_gate.T, prefix_up.T, prefix_down)
    weights += (action_gate[0], action_up[0], action_down[0], valid)
    kept = None
    results = {}

    def run(arrays, first, blocks, base, after):
        nonlocal kept
        where = where_parts(first, len(arrays), (HALF_A, HALF_B))
        layout = tuple((where[k, 0], where[k, 1]) for k in blocks)
        some = seeds[first : first + len(arrays)]
        done, kept = feed(arrays, some, weights, layout, base, kept, after)
        results.update(zip(blocks, done))
        return (done[0][0],)

    def feed_during(stage, arrays, sends):
        if stage == 3:
            return ()
        first, blocks, base = {1: (0, (0,), 3), 2: (1, (1, 3, 4), 0)}[stage]
        return run(arrays, first, blocks, base, sends)

    second_block = fence(second_block, *arrived["seeds", "sends", 3])
    arrays = relay_gather(second_block, HALF_A, mp_swap, feed_during)
    run(arrays[4:], 4, (2, 5, 7, 6), 4, ())
    product_d, deltas_d, rows_d, seeds_d, product_a, deltas_a, rows_a, seeds_a = kept

    grads = (
        t_dot(deltas_d, rows_d),
        t_dot(product_d, seeds_d),
        t_dot(rows_a, deltas_a),
        t_dot(product_a, seeds_a),
    )
    hidden = prefix_down.shape[0]
    grads = tuple(g.astype(bf16) for g in grads)
    after_grads = tuple(grads)
    grads = tuple(lax.psum(g, "dp") for g in grads)
    finished = (
        grads[0][:hidden].astype(f32),
        grads[0][HIDDEN_PAD : HIDDEN_PAD + hidden].astype(f32),
        grads[1][:hidden].astype(f32),
        grads[2][:, :slots].astype(f32),
        grads[2][:, slots:].astype(f32),
        grads[3].astype(f32),
    )

    pa = {k: v[0] for k, v in results.items()}
    pb = {k: v[1] for k, v in results.items()}
    delta_sent = {}
    delta_pieces = relay_scatter(pa, pb, mp_swap, sent=delta_sent)

    partial_d = dot(product_d[:, :hidden], prefix_down).astype(bf16)
    partial_a = dot(product_a, action_down[0]).astype(bf16)
    out = []
    for k in range(8):
        i = (1, 3, 4, 0, 2, 5, 7, 6).index(k)
        mine = partial_a[i * ACT_PAD : (i + 1) * ACT_PAD]
        out.append(block_of(partial_d[i * PREF : (i + 1) * PREF], mine))
    out_sent = []
    out = ring_scatter(out, mp_swap, delta_sent[3], out_sent)

    (hidden_delta_d, hidden_delta_a, low, terms_d, terms_a, query_delta), pa, pb = attend_back(
        *delta_pieces,
        hidden_d,
        hidden_a,
        prefix_cotangent[0],
        cotangent_a,
        row_share,
        gains_d,
        gains_a,
        wo_m,
        wo_e,
        wo_a,
        queries,
        tops,
        totals,
        own_cos,
        own_sin,
        own_codes,
        key_codes,
        keys,
        values,
        after=(),
    )
    low_d, low_a = low[:PREF], low[PREF:, :DA]

    kv_near = [join(pa[k], pb[k], pa[k ^ 4], pb[k ^ 4]) for k in range(4)]
    kv_part = kv_near[0].astype(f32)
    for k in (1, 3, 2):
        kv_part = kv_part + mp_swap(kv_near[k], k).astype(f32)
    pair = lambda table: join(
        own_cos if table is key_cos else own_sin,
        table[ROW_PAIR : ROW_PAIR + PREF],
        table[len(PARTS) * HALF_A + ACT_PAIR : len(PARTS) * HALF_A + ACT_PAIR + ACT_PAD],
    )
    kv_turned = jnp.concatenate(
        [unrotate(kv_part[:, :HD], pair(key_cos), pair(key_sin)), kv_part[:, HD:]], axis=1
    )
    kv_turned_low = kv_turned.astype(bf16)
    kv_rows_d = join(kv_turned_low[:PREF], kv_turned_low[BLOCK : BLOCK + PREF])
    kv_rows_a = join(kv_turned_low[PREF:BLOCK], kv_turned_low[BLOCK + PREF :])

    order_d, order_a = order_matrix(D, 9), order_matrix(DA, 8)
    turned_d = dot(normed_d, order_d).astype(bf16)
    turned_a = dot(normed_a, order_a).astype(bf16)
    turned_context = dot(context, order_a).astype(bf16)
    second_term_d = t_dot(dot(terms_d, order_d).astype(bf16), jnp.ones((PREF, 256), bf16))
    second_term_a = t_dot(dot(terms_a, order_a).astype(bf16), jnp.ones((ACT_PAD, 128), bf16))
    out_grad_d = t_dot(turned_context[:PREF], low_d).astype(bf16)
    out_grad_a = t_dot(turned_context[PREF:], low_a).astype(bf16)
    q_grad_d = t_dot(turned_d[:PREF], query_delta[:PREF]).astype(bf16)
    q_grad_a = t_dot(turned_a[:ACT_PAD], query_delta[PREF:]).astype(bf16)
    here = jnp.stack([mp, core])
    cuts = (
        (0, 8, 0, 0, 1024),
        (8, 8, 0, 0, 1024),
        (16, 9, 0, 0, 1024),
        (25, 8, 0, 0, 1024),
    )
    qo_sent, kv_sent = [], []
    qo_grads = (q_grad_a, out_grad_a, q_grad_d, out_grad_d)
    qo = sum_weights(qo_grads, cuts, 1024, here, qo_sent, ())
    kv_grad_d = t_dot(turned_d, kv_rows_d).astype(bf16)
    kv_grad_a = t_dot(turned_a, kv_rows_a).astype(bf16)
    cuts = (
        (0, 8, 0, 0, 512),
        (0, 8, 0, 512, 128),
        (0, 8, 1024, 640, 128),
        (8, 9, 0, 0, 512),
        (8, 9, 0, 512, 256),
    )
    kv_grads = (
        kv_grad_a,
        second_term_a.astype(bf16),
        out_grad_d,
        kv_grad_d,
        second_term_d.astype(bf16),
    )
    kv = sum_weights(kv_grads, cuts, 768, here, kv_sent, qo_sent)
    kv_a, kv_d = kv[:64], kv[64:, :640]
    qo_a, qo_b = qo[:128], qo[128:]
    kv_other = mp_swap(held(kv_part[BLOCK:].astype(bf16), tuple(kv_sent)), 4)
    kv_sum = kv_part[:BLOCK] + kv_other.astype(f32)
    kv_raw_delta = jnp.concatenate(
        [unrotate(kv_sum[:, :HD], own_cos, own_sin), kv_sum[:, HD:]], axis=1
    ).astype(bf16)

    out = pair_sum(out, mp_swap, (*qo_sent, *kv_sent))
    prefix_output = (hidden_d + out[:PREF]).astype(bf16)[None]
    action_output = (hidden_a + out[PREF:, :DA])[:ACT].astype(bf16)[None]

    last_d = jnp.concatenate([kv_d, qo_b[:72]], axis=1).reshape(8, 9, wide)
    last_a = jnp.concatenate(
        [kv_a[:, :640], qo_a[:64], qo_a[64:], qo_b[72:], kv_a[:, 640:]], axis=1
    ).reshape(8, 8, -1)
    last = jnp.concatenate(
        [
            last_d[:, :8],
            last_a,
            jnp.pad(last_d[:, 8:].reshape(8, 8, wide // 8), ((0, 0), (0, 0), (0, 48))),
        ],
        axis=2,
    )
    last = scatter_direct(fence(last, grads[0]), yz, yz_swap)
    ninth = last[:, last.shape[1] - 256 : last.shape[1] - 48].reshape(1, wide)
    grads_d = join(last[:, :wide], ninth)
    grads_a = last[:, wide : last.shape[1] - 256]

    def split_grads(grads, query, key, value, gain):
        key_grad = grads[:, :256]
        value_grad = grads[:, 256:512]
        second = grads[:, 512]
        query_grad = grads[:, 640:1664]
        first = (
            jnp.sum(query_grad * query.astype(f32), axis=1)
            + jnp.sum(key_grad * key.astype(f32), axis=1)
            + jnp.sum(value_grad * value.astype(f32), axis=1)
        ) / gain.astype(f32)
        return query_grad, key_grad, value_grad, first, second

    gd = split_grads(grads_d, prefix_query, prefix_key, prefix_value, prefix_first_gain)
    ga = split_grads(grads_a, action_query, action_key, action_value, action_first_gain)
    action_out_grad = grads_a[:, 1664:2688]
    prefix_out_grad = grads_a[:, 2688:]

    first_delta_d = dot_t(query_delta[:PREF], wq_d) + dot_t(kv_raw_delta[:PREF], wkv_d)
    first_delta_a = dot_t(query_delta[PREF:], wq_a) + dot_t(kv_raw_delta[PREF:], wkv_a)
    first_gain_d, first_gain_a = gain_rows(gains_d)[0], gain_rows(gains_a)[0]
    input_d = hidden_delta_d + normalize_back(x_d, rms_d, first_gain_d, first_delta_d)
    input_a = hidden_delta_a + normalize_back(x_a, rms_a, first_gain_a, first_delta_a)

    return (
        prefix_output,
        action_output,
        input_d.astype(bf16)[None],
        input_a[:ACT].astype(bf16)[None],
        gd[0],
        gd[1],
        gd[2],
        prefix_out_grad,
        gd[3],
        gd[4],
        ga[0],
        ga[1],
        ga[2],
        action_out_grad,
        ga[3],
        ga[4],
        finished[0].T,
        finished[1].T,
        finished[2],
        finished[3][None],
        finished[4][None],
        finished[5][None],
    )


def solution(mesh):
    rows = P("dp", "mp", None)
    both = P(("dp", "mp"), None)
    vector = P(("dp", "mp"))
    slots = P("mp", None, None)
    return jax.shard_map(
        on_device,
        mesh=mesh,
        in_specs=(rows,) * 4
        + (P("dp", None), P("dp", None), P())
        + (both,) * 4
        + (vector,) * 2
        + (both,) * 4
        + (vector,) * 2
        + (P(None, "mp"), P(None, "mp"), P("mp", None))
        + (slots,) * 3,
        out_specs=(rows,) * 4
        + (both,) * 4
        + (vector,) * 2
        + (both,) * 4
        + (vector,) * 2
        + (P(None, "mp"), P(None, "mp"), P("mp", None))
        + (slots,) * 3,
        check_vma=False,
    )
```

```python
import functools

import jax
import jax.numpy as jnp
import numpy as np
from jax import lax
from jax.experimental import pallas as pl
from jax.experimental.pallas import tpu as pltpu
from jax.sharding import PartitionSpec as P

ACT_LEN = 48
EPSILON = 1e-06
ROPE_BASE = 10000.0
HEADS = 4
HD = 256
PREF = 192
ACT = 12
ACT_PAD = 16
BLOCK = PREF + ACT_PAD
N_MP = 8
HALF_A = 96
HALF_B = BLOCK - HALF_A
HIDDEN_PAD = 896
VMEM_FEED = 50
bf16 = jnp.bfloat16
f32 = jnp.float32
ANY = pl.BlockSpec(memory_space=pl.ANY)
SMEM = pl.BlockSpec(memory_space=pltpu.SMEM)
VMEM = pl.BlockSpec(memory_space=pltpu.VMEM)
ARRIVALS = (
    ((0, 0), (0, 1)),
    ((1, 0), (1, 1)),
    ((3, 0), (3, 1)),
    ((4, 0), (4, 1)),
    ((5, 0), (7, 0)),
    ((2, 0), (5, 1)),
    ((2, 1), (7, 1)),
    ((6, 0),),
    ((6, 1),),
)
PARTS = tuple(part for parts in ARRIVALS for part in parts)
KEY_BLOCK = np.concatenate(
    [np.full(HALF_A, k) for k, _ in PARTS] + [np.full(ACT_PAD, k) for k, h in PARTS if h]
).astype(np.int32)
KEY_ROW = np.concatenate(
    [np.arange(HALF_A) + h * HALF_A for _, h in PARTS]
    + [np.arange(PREF, BLOCK) for _, h in PARTS if h]
).astype(np.int32)


ROW_PAIR, ACT_PAIR = 3 * PREF, 3 * ACT_PAD


def mp_swap(array, step):
    return lax.ppermute(array, "mp", [(i, i ^ step) for i in range(N_MP)])


def dp_swap(array, step):
    return lax.ppermute(array, "dp", [(i, i ^ step) for i in range(16)])


def yz_swap(array, step):
    return dp_swap(array, (step >> 2) * 8 + (step & 3) * 2)


def core_swap(array):
    return dp_swap(array, 1)


def where_parts(first, arrays, sizes):
    where = {}
    for i in range(arrays):
        at = 0
        for k, h in ARRIVALS[first + i]:
            where[k, h] = (i, at)
            at += sizes[h]
    return where


def fence_kernel(*refs):
    pass


def fence(array, *after):
    return pl.pallas_call(
        fence_kernel,
        in_specs=[pl.BlockSpec(memory_space=pl.ANY)] * (1 + len(after)),
        out_specs=pl.BlockSpec(memory_space=pl.ANY),
        out_shape=jax.ShapeDtypeStruct(array.shape, array.dtype),
        input_output_aliases={0: 0},
        cost_estimate=pl.CostEstimate(flops=0, bytes_accessed=0, transcendentals=0),
        name="fence",
    )(array, *after)


def join(*parts):
    return jnp.concatenate(parts, axis=0)


def add_low(*parts):
    total = parts[0].astype(f32)
    for part in parts[1:]:
        total = total + part.astype(f32)
    return total.astype(bf16)


def held(array, after):
    return fence(array, *after) if after else array


def sends_kernel(count, layout, *refs):
    for out, parts in zip(refs[len(refs) - len(layout) :], layout):
        at = 0
        for which, first, n in parts:
            out[at : at + n] = refs[which][first : first + n]
            at += n


def make_sends(arrays, layout, after=()):
    width = arrays[0].shape[1]
    low = lambda parts: jax.ShapeDtypeStruct((sum(n for _, _, n in parts), width), arrays[0].dtype)
    return pl.pallas_call(
        functools.partial(sends_kernel, len(arrays), layout),
        in_specs=[VMEM] * len(arrays) + [ANY] * len(after),
        out_specs=[VMEM] * len(layout),
        out_shape=[low(parts) for parts in layout],
        compiler_params=pltpu.CompilerParams(vmem_limit_bytes=16 * 1024 * 1024),
        cost_estimate=pl.CostEstimate(flops=0, bytes_accessed=0, transcendentals=0),
        name="sends",
    )(*arrays, *after)


class relay_stages:
    def __init__(self, own, na, swap):
        self.own, self.na, self.nb, self.swap = own, na, own.shape[0] - na, swap
        self.got, self.stage = (), 0

    def send(self, after=()):
        self.stage += 1
        na, nb = self.na, self.nb
        if self.stage == 1:
            self.own = held(self.own, after)
            sends = [self.own] * 3
            steps = (1, 3, 4)
        elif self.stage == 2:
            layout = (
                ((0, 0, na), (1, 0, na)),
                ((1, 0, na), (2, na, nb)),
                ((0, na, nb), (2, na, nb)),
            )
            sends = make_sends(self.got, layout, after)
            steps = (4, 1, 3)
        else:
            sends = make_sends(self.got[3:5], (((0, na, na),), ((1, na, nb),)), after)
            steps = (1, 3)
        self.flying = tuple(self.swap(x, step) for x, step in zip(sends, steps))
        return tuple(sends)

    def arrive(self):
        self.got += self.flying

    def finish(self):
        self.arrive()
        return (self.own, *self.got)


def relay_gather(own, na, swap, during=None, hold=None):
    nb = own.shape[0] - na
    during = during or (lambda stage, arrived, sends: ())
    hold = hold or {}
    own = held(own, hold.get(1, ()))
    s1, s3, s4 = swap(own, 1), swap(own, 3), swap(own, 4)
    after = during(1, (own,), (own,)) + hold.get(2, ())
    layout = (
        ((0, 0, na), (1, 0, na)),
        ((1, 0, na), (2, na, nb)),
        ((0, na, nb), (2, na, nb)),
    )
    sends = make_sends((s1, s3, s4), layout, after)
    zz, v1, v3 = swap(sends[0], 4), swap(sends[1], 1), swap(sends[2], 3)
    after = during(2, (s1, s3, s4), tuple(sends)) + hold.get(3, ())
    sends = make_sends((zz, v1), (((0, na, na),), ((1, na, nb),)), after)
    z2a, z2b = swap(sends[0], 1), swap(sends[1], 3)
    during(3, (zz, v1, v3), tuple(sends))
    return own, s1, s3, s4, zz, v1, v3, z2a, z2b


def relay_scatter(pa, pb, swap, hold=None, sent=None):
    na, nb = pa[0].shape[0], pb[0].shape[0]
    hold = hold or {}
    sent = {} if sent is None else sent
    get = lambda stage: hold[stage]() if stage in hold else ()
    after = get(1)
    sent[1] = (held(pa[6], after), held(pb[6], after))
    r1, r3 = swap(sent[1][0], 1), swap(sent[1][1], 3)
    p7a = add_low(pa[7], r1)
    p5b = add_low(pb[5], r3)
    after = get(2)
    sends = (join(pa[5], p7a), join(pa[2], p5b), join(pb[2], pb[7]))
    sent[2] = tuple(held(x, after) for x in sends)
    zz, v1, v3 = swap(sent[2][0], 4), swap(sent[2][1], 1), swap(sent[2][2], 3)
    p1 = join(add_low(pa[1], zz[:na]), add_low(pb[1], v3[:nb]))
    p3 = join(add_low(pa[3], zz[na:], v1[:na]), pb[3])
    p4 = join(pa[4], add_low(pb[4], v1[na:], v3[nb:]))
    after = get(3)
    sent[3] = tuple(held(x, after) for x in (p1, p3, p4))
    s1, s3, s4 = swap(sent[3][0], 1), swap(sent[3][1], 3), swap(sent[3][2], 4)
    return pa[0], pb[0], s1, s3, s4


def total_of(pieces):
    pa, pb, s1, s3, s4 = pieces
    na = pa.shape[0]
    total_a = pa.astype(f32) + s1[:na].astype(f32) + s3[:na].astype(f32) + s4[:na].astype(f32)
    total_b = pb.astype(f32) + s1[na:].astype(f32) + s3[na:].astype(f32) + s4[na:].astype(f32)
    return total_a, total_b


def ring_scatter(pieces, swap, after, sent):
    near = [join(pieces[j], pieces[j ^ 4]) for j in range(4)]
    near[1:] = [held(x, after) for x in near[1:]]
    sent += near[1:]
    total = near[0].astype(f32)
    for j in (1, 3, 2):
        total = total + swap(near[j], j).astype(f32)
    return total


def pair_sum(total, swap, after=()):
    half = total.shape[0] // 2
    return total[:half] + swap(held(total[half:].astype(bf16), after), 4).astype(f32)


def gather_direct(array, index, swap):
    pair = index & 4
    high = (index >> 2) & 1
    two = jnp.zeros((2,) + array.shape, array.dtype)
    two = lax.dynamic_update_index_in_dim(two, array, high, 0)
    two = lax.dynamic_update_index_in_dim(two, swap(array, 4), 1 - high, 0)
    ring = index & 3
    out = jnp.zeros((2, 4) + array.shape, array.dtype)
    out = lax.dynamic_update_index_in_dim(out, two, ring, 1)
    for step in (1, 3, 2):
        out = lax.dynamic_update_index_in_dim(out, swap(two, step), ring ^ step, 1)
    return out.reshape((8,) + array.shape), two


def scatter_direct(pieces, index, swap):
    high = (index >> 2) & 1
    ring = index & 3
    quads = pieces.reshape((2, 4) + pieces.shape[1:])
    total = lax.dynamic_index_in_dim(quads, ring, 1, keepdims=False).astype(f32)
    for step in (1, 3, 2):
        piece = lax.dynamic_index_in_dim(quads, ring ^ step, 1, keepdims=False)
        total = total + swap(piece, step).astype(f32)
    mine = lax.dynamic_index_in_dim(total, high, 0, keepdims=False)
    theirs = lax.dynamic_index_in_dim(total, 1 - high, 0, keepdims=False)
    return mine + swap(theirs.astype(bf16), 4).astype(f32)


def place_kernel(cuts, sizes, index_ref, *refs):
    arrays, outs = refs[:9], refs[len(refs) - len(cuts) :]
    for (k, h), (i, at) in where_parts(0, 9, sizes).items():
        for out, (which, first, n, width) in zip(outs, cuts):
            if which == h:
                rows = slice(at + first, at + first + n)
                out[index_ref[0] ^ k] = arrays[i][rows, :, :width]


def place(arrays, na, cuts, index, after):
    rows, columns = arrays[0].shape
    eights = [x.reshape(x.shape[0] // 8, 8, columns) for x in arrays]
    sizes = (na // 8, (rows - na) // 8)
    return pl.pallas_call(
        functools.partial(place_kernel, cuts, sizes),
        in_specs=[SMEM] + [VMEM] * 9 + [ANY] * len(after),
        out_specs=[VMEM] * len(cuts),
        out_shape=[jax.ShapeDtypeStruct((8, n, 8, width), bf16) for _, _, n, width in cuts],
        compiler_params=pltpu.CompilerParams(vmem_limit_bytes=24 * 1024 * 1024),
        name="place",
    )(index.reshape(1), *eights, *after)


def interleave_kernel(cuts, core_ref, *refs):
    count = 1 + max(which for which, _, _, _, _ in cuts)
    mine, theirs, outs = refs[:count], refs[count : 2 * count], refs[len(refs) - len(cuts) :]
    core = core_ref[0]
    for out, (which, first, n, column, width) in zip(outs, cuts):
        columns = slice(column, column + width)
        for i in range(8):
            out[i, core] = mine[which][i, first : first + n, :, columns]
            out[i, 1 - core] = theirs[which][i, first : first + n, :, columns]


def interleave(mine, theirs, cuts, core, after=()):
    outs = pl.pallas_call(
        functools.partial(interleave_kernel, cuts),
        in_specs=[SMEM] + [VMEM] * (2 * len(mine)) + [ANY] * len(after),
        out_specs=[VMEM] * len(cuts),
        out_shape=[jax.ShapeDtypeStruct((8, 2, n, 8, width), bf16) for _, _, n, _, width in cuts],
        compiler_params=pltpu.CompilerParams(vmem_limit_bytes=40 * 1024 * 1024),
        name="interleave",
    )(core.reshape(1), *mine, *theirs, *after)
    return [x.reshape(-1, x.shape[-1]) for x in outs]


def gain_rows(block):
    pick = lax.broadcasted_iota(jnp.int32, (ACT_PAD, 128), 0)
    pick = (pick == lax.broadcasted_iota(jnp.int32, (ACT_PAD, 128), 1)).astype(bf16)
    turned = dot_t(pick, block)
    return turned[0:1], turned[1:2]


def keys_kernel(*refs):
    rows, (gain_d, gain_a, weight_d, weight_a, cosine, sine) = refs[:9], refs[9:15]
    normed_d, normed_a, keys, values = refs[-4:]
    gain_d, gain_a = gain_rows(gain_d[...])[0], gain_rows(gain_a[...])[0]
    width = weight_a.shape[0]
    prefix, action = [], []
    for i, parts in enumerate(ARRIVALS):
        at = 0
        for _, h in parts:
            prefix.append(rows[i][at : at + HALF_A])
            if h:
                action.append(rows[i][at + HALF_A : at + HALF_B, :width])
            at += 2 * (HALF_A, HALF_B)[h]
    x = join(*prefix).astype(f32)
    low_d = (x * inverse_rms(x) * gain_d).astype(bf16)
    x = join(*action).astype(f32)
    low_a = (x * inverse_rms(x) * gain_a).astype(bf16)
    normed_d[:PREF] = low_d[:PREF]
    normed_a[:ACT_PAD] = low_a[:ACT_PAD]
    normed_d[PREF:] = low_d[ROW_PAIR : ROW_PAIR + PREF]
    normed_a[ACT_PAD:] = low_a[ACT_PAIR : ACT_PAIR + ACT_PAD]
    raw = join(dot(low_d, weight_d[...]), dot(low_a, weight_a[...]))
    keys[...] = rotate(raw[:, :HD], cosine[...], sine[...]).astype(bf16)
    values[...] = raw[:, HD:].astype(bf16)


def keys_of(rows, gain_d, gain_a, weight_d, weight_a, cosine, sine, after):
    width_d, width_a = gain_d.shape[0], gain_a.shape[0]
    count = cosine.shape[0]
    shape = lambda *dims: jax.ShapeDtypeStruct(dims, bf16)
    given = [*rows, gain_d, gain_a, weight_d, weight_a, cosine, sine]
    return pl.pallas_call(
        keys_kernel,
        in_specs=[VMEM] * len(given) + [ANY] * len(after),
        out_specs=[VMEM] * 4,
        out_shape=[
            shape(2 * PREF, width_d),
            shape(2 * ACT_PAD, width_a),
            shape(count, HD),
            shape(count, HD),
        ],
        compiler_params=pltpu.CompilerParams(vmem_limit_bytes=48 * 1024 * 1024),
        cost_estimate=pl.CostEstimate(
            flops=4 * count * width_d * HD, bytes_accessed=8 * 1024 * 1024, transcendentals=count
        ),
        name="keys_of",
    )(*given, *after)


def gelu_parts(gate):
    c0 = 0.7978845608028654
    c1 = 0.044715
    square = gate * gate
    tanh = jnp.tanh(c0 * gate * (1.0 + c1 * square))
    half = 0.5 * (1.0 + tanh)
    slope = half + 0.5 * gate * (1.0 - tanh * tanh) * c0 * (1.0 + 3.0 * c1 * square)
    return gate * half, slope


def feed_block(rows, seed, gate_weight, up_weight, down_weight, valid):
    into, out_of = (dot_t, dot) if valid is None else (dot, dot_t)
    gate = into(rows, gate_weight)
    up = into(rows, up_weight)
    active, slope = gelu_parts(gate)
    product_delta = dot_t(seed, down_weight)
    if valid is not None:
        active = active * valid
        product_delta = product_delta * valid
    product = (active * up).astype(bf16)
    gate_delta = (product_delta * up * slope).astype(bf16)
    up_delta = (product_delta * active).astype(bf16)
    rows_delta = out_of(gate_delta, gate_weight) + out_of(up_delta, up_weight)
    return product, gate_delta, up_delta, rows_delta.astype(bf16)


def feed_kernel(layout, seed_layout, *refs):
    arrays = 1 + max(i for parts in layout for i, _ in parts)
    rows_refs, seed_refs, refs = refs[:arrays], refs[arrays : 2 * arrays], refs[2 * arrays :]
    gate_ref, up_ref, down_ref = refs[:3]
    action_gate_ref, action_up_ref, action_down_ref, valid_ref = refs[3:7]
    count = len(layout)
    outs = refs[-(2 * count + 8) :]
    products, deltas, kept_rows, kept_seeds = outs[:4]
    action_products, action_deltas, action_rows, action_seeds = outs[4:8]
    width = action_gate_ref.shape[0]
    rest = PREF - HALF_A

    def prefix_of(blocks, layout):
        parts = []
        for (ia, a), (ib, b) in layout:
            parts += [blocks[ia][a : a + HALF_A], blocks[ib][b : b + rest]]
        return join(*parts)

    def action_of(blocks, layout):
        parts = []
        for _, (ib, b) in layout:
            parts.append(blocks[ib][b + rest : b + HALF_B, :width])
        return join(*parts) if count > 1 else parts[0]

    rows, seed = prefix_of(rows_refs, layout), prefix_of(seed_refs, seed_layout)
    product, gate_delta, up_delta, rows_delta = feed_block(
        rows, seed, gate_ref[...], up_ref[...], down_ref[...], None
    )
    hidden = product.shape[1]
    spare = jnp.zeros((count * PREF, HIDDEN_PAD - hidden), bf16)
    products[:, :hidden] = product
    products[:, hidden:] = spare
    deltas[:, :hidden] = gate_delta
    deltas[:, hidden:HIDDEN_PAD] = spare
    deltas[:, HIDDEN_PAD : HIDDEN_PAD + hidden] = up_delta
    deltas[:, HIDDEN_PAD + hidden :] = spare
    kept_rows[...] = rows
    kept_seeds[...] = seed
    rows, seed = action_of(rows_refs, layout), action_of(seed_refs, seed_layout)
    product, gate_delta, up_delta, action_rows_delta = feed_block(
        rows,
        seed,
        action_gate_ref[...],
        action_up_ref[...],
        action_down_ref[...],
        valid_ref[...],
    )
    slots = gate_delta.shape[1]
    action_products[...] = product
    action_deltas[:, :slots] = gate_delta
    action_deltas[:, slots:] = up_delta
    action_rows[...] = rows
    action_seeds[...] = seed
    blank = jnp.zeros((ACT_PAD, rows_delta.shape[1] - width), bf16)
    for i in range(count):
        a, b, c = i * PREF, i * PREF + HALF_A, (i + 1) * PREF
        extra = slice(i * ACT_PAD, (i + 1) * ACT_PAD)
        ref_a, ref_b = outs[8 + 2 * i : 10 + 2 * i]
        ref_a[...] = rows_delta[a:b]
        ref_b[:rest] = rows_delta[b:c]
        ref_b[rest:, :width] = action_rows_delta[extra]
        ref_b[rest:, width:] = blank


def feed(arrays, seeds, weights, layout, seed_layout, base, kept, after):
    count = len(layout)
    width = arrays[0].shape[1]
    hidden = weights[0].shape[0]
    action_width, slots = weights[3].shape
    once = pl.Buffered(1)
    at = base // count

    def whole(array):
        return pl.BlockSpec(array.shape, lambda i: (0, 0), pipeline_mode=once)

    def part(size, columns):
        return (
            jax.ShapeDtypeStruct((N_MP * size, columns), bf16),
            pl.BlockSpec((count * size, columns), lambda i: (at, 0), pipeline_mode=once),
        )

    def own(size):
        return (
            jax.ShapeDtypeStruct((size, width), bf16),
            pl.BlockSpec((size, width), lambda i: (0, 0), pipeline_mode=once),
        )

    outs = [
        part(PREF, HIDDEN_PAD),
        part(PREF, 2 * HIDDEN_PAD),
        part(PREF, width),
        part(PREF, width),
        part(ACT_PAD, slots),
        part(ACT_PAD, 2 * slots),
        part(ACT_PAD, action_width),
        part(ACT_PAD, action_width),
    ] + [own(HALF_A), own(HALF_B)] * count
    reused = [] if kept is None else list(kept)
    given = [*arrays, *seeds]
    placed = len(given) + len(weights)
    results = pl.pallas_call(
        functools.partial(feed_kernel, layout, seed_layout),
        grid=(1,),
        in_specs=[whole(x) for x in given]
        + [VMEM] * len(weights)
        + [ANY] * (len(reused) + len(after)),
        out_shape=[shape for shape, _ in outs],
        out_specs=[spec for _, spec in outs],
        input_output_aliases={placed + i: i for i in range(len(reused))},
        compiler_params=pltpu.CompilerParams(
            dimension_semantics=("arbitrary",), vmem_limit_bytes=VMEM_FEED * 1024 * 1024
        ),
        cost_estimate=pl.CostEstimate(
            flops=10 * count * (PREF * width * hidden + ACT_PAD * action_width * slots),
            bytes_accessed=6 * (width * hidden + action_width * slots),
            transcendentals=count * PREF * hidden,
        ),
        name="feed",
    )(*given, *weights, *reused, *after)
    blocks = [results[8 + 2 * i : 10 + 2 * i] for i in range(count)]
    return blocks, results[:8]


def see(own_ref, key_ref):
    own, key = own_ref[...], key_ref[...]
    return (own[:, 0:1] == key[0:1]) | (own[:, 1:2] == key[1:2])


def attend_kernel(*refs):
    (normed_d, normed_a, x_d, x_a, wq_d, wq_a, wo_m, wo_e, wo_a) = refs[:9]
    (gain_d, gain_a, cosine, sine, own_codes, key_codes) = refs[9:15]
    keys, values = refs[15][...], refs[16][...]
    (queries, context, tops, totals, hidden_d, hidden_a, block) = refs[-7:]
    gain_d, gain_a = gain_rows(gain_d[...])[1], gain_rows(gain_a[...])[1]
    raw = join(dot(normed_d[:PREF], wq_d[...]), dot(normed_a[:ACT_PAD], wq_a[...]))
    visible = see(own_codes, key_codes)
    cos, sin = cosine[...], sine[...]
    heads = []
    for h in range(HEADS):
        rows = slice(h * BLOCK, (h + 1) * BLOCK)
        query = (rotate(raw[:, h * HD : (h + 1) * HD], cos, sin) * HD**-0.5).astype(bf16)
        queries[rows] = query
        scores = jnp.where(visible, dot_t(query, keys), -1e30)
        top = jnp.max(scores, axis=1, keepdims=True)
        shifted = jnp.exp(scores - top)
        total = jnp.sum(shifted, axis=1, keepdims=True)
        tops[rows] = top
        totals[rows] = total
        heads.append(dot((shifted / total).astype(bf16), values).astype(bf16))
    mixed = jnp.concatenate(heads, axis=1)
    context[...] = mixed
    main, width_d, width_a = wo_m.shape[1], x_d.shape[1], x_a.shape[1]
    low_d, low_a = mixed[:PREF], mixed[PREF:]
    state = x_d[...].astype(f32) + jnp.concatenate(
        [dot(low_d, wo_m[...]), dot(low_d, wo_e[...])], axis=1
    )
    hidden_d[...] = state
    second_d = (state * inverse_rms(state) * gain_d).astype(bf16)
    real = lax.broadcasted_iota(jnp.int32, (ACT_PAD, width_a), 0) < ACT
    state = jnp.where(real, x_a[...].astype(f32) + dot(low_a, wo_a[...]), 0.0)
    hidden_a[...] = state
    second_a = (state * inverse_rms(state) * gain_a).astype(bf16)
    block[:PREF] = second_d
    block[PREF:, :width_a] = second_a
    block[PREF:, width_a:] = jnp.zeros((ACT_PAD, width_d - width_a), bf16)


def attend(*given, after):
    x_d, x_a = given[2:4]
    width_d, width_a = x_d.shape[1], x_a.shape[1]
    shape = jax.ShapeDtypeStruct
    stacked = HEADS * BLOCK
    return pl.pallas_call(
        attend_kernel,
        in_specs=[VMEM] * len(given) + [ANY] * len(after),
        out_specs=[VMEM] * 7,
        out_shape=[
            shape((stacked, HD), bf16),
            shape((BLOCK, HEADS * HD), bf16),
            shape((stacked, 1), f32),
            shape((stacked, 1), f32),
            shape((PREF, width_d), f32),
            shape((ACT_PAD, width_a), f32),
            shape((BLOCK, width_d), bf16),
        ],
        compiler_params=pltpu.CompilerParams(vmem_limit_bytes=50 * 1024 * 1024),
        cost_estimate=pl.CostEstimate(
            flops=4 * BLOCK * HEADS * HD * (N_MP * BLOCK + width_d),
            bytes_accessed=4 * 1024 * 1024 * 5,
            transcendentals=stacked * N_MP * BLOCK,
        ),
        name="attend",
    )(*given, *after)


def attend_back_kernel(*refs):
    pieces = refs[:5]
    (hidden_d, hidden_a, cotangent_d, cotangent_a, share, gain_d, gain_a) = refs[5:12]
    (wo_m, wo_e, wo_a, queries, tops, totals, cosine, sine, own_codes, key_codes) = refs[12:22]
    keys, values = refs[22][...], refs[23][...]
    outs = refs[-(6 + len(PARTS)) :]
    (hidden_delta_d, hidden_delta_a, low, terms_d, terms_a, query_delta) = outs[:6]
    kv_deltas = outs[6:]
    gain_d, gain_a = gain_rows(gain_d[...])[1], gain_rows(gain_a[...])[1]
    delta = join(*total_of([piece[...] for piece in pieces]))
    width_d, width_a = hidden_d.shape[1], hidden_a.shape[1]
    lows = []
    for rows, state_ref, cotangent, gain, out, terms in (
        (slice(0, PREF), hidden_d, cotangent_d, gain_d, hidden_delta_d, terms_d),
        (slice(PREF, BLOCK), hidden_a, cotangent_a, gain_a, hidden_delta_a, terms_a),
    ):
        state = state_ref[...]
        change = delta[rows, : state.shape[1]]
        scale = inverse_rms(state)
        seed = cotangent[...].astype(f32) * share[rows]
        back = seed + normalize_back(state, scale, gain, change)
        out[...] = back
        terms[...] = (change * state * scale).astype(bf16)
        lows.append(back.astype(bf16))
    low_d, low_a = lows
    low[:PREF] = low_d
    low[PREF:, :width_a] = low_a
    low[PREF:, width_a:] = jnp.zeros((ACT_PAD, width_d - width_a), bf16)
    main = wo_m.shape[1]
    context_delta = join(
        dot_t(low_d[:, :main], wo_m[...]) + dot_t(low_d[:, main:], wo_e[...]),
        dot_t(low_a, wo_a[...]),
    ).astype(bf16)
    visible = see(own_codes, key_codes)
    cos, sin = cosine[...], sine[...]
    keys_delta, values_delta = None, None
    for h in range(HEADS):
        rows = slice(h * BLOCK, (h + 1) * BLOCK)
        query = queries[rows]
        change = context_delta[:, h * HD : (h + 1) * HD]
        scores = jnp.where(visible, dot_t(query, keys), -1e30)
        probs = jnp.exp(scores - tops[rows]) / totals[rows]
        probs_delta = dot_t(change, values)
        row_dot = jnp.sum(probs * probs_delta, axis=1, keepdims=True)
        score_delta = (probs * (probs_delta - row_dot)).astype(bf16)
        turned = unrotate(dot(score_delta, keys), cos, sin) * HD**-0.5
        query_delta[:, h * HD : (h + 1) * HD] = turned.astype(bf16)
        key_part = t_dot(score_delta, query)
        value_part = t_dot(probs.astype(bf16), change)
        keys_delta = key_part if h == 0 else keys_delta + key_part
        values_delta = value_part if h == 0 else values_delta + value_part
    at, extra = 0, len(PARTS) * HALF_A
    for (_, half), out in zip(PARTS, kv_deltas):
        for columns, change in ((slice(0, HD), keys_delta), (slice(HD, 2 * HD), values_delta)):
            out[:HALF_A, columns] = change[at : at + HALF_A].astype(bf16)
            if half:
                out[HALF_A:, columns] = change[extra : extra + ACT_PAD].astype(bf16)
        at += HALF_A
        extra += half * ACT_PAD


def attend_back(*given, after):
    hidden_d, hidden_a = given[5:7]
    width_d, width_a = hidden_d.shape[1], hidden_a.shape[1]
    shape = jax.ShapeDtypeStruct
    stacked = HEADS * BLOCK
    outs = pl.pallas_call(
        attend_back_kernel,
        in_specs=[VMEM] * len(given) + [ANY] * len(after),
        out_specs=[VMEM] * (6 + len(PARTS)),
        out_shape=[
            shape((PREF, width_d), f32),
            shape((ACT_PAD, width_a), f32),
            shape((BLOCK, width_d), bf16),
            shape((PREF, width_d), bf16),
            shape((ACT_PAD, width_a), bf16),
            shape((BLOCK, HEADS * HD), bf16),
        ]
        + [shape(((HALF_A, HALF_B)[half], 2 * HD), bf16) for _, half in PARTS],
        compiler_params=pltpu.CompilerParams(vmem_limit_bytes=50 * 1024 * 1024),
        cost_estimate=pl.CostEstimate(
            flops=2 * BLOCK * HEADS * HD, bytes_accessed=4 * BLOCK, transcendentals=stacked
        ),
        name="attend_back",
    )(*given, *after)
    kv_deltas = dict(zip(PARTS, outs[6:]))
    pa = {k: kv_deltas[k, 0] for k in range(8)}
    pb = {k: kv_deltas[k, 1] for k in range(8)}
    return outs[:6], pa, pb


def theirs_kernel(cuts, place_ref, *refs):
    out = refs[-1]
    core = place_ref[1]
    for ref, (row, n, source, column, width) in zip(refs, cuts):
        out[:, row : row + n, :, column : column + width] = ref[
            1 - core, :, :, :, source : source + width
        ]


def near_kernel(cuts, place_ref, *refs):
    got, outs = refs[len(cuts)], refs[-4:]
    mp, core = place_ref[0], place_ref[1]
    for step, out in zip((0, 1, 3, 2), outs):
        for pair in range(2):
            block = mp ^ step ^ (4 * pair)
            base = pair * got.shape[1]
            for ref, (row, n, source, column, width) in zip(refs, cuts):
                columns = slice(column, column + width)
                mine = ref[core, block, :, :, source : source + width].astype(f32)
                total = mine + got[block, row : row + n, :, columns].astype(f32)
                out[base + row : base + row + n, :, columns] = total.astype(bf16)


def sum_weights(grads, cuts, columns, place, sent, got, after, before_last):
    views = [g.reshape(2, 8, -1, 8, g.shape[1]) for g in grads]
    eights = max(row + n for row, n, _, _, _ in cuts)
    params = pltpu.CompilerParams(vmem_limit_bytes=44 * 1024 * 1024)
    cost = pl.CostEstimate(flops=0, bytes_accessed=0, transcendentals=0)
    low = lambda *dims: jax.ShapeDtypeStruct(dims, bf16)
    theirs = pl.pallas_call(
        functools.partial(theirs_kernel, cuts),
        in_specs=[SMEM] + [VMEM] * len(views),
        out_specs=VMEM,
        out_shape=low(8, eights, 8, columns),
        compiler_params=params,
        cost_estimate=cost,
        name="theirs",
    )(place, *views)
    near = pl.pallas_call(
        functools.partial(near_kernel, cuts),
        in_specs=[SMEM] + [VMEM] * (len(views) + 1) + [ANY] * len(after),
        out_specs=[VMEM] * 4,
        out_shape=[low(2 * eights, 8, columns)] * 4,
        compiler_params=params,
        cost_estimate=cost,
        name="near",
    )(place, *views, core_swap(theirs), *after)
    near = [x.reshape(16 * eights, columns) for x in near]
    sent += near[1:]
    total = near[0].astype(f32)
    for step, x in zip((1, 3, 2), near[1:]):
        got.append(mp_swap(x, step))
        total = total + got[-1].astype(f32)
    half = 8 * eights
    last = held(total[half:].astype(bf16), before_last)
    return (total[:half] + mp_swap(last, 4).astype(f32)).astype(bf16)


def pad_action(rows):
    return jnp.pad(rows, ((0, ACT_PAD - ACT), (0, 0)))


def widen(rows, width):
    return jnp.pad(rows, ((0, 0), (0, width - rows.shape[1])))


def block_of(prefix_rows, action_rows):
    return join(prefix_rows, widen(action_rows, prefix_rows.shape[1]))


def order_matrix(size, rows):
    d = jnp.arange(size, dtype=jnp.int32)
    r = d % rows
    mp = (d // rows) % 8
    dp = d // (8 * rows)
    place = (dp % 2) * (size // 2) + mp * (8 * rows) + (dp // 2) * rows + r
    return (place[:, None] == jnp.arange(size, dtype=jnp.int32)[None, :]).astype(bf16)


def dot(a, b):
    return jnp.dot(a, b, preferred_element_type=f32)


def dot_t(a, b):
    return lax.dot_general(a, b, (((1,), (1,)), ((), ())), preferred_element_type=f32)


def t_dot(a, b):
    return lax.dot_general(a, b, (((0,), (0,)), ((), ())), preferred_element_type=f32)


def inverse_rms(rows):
    return lax.rsqrt(jnp.mean(rows * rows, axis=-1, keepdims=True) + EPSILON)


def normalize_back(rows, scale, gain, delta):
    a = delta * gain
    return scale * (a - rows * (scale * scale) * jnp.mean(a * rows, axis=-1, keepdims=True))


def rotate(rows, cosine, sine):
    half = HD // 2
    first, second = rows[:, :half], rows[:, half:]
    return jnp.concatenate(
        [first * cosine - second * sine, second * cosine + first * sine], axis=1
    )


def unrotate(rows, cosine, sine):
    return rotate(rows, cosine, -sine)


def angle_tables(place):
    half = HD // 2
    frequency = ROPE_BASE ** (-jnp.arange(half, dtype=f32) / half)
    angles = place.astype(f32)[:, None] * frequency[None, :]
    return jnp.cos(angles), jnp.sin(angles)


def on_device(
    prefix_input,
    action_input,
    prefix_cotangent,
    action_cotangent,
    prefix_lengths,
    mixture,
    cut_points,
    prefix_query,
    prefix_key,
    prefix_value,
    prefix_out,
    prefix_first_gain,
    prefix_second_gain,
    action_query,
    action_key,
    action_value,
    action_out,
    action_first_gain,
    action_second_gain,
    prefix_gate,
    prefix_up,
    prefix_down,
    action_gate,
    action_up,
    action_down,
):
    mp = lax.axis_index("mp")
    dp = lax.axis_index("dp")
    core = dp & 1
    yz = (dp >> 3) * 4 + ((dp >> 1) & 3)
    D = prefix_input.shape[2]
    DA = action_input.shape[2]

    def column_block(first, second):
        return jnp.pad(jnp.stack([first, second], axis=1), ((0, 0), (0, 126)))

    pack_d = jnp.concatenate(
        [
            prefix_key,
            prefix_value,
            column_block(prefix_first_gain, prefix_second_gain),
            prefix_query,
        ],
        axis=1,
    )
    wide = pack_d.shape[1]
    pack = jnp.concatenate(
        [
            pack_d[:8],
            action_key,
            action_value,
            column_block(action_first_gain, action_second_gain),
            action_query,
            action_out,
            prefix_out,
            jnp.pad(pack_d[8:].reshape(8, wide // 8), ((0, 0), (0, 48))),
        ],
        axis=1,
    )
    lengths = prefix_lengths[0]
    first_length = lengths[0]

    def tables(source, row):
        is_action = row >= PREF
        prefix_row = source * PREF + row
        prefix_item = (prefix_row >= first_length).astype(jnp.int32)
        prefix_place = prefix_row - jnp.where(prefix_item == 1, first_length, 0)
        action_row = source * ACT + row - PREF
        action_item = (action_row >= ACT_LEN).astype(jnp.int32)
        action_place = jnp.where(action_item == 1, lengths[1], first_length) + action_row % ACT_LEN
        action_item = jnp.where(row - PREF < ACT, action_item, 2)
        item = jnp.where(is_action, action_item, prefix_item)
        place = jnp.where(is_action, action_place, prefix_place)
        return item, place, is_action

    own_item, own_place, own_is_action = tables(mp, jnp.arange(BLOCK, dtype=jnp.int32))
    key_item, key_place, key_is_action = tables(jnp.asarray(KEY_BLOCK) ^ mp, jnp.asarray(KEY_ROW))
    key_cos, key_sin = angle_tables(key_place)
    own_codes = jnp.stack([own_item, jnp.where(own_is_action, own_item, -2)], axis=1)
    key_codes = jnp.stack(
        [jnp.where(key_is_action, -1, key_item), jnp.where(key_is_action, key_item, -1)], axis=0
    )
    own_cos, own_sin = angle_tables(own_place)

    share = mixture[0].astype(f32) / 32.0
    row_share = jnp.where(own_item == 1, share[1], share[0])[:, None]
    cotangent_a = pad_action(action_cotangent[0])
    prefix_seed = prefix_cotangent[0].astype(f32) * row_share[:PREF]
    action_seed = cotangent_a.astype(f32) * row_share[PREF:]
    seed_block = block_of(prefix_seed.astype(bf16), action_seed.astype(bf16))

    near, two = gather_direct(pack, mp, mp_swap)
    last_row = near[:, :, pack.shape[1] - 256 : pack.shape[1] - 48].reshape(8, 1, wide)
    near_d = jnp.concatenate([near[:, :, :wide], last_row], axis=1).reshape(72, wide)
    near_a = near[:, :, wide : pack.shape[1] - 256].reshape(64, -1)
    edge = near_a[:, 2688 + 1024 :]
    kv_a = widen(jnp.concatenate([near_a[:, :640], edge], axis=1), 1024)
    pack_a = join(near_a[:, 640:1664], near_a[:, 1664:2688], kv_a)
    pack_b = join(near_d[:, 640:], near_a[:, 2688 : 2688 + 1024], widen(near_d[:, :640], 1024))
    own_action = pad_action(action_input[0])
    own_block = block_of(prefix_input[0], own_action)
    pack = join(pack_a, pack_b)
    both = join(
        own_block[:HALF_A], seed_block[:HALF_A], own_block[HALF_A:], seed_block[HALF_A:]
    )
    gather = relay_stages(pack, pack_a.shape[0], yz_swap)
    other = relay_stages(both, 2 * HALF_A, mp_swap)
    other.send((two,))
    gather.send()
    gather.arrive()
    sends = gather.send()
    other.arrive()
    other.send(sends)
    gather.arrive()
    sends = gather.send()
    other.arrive()
    row_sends = other.send(sends)
    pieces = gather.finish()
    x_rows = seeds = other.finish()
    cuts = ((0, 16, 8, 768), (1, 17, 9, 640), (0, 0, 16, 1024), (1, 0, 17, 1024))
    mine = place(pieces, pack_a.shape[0], cuts, yz, (*row_sends, x_rows[6]))
    theirs = [core_swap(x) for x in mine]
    cuts = ((0, 0, 8, 0, 512), (0, 0, 8, 512, 128), (0, 0, 8, 640, 128))
    cuts += ((1, 0, 9, 0, 512), (1, 0, 9, 512, 128))
    wkv_a, gains_a, wo_e, wkv_d, gains_d = interleave(mine[:2], theirs[:2], cuts, core, x_rows[7:])
    cuts = ((0, 0, 8, 0, 1024), (0, 8, 8, 0, 1024), (1, 0, 9, 0, 1024), (1, 9, 8, 0, 1024))
    wq_a, wo_a, wq_d, wo_m = interleave(mine[2:], theirs[2:], cuts, core)
    normed_d, normed_a, keys, values = keys_of(
        x_rows,
        gains_d,
        gains_a,
        wkv_d,
        wkv_a,
        key_cos,
        key_sin,
        (),
    )
    x_d, x_a = prefix_input[0].astype(f32), own_action.astype(f32)
    rms_d, rms_a = inverse_rms(x_d), inverse_rms(x_a)
    queries, context, tops, totals, hidden_d, hidden_a, second_block = attend(
        normed_d,
        normed_a,
        prefix_input[0],
        own_action,
        wq_d,
        wq_a,
        wo_m,
        wo_e,
        wo_a,
        gains_d,
        gains_a,
        own_cos,
        own_sin,
        own_codes,
        key_codes,
        keys,
        values,
        after=(),
    )

    slots = action_gate.shape[2]
    cut_pair = lax.dynamic_slice_in_dim(cut_points, mp, 2)
    valid = (jnp.arange(slots, dtype=jnp.int32) < cut_pair[1] - cut_pair[0]).astype(f32)[None, :]
    weights = (prefix_gate.T, prefix_up.T, prefix_down)
    weights += (action_gate[0], action_up[0], action_down[0], valid)
    kept = None
    results = {}

    def run(arrays, first, blocks, base, after):
        nonlocal kept
        where = where_parts(first, len(arrays), (HALF_A, HALF_B))
        layout = tuple((where[k, 0], where[k, 1]) for k in blocks)
        some = seeds[first : first + len(arrays)]
        where = where_parts(first, len(arrays), (2 * HALF_A, 2 * HALF_B))
        skip = lambda k, h: (where[k, h][0], where[k, h][1] + (HALF_A, HALF_B)[h])
        seed_layout = tuple((skip(k, 0), skip(k, 1)) for k in blocks)
        done, kept = feed(arrays, some, weights, layout, seed_layout, base, kept, after)
        results.update(zip(blocks, done))
        return (done[0][0],)

    def feed_during(stage, arrays, sends):
        if stage == 3:
            return ()
        first, blocks, base = {1: (0, (0,), 3), 2: (1, (1, 3, 4), 0)}[stage]
        return run(arrays, first, blocks, base, sends)

    arrays = relay_gather(second_block, HALF_A, mp_swap, feed_during)
    run(arrays[4:], 4, (2, 5, 7, 6), 4, ())
    product_d, deltas_d, rows_d, seeds_d, product_a, deltas_a, rows_a, seeds_a = kept

    grads = (
        t_dot(deltas_d, rows_d),
        t_dot(product_d, seeds_d),
        t_dot(rows_a, deltas_a),
        t_dot(product_a, seeds_a),
    )
    hidden = prefix_down.shape[0]
    grads = tuple(g.astype(bf16) for g in grads)
    pa = {k: v[0] for k, v in results.items()}
    pb = {k: v[1] for k, v in results.items()}
    delta_sent = {}
    delta_pieces = relay_scatter(pa, pb, mp_swap, sent=delta_sent)
    grads = grads[:3] + (fence(grads[3], *delta_sent[3]),)
    grads = tuple(lax.psum(g, "dp") for g in grads)
    finished = (
        grads[0][:hidden].astype(f32),
        grads[0][HIDDEN_PAD : HIDDEN_PAD + hidden].astype(f32),
        grads[1][:hidden].astype(f32),
        grads[2][:, :slots].astype(f32),
        grads[2][:, slots:].astype(f32),
        grads[3].astype(f32),
    )

    (hidden_delta_d, hidden_delta_a, low, terms_d, terms_a, query_delta), pa, pb = attend_back(
        *delta_pieces,
        hidden_d,
        hidden_a,
        prefix_cotangent[0],
        cotangent_a,
        row_share,
        gains_d,
        gains_a,
        wo_m,
        wo_e,
        wo_a,
        queries,
        tops,
        totals,
        own_cos,
        own_sin,
        own_codes,
        key_codes,
        keys,
        values,
        after=(),
    )
    low_d, low_a = low[:PREF], low[PREF:, :DA]

    kv_near = [join(pa[k], pb[k], pa[k ^ 4], pb[k ^ 4]) for k in range(4)]
    kv_part = kv_near[0].astype(f32)
    for k in (1, 3, 2):
        kv_part = kv_part + mp_swap(kv_near[k], k).astype(f32)
    pair = lambda table: join(
        own_cos if table is key_cos else own_sin,
        table[ROW_PAIR : ROW_PAIR + PREF],
        table[len(PARTS) * HALF_A + ACT_PAIR : len(PARTS) * HALF_A + ACT_PAIR + ACT_PAD],
    )
    kv_turned = jnp.concatenate(
        [unrotate(kv_part[:, :HD], pair(key_cos), pair(key_sin)), kv_part[:, HD:]], axis=1
    )
    kv_turned_low = kv_turned.astype(bf16)
    kv_rows_d = join(kv_turned_low[:PREF], kv_turned_low[BLOCK : BLOCK + PREF])
    kv_rows_a = join(kv_turned_low[PREF:BLOCK], kv_turned_low[BLOCK + PREF :])

    order_d, order_a = order_matrix(D, 9), order_matrix(DA, 8)
    turned_d = dot(normed_d, order_d).astype(bf16)
    turned_a = dot(normed_a, order_a).astype(bf16)
    turned_context = dot(context, order_a).astype(bf16)
    second_term_d = t_dot(dot(terms_d, order_d).astype(bf16), jnp.ones((PREF, 256), bf16))
    second_term_a = t_dot(dot(terms_a, order_a).astype(bf16), jnp.ones((ACT_PAD, 128), bf16))
    out_grad_d = t_dot(turned_context[:PREF], low_d).astype(bf16)
    out_grad_a = t_dot(turned_context[PREF:], low_a).astype(bf16)
    q_grad_d = t_dot(turned_d[:PREF], query_delta[:PREF]).astype(bf16)
    q_grad_a = t_dot(turned_a[:ACT_PAD], query_delta[PREF:]).astype(bf16)
    here = jnp.stack([mp, core])
    cuts = (
        (0, 8, 0, 0, 1024),
        (8, 8, 0, 0, 1024),
        (16, 9, 0, 0, 1024),
        (25, 8, 0, 0, 1024),
    )
    qo_sent, kv_sent, got = [], [], []
    qo_grads = (q_grad_a, out_grad_a, q_grad_d, out_grad_d)
    qo = sum_weights(qo_grads, cuts, 1024, here, qo_sent, got, (), grads[:1])
    kv_grad_d = t_dot(turned_d, kv_rows_d).astype(bf16)
    kv_grad_a = t_dot(turned_a, kv_rows_a).astype(bf16)
    cuts = (
        (0, 8, 0, 0, 512),
        (0, 8, 0, 512, 128),
        (0, 8, 1024, 640, 128),
        (8, 9, 0, 0, 512),
        (8, 9, 0, 512, 256),
    )
    kv_grads = (
        kv_grad_a,
        second_term_a.astype(bf16),
        out_grad_d,
        kv_grad_d,
        second_term_d.astype(bf16),
    )
    kv = sum_weights(kv_grads, cuts, 768, here, kv_sent, got, qo_sent, grads[:1])
    kv_a, kv_d = kv[:64], kv[64:, :640]
    qo_a, qo_b = qo[:128], qo[128:]
    kv_other = mp_swap(held(kv_part[BLOCK:].astype(bf16), tuple(kv_sent)), 4)
    kv_sum = kv_part[:BLOCK] + kv_other.astype(f32)
    kv_raw_delta = jnp.concatenate(
        [unrotate(kv_sum[:, :HD], own_cos, own_sin), kv_sum[:, HD:]], axis=1
    ).astype(bf16)

    partial_d = dot(product_d[:, :hidden], prefix_down).astype(bf16)
    partial_a = dot(product_a, action_down[0]).astype(bf16)
    out = []
    for k in range(8):
        i = (1, 3, 4, 0, 2, 5, 7, 6).index(k)
        mine = partial_a[i * ACT_PAD : (i + 1) * ACT_PAD]
        out.append(block_of(partial_d[i * PREF : (i + 1) * PREF], mine))
    out_sent = []
    out = ring_scatter(out, mp_swap, tuple(got), out_sent)
    out = pair_sum(out, mp_swap)
    prefix_output = (hidden_d + out[:PREF]).astype(bf16)[None]
    action_output = (hidden_a + out[PREF:, :DA])[:ACT].astype(bf16)[None]

    last_d = jnp.concatenate([kv_d, qo_b[:72]], axis=1).reshape(8, 9, wide)
    last_a = jnp.concatenate(
        [kv_a[:, :640], qo_a[:64], qo_a[64:], qo_b[72:], kv_a[:, 640:]], axis=1
    ).reshape(8, 8, -1)
    last = jnp.concatenate(
        [
            last_d[:, :8],
            last_a,
            jnp.pad(last_d[:, 8:].reshape(8, 8, wide // 8), ((0, 0), (0, 0), (0, 48))),
        ],
        axis=2,
    )
    last = scatter_direct(last, yz, yz_swap)
    ninth = last[:, last.shape[1] - 256 : last.shape[1] - 48].reshape(1, wide)
    grads_d = join(last[:, :wide], ninth)
    grads_a = last[:, wide : last.shape[1] - 256]

    def split_grads(grads, query, key, value, gain):
        key_grad = grads[:, :256]
        value_grad = grads[:, 256:512]
        second = grads[:, 512]
        query_grad = grads[:, 640:1664]
        first = (
            jnp.sum(query_grad * query.astype(f32), axis=1)
            + jnp.sum(key_grad * key.astype(f32), axis=1)
            + jnp.sum(value_grad * value.astype(f32), axis=1)
        ) / gain.astype(f32)
        return query_grad, key_grad, value_grad, first, second

    gd = split_grads(grads_d, prefix_query, prefix_key, prefix_value, prefix_first_gain)
    ga = split_grads(grads_a, action_query, action_key, action_value, action_first_gain)
    action_out_grad = grads_a[:, 1664:2688]
    prefix_out_grad = grads_a[:, 2688:]

    first_delta_d = dot_t(query_delta[:PREF], wq_d) + dot_t(kv_raw_delta[:PREF], wkv_d)
    first_delta_a = dot_t(query_delta[PREF:], wq_a) + dot_t(kv_raw_delta[PREF:], wkv_a)
    first_gain_d, first_gain_a = gain_rows(gains_d)[0], gain_rows(gains_a)[0]
    input_d = hidden_delta_d + normalize_back(x_d, rms_d, first_gain_d, first_delta_d)
    input_a = hidden_delta_a + normalize_back(x_a, rms_a, first_gain_a, first_delta_a)

    return (
        prefix_output,
        action_output,
        input_d.astype(bf16)[None],
        input_a[:ACT].astype(bf16)[None],
        gd[0],
        gd[1],
        gd[2],
        prefix_out_grad,
        gd[3],
        gd[4],
        ga[0],
        ga[1],
        ga[2],
        action_out_grad,
        ga[3],
        ga[4],
        finished[0].T,
        finished[1].T,
        finished[2],
        finished[3][None],
        finished[4][None],
        finished[5][None],
    )


def solution(mesh):
    rows = P("dp", "mp", None)
    both = P(("dp", "mp"), None)
    vector = P(("dp", "mp"))
    slots = P("mp", None, None)
    return jax.shard_map(
        on_device,
        mesh=mesh,
        in_specs=(rows,) * 4
        + (P("dp", None), P("dp", None), P())
        + (both,) * 4
        + (vector,) * 2
        + (both,) * 4
        + (vector,) * 2
        + (P(None, "mp"), P(None, "mp"), P("mp", None))
        + (slots,) * 3,
        out_specs=(rows,) * 4
        + (both,) * 4
        + (vector,) * 2
        + (both,) * 4
        + (vector,) * 2
        + (P(None, "mp"), P(None, "mp"), P("mp", None))
        + (slots,) * 3,
        check_vma=False,
    )
```

```python
import functools

import jax
import jax.numpy as jnp
import numpy as np
from jax import lax
from jax.experimental import pallas as pl
from jax.experimental.pallas import tpu as pltpu
from jax.sharding import PartitionSpec as P

ACT_LEN = 48
EPSILON = 1e-06
ROPE_BASE = 10000.0
HEADS = 4
HD = 256
PREF = 192
ACT = 12
ACT_PAD = 16
BLOCK = PREF + ACT_PAD
N_MP = 8
HALF_A = 96
HALF_B = BLOCK - HALF_A
HIDDEN_PAD = 896
VMEM_FEED = 50
bf16 = jnp.bfloat16
f32 = jnp.float32
ANY = pl.BlockSpec(memory_space=pl.ANY)
SMEM = pl.BlockSpec(memory_space=pltpu.SMEM)
VMEM = pl.BlockSpec(memory_space=pltpu.VMEM)
ARRIVALS = (
    ((0, 0), (0, 1)),
    ((1, 0), (1, 1)),
    ((3, 0), (3, 1)),
    ((4, 0), (4, 1)),
    ((5, 0), (7, 0)),
    ((2, 0), (5, 1)),
    ((2, 1), (7, 1)),
    ((6, 0),),
    ((6, 1),),
)
PARTS = tuple(part for parts in ARRIVALS for part in parts)
KEY_BLOCK = np.concatenate(
    [np.full(HALF_A, k) for k, _ in PARTS] + [np.full(ACT_PAD, k) for k, h in PARTS if h]
).astype(np.int32)
KEY_ROW = np.concatenate(
    [np.arange(HALF_A) + h * HALF_A for _, h in PARTS]
    + [np.arange(PREF, BLOCK) for _, h in PARTS if h]
).astype(np.int32)


ROW_PAIR, ACT_PAIR = 3 * PREF, 3 * ACT_PAD


def mp_swap(array, step):
    return lax.ppermute(array, "mp", [(i, i ^ step) for i in range(N_MP)])


def dp_swap(array, step):
    return lax.ppermute(array, "dp", [(i, i ^ step) for i in range(16)])


def yz_swap(array, step):
    return dp_swap(array, (step >> 2) * 8 + (step & 3) * 2)


def core_swap(array):
    return dp_swap(array, 1)


def where_parts(first, arrays, sizes):
    where = {}
    for i in range(arrays):
        at = 0
        for k, h in ARRIVALS[first + i]:
            where[k, h] = (i, at)
            at += sizes[h]
    return where


def fence_kernel(*refs):
    pass


def fence(array, *after):
    return pl.pallas_call(
        fence_kernel,
        in_specs=[pl.BlockSpec(memory_space=pl.ANY)] * (1 + len(after)),
        out_specs=pl.BlockSpec(memory_space=pl.ANY),
        out_shape=jax.ShapeDtypeStruct(array.shape, array.dtype),
        input_output_aliases={0: 0},
        cost_estimate=pl.CostEstimate(flops=0, bytes_accessed=0, transcendentals=0),
        name="fence",
    )(array, *after)


def join(*parts):
    return jnp.concatenate(parts, axis=0)


def add_low(*parts):
    total = parts[0].astype(f32)
    for part in parts[1:]:
        total = total + part.astype(f32)
    return total.astype(bf16)


def held(array, after):
    return fence(array, *after) if after else array


def sends_kernel(count, layout, *refs):
    for out, parts in zip(refs[len(refs) - len(layout) :], layout):
        at = 0
        for which, first, n in parts:
            out[at : at + n] = refs[which][first : first + n]
            at += n


def make_sends(arrays, layout, after=()):
    width = arrays[0].shape[1]
    low = lambda parts: jax.ShapeDtypeStruct((sum(n for _, _, n in parts), width), arrays[0].dtype)
    return pl.pallas_call(
        functools.partial(sends_kernel, len(arrays), layout),
        in_specs=[VMEM] * len(arrays) + [ANY] * len(after),
        out_specs=[VMEM] * len(layout),
        out_shape=[low(parts) for parts in layout],
        compiler_params=pltpu.CompilerParams(vmem_limit_bytes=16 * 1024 * 1024),
        cost_estimate=pl.CostEstimate(flops=0, bytes_accessed=0, transcendentals=0),
        name="sends",
    )(*arrays, *after)


class relay_stages:
    def __init__(self, own, na, swap):
        self.own, self.na, self.nb, self.swap = own, na, own.shape[0] - na, swap
        self.got, self.stage = (), 0

    def send(self, after=()):
        self.stage += 1
        na, nb = self.na, self.nb
        if self.stage == 1:
            self.own = held(self.own, after)
            sends = [self.own] * 3
            steps = (1, 3, 4)
        elif self.stage == 2:
            layout = (
                ((0, 0, na), (1, 0, na)),
                ((1, 0, na), (2, na, nb)),
                ((0, na, nb), (2, na, nb)),
            )
            sends = make_sends(self.got, layout, after)
            steps = (4, 1, 3)
        else:
            sends = make_sends(self.got[3:5], (((0, na, na),), ((1, na, nb),)), after)
            steps = (1, 3)
        self.flying = tuple(self.swap(x, step) for x, step in zip(sends, steps))
        return tuple(sends)

    def arrive(self):
        self.got += self.flying

    def finish(self):
        self.arrive()
        return (self.own, *self.got)


def relay_gather(own, na, swap, during=None, hold=None):
    nb = own.shape[0] - na
    during = during or (lambda stage, arrived, sends: ())
    hold = hold or {}
    own = held(own, hold.get(1, ()))
    s1, s3, s4 = swap(own, 1), swap(own, 3), swap(own, 4)
    after = during(1, (own,), (own,)) + hold.get(2, ())
    layout = (
        ((0, 0, na), (1, 0, na)),
        ((1, 0, na), (2, na, nb)),
        ((0, na, nb), (2, na, nb)),
    )
    sends = make_sends((s1, s3, s4), layout, after)
    zz, v1, v3 = swap(sends[0], 4), swap(sends[1], 1), swap(sends[2], 3)
    after = during(2, (s1, s3, s4), tuple(sends)) + hold.get(3, ())
    sends = make_sends((zz, v1), (((0, na, na),), ((1, na, nb),)), after)
    z2a, z2b = swap(sends[0], 1), swap(sends[1], 3)
    during(3, (zz, v1, v3), tuple(sends))
    return own, s1, s3, s4, zz, v1, v3, z2a, z2b


def relay_scatter(pa, pb, swap, hold=None, sent=None):
    na, nb = pa[0].shape[0], pb[0].shape[0]
    hold = hold or {}
    sent = {} if sent is None else sent
    get = lambda stage: hold[stage]() if stage in hold else ()
    after = get(1)
    sent[1] = (held(pa[6], after), held(pb[6], after))
    r1, r3 = swap(sent[1][0], 1), swap(sent[1][1], 3)
    p7a = add_low(pa[7], r1)
    p5b = add_low(pb[5], r3)
    after = get(2)
    sends = (join(pa[5], p7a), join(pa[2], p5b), join(pb[2], pb[7]))
    sent[2] = tuple(held(x, after) for x in sends)
    zz, v1, v3 = swap(sent[2][0], 4), swap(sent[2][1], 1), swap(sent[2][2], 3)
    p1 = join(add_low(pa[1], zz[:na]), add_low(pb[1], v3[:nb]))
    p3 = join(add_low(pa[3], zz[na:], v1[:na]), pb[3])
    p4 = join(pa[4], add_low(pb[4], v1[na:], v3[nb:]))
    after = get(3)
    sent[3] = tuple(held(x, after) for x in (p1, p3, p4))
    s1, s3, s4 = swap(sent[3][0], 1), swap(sent[3][1], 3), swap(sent[3][2], 4)
    return pa[0], pb[0], s1, s3, s4


def total_of(pieces):
    pa, pb, s1, s3, s4 = pieces
    na = pa.shape[0]
    total_a = pa.astype(f32) + s1[:na].astype(f32) + s3[:na].astype(f32) + s4[:na].astype(f32)
    total_b = pb.astype(f32) + s1[na:].astype(f32) + s3[na:].astype(f32) + s4[na:].astype(f32)
    return total_a, total_b


def ring_scatter(pieces, swap, after, sent):
    near = [join(pieces[j], pieces[j ^ 4]) for j in range(4)]
    near[1:] = [held(x, after) for x in near[1:]]
    sent += near[1:]
    total = near[0].astype(f32)
    for j in (1, 3, 2):
        total = total + swap(near[j], j).astype(f32)
    return total


def pair_sum(total, swap, after=()):
    half = total.shape[0] // 2
    return total[:half] + swap(held(total[half:].astype(bf16), after), 4).astype(f32)


def gather_direct(array, index, swap):
    pair = index & 4
    high = (index >> 2) & 1
    two = jnp.zeros((2,) + array.shape, array.dtype)
    two = lax.dynamic_update_index_in_dim(two, array, high, 0)
    two = lax.dynamic_update_index_in_dim(two, swap(array, 4), 1 - high, 0)
    ring = index & 3
    out = jnp.zeros((2, 4) + array.shape, array.dtype)
    out = lax.dynamic_update_index_in_dim(out, two, ring, 1)
    for step in (1, 3, 2):
        out = lax.dynamic_update_index_in_dim(out, swap(two, step), ring ^ step, 1)
    return out.reshape((8,) + array.shape)


def scatter_direct(pieces, index, swap):
    high = (index >> 2) & 1
    ring = index & 3
    quads = pieces.reshape((2, 4) + pieces.shape[1:])
    total = lax.dynamic_index_in_dim(quads, ring, 1, keepdims=False).astype(f32)
    for step in (1, 3, 2):
        piece = lax.dynamic_index_in_dim(quads, ring ^ step, 1, keepdims=False)
        total = total + swap(piece, step).astype(f32)
    mine = lax.dynamic_index_in_dim(total, high, 0, keepdims=False)
    theirs = lax.dynamic_index_in_dim(total, 1 - high, 0, keepdims=False)
    return mine + swap(theirs.astype(bf16), 4).astype(f32)


def place_kernel(cuts, sizes, index_ref, *refs):
    arrays, outs = refs[:9], refs[len(refs) - len(cuts) :]
    for (k, h), (i, at) in where_parts(0, 9, sizes).items():
        for out, (which, first, n, width) in zip(outs, cuts):
            if which == h:
                rows = slice(at + first, at + first + n)
                out[index_ref[0] ^ k] = arrays[i][rows, :, :width]


def place(arrays, na, cuts, index, after):
    rows, columns = arrays[0].shape
    eights = [x.reshape(x.shape[0] // 8, 8, columns) for x in arrays]
    sizes = (na // 8, (rows - na) // 8)
    return pl.pallas_call(
        functools.partial(place_kernel, cuts, sizes),
        in_specs=[SMEM] + [VMEM] * 9 + [ANY] * len(after),
        out_specs=[VMEM] * len(cuts),
        out_shape=[jax.ShapeDtypeStruct((8, n, 8, width), bf16) for _, _, n, width in cuts],
        compiler_params=pltpu.CompilerParams(vmem_limit_bytes=24 * 1024 * 1024),
        name="place",
    )(index.reshape(1), *eights, *after)


def interleave_kernel(cuts, core_ref, *refs):
    count = 1 + max(which for which, _, _, _, _ in cuts)
    mine, theirs, outs = refs[:count], refs[count : 2 * count], refs[len(refs) - len(cuts) :]
    core = core_ref[0]
    for out, (which, first, n, column, width) in zip(outs, cuts):
        columns = slice(column, column + width)
        for i in range(8):
            out[i, core] = mine[which][i, first : first + n, :, columns]
            out[i, 1 - core] = theirs[which][i, first : first + n, :, columns]


def interleave(mine, theirs, cuts, core, after=()):
    outs = pl.pallas_call(
        functools.partial(interleave_kernel, cuts),
        in_specs=[SMEM] + [VMEM] * (2 * len(mine)) + [ANY] * len(after),
        out_specs=[VMEM] * len(cuts),
        out_shape=[jax.ShapeDtypeStruct((8, 2, n, 8, width), bf16) for _, _, n, _, width in cuts],
        compiler_params=pltpu.CompilerParams(vmem_limit_bytes=40 * 1024 * 1024),
        name="interleave",
    )(core.reshape(1), *mine, *theirs, *after)
    return [x.reshape(-1, x.shape[-1]) for x in outs]


def gain_rows(block):
    pick = lax.broadcasted_iota(jnp.int32, (ACT_PAD, 128), 0)
    pick = (pick == lax.broadcasted_iota(jnp.int32, (ACT_PAD, 128), 1)).astype(bf16)
    turned = dot_t(pick, block)
    return turned[0:1], turned[1:2]


def keys_kernel(*refs):
    rows, (gain_d, gain_a, weight_d, weight_a, cosine, sine) = refs[:9], refs[9:15]
    normed_d, normed_a, keys, values = refs[-4:]
    gain_d, gain_a = gain_rows(gain_d[...])[0], gain_rows(gain_a[...])[0]
    width = weight_a.shape[0]
    prefix, action = [], []
    for i, parts in enumerate(ARRIVALS):
        at = 0
        for _, h in parts:
            prefix.append(rows[i][at : at + HALF_A])
            at += HALF_A
            if h:
                action.append(rows[i][at : at + ACT_PAD, :width])
                at += ACT_PAD
    x = join(*prefix).astype(f32)
    low_d = (x * inverse_rms(x) * gain_d).astype(bf16)
    x = join(*action).astype(f32)
    low_a = (x * inverse_rms(x) * gain_a).astype(bf16)
    normed_d[:PREF] = low_d[:PREF]
    normed_a[:ACT_PAD] = low_a[:ACT_PAD]
    normed_d[PREF:] = low_d[ROW_PAIR : ROW_PAIR + PREF]
    normed_a[ACT_PAD:] = low_a[ACT_PAIR : ACT_PAIR + ACT_PAD]
    raw = join(dot(low_d, weight_d[...]), dot(low_a, weight_a[...]))
    keys[...] = rotate(raw[:, :HD], cosine[...], sine[...]).astype(bf16)
    values[...] = raw[:, HD:].astype(bf16)


def keys_of(rows, gain_d, gain_a, weight_d, weight_a, cosine, sine, after):
    width_d, width_a = gain_d.shape[0], gain_a.shape[0]
    count = cosine.shape[0]
    shape = lambda *dims: jax.ShapeDtypeStruct(dims, bf16)
    given = [*rows, gain_d, gain_a, weight_d, weight_a, cosine, sine]
    return pl.pallas_call(
        keys_kernel,
        in_specs=[VMEM] * len(given) + [ANY] * len(after),
        out_specs=[VMEM] * 4,
        out_shape=[
            shape(2 * PREF, width_d),
            shape(2 * ACT_PAD, width_a),
            shape(count, HD),
            shape(count, HD),
        ],
        compiler_params=pltpu.CompilerParams(vmem_limit_bytes=48 * 1024 * 1024),
        cost_estimate=pl.CostEstimate(
            flops=4 * count * width_d * HD, bytes_accessed=8 * 1024 * 1024, transcendentals=count
        ),
        name="keys_of",
    )(*given, *after)


def gelu_parts(gate):
    c0 = 0.7978845608028654
    c1 = 0.044715
    square = gate * gate
    tanh = jnp.tanh(c0 * gate * (1.0 + c1 * square))
    half = 0.5 * (1.0 + tanh)
    slope = half + 0.5 * gate * (1.0 - tanh * tanh) * c0 * (1.0 + 3.0 * c1 * square)
    return gate * half, slope


def feed_block(rows, seed, gate_weight, up_weight, down_weight, valid):
    into, out_of = (dot_t, dot) if valid is None else (dot, dot_t)
    gate = into(rows, gate_weight)
    up = into(rows, up_weight)
    active, slope = gelu_parts(gate)
    product_delta = dot_t(seed, down_weight)
    if valid is not None:
        active = active * valid
        product_delta = product_delta * valid
    product = (active * up).astype(bf16)
    gate_delta = (product_delta * up * slope).astype(bf16)
    up_delta = (product_delta * active).astype(bf16)
    rows_delta = out_of(gate_delta, gate_weight) + out_of(up_delta, up_weight)
    return product, gate_delta, up_delta, rows_delta.astype(bf16)


def feed_kernel(layout, *refs):
    arrays = 1 + max(i for parts in layout for i, _ in parts)
    rows_refs, seed_refs, refs = refs[:arrays], refs[arrays : 2 * arrays], refs[2 * arrays :]
    gate_ref, up_ref, down_ref = refs[:3]
    action_gate_ref, action_up_ref, action_down_ref, valid_ref = refs[3:7]
    count = len(layout)
    outs = refs[-(2 * count + 8) :]
    products, deltas, kept_rows, kept_seeds = outs[:4]
    action_products, action_deltas, action_rows, action_seeds = outs[4:8]
    width = action_gate_ref.shape[0]
    rest = PREF - HALF_A

    def prefix_of(blocks):
        parts = []
        for (ia, a), (ib, b) in layout:
            parts += [blocks[ia][a : a + HALF_A], blocks[ib][b : b + rest]]
        return join(*parts)

    def action_of(blocks):
        parts = []
        for _, (ib, b) in layout:
            parts.append(blocks[ib][b + rest : b + HALF_B, :width])
        return join(*parts) if count > 1 else parts[0]

    rows, seed = prefix_of(rows_refs), prefix_of(seed_refs)
    product, gate_delta, up_delta, rows_delta = feed_block(
        rows, seed, gate_ref[...], up_ref[...], down_ref[...], None
    )
    hidden = product.shape[1]
    spare = jnp.zeros((count * PREF, HIDDEN_PAD - hidden), bf16)
    products[:, :hidden] = product
    products[:, hidden:] = spare
    deltas[:, :hidden] = gate_delta
    deltas[:, hidden:HIDDEN_PAD] = spare
    deltas[:, HIDDEN_PAD : HIDDEN_PAD + hidden] = up_delta
    deltas[:, HIDDEN_PAD + hidden :] = spare
    kept_rows[...] = rows
    kept_seeds[...] = seed
    rows, seed = action_of(rows_refs), action_of(seed_refs)
    product, gate_delta, up_delta, action_rows_delta = feed_block(
        rows,
        seed,
        action_gate_ref[...],
        action_up_ref[...],
        action_down_ref[...],
        valid_ref[...],
    )
    slots = gate_delta.shape[1]
    action_products[...] = product
    action_deltas[:, :slots] = gate_delta
    action_deltas[:, slots:] = up_delta
    action_rows[...] = rows
    action_seeds[...] = seed
    blank = jnp.zeros((ACT_PAD, rows_delta.shape[1] - width), bf16)
    for i in range(count):
        a, b, c = i * PREF, i * PREF + HALF_A, (i + 1) * PREF
        extra = slice(i * ACT_PAD, (i + 1) * ACT_PAD)
        ref_a, ref_b = outs[8 + 2 * i : 10 + 2 * i]
        ref_a[...] = rows_delta[a:b]
        ref_b[:rest] = rows_delta[b:c]
        ref_b[rest:, :width] = action_rows_delta[extra]
        ref_b[rest:, width:] = blank


def feed(arrays, seeds, weights, layout, base, kept, after):
    count = len(layout)
    width = arrays[0].shape[1]
    hidden = weights[0].shape[0]
    action_width, slots = weights[3].shape
    once = pl.Buffered(1)
    at = base // count

    def whole(array):
        return pl.BlockSpec(array.shape, lambda i: (0, 0), pipeline_mode=once)

    def part(size, columns):
        return (
            jax.ShapeDtypeStruct((N_MP * size, columns), bf16),
            pl.BlockSpec((count * size, columns), lambda i: (at, 0), pipeline_mode=once),
        )

    def own(size):
        return (
            jax.ShapeDtypeStruct((size, width), bf16),
            pl.BlockSpec((size, width), lambda i: (0, 0), pipeline_mode=once),
        )

    outs = [
        part(PREF, HIDDEN_PAD),
        part(PREF, 2 * HIDDEN_PAD),
        part(PREF, width),
        part(PREF, width),
        part(ACT_PAD, slots),
        part(ACT_PAD, 2 * slots),
        part(ACT_PAD, action_width),
        part(ACT_PAD, action_width),
    ] + [own(HALF_A), own(HALF_B)] * count
    reused = [] if kept is None else list(kept)
    given = [*arrays, *seeds]
    placed = len(given) + len(weights)
    results = pl.pallas_call(
        functools.partial(feed_kernel, layout),
        grid=(1,),
        in_specs=[whole(x) for x in given]
        + [VMEM] * len(weights)
        + [ANY] * (len(reused) + len(after)),
        out_shape=[shape for shape, _ in outs],
        out_specs=[spec for _, spec in outs],
        input_output_aliases={placed + i: i for i in range(len(reused))},
        compiler_params=pltpu.CompilerParams(
            dimension_semantics=("arbitrary",), vmem_limit_bytes=VMEM_FEED * 1024 * 1024
        ),
        cost_estimate=pl.CostEstimate(
            flops=10 * count * (PREF * width * hidden + ACT_PAD * action_width * slots),
            bytes_accessed=6 * (width * hidden + action_width * slots),
            transcendentals=count * PREF * hidden,
        ),
        name="feed",
    )(*given, *weights, *reused, *after)
    blocks = [results[8 + 2 * i : 10 + 2 * i] for i in range(count)]
    return blocks, results[:8]


def see(own_ref, key_ref):
    own, key = own_ref[...], key_ref[...]
    return (own[:, 0:1] == key[0:1]) | (own[:, 1:2] == key[1:2])


def attend_kernel(*refs):
    (normed_d, normed_a, x_d, x_a, wq_d, wq_a, wo_m, wo_e, wo_a) = refs[:9]
    (gain_d, gain_a, cosine, sine, own_codes, key_codes) = refs[9:15]
    keys, values = refs[15][...], refs[16][...]
    (queries, context, tops, totals, hidden_d, hidden_a, block) = refs[-7:]
    gain_d, gain_a = gain_rows(gain_d[...])[1], gain_rows(gain_a[...])[1]
    raw = join(dot(normed_d[:PREF], wq_d[...]), dot(normed_a[:ACT_PAD], wq_a[...]))
    visible = see(own_codes, key_codes)
    cos, sin = cosine[...], sine[...]
    heads = []
    for h in range(HEADS):
        rows = slice(h * BLOCK, (h + 1) * BLOCK)
        query = (rotate(raw[:, h * HD : (h + 1) * HD], cos, sin) * HD**-0.5).astype(bf16)
        queries[rows] = query
        scores = jnp.where(visible, dot_t(query, keys), -1e30)
        top = jnp.max(scores, axis=1, keepdims=True)
        shifted = jnp.exp(scores - top)
        total = jnp.sum(shifted, axis=1, keepdims=True)
        tops[rows] = top
        totals[rows] = total
        heads.append(dot((shifted / total).astype(bf16), values).astype(bf16))
    mixed = jnp.concatenate(heads, axis=1)
    context[...] = mixed
    main, width_d, width_a = wo_m.shape[1], x_d.shape[1], x_a.shape[1]
    low_d, low_a = mixed[:PREF], mixed[PREF:]
    state = x_d[...].astype(f32) + jnp.concatenate(
        [dot(low_d, wo_m[...]), dot(low_d, wo_e[...])], axis=1
    )
    hidden_d[...] = state
    second_d = (state * inverse_rms(state) * gain_d).astype(bf16)
    real = lax.broadcasted_iota(jnp.int32, (ACT_PAD, width_a), 0) < ACT
    state = jnp.where(real, x_a[...].astype(f32) + dot(low_a, wo_a[...]), 0.0)
    hidden_a[...] = state
    second_a = (state * inverse_rms(state) * gain_a).astype(bf16)
    block[:PREF] = second_d
    block[PREF:, :width_a] = second_a
    block[PREF:, width_a:] = jnp.zeros((ACT_PAD, width_d - width_a), bf16)


def attend(*given, after):
    x_d, x_a = given[2:4]
    width_d, width_a = x_d.shape[1], x_a.shape[1]
    shape = jax.ShapeDtypeStruct
    stacked = HEADS * BLOCK
    return pl.pallas_call(
        attend_kernel,
        in_specs=[VMEM] * len(given) + [ANY] * len(after),
        out_specs=[VMEM] * 7,
        out_shape=[
            shape((stacked, HD), bf16),
            shape((BLOCK, HEADS * HD), bf16),
            shape((stacked, 1), f32),
            shape((stacked, 1), f32),
            shape((PREF, width_d), f32),
            shape((ACT_PAD, width_a), f32),
            shape((BLOCK, width_d), bf16),
        ],
        compiler_params=pltpu.CompilerParams(vmem_limit_bytes=50 * 1024 * 1024),
        cost_estimate=pl.CostEstimate(
            flops=4 * BLOCK * HEADS * HD * (N_MP * BLOCK + width_d),
            bytes_accessed=4 * 1024 * 1024 * 5,
            transcendentals=stacked * N_MP * BLOCK,
        ),
        name="attend",
    )(*given, *after)


def attend_back_kernel(*refs):
    pieces = refs[:5]
    (hidden_d, hidden_a, cotangent_d, cotangent_a, share, gain_d, gain_a) = refs[5:12]
    (wo_m, wo_e, wo_a, queries, tops, totals, cosine, sine, own_codes, key_codes) = refs[12:22]
    keys, values = refs[22][...], refs[23][...]
    outs = refs[-(6 + len(PARTS)) :]
    (hidden_delta_d, hidden_delta_a, low, terms_d, terms_a, query_delta) = outs[:6]
    kv_deltas = outs[6:]
    gain_d, gain_a = gain_rows(gain_d[...])[1], gain_rows(gain_a[...])[1]
    delta = join(*total_of([piece[...] for piece in pieces]))
    width_d, width_a = hidden_d.shape[1], hidden_a.shape[1]
    lows = []
    for rows, state_ref, cotangent, gain, out, terms in (
        (slice(0, PREF), hidden_d, cotangent_d, gain_d, hidden_delta_d, terms_d),
        (slice(PREF, BLOCK), hidden_a, cotangent_a, gain_a, hidden_delta_a, terms_a),
    ):
        state = state_ref[...]
        change = delta[rows, : state.shape[1]]
        scale = inverse_rms(state)
        seed = cotangent[...].astype(f32) * share[rows]
        back = seed + normalize_back(state, scale, gain, change)
        out[...] = back
        terms[...] = (change * state * scale).astype(bf16)
        lows.append(back.astype(bf16))
    low_d, low_a = lows
    low[:PREF] = low_d
    low[PREF:, :width_a] = low_a
    low[PREF:, width_a:] = jnp.zeros((ACT_PAD, width_d - width_a), bf16)
    main = wo_m.shape[1]
    context_delta = join(
        dot_t(low_d[:, :main], wo_m[...]) + dot_t(low_d[:, main:], wo_e[...]),
        dot_t(low_a, wo_a[...]),
    ).astype(bf16)
    visible = see(own_codes, key_codes)
    cos, sin = cosine[...], sine[...]
    keys_delta, values_delta = None, None
    for h in range(HEADS):
        rows = slice(h * BLOCK, (h + 1) * BLOCK)
        query = queries[rows]
        change = context_delta[:, h * HD : (h + 1) * HD]
        scores = jnp.where(visible, dot_t(query, keys), -1e30)
        probs = jnp.exp(scores - tops[rows]) / totals[rows]
        probs_delta = dot_t(change, values)
        row_dot = jnp.sum(probs * probs_delta, axis=1, keepdims=True)
        score_delta = (probs * (probs_delta - row_dot)).astype(bf16)
        turned = unrotate(dot(score_delta, keys), cos, sin) * HD**-0.5
        query_delta[:, h * HD : (h + 1) * HD] = turned.astype(bf16)
        key_part = t_dot(score_delta, query)
        value_part = t_dot(probs.astype(bf16), change)
        keys_delta = key_part if h == 0 else keys_delta + key_part
        values_delta = value_part if h == 0 else values_delta + value_part
    at, extra = 0, len(PARTS) * HALF_A
    for (_, half), out in zip(PARTS, kv_deltas):
        for columns, change in ((slice(0, HD), keys_delta), (slice(HD, 2 * HD), values_delta)):
            out[:HALF_A, columns] = change[at : at + HALF_A].astype(bf16)
            if half:
                out[HALF_A:, columns] = change[extra : extra + ACT_PAD].astype(bf16)
        at += HALF_A
        extra += half * ACT_PAD


def attend_back(*given, after):
    hidden_d, hidden_a = given[5:7]
    width_d, width_a = hidden_d.shape[1], hidden_a.shape[1]
    shape = jax.ShapeDtypeStruct
    stacked = HEADS * BLOCK
    outs = pl.pallas_call(
        attend_back_kernel,
        in_specs=[VMEM] * len(given) + [ANY] * len(after),
        out_specs=[VMEM] * (6 + len(PARTS)),
        out_shape=[
            shape((PREF, width_d), f32),
            shape((ACT_PAD, width_a), f32),
            shape((BLOCK, width_d), bf16),
            shape((PREF, width_d), bf16),
            shape((ACT_PAD, width_a), bf16),
            shape((BLOCK, HEADS * HD), bf16),
        ]
        + [shape(((HALF_A, HALF_B)[half], 2 * HD), bf16) for _, half in PARTS],
        compiler_params=pltpu.CompilerParams(vmem_limit_bytes=50 * 1024 * 1024),
        cost_estimate=pl.CostEstimate(
            flops=2 * BLOCK * HEADS * HD, bytes_accessed=4 * BLOCK, transcendentals=stacked
        ),
        name="attend_back",
    )(*given, *after)
    kv_deltas = dict(zip(PARTS, outs[6:]))
    pa = {k: kv_deltas[k, 0] for k in range(8)}
    pb = {k: kv_deltas[k, 1] for k in range(8)}
    return outs[:6], pa, pb


def theirs_kernel(cuts, place_ref, *refs):
    out = refs[-1]
    core = place_ref[1]
    for ref, (row, n, source, column, width) in zip(refs, cuts):
        out[:, row : row + n, :, column : column + width] = ref[
            1 - core, :, :, :, source : source + width
        ]


def near_kernel(cuts, place_ref, *refs):
    got, outs = refs[len(cuts)], refs[-4:]
    mp, core = place_ref[0], place_ref[1]
    for step, out in zip((0, 1, 3, 2), outs):
        for pair in range(2):
            block = mp ^ step ^ (4 * pair)
            base = pair * got.shape[1]
            for ref, (row, n, source, column, width) in zip(refs, cuts):
                columns = slice(column, column + width)
                mine = ref[core, block, :, :, source : source + width].astype(f32)
                total = mine + got[block, row : row + n, :, columns].astype(f32)
                out[base + row : base + row + n, :, columns] = total.astype(bf16)


def sum_weights(grads, cuts, columns, place, sent, got, after, before_last, last_sent):
    views = [g.reshape(2, 8, -1, 8, g.shape[1]) for g in grads]
    eights = max(row + n for row, n, _, _, _ in cuts)
    params = pltpu.CompilerParams(vmem_limit_bytes=44 * 1024 * 1024)
    cost = pl.CostEstimate(flops=0, bytes_accessed=0, transcendentals=0)
    low = lambda *dims: jax.ShapeDtypeStruct(dims, bf16)
    theirs = pl.pallas_call(
        functools.partial(theirs_kernel, cuts),
        in_specs=[SMEM] + [VMEM] * len(views),
        out_specs=VMEM,
        out_shape=low(8, eights, 8, columns),
        compiler_params=params,
        cost_estimate=cost,
        name="theirs",
    )(place, *views)
    near = pl.pallas_call(
        functools.partial(near_kernel, cuts),
        in_specs=[SMEM] + [VMEM] * (len(views) + 1) + [ANY] * len(after),
        out_specs=[VMEM] * 4,
        out_shape=[low(2 * eights, 8, columns)] * 4,
        compiler_params=params,
        cost_estimate=cost,
        name="near",
    )(place, *views, core_swap(theirs), *after)
    near = [x.reshape(16 * eights, columns) for x in near]
    sent += near[1:]
    total = near[0].astype(f32)
    for step, x in zip((1, 3, 2), near[1:]):
        got.append(mp_swap(x, step))
        total = total + got[-1].astype(f32)
    half = 8 * eights
    last_sent.append(held(total[half:].astype(bf16), before_last))
    return (total[:half] + mp_swap(last_sent[-1], 4).astype(f32)).astype(bf16)


def pad_action(rows):
    return jnp.pad(rows, ((0, ACT_PAD - ACT), (0, 0)))


def widen(rows, width):
    return jnp.pad(rows, ((0, 0), (0, width - rows.shape[1])))


def block_of(prefix_rows, action_rows):
    return join(prefix_rows, widen(action_rows, prefix_rows.shape[1]))


def order_matrix(size, rows):
    d = jnp.arange(size, dtype=jnp.int32)
    r = d % rows
    mp = (d // rows) % 8
    dp = d // (8 * rows)
    place = (dp % 2) * (size // 2) + mp * (8 * rows) + (dp // 2) * rows + r
    return (place[:, None] == jnp.arange(size, dtype=jnp.int32)[None, :]).astype(bf16)


def dot(a, b):
    return jnp.dot(a, b, preferred_element_type=f32)


def dot_t(a, b):
    return lax.dot_general(a, b, (((1,), (1,)), ((), ())), preferred_element_type=f32)


def t_dot(a, b):
    return lax.dot_general(a, b, (((0,), (0,)), ((), ())), preferred_element_type=f32)


def inverse_rms(rows):
    return lax.rsqrt(jnp.mean(rows * rows, axis=-1, keepdims=True) + EPSILON)


def normalize_back(rows, scale, gain, delta):
    a = delta * gain
    return scale * (a - rows * (scale * scale) * jnp.mean(a * rows, axis=-1, keepdims=True))


def rotate(rows, cosine, sine):
    half = HD // 2
    first, second = rows[:, :half], rows[:, half:]
    return jnp.concatenate(
        [first * cosine - second * sine, second * cosine + first * sine], axis=1
    )


def unrotate(rows, cosine, sine):
    return rotate(rows, cosine, -sine)


def angle_tables(place):
    half = HD // 2
    frequency = ROPE_BASE ** (-jnp.arange(half, dtype=f32) / half)
    angles = place.astype(f32)[:, None] * frequency[None, :]
    return jnp.cos(angles), jnp.sin(angles)


def on_device(
    prefix_input,
    action_input,
    prefix_cotangent,
    action_cotangent,
    prefix_lengths,
    mixture,
    cut_points,
    prefix_query,
    prefix_key,
    prefix_value,
    prefix_out,
    prefix_first_gain,
    prefix_second_gain,
    action_query,
    action_key,
    action_value,
    action_out,
    action_first_gain,
    action_second_gain,
    prefix_gate,
    prefix_up,
    prefix_down,
    action_gate,
    action_up,
    action_down,
):
    mp = lax.axis_index("mp")
    dp = lax.axis_index("dp")
    core = dp & 1
    yz = (dp >> 3) * 4 + ((dp >> 1) & 3)
    D = prefix_input.shape[2]
    DA = action_input.shape[2]

    def column_block(first, second):
        return jnp.pad(jnp.stack([first, second], axis=1), ((0, 0), (0, 126)))

    pack_d = jnp.concatenate(
        [
            prefix_key,
            prefix_value,
            column_block(prefix_first_gain, prefix_second_gain),
            prefix_query,
        ],
        axis=1,
    )
    wide = pack_d.shape[1]
    pack = jnp.concatenate(
        [
            pack_d[:8],
            action_key,
            action_value,
            column_block(action_first_gain, action_second_gain),
            action_query,
            action_out,
            prefix_out,
            jnp.pad(pack_d[8:].reshape(8, wide // 8), ((0, 0), (0, 48))),
        ],
        axis=1,
    )
    lengths = prefix_lengths[0]
    first_length = lengths[0]

    def tables(source, row):
        is_action = row >= PREF
        prefix_row = source * PREF + row
        prefix_item = (prefix_row >= first_length).astype(jnp.int32)
        prefix_place = prefix_row - jnp.where(prefix_item == 1, first_length, 0)
        action_row = source * ACT + row - PREF
        action_item = (action_row >= ACT_LEN).astype(jnp.int32)
        action_place = jnp.where(action_item == 1, lengths[1], first_length) + action_row % ACT_LEN
        action_item = jnp.where(row - PREF < ACT, action_item, 2)
        item = jnp.where(is_action, action_item, prefix_item)
        place = jnp.where(is_action, action_place, prefix_place)
        return item, place, is_action

    own_item, own_place, own_is_action = tables(mp, jnp.arange(BLOCK, dtype=jnp.int32))
    key_item, key_place, key_is_action = tables(jnp.asarray(KEY_BLOCK) ^ mp, jnp.asarray(KEY_ROW))
    key_cos, key_sin = angle_tables(key_place)
    own_codes = jnp.stack([own_item, jnp.where(own_is_action, own_item, -2)], axis=1)
    key_codes = jnp.stack(
        [jnp.where(key_is_action, -1, key_item), jnp.where(key_is_action, key_item, -1)], axis=0
    )
    own_cos, own_sin = angle_tables(own_place)

    share = mixture[0].astype(f32) / 32.0
    row_share = jnp.where(own_item == 1, share[1], share[0])[:, None]
    cotangent_a = pad_action(action_cotangent[0])
    prefix_seed = prefix_cotangent[0].astype(f32) * row_share[:PREF]
    action_seed = cotangent_a.astype(f32) * row_share[PREF:]
    seed_block = block_of(prefix_seed.astype(bf16), action_seed.astype(bf16))

    near = gather_direct(pack, mp, mp_swap)
    last_row = near[:, :, pack.shape[1] - 256 : pack.shape[1] - 48].reshape(8, 1, wide)
    near_d = jnp.concatenate([near[:, :, :wide], last_row], axis=1).reshape(72, wide)
    near_a = near[:, :, wide : pack.shape[1] - 256].reshape(64, -1)
    edge = near_a[:, 2688 + 1024 :]
    kv_a = widen(jnp.concatenate([near_a[:, :640], edge], axis=1), 1024)
    pack_a = join(near_a[:, 640:1664], near_a[:, 1664:2688], kv_a)
    pack_b = join(near_d[:, 640:], near_a[:, 2688 : 2688 + 1024], widen(near_d[:, :640], 1024))
    arrived = {}

    def note(name):
        def during(stage, blocks, sends):
            arrived[name, stage] = blocks
            arrived[name, "sends", stage] = sends
            return ()

        return during

    own_action = pad_action(action_input[0])
    own_block = block_of(prefix_input[0], own_action)
    own_block = fence(own_block, near)
    pack = join(pack_a, pack_b)
    gather = relay_stages(pack, pack_a.shape[0], yz_swap)
    other = relay_stages(own_block, HALF_A, mp_swap)
    gather.send()
    other.send()
    gather.arrive()
    other.arrive()
    sends = gather.send(other.got)
    other.send(sends)
    gather.arrive()
    other.arrive()
    sends = gather.send()
    row_sends = other.send(sends)
    pieces = gather.finish()
    x_rows = other.finish()
    cuts = ((0, 16, 8, 768), (1, 17, 9, 640), (0, 0, 16, 1024), (1, 0, 17, 1024))
    mine = place(pieces, pack_a.shape[0], cuts, yz, x_rows[6:])
    theirs = [core_swap(x) for x in mine]
    cuts = ((0, 0, 8, 0, 512), (0, 0, 8, 512, 128), (0, 0, 8, 640, 128))
    cuts += ((1, 0, 9, 0, 512), (1, 0, 9, 512, 128))
    wkv_a, gains_a, wo_e, wkv_d, gains_d = interleave(mine[:2], theirs[:2], cuts, core)
    normed_d, normed_a, keys, values = keys_of(
        x_rows,
        gains_d,
        gains_a,
        wkv_d,
        wkv_a,
        key_cos,
        key_sin,
        (),
    )
    seeds = relay_stages(seed_block, HALF_A, mp_swap)
    seed_sends = seeds.send((keys,))
    cuts = ((0, 0, 8, 0, 1024), (0, 8, 8, 0, 1024), (1, 0, 9, 0, 1024), (1, 9, 8, 0, 1024))
    wq_a, wo_a, wq_d, wo_m = interleave(mine[2:], theirs[2:], cuts, core, seed_sends[:1])
    x_d, x_a = prefix_input[0].astype(f32), own_action.astype(f32)
    rms_d, rms_a = inverse_rms(x_d), inverse_rms(x_a)
    queries, context, tops, totals, hidden_d, hidden_a, second_block = attend(
        normed_d,
        normed_a,
        prefix_input[0],
        own_action,
        wq_d,
        wq_a,
        wo_m,
        wo_e,
        wo_a,
        gains_d,
        gains_a,
        own_cos,
        own_sin,
        own_codes,
        key_codes,
        keys,
        values,
        after=(),
    )

    slots = action_gate.shape[2]
    cut_pair = lax.dynamic_slice_in_dim(cut_points, mp, 2)
    valid = (jnp.arange(slots, dtype=jnp.int32) < cut_pair[1] - cut_pair[0]).astype(f32)[None, :]
    weights = (prefix_gate.T, prefix_up.T, prefix_down)
    weights += (action_gate[0], action_up[0], action_down[0], valid)
    kept = None
    results = {}

    def run(arrays, first, blocks, base, after):
        nonlocal kept
        where = where_parts(first, len(arrays), (HALF_A, HALF_B))
        layout = tuple((where[k, 0], where[k, 1]) for k in blocks)
        some = (seeds.own, *seeds.got)[first : first + len(arrays)]
        done, kept = feed(arrays, some, weights, layout, base, kept, after)
        results.update(zip(blocks, done))
        return (done[0][0],)

    def feed_during(stage, arrays, sends):
        if stage < 3:
            seeds.arrive()
            seeds.send(sends)
        if stage == 3:
            return ()
        first, blocks, base = {1: (0, (0,), 3), 2: (1, (1, 3, 4), 0)}[stage]
        return run(arrays, first, blocks, base, sends)

    arrays = relay_gather(second_block, HALF_A, mp_swap, feed_during)
    seeds.arrive()
    run(arrays[4:], 4, (2, 5, 7, 6), 4, ())
    product_d, deltas_d, rows_d, seeds_d, product_a, deltas_a, rows_a, seeds_a = kept

    grads = (
        t_dot(deltas_d, rows_d),
        t_dot(product_d, seeds_d),
        t_dot(rows_a, deltas_a),
        t_dot(product_a, seeds_a),
    )
    hidden = prefix_down.shape[0]
    grads = tuple(g.astype(bf16) for g in grads)
    pa = {k: v[0] for k, v in results.items()}
    pb = {k: v[1] for k, v in results.items()}
    delta_sent = {}
    delta_pieces = relay_scatter(pa, pb, mp_swap, sent=delta_sent)
    grads = grads[:3] + (fence(grads[3], *delta_sent[3]),)
    grads = tuple(lax.psum(g, "dp") for g in grads)
    finished = (
        grads[0][:hidden].astype(f32),
        grads[0][HIDDEN_PAD : HIDDEN_PAD + hidden].astype(f32),
        grads[1][:hidden].astype(f32),
        grads[2][:, :slots].astype(f32),
        grads[2][:, slots:].astype(f32),
        grads[3].astype(f32),
    )

    (hidden_delta_d, hidden_delta_a, low, terms_d, terms_a, query_delta), pa, pb = attend_back(
        *delta_pieces,
        hidden_d,
        hidden_a,
        prefix_cotangent[0],
        cotangent_a,
        row_share,
        gains_d,
        gains_a,
        wo_m,
        wo_e,
        wo_a,
        queries,
        tops,
        totals,
        own_cos,
        own_sin,
        own_codes,
        key_codes,
        keys,
        values,
        after=(),
    )
    low_d, low_a = low[:PREF], low[PREF:, :DA]

    kv_near = [join(pa[k], pb[k], pa[k ^ 4], pb[k ^ 4]) for k in range(4)]
    kv_part = kv_near[0].astype(f32)
    for k in (1, 3, 2):
        kv_part = kv_part + mp_swap(kv_near[k], k).astype(f32)
    pair = lambda table: join(
        own_cos if table is key_cos else own_sin,
        table[ROW_PAIR : ROW_PAIR + PREF],
        table[len(PARTS) * HALF_A + ACT_PAIR : len(PARTS) * HALF_A + ACT_PAIR + ACT_PAD],
    )
    kv_turned = jnp.concatenate(
        [unrotate(kv_part[:, :HD], pair(key_cos), pair(key_sin)), kv_part[:, HD:]], axis=1
    )
    kv_turned_low = kv_turned.astype(bf16)
    kv_rows_d = join(kv_turned_low[:PREF], kv_turned_low[BLOCK : BLOCK + PREF])
    kv_rows_a = join(kv_turned_low[PREF:BLOCK], kv_turned_low[BLOCK + PREF :])

    order_d, order_a = order_matrix(D, 9), order_matrix(DA, 8)
    turned_d = dot(normed_d, order_d).astype(bf16)
    turned_a = dot(normed_a, order_a).astype(bf16)
    turned_context = dot(context, order_a).astype(bf16)
    second_term_d = t_dot(dot(terms_d, order_d).astype(bf16), jnp.ones((PREF, 256), bf16))
    second_term_a = t_dot(dot(terms_a, order_a).astype(bf16), jnp.ones((ACT_PAD, 128), bf16))
    out_grad_d = t_dot(turned_context[:PREF], low_d).astype(bf16)
    out_grad_a = t_dot(turned_context[PREF:], low_a).astype(bf16)
    q_grad_d = t_dot(turned_d[:PREF], query_delta[:PREF]).astype(bf16)
    q_grad_a = t_dot(turned_a[:ACT_PAD], query_delta[PREF:]).astype(bf16)
    here = jnp.stack([mp, core])
    cuts = (
        (0, 8, 0, 0, 1024),
        (8, 8, 0, 0, 1024),
        (16, 9, 0, 0, 1024),
        (25, 8, 0, 0, 1024),
    )
    qo_sent, kv_sent, got, last_sent = [], [], [], []
    qo_grads = (q_grad_a, out_grad_a, q_grad_d, out_grad_d)
    qo = sum_weights(qo_grads, cuts, 1024, here, qo_sent, got, (), grads[:1], last_sent)
    kv_grad_d = t_dot(turned_d, kv_rows_d).astype(bf16)
    kv_grad_a = t_dot(turned_a, kv_rows_a).astype(bf16)
    cuts = (
        (0, 8, 0, 0, 512),
        (0, 8, 0, 512, 128),
        (0, 8, 1024, 640, 128),
        (8, 9, 0, 0, 512),
        (8, 9, 0, 512, 256),
    )
    kv_grads = (
        kv_grad_a,
        second_term_a.astype(bf16),
        out_grad_d,
        kv_grad_d,
        second_term_d.astype(bf16),
    )
    kv = sum_weights(kv_grads, cuts, 768, here, kv_sent, got, qo_sent, grads[:1], last_sent)
    kv_a, kv_d = kv[:64], kv[64:, :640]
    qo_a, qo_b = qo[:128], qo[128:]
    kv_other = mp_swap(held(kv_part[BLOCK:].astype(bf16), tuple(kv_sent)), 4)
    kv_sum = kv_part[:BLOCK] + kv_other.astype(f32)
    kv_raw_delta = jnp.concatenate(
        [unrotate(kv_sum[:, :HD], own_cos, own_sin), kv_sum[:, HD:]], axis=1
    ).astype(bf16)

    partial_d = dot(product_d[:, :hidden], prefix_down).astype(bf16)
    partial_a = dot(product_a, action_down[0]).astype(bf16)
    out = []
    for k in range(8):
        i = (1, 3, 4, 0, 2, 5, 7, 6).index(k)
        mine = partial_a[i * ACT_PAD : (i + 1) * ACT_PAD]
        out.append(block_of(partial_d[i * PREF : (i + 1) * PREF], mine))
    out_sent = []
    out = ring_scatter(out, mp_swap, tuple(got), out_sent)
    out = pair_sum(out, mp_swap, tuple(last_sent))
    prefix_output = (hidden_d + out[:PREF]).astype(bf16)[None]
    action_output = (hidden_a + out[PREF:, :DA])[:ACT].astype(bf16)[None]

    last_d = jnp.concatenate([kv_d, qo_b[:72]], axis=1).reshape(8, 9, wide)
    last_a = jnp.concatenate(
        [kv_a[:, :640], qo_a[:64], qo_a[64:], qo_b[72:], kv_a[:, 640:]], axis=1
    ).reshape(8, 8, -1)
    last = jnp.concatenate(
        [
            last_d[:, :8],
            last_a,
            jnp.pad(last_d[:, 8:].reshape(8, 8, wide // 8), ((0, 0), (0, 0), (0, 48))),
        ],
        axis=2,
    )
    last = scatter_direct(last, yz, yz_swap)
    ninth = last[:, last.shape[1] - 256 : last.shape[1] - 48].reshape(1, wide)
    grads_d = join(last[:, :wide], ninth)
    grads_a = last[:, wide : last.shape[1] - 256]

    def split_grads(grads, query, key, value, gain):
        key_grad = grads[:, :256]
        value_grad = grads[:, 256:512]
        second = grads[:, 512]
        query_grad = grads[:, 640:1664]
        first = (
            jnp.sum(query_grad * query.astype(f32), axis=1)
            + jnp.sum(key_grad * key.astype(f32), axis=1)
            + jnp.sum(value_grad * value.astype(f32), axis=1)
        ) / gain.astype(f32)
        return query_grad, key_grad, value_grad, first, second

    gd = split_grads(grads_d, prefix_query, prefix_key, prefix_value, prefix_first_gain)
    ga = split_grads(grads_a, action_query, action_key, action_value, action_first_gain)
    action_out_grad = grads_a[:, 1664:2688]
    prefix_out_grad = grads_a[:, 2688:]

    first_delta_d = dot_t(query_delta[:PREF], wq_d) + dot_t(kv_raw_delta[:PREF], wkv_d)
    first_delta_a = dot_t(query_delta[PREF:], wq_a) + dot_t(kv_raw_delta[PREF:], wkv_a)
    first_gain_d, first_gain_a = gain_rows(gains_d)[0], gain_rows(gains_a)[0]
    input_d = hidden_delta_d + normalize_back(x_d, rms_d, first_gain_d, first_delta_d)
    input_a = hidden_delta_a + normalize_back(x_a, rms_a, first_gain_a, first_delta_a)

    return (
        prefix_output,
        action_output,
        input_d.astype(bf16)[None],
        input_a[:ACT].astype(bf16)[None],
        gd[0],
        gd[1],
        gd[2],
        prefix_out_grad,
        gd[3],
        gd[4],
        ga[0],
        ga[1],
        ga[2],
        action_out_grad,
        ga[3],
        ga[4],
        finished[0].T,
        finished[1].T,
        finished[2],
        finished[3][None],
        finished[4][None],
        finished[5][None],
    )


def solution(mesh):
    rows = P("dp", "mp", None)
    both = P(("dp", "mp"), None)
    vector = P(("dp", "mp"))
    slots = P("mp", None, None)
    return jax.shard_map(
        on_device,
        mesh=mesh,
        in_specs=(rows,) * 4
        + (P("dp", None), P("dp", None), P())
        + (both,) * 4
        + (vector,) * 2
        + (both,) * 4
        + (vector,) * 2
        + (P(None, "mp"), P(None, "mp"), P("mp", None))
        + (slots,) * 3,
        out_specs=(rows,) * 4
        + (both,) * 4
        + (vector,) * 2
        + (both,) * 4
        + (vector,) * 2
        + (P(None, "mp"), P(None, "mp"), P("mp", None))
        + (slots,) * 3,
        check_vma=False,
    )
```

```python
import functools

import jax
import jax.numpy as jnp
import numpy as np
from jax import lax
from jax.experimental import pallas as pl
from jax.experimental.pallas import tpu as pltpu
from jax.sharding import PartitionSpec as P

ACT_LEN = 48
EPSILON = 1e-06
ROPE_BASE = 10000.0
HEADS = 4
HD = 256
PREF = 192
ACT = 12
ACT_PAD = 16
BLOCK = PREF + ACT_PAD
N_MP = 8
HALF_A = 96
HALF_B = BLOCK - HALF_A
HIDDEN_PAD = 896
VMEM_FEED = 50
bf16 = jnp.bfloat16
f32 = jnp.float32
ANY = pl.BlockSpec(memory_space=pl.ANY)
SMEM = pl.BlockSpec(memory_space=pltpu.SMEM)
VMEM = pl.BlockSpec(memory_space=pltpu.VMEM)
ARRIVALS = (
    ((0, 0), (0, 1)),
    ((1, 0), (1, 1)),
    ((3, 0), (3, 1)),
    ((4, 0), (4, 1)),
    ((5, 0), (7, 0)),
    ((2, 0), (5, 1)),
    ((2, 1), (7, 1)),
    ((6, 0),),
    ((6, 1),),
)
PARTS = tuple(part for parts in ARRIVALS for part in parts)
KEY_BLOCK = np.concatenate(
    [np.full(HALF_A, k) for k, _ in PARTS] + [np.full(ACT_PAD, k) for k, h in PARTS if h]
).astype(np.int32)
KEY_ROW = np.concatenate(
    [np.arange(HALF_A) + h * HALF_A for _, h in PARTS]
    + [np.arange(PREF, BLOCK) for _, h in PARTS if h]
).astype(np.int32)


ROW_PAIR, ACT_PAIR = 3 * PREF, 3 * ACT_PAD


def mp_swap(array, step):
    return lax.ppermute(array, "mp", [(i, i ^ step) for i in range(N_MP)])


def dp_swap(array, step):
    return lax.ppermute(array, "dp", [(i, i ^ step) for i in range(16)])


def yz_swap(array, step):
    return dp_swap(array, (step >> 2) * 8 + (step & 3) * 2)


def core_swap(array):
    return dp_swap(array, 1)


def where_parts(first, arrays, sizes):
    where = {}
    for i in range(arrays):
        at = 0
        for k, h in ARRIVALS[first + i]:
            where[k, h] = (i, at)
            at += sizes[h]
    return where


def fence_kernel(*refs):
    pass


def fence(array, *after):
    return pl.pallas_call(
        fence_kernel,
        in_specs=[pl.BlockSpec(memory_space=pl.ANY)] * (1 + len(after)),
        out_specs=pl.BlockSpec(memory_space=pl.ANY),
        out_shape=jax.ShapeDtypeStruct(array.shape, array.dtype),
        input_output_aliases={0: 0},
        cost_estimate=pl.CostEstimate(flops=0, bytes_accessed=0, transcendentals=0),
        name="fence",
    )(array, *after)


def join(*parts):
    return jnp.concatenate(parts, axis=0)


def add_low(*parts):
    total = parts[0].astype(f32)
    for part in parts[1:]:
        total = total + part.astype(f32)
    return total.astype(bf16)


def held(array, after):
    return fence(array, *after) if after else array


def sends_kernel(count, layout, *refs):
    for out, parts in zip(refs[len(refs) - len(layout) :], layout):
        at = 0
        for which, first, n in parts:
            out[at : at + n] = refs[which][first : first + n]
            at += n


def make_sends(arrays, layout, after=()):
    width = arrays[0].shape[1]
    low = lambda parts: jax.ShapeDtypeStruct((sum(n for _, _, n in parts), width), arrays[0].dtype)
    return pl.pallas_call(
        functools.partial(sends_kernel, len(arrays), layout),
        in_specs=[VMEM] * len(arrays) + [ANY] * len(after),
        out_specs=[VMEM] * len(layout),
        out_shape=[low(parts) for parts in layout],
        compiler_params=pltpu.CompilerParams(vmem_limit_bytes=16 * 1024 * 1024),
        cost_estimate=pl.CostEstimate(flops=0, bytes_accessed=0, transcendentals=0),
        name="sends",
    )(*arrays, *after)


def relay_gather(own, na, swap, during=None, hold=None):
    nb = own.shape[0] - na
    during = during or (lambda stage, arrived, sends: ())
    hold = hold or {}
    own = held(own, hold.get(1, ()))
    s1, s3, s4 = swap(own, 1), swap(own, 3), swap(own, 4)
    after = during(1, (own,), (own,)) + hold.get(2, ())
    layout = (
        ((0, 0, na), (1, 0, na)),
        ((1, 0, na), (2, na, nb)),
        ((0, na, nb), (2, na, nb)),
    )
    sends = make_sends((s1, s3, s4), layout, after)
    zz, v1, v3 = swap(sends[0], 4), swap(sends[1], 1), swap(sends[2], 3)
    after = during(2, (s1, s3, s4), tuple(sends)) + hold.get(3, ())
    sends = make_sends((zz, v1), (((0, na, na),), ((1, na, nb),)), after)
    z2a, z2b = swap(sends[0], 1), swap(sends[1], 3)
    during(3, (zz, v1, v3), tuple(sends))
    return own, s1, s3, s4, zz, v1, v3, z2a, z2b


def relay_scatter(pa, pb, swap, hold=None, sent=None):
    na, nb = pa[0].shape[0], pb[0].shape[0]
    hold = hold or {}
    sent = {} if sent is None else sent
    get = lambda stage: hold[stage]() if stage in hold else ()
    after = get(1)
    sent[1] = (held(pa[6], after), held(pb[6], after))
    r1, r3 = swap(sent[1][0], 1), swap(sent[1][1], 3)
    p7a = add_low(pa[7], r1)
    p5b = add_low(pb[5], r3)
    after = get(2)
    sends = (join(pa[5], p7a), join(pa[2], p5b), join(pb[2], pb[7]))
    sent[2] = tuple(held(x, after) for x in sends)
    zz, v1, v3 = swap(sent[2][0], 4), swap(sent[2][1], 1), swap(sent[2][2], 3)
    p1 = join(add_low(pa[1], zz[:na]), add_low(pb[1], v3[:nb]))
    p3 = join(add_low(pa[3], zz[na:], v1[:na]), pb[3])
    p4 = join(pa[4], add_low(pb[4], v1[na:], v3[nb:]))
    after = get(3)
    sent[3] = tuple(held(x, after) for x in (p1, p3, p4))
    s1, s3, s4 = swap(sent[3][0], 1), swap(sent[3][1], 3), swap(sent[3][2], 4)
    return pa[0], pb[0], s1, s3, s4


def total_of(pieces):
    pa, pb, s1, s3, s4 = pieces
    na = pa.shape[0]
    total_a = pa.astype(f32) + s1[:na].astype(f32) + s3[:na].astype(f32) + s4[:na].astype(f32)
    total_b = pb.astype(f32) + s1[na:].astype(f32) + s3[na:].astype(f32) + s4[na:].astype(f32)
    return total_a, total_b


def ring_scatter(pieces, swap, after, sent):
    near = [join(pieces[j], pieces[j ^ 4]) for j in range(4)]
    near[1:] = [held(x, after) for x in near[1:]]
    sent += near[1:]
    total = near[0].astype(f32)
    for j in (1, 3, 2):
        total = total + swap(near[j], j).astype(f32)
    return total


def pair_sum(total, swap, after=()):
    half = total.shape[0] // 2
    return total[:half] + swap(held(total[half:].astype(bf16), after), 4).astype(f32)


def gather_direct(array, index, swap):
    pair = index & 4
    high = (index >> 2) & 1
    two = jnp.zeros((2,) + array.shape, array.dtype)
    two = lax.dynamic_update_index_in_dim(two, array, high, 0)
    two = lax.dynamic_update_index_in_dim(two, swap(array, 4), 1 - high, 0)
    ring = index & 3
    out = jnp.zeros((2, 4) + array.shape, array.dtype)
    out = lax.dynamic_update_index_in_dim(out, two, ring, 1)
    for step in (1, 3, 2):
        out = lax.dynamic_update_index_in_dim(out, swap(two, step), ring ^ step, 1)
    return out.reshape((8,) + array.shape)


def scatter_direct(pieces, index, swap):
    high = (index >> 2) & 1
    ring = index & 3
    quads = pieces.reshape((2, 4) + pieces.shape[1:])
    total = lax.dynamic_index_in_dim(quads, ring, 1, keepdims=False).astype(f32)
    for step in (1, 3, 2):
        piece = lax.dynamic_index_in_dim(quads, ring ^ step, 1, keepdims=False)
        total = total + swap(piece, step).astype(f32)
    mine = lax.dynamic_index_in_dim(total, high, 0, keepdims=False)
    theirs = lax.dynamic_index_in_dim(total, 1 - high, 0, keepdims=False)
    return mine + swap(theirs.astype(bf16), 4).astype(f32)


def assemble_kernel(cuts, sizes, place_ref, *refs):
    arrays, outs = refs[:18], refs[18:]
    index, core = place_ref[0], place_ref[1]
    for (k, h), (i, at) in where_parts(0, 9, sizes).items():
        for out, (which, first, n, column, width) in zip(outs, cuts):
            if which == h:
                rows, columns = slice(at + first, at + first + n), slice(column, column + width)
                out[index ^ k, core] = arrays[i][rows, :, columns]
                out[index ^ k, 1 - core] = arrays[9 + i][rows, :, columns]


def assemble(mine, theirs, na, cuts, index, core):
    rows, columns = mine[0].shape
    eights = [x.reshape(x.shape[0] // 8, 8, columns) for x in (*mine, *theirs)]
    sizes = (na // 8, (rows - na) // 8)
    outs = pl.pallas_call(
        functools.partial(assemble_kernel, cuts, sizes),
        in_specs=[SMEM] + [VMEM] * 18,
        out_specs=[VMEM] * len(cuts),
        out_shape=[jax.ShapeDtypeStruct((8, 2, n, 8, width), bf16) for _, _, n, _, width in cuts],
        compiler_params=pltpu.CompilerParams(vmem_limit_bytes=40 * 1024 * 1024),
        name="assemble",
    )(jnp.stack([index, core]), *eights)
    return [x.reshape(-1, x.shape[-1]) for x in outs]


def gain_rows(block):
    pick = lax.broadcasted_iota(jnp.int32, (ACT_PAD, 128), 0)
    pick = (pick == lax.broadcasted_iota(jnp.int32, (ACT_PAD, 128), 1)).astype(bf16)
    turned = dot_t(pick, block)
    return turned[0:1], turned[1:2]


def keys_kernel(*refs):
    rows, (gain_d, gain_a, weight_d, weight_a, cosine, sine) = refs[:9], refs[9:15]
    normed_d, normed_a, keys, values = refs[-4:]
    gain_d, gain_a = gain_rows(gain_d[...])[0], gain_rows(gain_a[...])[0]
    width = weight_a.shape[0]
    prefix, action = [], []
    for i, parts in enumerate(ARRIVALS):
        at = 0
        for _, h in parts:
            prefix.append(rows[i][at : at + HALF_A])
            at += HALF_A
            if h:
                action.append(rows[i][at : at + ACT_PAD, :width])
                at += ACT_PAD
    x = join(*prefix).astype(f32)
    low_d = (x * inverse_rms(x) * gain_d).astype(bf16)
    x = join(*action).astype(f32)
    low_a = (x * inverse_rms(x) * gain_a).astype(bf16)
    normed_d[:PREF] = low_d[:PREF]
    normed_a[:ACT_PAD] = low_a[:ACT_PAD]
    normed_d[PREF:] = low_d[ROW_PAIR : ROW_PAIR + PREF]
    normed_a[ACT_PAD:] = low_a[ACT_PAIR : ACT_PAIR + ACT_PAD]
    raw = join(dot(low_d, weight_d[...]), dot(low_a, weight_a[...]))
    keys[...] = rotate(raw[:, :HD], cosine[...], sine[...]).astype(bf16)
    values[...] = raw[:, HD:].astype(bf16)


def keys_of(rows, gain_d, gain_a, weight_d, weight_a, cosine, sine, after):
    width_d, width_a = gain_d.shape[0], gain_a.shape[0]
    count = cosine.shape[0]
    shape = lambda *dims: jax.ShapeDtypeStruct(dims, bf16)
    given = [*rows, gain_d, gain_a, weight_d, weight_a, cosine, sine]
    return pl.pallas_call(
        keys_kernel,
        in_specs=[VMEM] * len(given) + [ANY] * len(after),
        out_specs=[VMEM] * 4,
        out_shape=[
            shape(2 * PREF, width_d),
            shape(2 * ACT_PAD, width_a),
            shape(count, HD),
            shape(count, HD),
        ],
        compiler_params=pltpu.CompilerParams(vmem_limit_bytes=48 * 1024 * 1024),
        cost_estimate=pl.CostEstimate(
            flops=4 * count * width_d * HD, bytes_accessed=8 * 1024 * 1024, transcendentals=count
        ),
        name="keys_of",
    )(*given, *after)


def gelu_parts(gate):
    c0 = 0.7978845608028654
    c1 = 0.044715
    square = gate * gate
    tanh = jnp.tanh(c0 * gate * (1.0 + c1 * square))
    half = 0.5 * (1.0 + tanh)
    slope = half + 0.5 * gate * (1.0 - tanh * tanh) * c0 * (1.0 + 3.0 * c1 * square)
    return gate * half, slope


def feed_block(rows, seed, gate_weight, up_weight, down_weight, valid):
    into, out_of = (dot_t, dot) if valid is None else (dot, dot_t)
    gate = into(rows, gate_weight)
    up = into(rows, up_weight)
    active, slope = gelu_parts(gate)
    product_delta = dot_t(seed, down_weight)
    if valid is not None:
        active = active * valid
        product_delta = product_delta * valid
    product = (active * up).astype(bf16)
    gate_delta = (product_delta * up * slope).astype(bf16)
    up_delta = (product_delta * active).astype(bf16)
    rows_delta = out_of(gate_delta, gate_weight) + out_of(up_delta, up_weight)
    return product, gate_delta, up_delta, rows_delta.astype(bf16)


def feed_kernel(layout, *refs):
    arrays = 1 + max(i for parts in layout for i, _ in parts)
    rows_refs, seed_refs, refs = refs[:arrays], refs[arrays : 2 * arrays], refs[2 * arrays :]
    gate_ref, up_ref, down_ref = refs[:3]
    action_gate_ref, action_up_ref, action_down_ref, valid_ref = refs[3:7]
    count = len(layout)
    outs = refs[-(2 * count + 8) :]
    products, deltas, kept_rows, kept_seeds = outs[:4]
    action_products, action_deltas, action_rows, action_seeds = outs[4:8]
    width = action_gate_ref.shape[0]
    rest = PREF - HALF_A

    def prefix_of(blocks):
        parts = []
        for (ia, a), (ib, b) in layout:
            parts += [blocks[ia][a : a + HALF_A], blocks[ib][b : b + rest]]
        return join(*parts)

    def action_of(blocks):
        parts = []
        for _, (ib, b) in layout:
            parts.append(blocks[ib][b + rest : b + HALF_B, :width])
        return join(*parts) if count > 1 else parts[0]

    rows, seed = prefix_of(rows_refs), prefix_of(seed_refs)
    product, gate_delta, up_delta, rows_delta = feed_block(
        rows, seed, gate_ref[...], up_ref[...], down_ref[...], None
    )
    hidden = product.shape[1]
    spare = jnp.zeros((count * PREF, HIDDEN_PAD - hidden), bf16)
    products[:, :hidden] = product
    products[:, hidden:] = spare
    deltas[:, :hidden] = gate_delta
    deltas[:, hidden:HIDDEN_PAD] = spare
    deltas[:, HIDDEN_PAD : HIDDEN_PAD + hidden] = up_delta
    deltas[:, HIDDEN_PAD + hidden :] = spare
    kept_rows[...] = rows
    kept_seeds[...] = seed
    rows, seed = action_of(rows_refs), action_of(seed_refs)
    product, gate_delta, up_delta, action_rows_delta = feed_block(
        rows,
        seed,
        action_gate_ref[...],
        action_up_ref[...],
        action_down_ref[...],
        valid_ref[...],
    )
    slots = gate_delta.shape[1]
    action_products[...] = product
    action_deltas[:, :slots] = gate_delta
    action_deltas[:, slots:] = up_delta
    action_rows[...] = rows
    action_seeds[...] = seed
    blank = jnp.zeros((ACT_PAD, rows_delta.shape[1] - width), bf16)
    for i in range(count):
        a, b, c = i * PREF, i * PREF + HALF_A, (i + 1) * PREF
        extra = slice(i * ACT_PAD, (i + 1) * ACT_PAD)
        ref_a, ref_b = outs[8 + 2 * i : 10 + 2 * i]
        ref_a[...] = rows_delta[a:b]
        ref_b[:rest] = rows_delta[b:c]
        ref_b[rest:, :width] = action_rows_delta[extra]
        ref_b[rest:, width:] = blank


def feed(arrays, seeds, weights, layout, base, kept, after):
    count = len(layout)
    width = arrays[0].shape[1]
    hidden = weights[0].shape[0]
    action_width, slots = weights[3].shape
    once = pl.Buffered(1)
    at = base // count

    def whole(array):
        return pl.BlockSpec(array.shape, lambda i: (0, 0), pipeline_mode=once)

    def part(size, columns):
        return (
            jax.ShapeDtypeStruct((N_MP * size, columns), bf16),
            pl.BlockSpec((count * size, columns), lambda i: (at, 0), pipeline_mode=once),
        )

    def own(size):
        return (
            jax.ShapeDtypeStruct((size, width), bf16),
            pl.BlockSpec((size, width), lambda i: (0, 0), pipeline_mode=once),
        )

    outs = [
        part(PREF, HIDDEN_PAD),
        part(PREF, 2 * HIDDEN_PAD),
        part(PREF, width),
        part(PREF, width),
        part(ACT_PAD, slots),
        part(ACT_PAD, 2 * slots),
        part(ACT_PAD, action_width),
        part(ACT_PAD, action_width),
    ] + [own(HALF_A), own(HALF_B)] * count
    reused = [] if kept is None else list(kept)
    given = [*arrays, *seeds]
    placed = len(given) + len(weights)
    results = pl.pallas_call(
        functools.partial(feed_kernel, layout),
        grid=(1,),
        in_specs=[whole(x) for x in given]
        + [VMEM] * len(weights)
        + [ANY] * (len(reused) + len(after)),
        out_shape=[shape for shape, _ in outs],
        out_specs=[spec for _, spec in outs],
        input_output_aliases={placed + i: i for i in range(len(reused))},
        compiler_params=pltpu.CompilerParams(
            dimension_semantics=("arbitrary",), vmem_limit_bytes=VMEM_FEED * 1024 * 1024
        ),
        cost_estimate=pl.CostEstimate(
            flops=10 * count * (PREF * width * hidden + ACT_PAD * action_width * slots),
            bytes_accessed=6 * (width * hidden + action_width * slots),
            transcendentals=count * PREF * hidden,
        ),
        name="feed",
    )(*given, *weights, *reused, *after)
    blocks = [results[8 + 2 * i : 10 + 2 * i] for i in range(count)]
    return blocks, results[:8]


def see(own_ref, key_ref):
    own, key = own_ref[...], key_ref[...]
    return (own[:, 0:1] == key[0:1]) | (own[:, 1:2] == key[1:2])


def attend_kernel(*refs):
    (normed_d, normed_a, x_d, x_a, wq_d, wq_a, wo_m, wo_e, wo_a) = refs[:9]
    (gain_d, gain_a, cosine, sine, own_codes, key_codes) = refs[9:15]
    keys, values = refs[15][...], refs[16][...]
    (queries, context, tops, totals, hidden_d, hidden_a, block) = refs[-7:]
    gain_d, gain_a = gain_rows(gain_d[...])[1], gain_rows(gain_a[...])[1]
    raw = join(dot(normed_d[:PREF], wq_d[...]), dot(normed_a[:ACT_PAD], wq_a[...]))
    visible = see(own_codes, key_codes)
    cos, sin = cosine[...], sine[...]
    heads = []
    for h in range(HEADS):
        rows = slice(h * BLOCK, (h + 1) * BLOCK)
        query = (rotate(raw[:, h * HD : (h + 1) * HD], cos, sin) * HD**-0.5).astype(bf16)
        queries[rows] = query
        scores = jnp.where(visible, dot_t(query, keys), -1e30)
        top = jnp.max(scores, axis=1, keepdims=True)
        shifted = jnp.exp(scores - top)
        total = jnp.sum(shifted, axis=1, keepdims=True)
        tops[rows] = top
        totals[rows] = total
        heads.append(dot((shifted / total).astype(bf16), values).astype(bf16))
    mixed = jnp.concatenate(heads, axis=1)
    context[...] = mixed
    main, width_d, width_a = wo_m.shape[1], x_d.shape[1], x_a.shape[1]
    low_d, low_a = mixed[:PREF], mixed[PREF:]
    state = x_d[...].astype(f32) + jnp.concatenate(
        [dot(low_d, wo_m[...]), dot(low_d, wo_e[...])], axis=1
    )
    hidden_d[...] = state
    second_d = (state * inverse_rms(state) * gain_d).astype(bf16)
    real = lax.broadcasted_iota(jnp.int32, (ACT_PAD, width_a), 0) < ACT
    state = jnp.where(real, x_a[...].astype(f32) + dot(low_a, wo_a[...]), 0.0)
    hidden_a[...] = state
    second_a = (state * inverse_rms(state) * gain_a).astype(bf16)
    block[:PREF] = second_d
    block[PREF:, :width_a] = second_a
    block[PREF:, width_a:] = jnp.zeros((ACT_PAD, width_d - width_a), bf16)


def attend(*given, after):
    x_d, x_a = given[2:4]
    width_d, width_a = x_d.shape[1], x_a.shape[1]
    shape = jax.ShapeDtypeStruct
    stacked = HEADS * BLOCK
    return pl.pallas_call(
        attend_kernel,
        in_specs=[VMEM] * len(given) + [ANY] * len(after),
        out_specs=[VMEM] * 7,
        out_shape=[
            shape((stacked, HD), bf16),
            shape((BLOCK, HEADS * HD), bf16),
            shape((stacked, 1), f32),
            shape((stacked, 1), f32),
            shape((PREF, width_d), f32),
            shape((ACT_PAD, width_a), f32),
            shape((BLOCK, width_d), bf16),
        ],
        compiler_params=pltpu.CompilerParams(vmem_limit_bytes=50 * 1024 * 1024),
        cost_estimate=pl.CostEstimate(
            flops=4 * BLOCK * HEADS * HD * (N_MP * BLOCK + width_d),
            bytes_accessed=4 * 1024 * 1024 * 5,
            transcendentals=stacked * N_MP * BLOCK,
        ),
        name="attend",
    )(*given, *after)


def attend_back_kernel(*refs):
    pieces = refs[:5]
    (hidden_d, hidden_a, cotangent_d, cotangent_a, share, gain_d, gain_a) = refs[5:12]
    (wo_m, wo_e, wo_a, queries, tops, totals, cosine, sine, own_codes, key_codes) = refs[12:22]
    keys, values = refs[22][...], refs[23][...]
    outs = refs[-(6 + len(PARTS)) :]
    (hidden_delta_d, hidden_delta_a, low, terms_d, terms_a, query_delta) = outs[:6]
    kv_deltas = outs[6:]
    gain_d, gain_a = gain_rows(gain_d[...])[1], gain_rows(gain_a[...])[1]
    delta = join(*total_of([piece[...] for piece in pieces]))
    width_d, width_a = hidden_d.shape[1], hidden_a.shape[1]
    lows = []
    for rows, state_ref, cotangent, gain, out, terms in (
        (slice(0, PREF), hidden_d, cotangent_d, gain_d, hidden_delta_d, terms_d),
        (slice(PREF, BLOCK), hidden_a, cotangent_a, gain_a, hidden_delta_a, terms_a),
    ):
        state = state_ref[...]
        change = delta[rows, : state.shape[1]]
        scale = inverse_rms(state)
        seed = cotangent[...].astype(f32) * share[rows]
        back = seed + normalize_back(state, scale, gain, change)
        out[...] = back
        terms[...] = (change * state * scale).astype(bf16)
        lows.append(back.astype(bf16))
    low_d, low_a = lows
    low[:PREF] = low_d
    low[PREF:, :width_a] = low_a
    low[PREF:, width_a:] = jnp.zeros((ACT_PAD, width_d - width_a), bf16)
    main = wo_m.shape[1]
    context_delta = join(
        dot_t(low_d[:, :main], wo_m[...]) + dot_t(low_d[:, main:], wo_e[...]),
        dot_t(low_a, wo_a[...]),
    ).astype(bf16)
    visible = see(own_codes, key_codes)
    cos, sin = cosine[...], sine[...]
    keys_delta, values_delta = None, None
    for h in range(HEADS):
        rows = slice(h * BLOCK, (h + 1) * BLOCK)
        query = queries[rows]
        change = context_delta[:, h * HD : (h + 1) * HD]
        scores = jnp.where(visible, dot_t(query, keys), -1e30)
        probs = jnp.exp(scores - tops[rows]) / totals[rows]
        probs_delta = dot_t(change, values)
        row_dot = jnp.sum(probs * probs_delta, axis=1, keepdims=True)
        score_delta = (probs * (probs_delta - row_dot)).astype(bf16)
        turned = unrotate(dot(score_delta, keys), cos, sin) * HD**-0.5
        query_delta[:, h * HD : (h + 1) * HD] = turned.astype(bf16)
        key_part = t_dot(score_delta, query)
        value_part = t_dot(probs.astype(bf16), change)
        keys_delta = key_part if h == 0 else keys_delta + key_part
        values_delta = value_part if h == 0 else values_delta + value_part
    at, extra = 0, len(PARTS) * HALF_A
    for (_, half), out in zip(PARTS, kv_deltas):
        for columns, change in ((slice(0, HD), keys_delta), (slice(HD, 2 * HD), values_delta)):
            out[:HALF_A, columns] = change[at : at + HALF_A].astype(bf16)
            if half:
                out[HALF_A:, columns] = change[extra : extra + ACT_PAD].astype(bf16)
        at += HALF_A
        extra += half * ACT_PAD


def attend_back(*given, after):
    hidden_d, hidden_a = given[5:7]
    width_d, width_a = hidden_d.shape[1], hidden_a.shape[1]
    shape = jax.ShapeDtypeStruct
    stacked = HEADS * BLOCK
    outs = pl.pallas_call(
        attend_back_kernel,
        in_specs=[VMEM] * len(given) + [ANY] * len(after),
        out_specs=[VMEM] * (6 + len(PARTS)),
        out_shape=[
            shape((PREF, width_d), f32),
            shape((ACT_PAD, width_a), f32),
            shape((BLOCK, width_d), bf16),
            shape((PREF, width_d), bf16),
            shape((ACT_PAD, width_a), bf16),
            shape((BLOCK, HEADS * HD), bf16),
        ]
        + [shape(((HALF_A, HALF_B)[half], 2 * HD), bf16) for _, half in PARTS],
        compiler_params=pltpu.CompilerParams(vmem_limit_bytes=50 * 1024 * 1024),
        cost_estimate=pl.CostEstimate(
            flops=2 * BLOCK * HEADS * HD, bytes_accessed=4 * BLOCK, transcendentals=stacked
        ),
        name="attend_back",
    )(*given, *after)
    kv_deltas = dict(zip(PARTS, outs[6:]))
    pa = {k: kv_deltas[k, 0] for k in range(8)}
    pb = {k: kv_deltas[k, 1] for k in range(8)}
    return outs[:6], pa, pb


def theirs_kernel(cuts, place_ref, *refs):
    out = refs[-1]
    core = place_ref[1]
    for ref, (row, n, source, column, width) in zip(refs, cuts):
        out[:, row : row + n, :, column : column + width] = ref[
            1 - core, :, :, :, source : source + width
        ]


def near_kernel(cuts, place_ref, *refs):
    got, outs = refs[len(cuts)], refs[-4:]
    mp, core = place_ref[0], place_ref[1]
    for step, out in zip((0, 1, 3, 2), outs):
        for pair in range(2):
            block = mp ^ step ^ (4 * pair)
            base = pair * got.shape[1]
            for ref, (row, n, source, column, width) in zip(refs, cuts):
                columns = slice(column, column + width)
                mine = ref[core, block, :, :, source : source + width].astype(f32)
                total = mine + got[block, row : row + n, :, columns].astype(f32)
                out[base + row : base + row + n, :, columns] = total.astype(bf16)


def sum_weights(grads, cuts, columns, place, sent, got, after, before_last, last_sent):
    views = [g.reshape(2, 8, -1, 8, g.shape[1]) for g in grads]
    eights = max(row + n for row, n, _, _, _ in cuts)
    params = pltpu.CompilerParams(vmem_limit_bytes=44 * 1024 * 1024)
    cost = pl.CostEstimate(flops=0, bytes_accessed=0, transcendentals=0)
    low = lambda *dims: jax.ShapeDtypeStruct(dims, bf16)
    theirs = pl.pallas_call(
        functools.partial(theirs_kernel, cuts),
        in_specs=[SMEM] + [VMEM] * len(views),
        out_specs=VMEM,
        out_shape=low(8, eights, 8, columns),
        compiler_params=params,
        cost_estimate=cost,
        name="theirs",
    )(place, *views)
    near = pl.pallas_call(
        functools.partial(near_kernel, cuts),
        in_specs=[SMEM] + [VMEM] * (len(views) + 1) + [ANY] * len(after),
        out_specs=[VMEM] * 4,
        out_shape=[low(2 * eights, 8, columns)] * 4,
        compiler_params=params,
        cost_estimate=cost,
        name="near",
    )(place, *views, core_swap(theirs), *after)
    near = [x.reshape(16 * eights, columns) for x in near]
    sent += near[1:]
    total = near[0].astype(f32)
    for step, x in zip((1, 3, 2), near[1:]):
        got.append(mp_swap(x, step))
        total = total + got[-1].astype(f32)
    half = 8 * eights
    last_sent.append(held(total[half:].astype(bf16), before_last))
    return (total[:half] + mp_swap(last_sent[-1], 4).astype(f32)).astype(bf16)


def pad_action(rows):
    return jnp.pad(rows, ((0, ACT_PAD - ACT), (0, 0)))


def widen(rows, width):
    return jnp.pad(rows, ((0, 0), (0, width - rows.shape[1])))


def block_of(prefix_rows, action_rows):
    return join(prefix_rows, widen(action_rows, prefix_rows.shape[1]))


def order_matrix(size, rows):
    d = jnp.arange(size, dtype=jnp.int32)
    r = d % rows
    mp = (d // rows) % 8
    dp = d // (8 * rows)
    place = (dp % 2) * (size // 2) + mp * (8 * rows) + (dp // 2) * rows + r
    return (place[:, None] == jnp.arange(size, dtype=jnp.int32)[None, :]).astype(bf16)


def dot(a, b):
    return jnp.dot(a, b, preferred_element_type=f32)


def dot_t(a, b):
    return lax.dot_general(a, b, (((1,), (1,)), ((), ())), preferred_element_type=f32)


def t_dot(a, b):
    return lax.dot_general(a, b, (((0,), (0,)), ((), ())), preferred_element_type=f32)


def inverse_rms(rows):
    return lax.rsqrt(jnp.mean(rows * rows, axis=-1, keepdims=True) + EPSILON)


def normalize_back(rows, scale, gain, delta):
    a = delta * gain
    return scale * (a - rows * (scale * scale) * jnp.mean(a * rows, axis=-1, keepdims=True))


def rotate(rows, cosine, sine):
    half = HD // 2
    first, second = rows[:, :half], rows[:, half:]
    return jnp.concatenate(
        [first * cosine - second * sine, second * cosine + first * sine], axis=1
    )


def unrotate(rows, cosine, sine):
    return rotate(rows, cosine, -sine)


def angle_tables(place):
    half = HD // 2
    frequency = ROPE_BASE ** (-jnp.arange(half, dtype=f32) / half)
    angles = place.astype(f32)[:, None] * frequency[None, :]
    return jnp.cos(angles), jnp.sin(angles)


def on_device(
    prefix_input,
    action_input,
    prefix_cotangent,
    action_cotangent,
    prefix_lengths,
    mixture,
    cut_points,
    prefix_query,
    prefix_key,
    prefix_value,
    prefix_out,
    prefix_first_gain,
    prefix_second_gain,
    action_query,
    action_key,
    action_value,
    action_out,
    action_first_gain,
    action_second_gain,
    prefix_gate,
    prefix_up,
    prefix_down,
    action_gate,
    action_up,
    action_down,
):
    mp = lax.axis_index("mp")
    dp = lax.axis_index("dp")
    core = dp & 1
    yz = (dp >> 3) * 4 + ((dp >> 1) & 3)
    D = prefix_input.shape[2]
    DA = action_input.shape[2]

    def column_block(first, second):
        return jnp.pad(jnp.stack([first, second], axis=1), ((0, 0), (0, 126)))

    pack_d = jnp.concatenate(
        [
            prefix_key,
            prefix_value,
            column_block(prefix_first_gain, prefix_second_gain),
            prefix_query,
        ],
        axis=1,
    )
    wide = pack_d.shape[1]
    pack = jnp.concatenate(
        [
            pack_d[:8],
            action_key,
            action_value,
            column_block(action_first_gain, action_second_gain),
            action_query,
            action_out,
            prefix_out,
            jnp.pad(pack_d[8:].reshape(8, wide // 8), ((0, 0), (0, 48))),
        ],
        axis=1,
    )
    lengths = prefix_lengths[0]
    first_length = lengths[0]

    def tables(source, row):
        is_action = row >= PREF
        prefix_row = source * PREF + row
        prefix_item = (prefix_row >= first_length).astype(jnp.int32)
        prefix_place = prefix_row - jnp.where(prefix_item == 1, first_length, 0)
        action_row = source * ACT + row - PREF
        action_item = (action_row >= ACT_LEN).astype(jnp.int32)
        action_place = jnp.where(action_item == 1, lengths[1], first_length) + action_row % ACT_LEN
        action_item = jnp.where(row - PREF < ACT, action_item, 2)
        item = jnp.where(is_action, action_item, prefix_item)
        place = jnp.where(is_action, action_place, prefix_place)
        return item, place, is_action

    own_item, own_place, own_is_action = tables(mp, jnp.arange(BLOCK, dtype=jnp.int32))
    key_item, key_place, key_is_action = tables(jnp.asarray(KEY_BLOCK) ^ mp, jnp.asarray(KEY_ROW))
    key_cos, key_sin = angle_tables(key_place)
    own_codes = jnp.stack([own_item, jnp.where(own_is_action, own_item, -2)], axis=1)
    key_codes = jnp.stack(
        [jnp.where(key_is_action, -1, key_item), jnp.where(key_is_action, key_item, -1)], axis=0
    )
    own_cos, own_sin = angle_tables(own_place)

    share = mixture[0].astype(f32) / 32.0
    row_share = jnp.where(own_item == 1, share[1], share[0])[:, None]
    cotangent_a = pad_action(action_cotangent[0])
    prefix_seed = prefix_cotangent[0].astype(f32) * row_share[:PREF]
    action_seed = cotangent_a.astype(f32) * row_share[PREF:]
    seed_block = block_of(prefix_seed.astype(bf16), action_seed.astype(bf16))

    near = gather_direct(pack, mp, mp_swap)
    last_row = near[:, :, pack.shape[1] - 256 : pack.shape[1] - 48].reshape(8, 1, wide)
    near_d = jnp.concatenate([near[:, :, :wide], last_row], axis=1).reshape(72, wide)
    near_a = near[:, :, wide : pack.shape[1] - 256].reshape(64, -1)
    edge = near_a[:, 2688 + 1024 :]
    kv_a = widen(jnp.concatenate([near_a[:, :640], edge], axis=1), 1024)
    pack_a = join(near_a[:, 640:1664], near_a[:, 1664:2688], kv_a)
    pack_b = join(near_d[:, 640:], near_a[:, 2688 : 2688 + 1024], widen(near_d[:, :640], 1024))
    arrived = {}

    def note(name):
        def during(stage, blocks, sends):
            arrived[name, stage] = blocks
            arrived[name, "sends", stage] = sends
            return ()

        return during

    own_action = pad_action(action_input[0])
    own_block = block_of(prefix_input[0], own_action)
    own_block = fence(own_block, near)
    x_rows = relay_gather(own_block, HALF_A, mp_swap)
    hold = {2: x_rows[1:4], 3: x_rows[4:7]}
    mine = relay_gather(join(pack_a, pack_b), pack_a.shape[0], yz_swap, note("weights"), hold)
    theirs = [core_swap(x) for x in mine]
    cuts = (
        (0, 0, 8, 0, 1024),
        (0, 8, 8, 0, 1024),
        (0, 16, 8, 0, 512),
        (0, 16, 8, 512, 128),
        (0, 16, 8, 640, 128),
        (1, 0, 9, 0, 1024),
        (1, 9, 8, 0, 1024),
        (1, 17, 9, 0, 512),
        (1, 17, 9, 512, 128),
    )
    wq_a, wo_a, wkv_a, gains_a, wo_e, wq_d, wo_m, wkv_d, gains_d = assemble(
        mine, theirs, pack_a.shape[0], cuts, yz, core
    )
    seeds = relay_gather(
        seed_block,
        HALF_A,
        mp_swap,
        note("seeds"),
        {1: arrived["weights", "sends", 3][:1]},
    )

    normed_d, normed_a, keys, values = keys_of(
        x_rows,
        gains_d,
        gains_a,
        wkv_d,
        wkv_a,
        key_cos,
        key_sin,
        arrived["seeds", "sends", 2],
    )
    x_d, x_a = prefix_input[0].astype(f32), own_action.astype(f32)
    rms_d, rms_a = inverse_rms(x_d), inverse_rms(x_a)
    queries, context, tops, totals, hidden_d, hidden_a, second_block = attend(
        normed_d,
        normed_a,
        prefix_input[0],
        own_action,
        wq_d,
        wq_a,
        wo_m,
        wo_e,
        wo_a,
        gains_d,
        gains_a,
        own_cos,
        own_sin,
        own_codes,
        key_codes,
        keys,
        values,
        after=arrived["seeds", "sends", 3],
    )

    slots = action_gate.shape[2]
    cut_pair = lax.dynamic_slice_in_dim(cut_points, mp, 2)
    valid = (jnp.arange(slots, dtype=jnp.int32) < cut_pair[1] - cut_pair[0]).astype(f32)[None, :]
    weights = (prefix_gate.T, prefix_up.T, prefix_down)
    weights += (action_gate[0], action_up[0], action_down[0], valid)
    kept = None
    results = {}

    def run(arrays, first, blocks, base, after):
        nonlocal kept
        where = where_parts(first, len(arrays), (HALF_A, HALF_B))
        layout = tuple((where[k, 0], where[k, 1]) for k in blocks)
        some = seeds[first : first + len(arrays)]
        done, kept = feed(arrays, some, weights, layout, base, kept, after)
        results.update(zip(blocks, done))
        return (done[0][0],)

    def feed_during(stage, arrays, sends):
        if stage == 3:
            return ()
        first, blocks, base = {1: (0, (0,), 3), 2: (1, (1, 3, 4), 0)}[stage]
        return run(arrays, first, blocks, base, sends)

    second_block = fence(second_block, seeds[8])
    arrays = relay_gather(second_block, HALF_A, mp_swap, feed_during)
    run(arrays[4:], 4, (2, 5, 7, 6), 4, ())
    product_d, deltas_d, rows_d, seeds_d, product_a, deltas_a, rows_a, seeds_a = kept

    grads = (
        t_dot(deltas_d, rows_d),
        t_dot(product_d, seeds_d),
        t_dot(rows_a, deltas_a),
        t_dot(product_a, seeds_a),
    )
    hidden = prefix_down.shape[0]
    grads = tuple(g.astype(bf16) for g in grads)
    pa = {k: v[0] for k, v in results.items()}
    pb = {k: v[1] for k, v in results.items()}
    delta_pieces = relay_scatter(pa, pb, mp_swap)
    grads = grads[:3] + (fence(grads[3], *delta_pieces[2:]),)
    grads = tuple(lax.psum(g, "dp") for g in grads)
    finished = (
        grads[0][:hidden].astype(f32),
        grads[0][HIDDEN_PAD : HIDDEN_PAD + hidden].astype(f32),
        grads[1][:hidden].astype(f32),
        grads[2][:, :slots].astype(f32),
        grads[2][:, slots:].astype(f32),
        grads[3].astype(f32),
    )

    (hidden_delta_d, hidden_delta_a, low, terms_d, terms_a, query_delta), pa, pb = attend_back(
        *delta_pieces,
        hidden_d,
        hidden_a,
        prefix_cotangent[0],
        cotangent_a,
        row_share,
        gains_d,
        gains_a,
        wo_m,
        wo_e,
        wo_a,
        queries,
        tops,
        totals,
        own_cos,
        own_sin,
        own_codes,
        key_codes,
        keys,
        values,
        after=(),
    )
    low_d, low_a = low[:PREF], low[PREF:, :DA]

    kv_near = [join(pa[k], pb[k], pa[k ^ 4], pb[k ^ 4]) for k in range(4)]
    kv_part = kv_near[0].astype(f32)
    for k in (1, 3, 2):
        kv_part = kv_part + mp_swap(kv_near[k], k).astype(f32)
    pair = lambda table: join(
        own_cos if table is key_cos else own_sin,
        table[ROW_PAIR : ROW_PAIR + PREF],
        table[len(PARTS) * HALF_A + ACT_PAIR : len(PARTS) * HALF_A + ACT_PAIR + ACT_PAD],
    )
    kv_turned = jnp.concatenate(
        [unrotate(kv_part[:, :HD], pair(key_cos), pair(key_sin)), kv_part[:, HD:]], axis=1
    )
    kv_turned_low = kv_turned.astype(bf16)
    kv_rows_d = join(kv_turned_low[:PREF], kv_turned_low[BLOCK : BLOCK + PREF])
    kv_rows_a = join(kv_turned_low[PREF:BLOCK], kv_turned_low[BLOCK + PREF :])

    order_d, order_a = order_matrix(D, 9), order_matrix(DA, 8)
    turned_d = dot(normed_d, order_d).astype(bf16)
    turned_a = dot(normed_a, order_a).astype(bf16)
    turned_context = dot(context, order_a).astype(bf16)
    second_term_d = t_dot(dot(terms_d, order_d).astype(bf16), jnp.ones((PREF, 256), bf16))
    second_term_a = t_dot(dot(terms_a, order_a).astype(bf16), jnp.ones((ACT_PAD, 128), bf16))
    out_grad_d = t_dot(turned_context[:PREF], low_d).astype(bf16)
    out_grad_a = t_dot(turned_context[PREF:], low_a).astype(bf16)
    q_grad_d = t_dot(turned_d[:PREF], query_delta[:PREF]).astype(bf16)
    q_grad_a = t_dot(turned_a[:ACT_PAD], query_delta[PREF:]).astype(bf16)
    place = jnp.stack([mp, core])
    cuts = (
        (0, 8, 0, 0, 1024),
        (8, 8, 0, 0, 1024),
        (16, 9, 0, 0, 1024),
        (25, 8, 0, 0, 1024),
    )
    qo_sent, kv_sent, got, last_sent = [], [], [], []
    qo_grads = (q_grad_a, out_grad_a, q_grad_d, out_grad_d)
    qo = sum_weights(qo_grads, cuts, 1024, place, qo_sent, got, (), (), last_sent)
    kv_grad_d = t_dot(turned_d, kv_rows_d).astype(bf16)
    kv_grad_a = t_dot(turned_a, kv_rows_a).astype(bf16)
    cuts = (
        (0, 8, 0, 0, 512),
        (0, 8, 0, 512, 128),
        (0, 8, 1024, 640, 128),
        (8, 9, 0, 0, 512),
        (8, 9, 0, 512, 256),
    )
    kv_grads = (
        kv_grad_a,
        second_term_a.astype(bf16),
        out_grad_d,
        kv_grad_d,
        second_term_d.astype(bf16),
    )
    kv = sum_weights(kv_grads, cuts, 768, place, kv_sent, got, qo_sent, grads[:1], last_sent)
    kv_a, kv_d = kv[:64], kv[64:, :640]
    qo_a, qo_b = qo[:128], qo[128:]
    kv_other = mp_swap(held(kv_part[BLOCK:].astype(bf16), (*kv_sent, grads[0])), 4)
    kv_sum = kv_part[:BLOCK] + kv_other.astype(f32)
    kv_raw_delta = jnp.concatenate(
        [unrotate(kv_sum[:, :HD], own_cos, own_sin), kv_sum[:, HD:]], axis=1
    ).astype(bf16)

    partial_d = dot(product_d[:, :hidden], prefix_down).astype(bf16)
    partial_a = dot(product_a, action_down[0]).astype(bf16)
    out = []
    for k in range(8):
        i = (1, 3, 4, 0, 2, 5, 7, 6).index(k)
        mine = partial_a[i * ACT_PAD : (i + 1) * ACT_PAD]
        out.append(block_of(partial_d[i * PREF : (i + 1) * PREF], mine))
    out_sent = []
    out = ring_scatter(out, mp_swap, tuple(got), out_sent)
    out = pair_sum(out, mp_swap, tuple(last_sent))
    prefix_output = (hidden_d + out[:PREF]).astype(bf16)[None]
    action_output = (hidden_a + out[PREF:, :DA])[:ACT].astype(bf16)[None]

    last_d = jnp.concatenate([kv_d, qo_b[:72]], axis=1).reshape(8, 9, wide)
    last_a = jnp.concatenate(
        [kv_a[:, :640], qo_a[:64], qo_a[64:], qo_b[72:], kv_a[:, 640:]], axis=1
    ).reshape(8, 8, -1)
    last = jnp.concatenate(
        [
            last_d[:, :8],
            last_a,
            jnp.pad(last_d[:, 8:].reshape(8, 8, wide // 8), ((0, 0), (0, 0), (0, 48))),
        ],
        axis=2,
    )
    last = scatter_direct(last, yz, yz_swap)
    ninth = last[:, last.shape[1] - 256 : last.shape[1] - 48].reshape(1, wide)
    grads_d = join(last[:, :wide], ninth)
    grads_a = last[:, wide : last.shape[1] - 256]

    def split_grads(grads, query, key, value, gain):
        key_grad = grads[:, :256]
        value_grad = grads[:, 256:512]
        second = grads[:, 512]
        query_grad = grads[:, 640:1664]
        first = (
            jnp.sum(query_grad * query.astype(f32), axis=1)
            + jnp.sum(key_grad * key.astype(f32), axis=1)
            + jnp.sum(value_grad * value.astype(f32), axis=1)
        ) / gain.astype(f32)
        return query_grad, key_grad, value_grad, first, second

    gd = split_grads(grads_d, prefix_query, prefix_key, prefix_value, prefix_first_gain)
    ga = split_grads(grads_a, action_query, action_key, action_value, action_first_gain)
    action_out_grad = grads_a[:, 1664:2688]
    prefix_out_grad = grads_a[:, 2688:]

    first_delta_d = dot_t(query_delta[:PREF], wq_d) + dot_t(kv_raw_delta[:PREF], wkv_d)
    first_delta_a = dot_t(query_delta[PREF:], wq_a) + dot_t(kv_raw_delta[PREF:], wkv_a)
    first_gain_d, first_gain_a = gain_rows(gains_d)[0], gain_rows(gains_a)[0]
    input_d = hidden_delta_d + normalize_back(x_d, rms_d, first_gain_d, first_delta_d)
    input_a = hidden_delta_a + normalize_back(x_a, rms_a, first_gain_a, first_delta_a)

    return (
        prefix_output,
        action_output,
        input_d.astype(bf16)[None],
        input_a[:ACT].astype(bf16)[None],
        gd[0],
        gd[1],
        gd[2],
        prefix_out_grad,
        gd[3],
        gd[4],
        ga[0],
        ga[1],
        ga[2],
        action_out_grad,
        ga[3],
        ga[4],
        finished[0].T,
        finished[1].T,
        finished[2],
        finished[3][None],
        finished[4][None],
        finished[5][None],
    )


def solution(mesh):
    rows = P("dp", "mp", None)
    both = P(("dp", "mp"), None)
    vector = P(("dp", "mp"))
    slots = P("mp", None, None)
    return jax.shard_map(
        on_device,
        mesh=mesh,
        in_specs=(rows,) * 4
        + (P("dp", None), P("dp", None), P())
        + (both,) * 4
        + (vector,) * 2
        + (both,) * 4
        + (vector,) * 2
        + (P(None, "mp"), P(None, "mp"), P("mp", None))
        + (slots,) * 3,
        out_specs=(rows,) * 4
        + (both,) * 4
        + (vector,) * 2
        + (both,) * 4
        + (vector,) * 2
        + (P(None, "mp"), P(None, "mp"), P("mp", None))
        + (slots,) * 3,
        check_vma=False,
    )
```

```python
import functools

import jax
import jax.numpy as jnp
import numpy as np
from jax import lax
from jax.experimental import pallas as pl
from jax.experimental.pallas import tpu as pltpu
from jax.sharding import PartitionSpec as P

ACT_LEN = 48
EPSILON = 1e-06
ROPE_BASE = 10000.0
HEADS = 4
HD = 256
PREF = 192
ACT = 12
ACT_PAD = 16
BLOCK = PREF + ACT_PAD
N_MP = 8
HALF_A = 96
HALF_B = BLOCK - HALF_A
HIDDEN_PAD = 896
VMEM_FEED = 50
bf16 = jnp.bfloat16
f32 = jnp.float32
ANY = pl.BlockSpec(memory_space=pl.ANY)
SMEM = pl.BlockSpec(memory_space=pltpu.SMEM)
VMEM = pl.BlockSpec(memory_space=pltpu.VMEM)
ARRIVALS = (
    ((0, 0), (0, 1)),
    ((1, 0), (1, 1)),
    ((3, 0), (3, 1)),
    ((4, 0), (4, 1)),
    ((5, 0), (7, 0)),
    ((2, 0), (5, 1)),
    ((2, 1), (7, 1)),
    ((6, 0),),
    ((6, 1),),
)
PARTS = tuple(part for parts in ARRIVALS for part in parts)
KEY_BLOCK = np.concatenate(
    [np.full(HALF_A, k) for k, _ in PARTS] + [np.full(ACT_PAD, k) for k, h in PARTS if h]
).astype(np.int32)
KEY_ROW = np.concatenate(
    [np.arange(HALF_A) + h * HALF_A for _, h in PARTS]
    + [np.arange(PREF, BLOCK) for _, h in PARTS if h]
).astype(np.int32)


ROW_PAIR, ACT_PAIR = 3 * PREF, 3 * ACT_PAD


def mp_swap(array, step):
    return lax.ppermute(array, "mp", [(i, i ^ step) for i in range(N_MP)])


def dp_swap(array, step):
    return lax.ppermute(array, "dp", [(i, i ^ step) for i in range(16)])


def yz_swap(array, step):
    return dp_swap(array, (step >> 2) * 8 + (step & 3) * 2)


def core_swap(array):
    return dp_swap(array, 1)


def where_parts(first, arrays, sizes):
    where = {}
    for i in range(arrays):
        at = 0
        for k, h in ARRIVALS[first + i]:
            where[k, h] = (i, at)
            at += sizes[h]
    return where


def fence_kernel(*refs):
    pass


def fence(array, *after):
    return pl.pallas_call(
        fence_kernel,
        in_specs=[pl.BlockSpec(memory_space=pl.ANY)] * (1 + len(after)),
        out_specs=pl.BlockSpec(memory_space=pl.ANY),
        out_shape=jax.ShapeDtypeStruct(array.shape, array.dtype),
        input_output_aliases={0: 0},
        cost_estimate=pl.CostEstimate(flops=0, bytes_accessed=0, transcendentals=0),
        name="fence",
    )(array, *after)


def join(*parts):
    return jnp.concatenate(parts, axis=0)


def add_low(*parts):
    total = parts[0].astype(f32)
    for part in parts[1:]:
        total = total + part.astype(f32)
    return total.astype(bf16)


def held(array, after):
    return fence(array, *after) if after else array


def sends_kernel(count, layout, *refs):
    for out, parts in zip(refs[len(refs) - len(layout) :], layout):
        at = 0
        for which, first, n in parts:
            out[at : at + n] = refs[which][first : first + n]
            at += n


def make_sends(arrays, layout, after=()):
    width = arrays[0].shape[1]
    low = lambda parts: jax.ShapeDtypeStruct((sum(n for _, _, n in parts), width), arrays[0].dtype)
    return pl.pallas_call(
        functools.partial(sends_kernel, len(arrays), layout),
        in_specs=[VMEM] * len(arrays) + [ANY] * len(after),
        out_specs=[VMEM] * len(layout),
        out_shape=[low(parts) for parts in layout],
        compiler_params=pltpu.CompilerParams(vmem_limit_bytes=16 * 1024 * 1024),
        cost_estimate=pl.CostEstimate(flops=0, bytes_accessed=0, transcendentals=0),
        name="sends",
    )(*arrays, *after)


def relay_gather(own, na, swap, during=None, hold=None):
    nb = own.shape[0] - na
    during = during or (lambda stage, arrived, sends: ())
    hold = hold or {}
    own = held(own, hold.get(1, ()))
    s1, s3, s4 = swap(own, 1), swap(own, 3), swap(own, 4)
    after = during(1, (own,), (own,)) + hold.get(2, ())
    layout = (
        ((0, 0, na), (1, 0, na)),
        ((1, 0, na), (2, na, nb)),
        ((0, na, nb), (2, na, nb)),
    )
    sends = make_sends((s1, s3, s4), layout, after)
    zz, v1, v3 = swap(sends[0], 4), swap(sends[1], 1), swap(sends[2], 3)
    after = during(2, (s1, s3, s4), tuple(sends)) + hold.get(3, ())
    sends = make_sends((zz, v1), (((0, na, na),), ((1, na, nb),)), after)
    z2a, z2b = swap(sends[0], 1), swap(sends[1], 3)
    during(3, (zz, v1, v3), tuple(sends))
    return own, s1, s3, s4, zz, v1, v3, z2a, z2b


def relay_scatter(pa, pb, swap, hold=None, sent=None):
    na, nb = pa[0].shape[0], pb[0].shape[0]
    hold = hold or {}
    sent = {} if sent is None else sent
    get = lambda stage: hold[stage]() if stage in hold else ()
    after = get(1)
    sent[1] = (held(pa[6], after), held(pb[6], after))
    r1, r3 = swap(sent[1][0], 1), swap(sent[1][1], 3)
    p7a = add_low(pa[7], r1)
    p5b = add_low(pb[5], r3)
    after = get(2)
    sends = (join(pa[5], p7a), join(pa[2], p5b), join(pb[2], pb[7]))
    sent[2] = tuple(held(x, after) for x in sends)
    zz, v1, v3 = swap(sent[2][0], 4), swap(sent[2][1], 1), swap(sent[2][2], 3)
    p1 = join(add_low(pa[1], zz[:na]), add_low(pb[1], v3[:nb]))
    p3 = join(add_low(pa[3], zz[na:], v1[:na]), pb[3])
    p4 = join(pa[4], add_low(pb[4], v1[na:], v3[nb:]))
    after = get(3)
    sent[3] = tuple(held(x, after) for x in (p1, p3, p4))
    s1, s3, s4 = swap(sent[3][0], 1), swap(sent[3][1], 3), swap(sent[3][2], 4)
    return pa[0], pb[0], s1, s3, s4


def total_of(pieces):
    pa, pb, s1, s3, s4 = pieces
    na = pa.shape[0]
    total_a = pa.astype(f32) + s1[:na].astype(f32) + s3[:na].astype(f32) + s4[:na].astype(f32)
    total_b = pb.astype(f32) + s1[na:].astype(f32) + s3[na:].astype(f32) + s4[na:].astype(f32)
    return total_a, total_b


def ring_scatter(pieces, swap, after, sent):
    near = [join(pieces[j], pieces[j ^ 4]) for j in range(4)]
    near[1:] = [held(x, after) for x in near[1:]]
    sent += near[1:]
    total = near[0].astype(f32)
    for j in (1, 3, 2):
        total = total + swap(near[j], j).astype(f32)
    return total


def pair_sum(total, swap, after=()):
    half = total.shape[0] // 2
    return total[:half] + swap(held(total[half:].astype(bf16), after), 4).astype(f32)


def gather_direct(array, index, swap):
    pair = index & 4
    high = (index >> 2) & 1
    two = jnp.zeros((2,) + array.shape, array.dtype)
    two = lax.dynamic_update_index_in_dim(two, array, high, 0)
    two = lax.dynamic_update_index_in_dim(two, swap(array, 4), 1 - high, 0)
    ring = index & 3
    out = jnp.zeros((2, 4) + array.shape, array.dtype)
    out = lax.dynamic_update_index_in_dim(out, two, ring, 1)
    for step in (1, 3, 2):
        out = lax.dynamic_update_index_in_dim(out, swap(two, step), ring ^ step, 1)
    return out.reshape((8,) + array.shape)


def scatter_direct(pieces, index, swap):
    high = (index >> 2) & 1
    ring = index & 3
    quads = pieces.reshape((2, 4) + pieces.shape[1:])
    total = lax.dynamic_index_in_dim(quads, ring, 1, keepdims=False).astype(f32)
    for step in (1, 3, 2):
        piece = lax.dynamic_index_in_dim(quads, ring ^ step, 1, keepdims=False)
        total = total + swap(piece, step).astype(f32)
    mine = lax.dynamic_index_in_dim(total, high, 0, keepdims=False)
    theirs = lax.dynamic_index_in_dim(total, 1 - high, 0, keepdims=False)
    return mine + swap(theirs.astype(bf16), 4).astype(f32)


def assemble_kernel(cuts, sizes, place_ref, *refs):
    arrays, outs = refs[:18], refs[18:]
    index, core = place_ref[0], place_ref[1]
    for (k, h), (i, at) in where_parts(0, 9, sizes).items():
        for out, (which, first, n, column, width) in zip(outs, cuts):
            if which == h:
                rows, columns = slice(at + first, at + first + n), slice(column, column + width)
                out[index ^ k, core] = arrays[i][rows, :, columns]
                out[index ^ k, 1 - core] = arrays[9 + i][rows, :, columns]


def assemble(mine, theirs, na, cuts, index, core):
    rows, columns = mine[0].shape
    eights = [x.reshape(x.shape[0] // 8, 8, columns) for x in (*mine, *theirs)]
    sizes = (na // 8, (rows - na) // 8)
    outs = pl.pallas_call(
        functools.partial(assemble_kernel, cuts, sizes),
        in_specs=[SMEM] + [VMEM] * 18,
        out_specs=[VMEM] * len(cuts),
        out_shape=[jax.ShapeDtypeStruct((8, 2, n, 8, width), bf16) for _, _, n, _, width in cuts],
        compiler_params=pltpu.CompilerParams(vmem_limit_bytes=40 * 1024 * 1024),
        name="assemble",
    )(jnp.stack([index, core]), *eights)
    return [x.reshape(-1, x.shape[-1]) for x in outs]


def gain_rows(block):
    pick = lax.broadcasted_iota(jnp.int32, (ACT_PAD, 128), 0)
    pick = (pick == lax.broadcasted_iota(jnp.int32, (ACT_PAD, 128), 1)).astype(bf16)
    turned = dot_t(pick, block)
    return turned[0:1], turned[1:2]


def keys_kernel(*refs):
    rows, (gain_d, gain_a, weight_d, weight_a, cosine, sine) = refs[:9], refs[9:15]
    normed_d, normed_a, keys, values = refs[-4:]
    gain_d, gain_a = gain_rows(gain_d[...])[0], gain_rows(gain_a[...])[0]
    width = weight_a.shape[0]
    prefix, action = [], []
    for i, parts in enumerate(ARRIVALS):
        at = 0
        for _, h in parts:
            prefix.append(rows[i][at : at + HALF_A])
            at += HALF_A
            if h:
                action.append(rows[i][at : at + ACT_PAD, :width])
                at += ACT_PAD
    x = join(*prefix).astype(f32)
    low_d = (x * inverse_rms(x) * gain_d).astype(bf16)
    x = join(*action).astype(f32)
    low_a = (x * inverse_rms(x) * gain_a).astype(bf16)
    normed_d[:PREF] = low_d[:PREF]
    normed_a[:ACT_PAD] = low_a[:ACT_PAD]
    normed_d[PREF:] = low_d[ROW_PAIR : ROW_PAIR + PREF]
    normed_a[ACT_PAD:] = low_a[ACT_PAIR : ACT_PAIR + ACT_PAD]
    raw = join(dot(low_d, weight_d[...]), dot(low_a, weight_a[...]))
    keys[...] = rotate(raw[:, :HD], cosine[...], sine[...]).astype(bf16)
    values[...] = raw[:, HD:].astype(bf16)


def keys_of(rows, gain_d, gain_a, weight_d, weight_a, cosine, sine, after):
    width_d, width_a = gain_d.shape[0], gain_a.shape[0]
    count = cosine.shape[0]
    shape = lambda *dims: jax.ShapeDtypeStruct(dims, bf16)
    given = [*rows, gain_d, gain_a, weight_d, weight_a, cosine, sine]
    return pl.pallas_call(
        keys_kernel,
        in_specs=[VMEM] * len(given) + [ANY] * len(after),
        out_specs=[VMEM] * 4,
        out_shape=[
            shape(2 * PREF, width_d),
            shape(2 * ACT_PAD, width_a),
            shape(count, HD),
            shape(count, HD),
        ],
        compiler_params=pltpu.CompilerParams(vmem_limit_bytes=48 * 1024 * 1024),
        cost_estimate=pl.CostEstimate(
            flops=4 * count * width_d * HD, bytes_accessed=8 * 1024 * 1024, transcendentals=count
        ),
        name="keys_of",
    )(*given, *after)


def gelu_parts(gate):
    c0 = 0.7978845608028654
    c1 = 0.044715
    square = gate * gate
    tanh = jnp.tanh(c0 * gate * (1.0 + c1 * square))
    half = 0.5 * (1.0 + tanh)
    slope = half + 0.5 * gate * (1.0 - tanh * tanh) * c0 * (1.0 + 3.0 * c1 * square)
    return gate * half, slope


def feed_block(rows, seed, gate_weight, up_weight, down_weight, valid):
    into, out_of = (dot_t, dot) if valid is None else (dot, dot_t)
    gate = into(rows, gate_weight)
    up = into(rows, up_weight)
    active, slope = gelu_parts(gate)
    product_delta = dot_t(seed, down_weight)
    if valid is not None:
        active = active * valid
        product_delta = product_delta * valid
    product = (active * up).astype(bf16)
    gate_delta = (product_delta * up * slope).astype(bf16)
    up_delta = (product_delta * active).astype(bf16)
    rows_delta = out_of(gate_delta, gate_weight) + out_of(up_delta, up_weight)
    return product, gate_delta, up_delta, rows_delta.astype(bf16)


def feed_kernel(layout, *refs):
    arrays = 1 + max(i for parts in layout for i, _ in parts)
    rows_refs, seed_refs, refs = refs[:arrays], refs[arrays : 2 * arrays], refs[2 * arrays :]
    gate_ref, up_ref, down_ref = refs[:3]
    action_gate_ref, action_up_ref, action_down_ref, valid_ref = refs[3:7]
    count = len(layout)
    outs = refs[-(2 * count + 8) :]
    products, deltas, kept_rows, kept_seeds = outs[:4]
    action_products, action_deltas, action_rows, action_seeds = outs[4:8]
    width = action_gate_ref.shape[0]
    rest = PREF - HALF_A

    def prefix_of(blocks):
        parts = []
        for (ia, a), (ib, b) in layout:
            parts += [blocks[ia][a : a + HALF_A], blocks[ib][b : b + rest]]
        return join(*parts)

    def action_of(blocks):
        parts = []
        for _, (ib, b) in layout:
            parts.append(blocks[ib][b + rest : b + HALF_B, :width])
        return join(*parts) if count > 1 else parts[0]

    rows, seed = prefix_of(rows_refs), prefix_of(seed_refs)
    product, gate_delta, up_delta, rows_delta = feed_block(
        rows, seed, gate_ref[...], up_ref[...], down_ref[...], None
    )
    hidden = product.shape[1]
    spare = jnp.zeros((count * PREF, HIDDEN_PAD - hidden), bf16)
    products[:, :hidden] = product
    products[:, hidden:] = spare
    deltas[:, :hidden] = gate_delta
    deltas[:, hidden:HIDDEN_PAD] = spare
    deltas[:, HIDDEN_PAD : HIDDEN_PAD + hidden] = up_delta
    deltas[:, HIDDEN_PAD + hidden :] = spare
    kept_rows[...] = rows
    kept_seeds[...] = seed
    rows, seed = action_of(rows_refs), action_of(seed_refs)
    product, gate_delta, up_delta, action_rows_delta = feed_block(
        rows,
        seed,
        action_gate_ref[...],
        action_up_ref[...],
        action_down_ref[...],
        valid_ref[...],
    )
    slots = gate_delta.shape[1]
    action_products[...] = product
    action_deltas[:, :slots] = gate_delta
    action_deltas[:, slots:] = up_delta
    action_rows[...] = rows
    action_seeds[...] = seed
    blank = jnp.zeros((ACT_PAD, rows_delta.shape[1] - width), bf16)
    for i in range(count):
        a, b, c = i * PREF, i * PREF + HALF_A, (i + 1) * PREF
        extra = slice(i * ACT_PAD, (i + 1) * ACT_PAD)
        ref_a, ref_b = outs[8 + 2 * i : 10 + 2 * i]
        ref_a[...] = rows_delta[a:b]
        ref_b[:rest] = rows_delta[b:c]
        ref_b[rest:, :width] = action_rows_delta[extra]
        ref_b[rest:, width:] = blank


def feed(arrays, seeds, weights, layout, base, kept, after):
    count = len(layout)
    width = arrays[0].shape[1]
    hidden = weights[0].shape[0]
    action_width, slots = weights[3].shape
    once = pl.Buffered(1)
    at = base // count

    def whole(array):
        return pl.BlockSpec(array.shape, lambda i: (0, 0), pipeline_mode=once)

    def part(size, columns):
        return (
            jax.ShapeDtypeStruct((N_MP * size, columns), bf16),
            pl.BlockSpec((count * size, columns), lambda i: (at, 0), pipeline_mode=once),
        )

    def own(size):
        return (
            jax.ShapeDtypeStruct((size, width), bf16),
            pl.BlockSpec((size, width), lambda i: (0, 0), pipeline_mode=once),
        )

    outs = [
        part(PREF, HIDDEN_PAD),
        part(PREF, 2 * HIDDEN_PAD),
        part(PREF, width),
        part(PREF, width),
        part(ACT_PAD, slots),
        part(ACT_PAD, 2 * slots),
        part(ACT_PAD, action_width),
        part(ACT_PAD, action_width),
    ] + [own(HALF_A), own(HALF_B)] * count
    reused = [] if kept is None else list(kept)
    given = [*arrays, *seeds]
    placed = len(given) + len(weights)
    results = pl.pallas_call(
        functools.partial(feed_kernel, layout),
        grid=(1,),
        in_specs=[whole(x) for x in given]
        + [VMEM] * len(weights)
        + [ANY] * (len(reused) + len(after)),
        out_shape=[shape for shape, _ in outs],
        out_specs=[spec for _, spec in outs],
        input_output_aliases={placed + i: i for i in range(len(reused))},
        compiler_params=pltpu.CompilerParams(
            dimension_semantics=("arbitrary",), vmem_limit_bytes=VMEM_FEED * 1024 * 1024
        ),
        cost_estimate=pl.CostEstimate(
            flops=10 * count * (PREF * width * hidden + ACT_PAD * action_width * slots),
            bytes_accessed=6 * (width * hidden + action_width * slots),
            transcendentals=count * PREF * hidden,
        ),
        name="feed",
    )(*given, *weights, *reused, *after)
    blocks = [results[8 + 2 * i : 10 + 2 * i] for i in range(count)]
    return blocks, results[:8]


def see(own_ref, key_ref):
    own, key = own_ref[...], key_ref[...]
    return (own[:, 0:1] == key[0:1]) | (own[:, 1:2] == key[1:2])


def attend_kernel(*refs):
    (normed_d, normed_a, x_d, x_a, wq_d, wq_a, wo_m, wo_e, wo_a) = refs[:9]
    (gain_d, gain_a, cosine, sine, own_codes, key_codes) = refs[9:15]
    keys, values = refs[15][...], refs[16][...]
    (queries, context, tops, totals, hidden_d, hidden_a, block) = refs[-7:]
    gain_d, gain_a = gain_rows(gain_d[...])[1], gain_rows(gain_a[...])[1]
    raw = join(dot(normed_d[:PREF], wq_d[...]), dot(normed_a[:ACT_PAD], wq_a[...]))
    visible = see(own_codes, key_codes)
    cos, sin = cosine[...], sine[...]
    heads = []
    for h in range(HEADS):
        rows = slice(h * BLOCK, (h + 1) * BLOCK)
        query = (rotate(raw[:, h * HD : (h + 1) * HD], cos, sin) * HD**-0.5).astype(bf16)
        queries[rows] = query
        scores = jnp.where(visible, dot_t(query, keys), -1e30)
        top = jnp.max(scores, axis=1, keepdims=True)
        shifted = jnp.exp(scores - top)
        total = jnp.sum(shifted, axis=1, keepdims=True)
        tops[rows] = top
        totals[rows] = total
        heads.append(dot((shifted / total).astype(bf16), values).astype(bf16))
    mixed = jnp.concatenate(heads, axis=1)
    context[...] = mixed
    main, width_d, width_a = wo_m.shape[1], x_d.shape[1], x_a.shape[1]
    low_d, low_a = mixed[:PREF], mixed[PREF:]
    state = x_d[...].astype(f32) + jnp.concatenate(
        [dot(low_d, wo_m[...]), dot(low_d, wo_e[...])], axis=1
    )
    hidden_d[...] = state
    second_d = (state * inverse_rms(state) * gain_d).astype(bf16)
    real = lax.broadcasted_iota(jnp.int32, (ACT_PAD, width_a), 0) < ACT
    state = jnp.where(real, x_a[...].astype(f32) + dot(low_a, wo_a[...]), 0.0)
    hidden_a[...] = state
    second_a = (state * inverse_rms(state) * gain_a).astype(bf16)
    block[:PREF] = second_d
    block[PREF:, :width_a] = second_a
    block[PREF:, width_a:] = jnp.zeros((ACT_PAD, width_d - width_a), bf16)


def attend(*given, after):
    x_d, x_a = given[2:4]
    width_d, width_a = x_d.shape[1], x_a.shape[1]
    shape = jax.ShapeDtypeStruct
    stacked = HEADS * BLOCK
    return pl.pallas_call(
        attend_kernel,
        in_specs=[VMEM] * len(given) + [ANY] * len(after),
        out_specs=[VMEM] * 7,
        out_shape=[
            shape((stacked, HD), bf16),
            shape((BLOCK, HEADS * HD), bf16),
            shape((stacked, 1), f32),
            shape((stacked, 1), f32),
            shape((PREF, width_d), f32),
            shape((ACT_PAD, width_a), f32),
            shape((BLOCK, width_d), bf16),
        ],
        compiler_params=pltpu.CompilerParams(vmem_limit_bytes=50 * 1024 * 1024),
        cost_estimate=pl.CostEstimate(
            flops=4 * BLOCK * HEADS * HD * (N_MP * BLOCK + width_d),
            bytes_accessed=4 * 1024 * 1024 * 5,
            transcendentals=stacked * N_MP * BLOCK,
        ),
        name="attend",
    )(*given, *after)


def attend_back_kernel(*refs):
    pieces = refs[:5]
    (hidden_d, hidden_a, cotangent_d, cotangent_a, share, gain_d, gain_a) = refs[5:12]
    (wo_m, wo_e, wo_a, queries, tops, totals, cosine, sine, own_codes, key_codes) = refs[12:22]
    keys, values = refs[22][...], refs[23][...]
    outs = refs[-(6 + len(PARTS)) :]
    (hidden_delta_d, hidden_delta_a, low, terms_d, terms_a, query_delta) = outs[:6]
    kv_deltas = outs[6:]
    gain_d, gain_a = gain_rows(gain_d[...])[1], gain_rows(gain_a[...])[1]
    delta = join(*total_of([piece[...] for piece in pieces]))
    width_d, width_a = hidden_d.shape[1], hidden_a.shape[1]
    lows = []
    for rows, state_ref, cotangent, gain, out, terms in (
        (slice(0, PREF), hidden_d, cotangent_d, gain_d, hidden_delta_d, terms_d),
        (slice(PREF, BLOCK), hidden_a, cotangent_a, gain_a, hidden_delta_a, terms_a),
    ):
        state = state_ref[...]
        change = delta[rows, : state.shape[1]]
        scale = inverse_rms(state)
        seed = cotangent[...].astype(f32) * share[rows]
        back = seed + normalize_back(state, scale, gain, change)
        out[...] = back
        terms[...] = (change * state * scale).astype(bf16)
        lows.append(back.astype(bf16))
    low_d, low_a = lows
    low[:PREF] = low_d
    low[PREF:, :width_a] = low_a
    low[PREF:, width_a:] = jnp.zeros((ACT_PAD, width_d - width_a), bf16)
    main = wo_m.shape[1]
    context_delta = join(
        dot_t(low_d[:, :main], wo_m[...]) + dot_t(low_d[:, main:], wo_e[...]),
        dot_t(low_a, wo_a[...]),
    ).astype(bf16)
    visible = see(own_codes, key_codes)
    cos, sin = cosine[...], sine[...]
    keys_delta, values_delta = None, None
    for h in range(HEADS):
        rows = slice(h * BLOCK, (h + 1) * BLOCK)
        query = queries[rows]
        change = context_delta[:, h * HD : (h + 1) * HD]
        scores = jnp.where(visible, dot_t(query, keys), -1e30)
        probs = jnp.exp(scores - tops[rows]) / totals[rows]
        probs_delta = dot_t(change, values)
        row_dot = jnp.sum(probs * probs_delta, axis=1, keepdims=True)
        score_delta = (probs * (probs_delta - row_dot)).astype(bf16)
        turned = unrotate(dot(score_delta, keys), cos, sin) * HD**-0.5
        query_delta[:, h * HD : (h + 1) * HD] = turned.astype(bf16)
        key_part = t_dot(score_delta, query)
        value_part = t_dot(probs.astype(bf16), change)
        keys_delta = key_part if h == 0 else keys_delta + key_part
        values_delta = value_part if h == 0 else values_delta + value_part
    at, extra = 0, len(PARTS) * HALF_A
    for (_, half), out in zip(PARTS, kv_deltas):
        for columns, change in ((slice(0, HD), keys_delta), (slice(HD, 2 * HD), values_delta)):
            out[:HALF_A, columns] = change[at : at + HALF_A].astype(bf16)
            if half:
                out[HALF_A:, columns] = change[extra : extra + ACT_PAD].astype(bf16)
        at += HALF_A
        extra += half * ACT_PAD


def attend_back(*given, after):
    hidden_d, hidden_a = given[5:7]
    width_d, width_a = hidden_d.shape[1], hidden_a.shape[1]
    shape = jax.ShapeDtypeStruct
    stacked = HEADS * BLOCK
    outs = pl.pallas_call(
        attend_back_kernel,
        in_specs=[VMEM] * len(given) + [ANY] * len(after),
        out_specs=[VMEM] * (6 + len(PARTS)),
        out_shape=[
            shape((PREF, width_d), f32),
            shape((ACT_PAD, width_a), f32),
            shape((BLOCK, width_d), bf16),
            shape((PREF, width_d), bf16),
            shape((ACT_PAD, width_a), bf16),
            shape((BLOCK, HEADS * HD), bf16),
        ]
        + [shape(((HALF_A, HALF_B)[half], 2 * HD), bf16) for _, half in PARTS],
        compiler_params=pltpu.CompilerParams(vmem_limit_bytes=50 * 1024 * 1024),
        cost_estimate=pl.CostEstimate(
            flops=2 * BLOCK * HEADS * HD, bytes_accessed=4 * BLOCK, transcendentals=stacked
        ),
        name="attend_back",
    )(*given, *after)
    kv_deltas = dict(zip(PARTS, outs[6:]))
    pa = {k: kv_deltas[k, 0] for k in range(8)}
    pb = {k: kv_deltas[k, 1] for k in range(8)}
    return outs[:6], pa, pb


def theirs_kernel(cuts, place_ref, *refs):
    out = refs[-1]
    core = place_ref[1]
    for ref, (row, n, source, column, width) in zip(refs, cuts):
        out[:, row : row + n, :, column : column + width] = ref[
            1 - core, :, :, :, source : source + width
        ]


def near_kernel(cuts, place_ref, *refs):
    got, outs = refs[len(cuts)], refs[-4:]
    mp, core = place_ref[0], place_ref[1]
    for step, out in zip((0, 1, 3, 2), outs):
        for pair in range(2):
            block = mp ^ step ^ (4 * pair)
            base = pair * got.shape[1]
            for ref, (row, n, source, column, width) in zip(refs, cuts):
                columns = slice(column, column + width)
                mine = ref[core, block, :, :, source : source + width].astype(f32)
                total = mine + got[block, row : row + n, :, columns].astype(f32)
                out[base + row : base + row + n, :, columns] = total.astype(bf16)


def sum_weights(grads, cuts, columns, place, sent, got, after, before_last, last_sent):
    views = [g.reshape(2, 8, -1, 8, g.shape[1]) for g in grads]
    eights = max(row + n for row, n, _, _, _ in cuts)
    params = pltpu.CompilerParams(vmem_limit_bytes=44 * 1024 * 1024)
    cost = pl.CostEstimate(flops=0, bytes_accessed=0, transcendentals=0)
    low = lambda *dims: jax.ShapeDtypeStruct(dims, bf16)
    theirs = pl.pallas_call(
        functools.partial(theirs_kernel, cuts),
        in_specs=[SMEM] + [VMEM] * len(views),
        out_specs=VMEM,
        out_shape=low(8, eights, 8, columns),
        compiler_params=params,
        cost_estimate=cost,
        name="theirs",
    )(place, *views)
    near = pl.pallas_call(
        functools.partial(near_kernel, cuts),
        in_specs=[SMEM] + [VMEM] * (len(views) + 1) + [ANY] * len(after),
        out_specs=[VMEM] * 4,
        out_shape=[low(2 * eights, 8, columns)] * 4,
        compiler_params=params,
        cost_estimate=cost,
        name="near",
    )(place, *views, core_swap(theirs), *after)
    near = [x.reshape(16 * eights, columns) for x in near]
    sent += near[1:]
    total = near[0].astype(f32)
    for step, x in zip((1, 3, 2), near[1:]):
        got.append(mp_swap(x, step))
        total = total + got[-1].astype(f32)
    half = 8 * eights
    last_sent.append(held(total[half:].astype(bf16), before_last))
    return (total[:half] + mp_swap(last_sent[-1], 4).astype(f32)).astype(bf16)


def pad_action(rows):
    return jnp.pad(rows, ((0, ACT_PAD - ACT), (0, 0)))


def widen(rows, width):
    return jnp.pad(rows, ((0, 0), (0, width - rows.shape[1])))


def block_of(prefix_rows, action_rows):
    return join(prefix_rows, widen(action_rows, prefix_rows.shape[1]))


def order_matrix(size, rows):
    d = jnp.arange(size, dtype=jnp.int32)
    r = d % rows
    mp = (d // rows) % 8
    dp = d // (8 * rows)
    place = (dp % 2) * (size // 2) + mp * (8 * rows) + (dp // 2) * rows + r
    return (place[:, None] == jnp.arange(size, dtype=jnp.int32)[None, :]).astype(bf16)


def dot(a, b):
    return jnp.dot(a, b, preferred_element_type=f32)


def dot_t(a, b):
    return lax.dot_general(a, b, (((1,), (1,)), ((), ())), preferred_element_type=f32)


def t_dot(a, b):
    return lax.dot_general(a, b, (((0,), (0,)), ((), ())), preferred_element_type=f32)


def inverse_rms(rows):
    return lax.rsqrt(jnp.mean(rows * rows, axis=-1, keepdims=True) + EPSILON)


def normalize_back(rows, scale, gain, delta):
    a = delta * gain
    return scale * (a - rows * (scale * scale) * jnp.mean(a * rows, axis=-1, keepdims=True))


def rotate(rows, cosine, sine):
    half = HD // 2
    first, second = rows[:, :half], rows[:, half:]
    return jnp.concatenate(
        [first * cosine - second * sine, second * cosine + first * sine], axis=1
    )


def unrotate(rows, cosine, sine):
    return rotate(rows, cosine, -sine)


def angle_tables(place):
    half = HD // 2
    frequency = ROPE_BASE ** (-jnp.arange(half, dtype=f32) / half)
    angles = place.astype(f32)[:, None] * frequency[None, :]
    return jnp.cos(angles), jnp.sin(angles)


def on_device(
    prefix_input,
    action_input,
    prefix_cotangent,
    action_cotangent,
    prefix_lengths,
    mixture,
    cut_points,
    prefix_query,
    prefix_key,
    prefix_value,
    prefix_out,
    prefix_first_gain,
    prefix_second_gain,
    action_query,
    action_key,
    action_value,
    action_out,
    action_first_gain,
    action_second_gain,
    prefix_gate,
    prefix_up,
    prefix_down,
    action_gate,
    action_up,
    action_down,
):
    mp = lax.axis_index("mp")
    dp = lax.axis_index("dp")
    core = dp & 1
    yz = (dp >> 3) * 4 + ((dp >> 1) & 3)
    D = prefix_input.shape[2]
    DA = action_input.shape[2]

    def column_block(first, second):
        return jnp.pad(jnp.stack([first, second], axis=1), ((0, 0), (0, 126)))

    pack_d = jnp.concatenate(
        [
            prefix_key,
            prefix_value,
            column_block(prefix_first_gain, prefix_second_gain),
            prefix_query,
        ],
        axis=1,
    )
    wide = pack_d.shape[1]
    pack = jnp.concatenate(
        [
            pack_d[:8],
            action_key,
            action_value,
            column_block(action_first_gain, action_second_gain),
            action_query,
            action_out,
            prefix_out,
            jnp.pad(pack_d[8:].reshape(8, wide // 8), ((0, 0), (0, 48))),
        ],
        axis=1,
    )
    lengths = prefix_lengths[0]
    first_length = lengths[0]

    def tables(source, row):
        is_action = row >= PREF
        prefix_row = source * PREF + row
        prefix_item = (prefix_row >= first_length).astype(jnp.int32)
        prefix_place = prefix_row - jnp.where(prefix_item == 1, first_length, 0)
        action_row = source * ACT + row - PREF
        action_item = (action_row >= ACT_LEN).astype(jnp.int32)
        action_place = jnp.where(action_item == 1, lengths[1], first_length) + action_row % ACT_LEN
        action_item = jnp.where(row - PREF < ACT, action_item, 2)
        item = jnp.where(is_action, action_item, prefix_item)
        place = jnp.where(is_action, action_place, prefix_place)
        return item, place, is_action

    own_item, own_place, own_is_action = tables(mp, jnp.arange(BLOCK, dtype=jnp.int32))
    key_item, key_place, key_is_action = tables(jnp.asarray(KEY_BLOCK) ^ mp, jnp.asarray(KEY_ROW))
    key_cos, key_sin = angle_tables(key_place)
    own_codes = jnp.stack([own_item, jnp.where(own_is_action, own_item, -2)], axis=1)
    key_codes = jnp.stack(
        [jnp.where(key_is_action, -1, key_item), jnp.where(key_is_action, key_item, -1)], axis=0
    )
    own_cos, own_sin = angle_tables(own_place)

    share = mixture[0].astype(f32) / 32.0
    row_share = jnp.where(own_item == 1, share[1], share[0])[:, None]
    cotangent_a = pad_action(action_cotangent[0])
    prefix_seed = prefix_cotangent[0].astype(f32) * row_share[:PREF]
    action_seed = cotangent_a.astype(f32) * row_share[PREF:]
    seed_block = block_of(prefix_seed.astype(bf16), action_seed.astype(bf16))

    near = gather_direct(pack, mp, mp_swap)
    last_row = near[:, :, pack.shape[1] - 256 : pack.shape[1] - 48].reshape(8, 1, wide)
    near_d = jnp.concatenate([near[:, :, :wide], last_row], axis=1).reshape(72, wide)
    near_a = near[:, :, wide : pack.shape[1] - 256].reshape(64, -1)
    edge = near_a[:, 2688 + 1024 :]
    kv_a = widen(jnp.concatenate([near_a[:, :640], edge], axis=1), 1024)
    pack_a = join(near_a[:, 640:1664], near_a[:, 1664:2688], kv_a)
    pack_b = join(near_d[:, 640:], near_a[:, 2688 : 2688 + 1024], widen(near_d[:, :640], 1024))
    arrived = {}

    def note(name):
        def during(stage, blocks, sends):
            arrived[name, stage] = blocks
            arrived[name, "sends", stage] = sends
            return ()

        return during

    own_action = pad_action(action_input[0])
    own_block = block_of(prefix_input[0], own_action)
    own_block = fence(own_block, near)
    x_rows = relay_gather(own_block, HALF_A, mp_swap)
    hold = {2: x_rows[1:4], 3: x_rows[4:7]}
    mine = relay_gather(join(pack_a, pack_b), pack_a.shape[0], yz_swap, note("weights"), hold)
    theirs = [core_swap(x) for x in mine]
    cuts = (
        (0, 0, 8, 0, 1024),
        (0, 8, 8, 0, 1024),
        (0, 16, 8, 0, 512),
        (0, 16, 8, 512, 128),
        (0, 16, 8, 640, 128),
        (1, 0, 9, 0, 1024),
        (1, 9, 8, 0, 1024),
        (1, 17, 9, 0, 512),
        (1, 17, 9, 512, 128),
    )
    wq_a, wo_a, wkv_a, gains_a, wo_e, wq_d, wo_m, wkv_d, gains_d = assemble(
        mine, theirs, pack_a.shape[0], cuts, yz, core
    )
    seeds = relay_gather(
        seed_block,
        HALF_A,
        mp_swap,
        note("seeds"),
        {1: arrived["weights", "sends", 3][:1]},
    )

    normed_d, normed_a, keys, values = keys_of(
        x_rows,
        gains_d,
        gains_a,
        wkv_d,
        wkv_a,
        key_cos,
        key_sin,
        arrived["seeds", "sends", 2],
    )
    x_d, x_a = prefix_input[0].astype(f32), own_action.astype(f32)
    rms_d, rms_a = inverse_rms(x_d), inverse_rms(x_a)
    queries, context, tops, totals, hidden_d, hidden_a, second_block = attend(
        normed_d,
        normed_a,
        prefix_input[0],
        own_action,
        wq_d,
        wq_a,
        wo_m,
        wo_e,
        wo_a,
        gains_d,
        gains_a,
        own_cos,
        own_sin,
        own_codes,
        key_codes,
        keys,
        values,
        after=arrived["seeds", "sends", 3],
    )

    slots = action_gate.shape[2]
    cut_pair = lax.dynamic_slice_in_dim(cut_points, mp, 2)
    valid = (jnp.arange(slots, dtype=jnp.int32) < cut_pair[1] - cut_pair[0]).astype(f32)[None, :]
    weights = (prefix_gate.T, prefix_up.T, prefix_down)
    weights += (action_gate[0], action_up[0], action_down[0], valid)
    kept = None
    results = {}

    def run(arrays, first, blocks, base, after):
        nonlocal kept
        where = where_parts(first, len(arrays), (HALF_A, HALF_B))
        layout = tuple((where[k, 0], where[k, 1]) for k in blocks)
        some = seeds[first : first + len(arrays)]
        done, kept = feed(arrays, some, weights, layout, base, kept, after)
        results.update(zip(blocks, done))
        return (done[0][0],)

    def feed_during(stage, arrays, sends):
        if stage == 3:
            return ()
        first, blocks, base = {1: (0, (0,), 3), 2: (1, (1, 3, 4), 0)}[stage]
        return run(arrays, first, blocks, base, sends)

    second_block = fence(second_block, seeds[8])
    arrays = relay_gather(second_block, HALF_A, mp_swap, feed_during)
    run(arrays[4:], 4, (2, 5, 7, 6), 4, ())
    product_d, deltas_d, rows_d, seeds_d, product_a, deltas_a, rows_a, seeds_a = kept

    grads = (
        t_dot(deltas_d, rows_d),
        t_dot(product_d, seeds_d),
        t_dot(rows_a, deltas_a),
        t_dot(product_a, seeds_a),
    )
    hidden = prefix_down.shape[0]
    grads = tuple(g.astype(bf16) for g in grads)
    pa = {k: v[0] for k, v in results.items()}
    pb = {k: v[1] for k, v in results.items()}
    delta_pieces = relay_scatter(pa, pb, mp_swap)
    grads = grads[:3] + (fence(grads[3], *delta_pieces[2:]),)
    grads = tuple(lax.psum(g, "dp") for g in grads)
    finished = (
        grads[0][:hidden].astype(f32),
        grads[0][HIDDEN_PAD : HIDDEN_PAD + hidden].astype(f32),
        grads[1][:hidden].astype(f32),
        grads[2][:, :slots].astype(f32),
        grads[2][:, slots:].astype(f32),
        grads[3].astype(f32),
    )

    partial_d = dot(product_d[:, :hidden], prefix_down).astype(bf16)
    partial_a = dot(product_a, action_down[0]).astype(bf16)
    out = []
    for k in range(8):
        i = (1, 3, 4, 0, 2, 5, 7, 6).index(k)
        mine = partial_a[i * ACT_PAD : (i + 1) * ACT_PAD]
        out.append(block_of(partial_d[i * PREF : (i + 1) * PREF], mine))
    out_sent = []
    out = ring_scatter(out, mp_swap, delta_pieces[2:], out_sent)
    (hidden_delta_d, hidden_delta_a, low, terms_d, terms_a, query_delta), pa, pb = attend_back(
        *delta_pieces,
        hidden_d,
        hidden_a,
        prefix_cotangent[0],
        cotangent_a,
        row_share,
        gains_d,
        gains_a,
        wo_m,
        wo_e,
        wo_a,
        queries,
        tops,
        totals,
        own_cos,
        own_sin,
        own_codes,
        key_codes,
        keys,
        values,
        after=tuple(out_sent),
    )
    low_d, low_a = low[:PREF], low[PREF:, :DA]

    kv_near = [join(pa[k], pb[k], pa[k ^ 4], pb[k ^ 4]) for k in range(4)]
    kv_part = kv_near[0].astype(f32)
    for k in (1, 3, 2):
        kv_part = kv_part + mp_swap(kv_near[k], k).astype(f32)
    pair = lambda table: join(
        own_cos if table is key_cos else own_sin,
        table[ROW_PAIR : ROW_PAIR + PREF],
        table[len(PARTS) * HALF_A + ACT_PAIR : len(PARTS) * HALF_A + ACT_PAIR + ACT_PAD],
    )
    kv_turned = jnp.concatenate(
        [unrotate(kv_part[:, :HD], pair(key_cos), pair(key_sin)), kv_part[:, HD:]], axis=1
    )
    kv_turned_low = kv_turned.astype(bf16)
    kv_rows_d = join(kv_turned_low[:PREF], kv_turned_low[BLOCK : BLOCK + PREF])
    kv_rows_a = join(kv_turned_low[PREF:BLOCK], kv_turned_low[BLOCK + PREF :])

    order_d, order_a = order_matrix(D, 9), order_matrix(DA, 8)
    turned_d = dot(normed_d, order_d).astype(bf16)
    turned_a = dot(normed_a, order_a).astype(bf16)
    turned_context = dot(context, order_a).astype(bf16)
    second_term_d = t_dot(dot(terms_d, order_d).astype(bf16), jnp.ones((PREF, 256), bf16))
    second_term_a = t_dot(dot(terms_a, order_a).astype(bf16), jnp.ones((ACT_PAD, 128), bf16))
    out_grad_d = t_dot(turned_context[:PREF], low_d).astype(bf16)
    out_grad_a = t_dot(turned_context[PREF:], low_a).astype(bf16)
    q_grad_d = t_dot(turned_d[:PREF], query_delta[:PREF]).astype(bf16)
    q_grad_a = t_dot(turned_a[:ACT_PAD], query_delta[PREF:]).astype(bf16)
    place = jnp.stack([mp, core])
    cuts = (
        (0, 8, 0, 0, 1024),
        (8, 8, 0, 0, 1024),
        (16, 9, 0, 0, 1024),
        (25, 8, 0, 0, 1024),
    )
    qo_sent, kv_sent, got, last_sent = [], [], [], []
    qo_grads = (q_grad_a, out_grad_a, q_grad_d, out_grad_d)
    qo = sum_weights(qo_grads, cuts, 1024, place, qo_sent, got, (), (), last_sent)
    kv_grad_d = t_dot(turned_d, kv_rows_d).astype(bf16)
    kv_grad_a = t_dot(turned_a, kv_rows_a).astype(bf16)
    cuts = (
        (0, 8, 0, 0, 512),
        (0, 8, 0, 512, 128),
        (0, 8, 1024, 640, 128),
        (8, 9, 0, 0, 512),
        (8, 9, 0, 512, 256),
    )
    kv_grads = (
        kv_grad_a,
        second_term_a.astype(bf16),
        out_grad_d,
        kv_grad_d,
        second_term_d.astype(bf16),
    )
    kv = sum_weights(kv_grads, cuts, 768, place, kv_sent, got, qo_sent, (), last_sent)
    kv_a, kv_d = kv[:64], kv[64:, :640]
    qo_a, qo_b = qo[:128], qo[128:]
    kv_other = mp_swap(held(kv_part[BLOCK:].astype(bf16), (*kv_sent, grads[0])), 4)
    kv_sum = kv_part[:BLOCK] + kv_other.astype(f32)
    kv_raw_delta = jnp.concatenate(
        [unrotate(kv_sum[:, :HD], own_cos, own_sin), kv_sum[:, HD:]], axis=1
    ).astype(bf16)

    out = pair_sum(out, mp_swap, tuple(last_sent))
    prefix_output = (hidden_d + out[:PREF]).astype(bf16)[None]
    action_output = (hidden_a + out[PREF:, :DA])[:ACT].astype(bf16)[None]

    last_d = jnp.concatenate([kv_d, qo_b[:72]], axis=1).reshape(8, 9, wide)
    last_a = jnp.concatenate(
        [kv_a[:, :640], qo_a[:64], qo_a[64:], qo_b[72:], kv_a[:, 640:]], axis=1
    ).reshape(8, 8, -1)
    last = jnp.concatenate(
        [
            last_d[:, :8],
            last_a,
            jnp.pad(last_d[:, 8:].reshape(8, 8, wide // 8), ((0, 0), (0, 0), (0, 48))),
        ],
        axis=2,
    )
    last = scatter_direct(fence(last, grads[0]), yz, yz_swap)
    ninth = last[:, last.shape[1] - 256 : last.shape[1] - 48].reshape(1, wide)
    grads_d = join(last[:, :wide], ninth)
    grads_a = last[:, wide : last.shape[1] - 256]

    def split_grads(grads, query, key, value, gain):
        key_grad = grads[:, :256]
        value_grad = grads[:, 256:512]
        second = grads[:, 512]
        query_grad = grads[:, 640:1664]
        first = (
            jnp.sum(query_grad * query.astype(f32), axis=1)
            + jnp.sum(key_grad * key.astype(f32), axis=1)
            + jnp.sum(value_grad * value.astype(f32), axis=1)
        ) / gain.astype(f32)
        return query_grad, key_grad, value_grad, first, second

    gd = split_grads(grads_d, prefix_query, prefix_key, prefix_value, prefix_first_gain)
    ga = split_grads(grads_a, action_query, action_key, action_value, action_first_gain)
    action_out_grad = grads_a[:, 1664:2688]
    prefix_out_grad = grads_a[:, 2688:]

    first_delta_d = dot_t(query_delta[:PREF], wq_d) + dot_t(kv_raw_delta[:PREF], wkv_d)
    first_delta_a = dot_t(query_delta[PREF:], wq_a) + dot_t(kv_raw_delta[PREF:], wkv_a)
    first_gain_d, first_gain_a = gain_rows(gains_d)[0], gain_rows(gains_a)[0]
    input_d = hidden_delta_d + normalize_back(x_d, rms_d, first_gain_d, first_delta_d)
    input_a = hidden_delta_a + normalize_back(x_a, rms_a, first_gain_a, first_delta_a)

    return (
        prefix_output,
        action_output,
        input_d.astype(bf16)[None],
        input_a[:ACT].astype(bf16)[None],
        gd[0],
        gd[1],
        gd[2],
        prefix_out_grad,
        gd[3],
        gd[4],
        ga[0],
        ga[1],
        ga[2],
        action_out_grad,
        ga[3],
        ga[4],
        finished[0].T,
        finished[1].T,
        finished[2],
        finished[3][None],
        finished[4][None],
        finished[5][None],
    )


def solution(mesh):
    rows = P("dp", "mp", None)
    both = P(("dp", "mp"), None)
    vector = P(("dp", "mp"))
    slots = P("mp", None, None)
    return jax.shard_map(
        on_device,
        mesh=mesh,
        in_specs=(rows,) * 4
        + (P("dp", None), P("dp", None), P())
        + (both,) * 4
        + (vector,) * 2
        + (both,) * 4
        + (vector,) * 2
        + (P(None, "mp"), P(None, "mp"), P("mp", None))
        + (slots,) * 3,
        out_specs=(rows,) * 4
        + (both,) * 4
        + (vector,) * 2
        + (both,) * 4
        + (vector,) * 2
        + (P(None, "mp"), P(None, "mp"), P("mp", None))
        + (slots,) * 3,
        check_vma=False,
    )
```

```python
import functools

import jax
import jax.numpy as jnp
import numpy as np
from jax import lax
from jax.experimental import pallas as pl
from jax.experimental.pallas import tpu as pltpu
from jax.sharding import PartitionSpec as P

ACT_LEN = 48
EPSILON = 1e-06
ROPE_BASE = 10000.0
HEADS = 4
HD = 256
PREF = 192
ACT = 12
ACT_PAD = 16
BLOCK = PREF + ACT_PAD
N_MP = 8
HALF_A = 96
HALF_B = BLOCK - HALF_A
HIDDEN_PAD = 896
VMEM_FEED = 50
bf16 = jnp.bfloat16
f32 = jnp.float32
ANY = pl.BlockSpec(memory_space=pl.ANY)
SMEM = pl.BlockSpec(memory_space=pltpu.SMEM)
VMEM = pl.BlockSpec(memory_space=pltpu.VMEM)
ARRIVALS = (
    ((0, 0), (0, 1)),
    ((1, 0), (1, 1)),
    ((3, 0), (3, 1)),
    ((4, 0), (4, 1)),
    ((5, 0), (7, 0)),
    ((2, 0), (5, 1)),
    ((2, 1), (7, 1)),
    ((6, 0),),
    ((6, 1),),
)
PARTS = tuple(part for parts in ARRIVALS for part in parts)
KEY_BLOCK = np.concatenate(
    [np.full(HALF_A, k) for k, _ in PARTS] + [np.full(ACT_PAD, k) for k, h in PARTS if h]
).astype(np.int32)
KEY_ROW = np.concatenate(
    [np.arange(HALF_A) + h * HALF_A for _, h in PARTS]
    + [np.arange(PREF, BLOCK) for _, h in PARTS if h]
).astype(np.int32)


ROW_PAIR, ACT_PAIR = 3 * PREF, 3 * ACT_PAD


def mp_swap(array, step):
    return lax.ppermute(array, "mp", [(i, i ^ step) for i in range(N_MP)])


def dp_swap(array, step):
    return lax.ppermute(array, "dp", [(i, i ^ step) for i in range(16)])


def yz_swap(array, step):
    return dp_swap(array, (step >> 2) * 8 + (step & 3) * 2)


def core_swap(array):
    return dp_swap(array, 1)


def where_parts(first, arrays, sizes):
    where = {}
    for i in range(arrays):
        at = 0
        for k, h in ARRIVALS[first + i]:
            where[k, h] = (i, at)
            at += sizes[h]
    return where


def fence_kernel(*refs):
    pass


def fence(array, *after):
    return pl.pallas_call(
        fence_kernel,
        in_specs=[pl.BlockSpec(memory_space=pl.ANY)] * (1 + len(after)),
        out_specs=pl.BlockSpec(memory_space=pl.ANY),
        out_shape=jax.ShapeDtypeStruct(array.shape, array.dtype),
        input_output_aliases={0: 0},
        cost_estimate=pl.CostEstimate(flops=0, bytes_accessed=0, transcendentals=0),
        name="fence",
    )(array, *after)


def join(*parts):
    return jnp.concatenate(parts, axis=0)


def add_low(*parts):
    total = parts[0].astype(f32)
    for part in parts[1:]:
        total = total + part.astype(f32)
    return total.astype(bf16)


def held(array, after):
    return fence(array, *after) if after else array


def sends_kernel(count, layout, *refs):
    for out, parts in zip(refs[len(refs) - len(layout) :], layout):
        at = 0
        for which, first, n in parts:
            out[at : at + n] = refs[which][first : first + n]
            at += n


def make_sends(arrays, layout, after=()):
    width = arrays[0].shape[1]
    low = lambda parts: jax.ShapeDtypeStruct((sum(n for _, _, n in parts), width), arrays[0].dtype)
    return pl.pallas_call(
        functools.partial(sends_kernel, len(arrays), layout),
        in_specs=[VMEM] * len(arrays) + [ANY] * len(after),
        out_specs=[VMEM] * len(layout),
        out_shape=[low(parts) for parts in layout],
        compiler_params=pltpu.CompilerParams(vmem_limit_bytes=16 * 1024 * 1024),
        cost_estimate=pl.CostEstimate(flops=0, bytes_accessed=0, transcendentals=0),
        name="sends",
    )(*arrays, *after)


def relay_gather(own, na, swap, during=None, hold=None):
    nb = own.shape[0] - na
    during = during or (lambda stage, arrived, sends: ())
    hold = hold or {}
    own = held(own, hold.get(1, ()))
    s1, s3, s4 = swap(own, 1), swap(own, 3), swap(own, 4)
    after = during(1, (own,), (own,)) + hold.get(2, ())
    layout = (
        ((0, 0, na), (1, 0, na)),
        ((1, 0, na), (2, na, nb)),
        ((0, na, nb), (2, na, nb)),
    )
    sends = make_sends((s1, s3, s4), layout, after)
    zz, v1, v3 = swap(sends[0], 4), swap(sends[1], 1), swap(sends[2], 3)
    after = during(2, (s1, s3, s4), tuple(sends)) + hold.get(3, ())
    sends = make_sends((zz, v1), (((0, na, na),), ((1, na, nb),)), after)
    z2a, z2b = swap(sends[0], 1), swap(sends[1], 3)
    during(3, (zz, v1, v3), tuple(sends))
    return own, s1, s3, s4, zz, v1, v3, z2a, z2b


def relay_scatter(pa, pb, swap, hold=None, sent=None):
    na, nb = pa[0].shape[0], pb[0].shape[0]
    hold = hold or {}
    sent = {} if sent is None else sent
    get = lambda stage: hold[stage]() if stage in hold else ()
    after = get(1)
    sent[1] = (held(pa[6], after), held(pb[6], after))
    r1, r3 = swap(sent[1][0], 1), swap(sent[1][1], 3)
    p7a = add_low(pa[7], r1)
    p5b = add_low(pb[5], r3)
    after = get(2)
    sends = (join(pa[5], p7a), join(pa[2], p5b), join(pb[2], pb[7]))
    sent[2] = tuple(held(x, after) for x in sends)
    zz, v1, v3 = swap(sent[2][0], 4), swap(sent[2][1], 1), swap(sent[2][2], 3)
    p1 = join(add_low(pa[1], zz[:na]), add_low(pb[1], v3[:nb]))
    p3 = join(add_low(pa[3], zz[na:], v1[:na]), pb[3])
    p4 = join(pa[4], add_low(pb[4], v1[na:], v3[nb:]))
    after = get(3)
    sent[3] = tuple(held(x, after) for x in (p1, p3, p4))
    s1, s3, s4 = swap(sent[3][0], 1), swap(sent[3][1], 3), swap(sent[3][2], 4)
    return pa[0], pb[0], s1, s3, s4


def total_of(pieces):
    pa, pb, s1, s3, s4 = pieces
    na = pa.shape[0]
    total_a = pa.astype(f32) + s1[:na].astype(f32) + s3[:na].astype(f32) + s4[:na].astype(f32)
    total_b = pb.astype(f32) + s1[na:].astype(f32) + s3[na:].astype(f32) + s4[na:].astype(f32)
    return total_a, total_b


def ring_scatter(pieces, swap, after, sent):
    near = [join(pieces[j], pieces[j ^ 4]) for j in range(4)]
    near[1:] = [held(x, after) for x in near[1:]]
    sent += near[1:]
    total = near[0].astype(f32)
    for j in (1, 3, 2):
        total = total + swap(near[j], j).astype(f32)
    return total


def pair_sum(total, swap, after=()):
    half = total.shape[0] // 2
    return total[:half] + swap(held(total[half:].astype(bf16), after), 4).astype(f32)


def gather_direct(array, index, swap):
    pair = index & 4
    high = (index >> 2) & 1
    two = jnp.zeros((2,) + array.shape, array.dtype)
    two = lax.dynamic_update_index_in_dim(two, array, high, 0)
    two = lax.dynamic_update_index_in_dim(two, swap(array, 4), 1 - high, 0)
    ring = index & 3
    out = jnp.zeros((2, 4) + array.shape, array.dtype)
    out = lax.dynamic_update_index_in_dim(out, two, ring, 1)
    for step in (1, 3, 2):
        out = lax.dynamic_update_index_in_dim(out, swap(two, step), ring ^ step, 1)
    return out.reshape((8,) + array.shape)


def scatter_direct(pieces, index, swap):
    high = (index >> 2) & 1
    ring = index & 3
    quads = pieces.reshape((2, 4) + pieces.shape[1:])
    total = lax.dynamic_index_in_dim(quads, ring, 1, keepdims=False).astype(f32)
    for step in (1, 3, 2):
        piece = lax.dynamic_index_in_dim(quads, ring ^ step, 1, keepdims=False)
        total = total + swap(piece, step).astype(f32)
    mine = lax.dynamic_index_in_dim(total, high, 0, keepdims=False)
    theirs = lax.dynamic_index_in_dim(total, 1 - high, 0, keepdims=False)
    return mine + swap(theirs.astype(bf16), 4).astype(f32)


def assemble_kernel(cuts, sizes, place_ref, *refs):
    arrays, outs = refs[:18], refs[18:]
    index, core = place_ref[0], place_ref[1]
    for (k, h), (i, at) in where_parts(0, 9, sizes).items():
        for out, (which, first, n, column, width) in zip(outs, cuts):
            if which == h:
                rows, columns = slice(at + first, at + first + n), slice(column, column + width)
                out[index ^ k, core] = arrays[i][rows, :, columns]
                out[index ^ k, 1 - core] = arrays[9 + i][rows, :, columns]


def assemble(mine, theirs, na, cuts, index, core):
    rows, columns = mine[0].shape
    eights = [x.reshape(x.shape[0] // 8, 8, columns) for x in (*mine, *theirs)]
    sizes = (na // 8, (rows - na) // 8)
    outs = pl.pallas_call(
        functools.partial(assemble_kernel, cuts, sizes),
        in_specs=[SMEM] + [VMEM] * 18,
        out_specs=[VMEM] * len(cuts),
        out_shape=[jax.ShapeDtypeStruct((8, 2, n, 8, width), bf16) for _, _, n, _, width in cuts],
        compiler_params=pltpu.CompilerParams(vmem_limit_bytes=40 * 1024 * 1024),
        name="assemble",
    )(jnp.stack([index, core]), *eights)
    return [x.reshape(-1, x.shape[-1]) for x in outs]


def gain_rows(block):
    pick = lax.broadcasted_iota(jnp.int32, (ACT_PAD, 128), 0)
    pick = (pick == lax.broadcasted_iota(jnp.int32, (ACT_PAD, 128), 1)).astype(bf16)
    turned = dot_t(pick, block)
    return turned[0:1], turned[1:2]


def keys_kernel(*refs):
    rows, (gain_d, gain_a, weight_d, weight_a, cosine, sine) = refs[:9], refs[9:15]
    normed_d, normed_a, keys, values = refs[-4:]
    gain_d, gain_a = gain_rows(gain_d[...])[0], gain_rows(gain_a[...])[0]
    width = weight_a.shape[0]
    prefix, action = [], []
    for i, parts in enumerate(ARRIVALS):
        at = 0
        for _, h in parts:
            prefix.append(rows[i][at : at + HALF_A])
            at += HALF_A
            if h:
                action.append(rows[i][at : at + ACT_PAD, :width])
                at += ACT_PAD
    x = join(*prefix).astype(f32)
    low_d = (x * inverse_rms(x) * gain_d).astype(bf16)
    x = join(*action).astype(f32)
    low_a = (x * inverse_rms(x) * gain_a).astype(bf16)
    normed_d[:PREF] = low_d[:PREF]
    normed_a[:ACT_PAD] = low_a[:ACT_PAD]
    normed_d[PREF:] = low_d[ROW_PAIR : ROW_PAIR + PREF]
    normed_a[ACT_PAD:] = low_a[ACT_PAIR : ACT_PAIR + ACT_PAD]
    raw = join(dot(low_d, weight_d[...]), dot(low_a, weight_a[...]))
    keys[...] = rotate(raw[:, :HD], cosine[...], sine[...]).astype(bf16)
    values[...] = raw[:, HD:].astype(bf16)


def keys_of(rows, gain_d, gain_a, weight_d, weight_a, cosine, sine, after):
    width_d, width_a = gain_d.shape[0], gain_a.shape[0]
    count = cosine.shape[0]
    shape = lambda *dims: jax.ShapeDtypeStruct(dims, bf16)
    given = [*rows, gain_d, gain_a, weight_d, weight_a, cosine, sine]
    return pl.pallas_call(
        keys_kernel,
        in_specs=[VMEM] * len(given) + [ANY] * len(after),
        out_specs=[VMEM] * 4,
        out_shape=[
            shape(2 * PREF, width_d),
            shape(2 * ACT_PAD, width_a),
            shape(count, HD),
            shape(count, HD),
        ],
        compiler_params=pltpu.CompilerParams(vmem_limit_bytes=48 * 1024 * 1024),
        cost_estimate=pl.CostEstimate(
            flops=4 * count * width_d * HD, bytes_accessed=8 * 1024 * 1024, transcendentals=count
        ),
        name="keys_of",
    )(*given, *after)


def gelu_parts(gate):
    c0 = 0.7978845608028654
    c1 = 0.044715
    square = gate * gate
    tanh = jnp.tanh(c0 * gate * (1.0 + c1 * square))
    half = 0.5 * (1.0 + tanh)
    slope = half + 0.5 * gate * (1.0 - tanh * tanh) * c0 * (1.0 + 3.0 * c1 * square)
    return gate * half, slope


def feed_block(rows, seed, gate_weight, up_weight, down_weight, valid):
    into, out_of = (dot_t, dot) if valid is None else (dot, dot_t)
    gate = into(rows, gate_weight)
    up = into(rows, up_weight)
    active, slope = gelu_parts(gate)
    product_delta = dot_t(seed, down_weight)
    if valid is not None:
        active = active * valid
        product_delta = product_delta * valid
    product = (active * up).astype(bf16)
    gate_delta = (product_delta * up * slope).astype(bf16)
    up_delta = (product_delta * active).astype(bf16)
    rows_delta = out_of(gate_delta, gate_weight) + out_of(up_delta, up_weight)
    return product, gate_delta, up_delta, rows_delta.astype(bf16)


def feed_kernel(layout, *refs):
    arrays = 1 + max(i for parts in layout for i, _ in parts)
    rows_refs, seed_refs, refs = refs[:arrays], refs[arrays : 2 * arrays], refs[2 * arrays :]
    gate_ref, up_ref, down_ref = refs[:3]
    action_gate_ref, action_up_ref, action_down_ref, valid_ref = refs[3:7]
    count = len(layout)
    outs = refs[-(2 * count + 8) :]
    products, deltas, kept_rows, kept_seeds = outs[:4]
    action_products, action_deltas, action_rows, action_seeds = outs[4:8]
    width = action_gate_ref.shape[0]
    rest = PREF - HALF_A

    def prefix_of(blocks):
        parts = []
        for (ia, a), (ib, b) in layout:
            parts += [blocks[ia][a : a + HALF_A], blocks[ib][b : b + rest]]
        return join(*parts)

    def action_of(blocks):
        parts = []
        for _, (ib, b) in layout:
            parts.append(blocks[ib][b + rest : b + HALF_B, :width])
        return join(*parts) if count > 1 else parts[0]

    rows, seed = prefix_of(rows_refs), prefix_of(seed_refs)
    product, gate_delta, up_delta, rows_delta = feed_block(
        rows, seed, gate_ref[...], up_ref[...], down_ref[...], None
    )
    hidden = product.shape[1]
    spare = jnp.zeros((count * PREF, HIDDEN_PAD - hidden), bf16)
    products[:, :hidden] = product
    products[:, hidden:] = spare
    deltas[:, :hidden] = gate_delta
    deltas[:, hidden:HIDDEN_PAD] = spare
    deltas[:, HIDDEN_PAD : HIDDEN_PAD + hidden] = up_delta
    deltas[:, HIDDEN_PAD + hidden :] = spare
    kept_rows[...] = rows
    kept_seeds[...] = seed
    rows, seed = action_of(rows_refs), action_of(seed_refs)
    product, gate_delta, up_delta, action_rows_delta = feed_block(
        rows,
        seed,
        action_gate_ref[...],
        action_up_ref[...],
        action_down_ref[...],
        valid_ref[...],
    )
    slots = gate_delta.shape[1]
    action_products[...] = product
    action_deltas[:, :slots] = gate_delta
    action_deltas[:, slots:] = up_delta
    action_rows[...] = rows
    action_seeds[...] = seed
    blank = jnp.zeros((ACT_PAD, rows_delta.shape[1] - width), bf16)
    for i in range(count):
        a, b, c = i * PREF, i * PREF + HALF_A, (i + 1) * PREF
        extra = slice(i * ACT_PAD, (i + 1) * ACT_PAD)
        ref_a, ref_b = outs[8 + 2 * i : 10 + 2 * i]
        ref_a[...] = rows_delta[a:b]
        ref_b[:rest] = rows_delta[b:c]
        ref_b[rest:, :width] = action_rows_delta[extra]
        ref_b[rest:, width:] = blank


def feed(arrays, seeds, weights, layout, base, kept, after):
    count = len(layout)
    width = arrays[0].shape[1]
    hidden = weights[0].shape[0]
    action_width, slots = weights[3].shape
    once = pl.Buffered(1)
    at = base // count

    def whole(array):
        return pl.BlockSpec(array.shape, lambda i: (0, 0), pipeline_mode=once)

    def part(size, columns):
        return (
            jax.ShapeDtypeStruct((N_MP * size, columns), bf16),
            pl.BlockSpec((count * size, columns), lambda i: (at, 0), pipeline_mode=once),
        )

    def own(size):
        return (
            jax.ShapeDtypeStruct((size, width), bf16),
            pl.BlockSpec((size, width), lambda i: (0, 0), pipeline_mode=once),
        )

    outs = [
        part(PREF, HIDDEN_PAD),
        part(PREF, 2 * HIDDEN_PAD),
        part(PREF, width),
        part(PREF, width),
        part(ACT_PAD, slots),
        part(ACT_PAD, 2 * slots),
        part(ACT_PAD, action_width),
        part(ACT_PAD, action_width),
    ] + [own(HALF_A), own(HALF_B)] * count
    reused = [] if kept is None else list(kept)
    given = [*arrays, *seeds]
    placed = len(given) + len(weights)
    results = pl.pallas_call(
        functools.partial(feed_kernel, layout),
        grid=(1,),
        in_specs=[whole(x) for x in given]
        + [VMEM] * len(weights)
        + [ANY] * (len(reused) + len(after)),
        out_shape=[shape for shape, _ in outs],
        out_specs=[spec for _, spec in outs],
        input_output_aliases={placed + i: i for i in range(len(reused))},
        compiler_params=pltpu.CompilerParams(
            dimension_semantics=("arbitrary",), vmem_limit_bytes=VMEM_FEED * 1024 * 1024
        ),
        cost_estimate=pl.CostEstimate(
            flops=10 * count * (PREF * width * hidden + ACT_PAD * action_width * slots),
            bytes_accessed=6 * (width * hidden + action_width * slots),
            transcendentals=count * PREF * hidden,
        ),
        name="feed",
    )(*given, *weights, *reused, *after)
    blocks = [results[8 + 2 * i : 10 + 2 * i] for i in range(count)]
    return blocks, results[:8]


def see(own_ref, key_ref):
    own, key = own_ref[...], key_ref[...]
    return (own[:, 0:1] == key[0:1]) | (own[:, 1:2] == key[1:2])


def attend_kernel(*refs):
    (normed_d, normed_a, x_d, x_a, wq_d, wq_a, wo_m, wo_e, wo_a) = refs[:9]
    (gain_d, gain_a, cosine, sine, own_codes, key_codes) = refs[9:15]
    keys, values = refs[15][...], refs[16][...]
    (queries, context, tops, totals, hidden_d, hidden_a, block) = refs[-7:]
    gain_d, gain_a = gain_rows(gain_d[...])[1], gain_rows(gain_a[...])[1]
    raw = join(dot(normed_d[:PREF], wq_d[...]), dot(normed_a[:ACT_PAD], wq_a[...]))
    visible = see(own_codes, key_codes)
    cos, sin = cosine[...], sine[...]
    heads = []
    for h in range(HEADS):
        rows = slice(h * BLOCK, (h + 1) * BLOCK)
        query = (rotate(raw[:, h * HD : (h + 1) * HD], cos, sin) * HD**-0.5).astype(bf16)
        queries[rows] = query
        scores = jnp.where(visible, dot_t(query, keys), -1e30)
        top = jnp.max(scores, axis=1, keepdims=True)
        shifted = jnp.exp(scores - top)
        total = jnp.sum(shifted, axis=1, keepdims=True)
        tops[rows] = top
        totals[rows] = total
        heads.append(dot((shifted / total).astype(bf16), values).astype(bf16))
    mixed = jnp.concatenate(heads, axis=1)
    context[...] = mixed
    main, width_d, width_a = wo_m.shape[1], x_d.shape[1], x_a.shape[1]
    low_d, low_a = mixed[:PREF], mixed[PREF:]
    state = x_d[...].astype(f32) + jnp.concatenate(
        [dot(low_d, wo_m[...]), dot(low_d, wo_e[...])], axis=1
    )
    hidden_d[...] = state
    second_d = (state * inverse_rms(state) * gain_d).astype(bf16)
    real = lax.broadcasted_iota(jnp.int32, (ACT_PAD, width_a), 0) < ACT
    state = jnp.where(real, x_a[...].astype(f32) + dot(low_a, wo_a[...]), 0.0)
    hidden_a[...] = state
    second_a = (state * inverse_rms(state) * gain_a).astype(bf16)
    block[:PREF] = second_d
    block[PREF:, :width_a] = second_a
    block[PREF:, width_a:] = jnp.zeros((ACT_PAD, width_d - width_a), bf16)


def attend(*given, after):
    x_d, x_a = given[2:4]
    width_d, width_a = x_d.shape[1], x_a.shape[1]
    shape = jax.ShapeDtypeStruct
    stacked = HEADS * BLOCK
    return pl.pallas_call(
        attend_kernel,
        in_specs=[VMEM] * len(given) + [ANY] * len(after),
        out_specs=[VMEM] * 7,
        out_shape=[
            shape((stacked, HD), bf16),
            shape((BLOCK, HEADS * HD), bf16),
            shape((stacked, 1), f32),
            shape((stacked, 1), f32),
            shape((PREF, width_d), f32),
            shape((ACT_PAD, width_a), f32),
            shape((BLOCK, width_d), bf16),
        ],
        compiler_params=pltpu.CompilerParams(vmem_limit_bytes=50 * 1024 * 1024),
        cost_estimate=pl.CostEstimate(
            flops=4 * BLOCK * HEADS * HD * (N_MP * BLOCK + width_d),
            bytes_accessed=4 * 1024 * 1024 * 5,
            transcendentals=stacked * N_MP * BLOCK,
        ),
        name="attend",
    )(*given, *after)


def attend_back_kernel(*refs):
    pieces = refs[:5]
    (hidden_d, hidden_a, cotangent_d, cotangent_a, share, gain_d, gain_a) = refs[5:12]
    (wo_m, wo_e, wo_a, queries, tops, totals, cosine, sine, own_codes, key_codes) = refs[12:22]
    keys, values = refs[22][...], refs[23][...]
    outs = refs[-(6 + len(PARTS)) :]
    (hidden_delta_d, hidden_delta_a, low, terms_d, terms_a, query_delta) = outs[:6]
    kv_deltas = outs[6:]
    gain_d, gain_a = gain_rows(gain_d[...])[1], gain_rows(gain_a[...])[1]
    delta = join(*total_of([piece[...] for piece in pieces]))
    width_d, width_a = hidden_d.shape[1], hidden_a.shape[1]
    lows = []
    for rows, state_ref, cotangent, gain, out, terms in (
        (slice(0, PREF), hidden_d, cotangent_d, gain_d, hidden_delta_d, terms_d),
        (slice(PREF, BLOCK), hidden_a, cotangent_a, gain_a, hidden_delta_a, terms_a),
    ):
        state = state_ref[...]
        change = delta[rows, : state.shape[1]]
        scale = inverse_rms(state)
        seed = cotangent[...].astype(f32) * share[rows]
        back = seed + normalize_back(state, scale, gain, change)
        out[...] = back
        terms[...] = (change * state * scale).astype(bf16)
        lows.append(back.astype(bf16))
    low_d, low_a = lows
    low[:PREF] = low_d
    low[PREF:, :width_a] = low_a
    low[PREF:, width_a:] = jnp.zeros((ACT_PAD, width_d - width_a), bf16)
    main = wo_m.shape[1]
    context_delta = join(
        dot_t(low_d[:, :main], wo_m[...]) + dot_t(low_d[:, main:], wo_e[...]),
        dot_t(low_a, wo_a[...]),
    ).astype(bf16)
    visible = see(own_codes, key_codes)
    cos, sin = cosine[...], sine[...]
    keys_delta, values_delta = None, None
    for h in range(HEADS):
        rows = slice(h * BLOCK, (h + 1) * BLOCK)
        query = queries[rows]
        change = context_delta[:, h * HD : (h + 1) * HD]
        scores = jnp.where(visible, dot_t(query, keys), -1e30)
        probs = jnp.exp(scores - tops[rows]) / totals[rows]
        probs_delta = dot_t(change, values)
        row_dot = jnp.sum(probs * probs_delta, axis=1, keepdims=True)
        score_delta = (probs * (probs_delta - row_dot)).astype(bf16)
        turned = unrotate(dot(score_delta, keys), cos, sin) * HD**-0.5
        query_delta[:, h * HD : (h + 1) * HD] = turned.astype(bf16)
        key_part = t_dot(score_delta, query)
        value_part = t_dot(probs.astype(bf16), change)
        keys_delta = key_part if h == 0 else keys_delta + key_part
        values_delta = value_part if h == 0 else values_delta + value_part
    at, extra = 0, len(PARTS) * HALF_A
    for (_, half), out in zip(PARTS, kv_deltas):
        for columns, change in ((slice(0, HD), keys_delta), (slice(HD, 2 * HD), values_delta)):
            out[:HALF_A, columns] = change[at : at + HALF_A].astype(bf16)
            if half:
                out[HALF_A:, columns] = change[extra : extra + ACT_PAD].astype(bf16)
        at += HALF_A
        extra += half * ACT_PAD


def attend_back(*given, after):
    hidden_d, hidden_a = given[5:7]
    width_d, width_a = hidden_d.shape[1], hidden_a.shape[1]
    shape = jax.ShapeDtypeStruct
    stacked = HEADS * BLOCK
    outs = pl.pallas_call(
        attend_back_kernel,
        in_specs=[VMEM] * len(given) + [ANY] * len(after),
        out_specs=[VMEM] * (6 + len(PARTS)),
        out_shape=[
            shape((PREF, width_d), f32),
            shape((ACT_PAD, width_a), f32),
            shape((BLOCK, width_d), bf16),
            shape((PREF, width_d), bf16),
            shape((ACT_PAD, width_a), bf16),
            shape((BLOCK, HEADS * HD), bf16),
        ]
        + [shape(((HALF_A, HALF_B)[half], 2 * HD), bf16) for _, half in PARTS],
        compiler_params=pltpu.CompilerParams(vmem_limit_bytes=50 * 1024 * 1024),
        cost_estimate=pl.CostEstimate(
            flops=2 * BLOCK * HEADS * HD, bytes_accessed=4 * BLOCK, transcendentals=stacked
        ),
        name="attend_back",
    )(*given, *after)
    kv_deltas = dict(zip(PARTS, outs[6:]))
    pa = {k: kv_deltas[k, 0] for k in range(8)}
    pb = {k: kv_deltas[k, 1] for k in range(8)}
    return outs[:6], pa, pb


def theirs_kernel(cuts, place_ref, *refs):
    out = refs[-1]
    core = place_ref[1]
    for ref, (row, n, source, column, width) in zip(refs, cuts):
        out[:, row : row + n, :, column : column + width] = ref[
            1 - core, :, :, :, source : source + width
        ]


def near_kernel(cuts, place_ref, *refs):
    got, outs = refs[len(cuts)], refs[-4:]
    mp, core = place_ref[0], place_ref[1]
    for step, out in zip((0, 1, 3, 2), outs):
        for pair in range(2):
            block = mp ^ step ^ (4 * pair)
            base = pair * got.shape[1]
            for ref, (row, n, source, column, width) in zip(refs, cuts):
                columns = slice(column, column + width)
                mine = ref[core, block, :, :, source : source + width].astype(f32)
                total = mine + got[block, row : row + n, :, columns].astype(f32)
                out[base + row : base + row + n, :, columns] = total.astype(bf16)


def sum_weights(grads, cuts, columns, place, sent, got, after, before_last, last_sent):
    views = [g.reshape(2, 8, -1, 8, g.shape[1]) for g in grads]
    eights = max(row + n for row, n, _, _, _ in cuts)
    params = pltpu.CompilerParams(vmem_limit_bytes=44 * 1024 * 1024)
    cost = pl.CostEstimate(flops=0, bytes_accessed=0, transcendentals=0)
    low = lambda *dims: jax.ShapeDtypeStruct(dims, bf16)
    theirs = pl.pallas_call(
        functools.partial(theirs_kernel, cuts),
        in_specs=[SMEM] + [VMEM] * len(views),
        out_specs=VMEM,
        out_shape=low(8, eights, 8, columns),
        compiler_params=params,
        cost_estimate=cost,
        name="theirs",
    )(place, *views)
    near = pl.pallas_call(
        functools.partial(near_kernel, cuts),
        in_specs=[SMEM] + [VMEM] * (len(views) + 1) + [ANY] * len(after),
        out_specs=[VMEM] * 4,
        out_shape=[low(2 * eights, 8, columns)] * 4,
        compiler_params=params,
        cost_estimate=cost,
        name="near",
    )(place, *views, core_swap(theirs), *after)
    near = [x.reshape(16 * eights, columns) for x in near]
    sent += near[1:]
    total = near[0].astype(f32)
    for step, x in zip((1, 3, 2), near[1:]):
        got.append(mp_swap(x, step))
        total = total + got[-1].astype(f32)
    half = 8 * eights
    last_sent.append(held(total[half:].astype(bf16), before_last))
    return (total[:half] + mp_swap(last_sent[-1], 4).astype(f32)).astype(bf16)


def pad_action(rows):
    return jnp.pad(rows, ((0, ACT_PAD - ACT), (0, 0)))


def widen(rows, width):
    return jnp.pad(rows, ((0, 0), (0, width - rows.shape[1])))


def block_of(prefix_rows, action_rows):
    return join(prefix_rows, widen(action_rows, prefix_rows.shape[1]))


def order_matrix(size, rows):
    d = jnp.arange(size, dtype=jnp.int32)
    r = d % rows
    mp = (d // rows) % 8
    dp = d // (8 * rows)
    place = (dp % 2) * (size // 2) + mp * (8 * rows) + (dp // 2) * rows + r
    return (place[:, None] == jnp.arange(size, dtype=jnp.int32)[None, :]).astype(bf16)


def dot(a, b):
    return jnp.dot(a, b, preferred_element_type=f32)


def dot_t(a, b):
    return lax.dot_general(a, b, (((1,), (1,)), ((), ())), preferred_element_type=f32)


def t_dot(a, b):
    return lax.dot_general(a, b, (((0,), (0,)), ((), ())), preferred_element_type=f32)


def inverse_rms(rows):
    return lax.rsqrt(jnp.mean(rows * rows, axis=-1, keepdims=True) + EPSILON)


def normalize_back(rows, scale, gain, delta):
    a = delta * gain
    return scale * (a - rows * (scale * scale) * jnp.mean(a * rows, axis=-1, keepdims=True))


def rotate(rows, cosine, sine):
    half = HD // 2
    first, second = rows[:, :half], rows[:, half:]
    return jnp.concatenate(
        [first * cosine - second * sine, second * cosine + first * sine], axis=1
    )


def unrotate(rows, cosine, sine):
    return rotate(rows, cosine, -sine)


def angle_tables(place):
    half = HD // 2
    frequency = ROPE_BASE ** (-jnp.arange(half, dtype=f32) / half)
    angles = place.astype(f32)[:, None] * frequency[None, :]
    return jnp.cos(angles), jnp.sin(angles)


def on_device(
    prefix_input,
    action_input,
    prefix_cotangent,
    action_cotangent,
    prefix_lengths,
    mixture,
    cut_points,
    prefix_query,
    prefix_key,
    prefix_value,
    prefix_out,
    prefix_first_gain,
    prefix_second_gain,
    action_query,
    action_key,
    action_value,
    action_out,
    action_first_gain,
    action_second_gain,
    prefix_gate,
    prefix_up,
    prefix_down,
    action_gate,
    action_up,
    action_down,
):
    mp = lax.axis_index("mp")
    dp = lax.axis_index("dp")
    core = dp & 1
    yz = (dp >> 3) * 4 + ((dp >> 1) & 3)
    D = prefix_input.shape[2]
    DA = action_input.shape[2]

    def column_block(first, second):
        return jnp.pad(jnp.stack([first, second], axis=1), ((0, 0), (0, 126)))

    pack_d = jnp.concatenate(
        [
            prefix_key,
            prefix_value,
            column_block(prefix_first_gain, prefix_second_gain),
            prefix_query,
        ],
        axis=1,
    )
    wide = pack_d.shape[1]
    pack = jnp.concatenate(
        [
            pack_d[:8],
            action_key,
            action_value,
            column_block(action_first_gain, action_second_gain),
            action_query,
            action_out,
            prefix_out,
            jnp.pad(pack_d[8:].reshape(8, wide // 8), ((0, 0), (0, 48))),
        ],
        axis=1,
    )
    lengths = prefix_lengths[0]
    first_length = lengths[0]

    def tables(source, row):
        is_action = row >= PREF
        prefix_row = source * PREF + row
        prefix_item = (prefix_row >= first_length).astype(jnp.int32)
        prefix_place = prefix_row - jnp.where(prefix_item == 1, first_length, 0)
        action_row = source * ACT + row - PREF
        action_item = (action_row >= ACT_LEN).astype(jnp.int32)
        action_place = jnp.where(action_item == 1, lengths[1], first_length) + action_row % ACT_LEN
        action_item = jnp.where(row - PREF < ACT, action_item, 2)
        item = jnp.where(is_action, action_item, prefix_item)
        place = jnp.where(is_action, action_place, prefix_place)
        return item, place, is_action

    own_item, own_place, own_is_action = tables(mp, jnp.arange(BLOCK, dtype=jnp.int32))
    key_item, key_place, key_is_action = tables(jnp.asarray(KEY_BLOCK) ^ mp, jnp.asarray(KEY_ROW))
    key_cos, key_sin = angle_tables(key_place)
    own_codes = jnp.stack([own_item, jnp.where(own_is_action, own_item, -2)], axis=1)
    key_codes = jnp.stack(
        [jnp.where(key_is_action, -1, key_item), jnp.where(key_is_action, key_item, -1)], axis=0
    )
    own_cos, own_sin = angle_tables(own_place)

    share = mixture[0].astype(f32) / 32.0
    row_share = jnp.where(own_item == 1, share[1], share[0])[:, None]
    cotangent_a = pad_action(action_cotangent[0])
    prefix_seed = prefix_cotangent[0].astype(f32) * row_share[:PREF]
    action_seed = cotangent_a.astype(f32) * row_share[PREF:]
    seed_block = block_of(prefix_seed.astype(bf16), action_seed.astype(bf16))

    near = gather_direct(pack, mp, mp_swap)
    last_row = near[:, :, pack.shape[1] - 256 : pack.shape[1] - 48].reshape(8, 1, wide)
    near_d = jnp.concatenate([near[:, :, :wide], last_row], axis=1).reshape(72, wide)
    near_a = near[:, :, wide : pack.shape[1] - 256].reshape(64, -1)
    edge = near_a[:, 2688 + 1024 :]
    kv_a = widen(jnp.concatenate([near_a[:, :640], edge], axis=1), 1024)
    pack_a = join(near_a[:, 640:1664], near_a[:, 1664:2688], kv_a)
    pack_b = join(near_d[:, 640:], near_a[:, 2688 : 2688 + 1024], widen(near_d[:, :640], 1024))
    arrived = {}

    def note(name):
        def during(stage, blocks, sends):
            arrived[name, stage] = blocks
            arrived[name, "sends", stage] = sends
            return ()

        return during

    own_action = pad_action(action_input[0])
    own_block = block_of(prefix_input[0], own_action)
    own_block = fence(own_block, near)
    x_rows = relay_gather(own_block, HALF_A, mp_swap)
    hold = {2: x_rows[1:4], 3: x_rows[4:7]}
    mine = relay_gather(join(pack_a, pack_b), pack_a.shape[0], yz_swap, note("weights"), hold)
    theirs = [core_swap(x) for x in mine]
    cuts = (
        (0, 0, 8, 0, 1024),
        (0, 8, 8, 0, 1024),
        (0, 16, 8, 0, 512),
        (0, 16, 8, 512, 128),
        (0, 16, 8, 640, 128),
        (1, 0, 9, 0, 1024),
        (1, 9, 8, 0, 1024),
        (1, 17, 9, 0, 512),
        (1, 17, 9, 512, 128),
    )
    wq_a, wo_a, wkv_a, gains_a, wo_e, wq_d, wo_m, wkv_d, gains_d = assemble(
        mine, theirs, pack_a.shape[0], cuts, yz, core
    )
    seeds = relay_gather(
        seed_block,
        HALF_A,
        mp_swap,
        note("seeds"),
        {1: arrived["weights", "sends", 3][:1]},
    )

    normed_d, normed_a, keys, values = keys_of(
        x_rows,
        gains_d,
        gains_a,
        wkv_d,
        wkv_a,
        key_cos,
        key_sin,
        arrived["seeds", "sends", 2],
    )
    x_d, x_a = prefix_input[0].astype(f32), own_action.astype(f32)
    rms_d, rms_a = inverse_rms(x_d), inverse_rms(x_a)
    queries, context, tops, totals, hidden_d, hidden_a, second_block = attend(
        normed_d,
        normed_a,
        prefix_input[0],
        own_action,
        wq_d,
        wq_a,
        wo_m,
        wo_e,
        wo_a,
        gains_d,
        gains_a,
        own_cos,
        own_sin,
        own_codes,
        key_codes,
        keys,
        values,
        after=arrived["seeds", "sends", 3],
    )

    slots = action_gate.shape[2]
    cut_pair = lax.dynamic_slice_in_dim(cut_points, mp, 2)
    valid = (jnp.arange(slots, dtype=jnp.int32) < cut_pair[1] - cut_pair[0]).astype(f32)[None, :]
    weights = (prefix_gate.T, prefix_up.T, prefix_down)
    weights += (action_gate[0], action_up[0], action_down[0], valid)
    kept = None
    results = {}

    def run(arrays, first, blocks, base, after):
        nonlocal kept
        where = where_parts(first, len(arrays), (HALF_A, HALF_B))
        layout = tuple((where[k, 0], where[k, 1]) for k in blocks)
        some = seeds[first : first + len(arrays)]
        done, kept = feed(arrays, some, weights, layout, base, kept, after)
        results.update(zip(blocks, done))
        return (done[0][0],)

    def feed_during(stage, arrays, sends):
        if stage == 3:
            return ()
        first, blocks, base = {1: (0, (0,), 3), 2: (1, (1, 3, 4), 0)}[stage]
        return run(arrays, first, blocks, base, sends)

    second_block = fence(second_block, seeds[8])
    arrays = relay_gather(second_block, HALF_A, mp_swap, feed_during)
    run(arrays[4:], 4, (2, 5, 7, 6), 4, ())
    product_d, deltas_d, rows_d, seeds_d, product_a, deltas_a, rows_a, seeds_a = kept

    grads = (
        t_dot(deltas_d, rows_d),
        t_dot(product_d, seeds_d),
        t_dot(rows_a, deltas_a),
        t_dot(product_a, seeds_a),
    )
    hidden = prefix_down.shape[0]
    grads = tuple(g.astype(bf16) for g in grads)
    pa = {k: v[0] for k, v in results.items()}
    pb = {k: v[1] for k, v in results.items()}
    delta_pieces = relay_scatter(pa, pb, mp_swap)
    grads = grads[:3] + (fence(grads[3], *delta_pieces[2:]),)
    grads = tuple(lax.psum(g, "dp") for g in grads)
    finished = (
        grads[0][:hidden].astype(f32),
        grads[0][HIDDEN_PAD : HIDDEN_PAD + hidden].astype(f32),
        grads[1][:hidden].astype(f32),
        grads[2][:, :slots].astype(f32),
        grads[2][:, slots:].astype(f32),
        grads[3].astype(f32),
    )

    partial_d = dot(product_d[:, :hidden], prefix_down).astype(bf16)
    partial_a = dot(product_a, action_down[0]).astype(bf16)
    out = []
    for k in range(8):
        i = (1, 3, 4, 0, 2, 5, 7, 6).index(k)
        mine = partial_a[i * ACT_PAD : (i + 1) * ACT_PAD]
        out.append(block_of(partial_d[i * PREF : (i + 1) * PREF], mine))
    out_sent = []
    out = ring_scatter(out, mp_swap, delta_pieces[2:], out_sent)
    (hidden_delta_d, hidden_delta_a, low, terms_d, terms_a, query_delta), pa, pb = attend_back(
        *delta_pieces,
        hidden_d,
        hidden_a,
        prefix_cotangent[0],
        cotangent_a,
        row_share,
        gains_d,
        gains_a,
        wo_m,
        wo_e,
        wo_a,
        queries,
        tops,
        totals,
        own_cos,
        own_sin,
        own_codes,
        key_codes,
        keys,
        values,
        after=tuple(out_sent),
    )
    low_d, low_a = low[:PREF], low[PREF:, :DA]

    kv_near = [join(pa[k], pb[k], pa[k ^ 4], pb[k ^ 4]) for k in range(4)]
    kv_part = kv_near[0].astype(f32)
    for k in (1, 3, 2):
        kv_part = kv_part + mp_swap(kv_near[k], k).astype(f32)
    pair = lambda table: join(
        own_cos if table is key_cos else own_sin,
        table[ROW_PAIR : ROW_PAIR + PREF],
        table[len(PARTS) * HALF_A + ACT_PAIR : len(PARTS) * HALF_A + ACT_PAIR + ACT_PAD],
    )
    kv_turned = jnp.concatenate(
        [unrotate(kv_part[:, :HD], pair(key_cos), pair(key_sin)), kv_part[:, HD:]], axis=1
    )
    kv_turned_low = kv_turned.astype(bf16)
    kv_rows_d = join(kv_turned_low[:PREF], kv_turned_low[BLOCK : BLOCK + PREF])
    kv_rows_a = join(kv_turned_low[PREF:BLOCK], kv_turned_low[BLOCK + PREF :])

    order_d, order_a = order_matrix(D, 9), order_matrix(DA, 8)
    turned_d = dot(normed_d, order_d).astype(bf16)
    turned_a = dot(normed_a, order_a).astype(bf16)
    turned_context = dot(context, order_a).astype(bf16)
    second_term_d = t_dot(dot(terms_d, order_d).astype(bf16), jnp.ones((PREF, 256), bf16))
    second_term_a = t_dot(dot(terms_a, order_a).astype(bf16), jnp.ones((ACT_PAD, 128), bf16))
    out_grad_d = t_dot(turned_context[:PREF], low_d).astype(bf16)
    out_grad_a = t_dot(turned_context[PREF:], low_a).astype(bf16)
    q_grad_d = t_dot(turned_d[:PREF], query_delta[:PREF]).astype(bf16)
    q_grad_a = t_dot(turned_a[:ACT_PAD], query_delta[PREF:]).astype(bf16)
    place = jnp.stack([mp, core])
    cuts = (
        (0, 8, 0, 0, 1024),
        (8, 8, 0, 0, 1024),
        (16, 9, 0, 0, 1024),
        (25, 8, 0, 0, 1024),
    )
    qo_sent, kv_sent, got, last_sent = [], [], [], []
    qo_grads = (q_grad_a, out_grad_a, q_grad_d, out_grad_d)
    qo = sum_weights(qo_grads, cuts, 1024, place, qo_sent, got, (), grads[:1], last_sent)
    kv_grad_d = t_dot(turned_d, kv_rows_d).astype(bf16)
    kv_grad_a = t_dot(turned_a, kv_rows_a).astype(bf16)
    cuts = (
        (0, 8, 0, 0, 512),
        (0, 8, 0, 512, 128),
        (0, 8, 1024, 640, 128),
        (8, 9, 0, 0, 512),
        (8, 9, 0, 512, 256),
    )
    kv_grads = (
        kv_grad_a,
        second_term_a.astype(bf16),
        out_grad_d,
        kv_grad_d,
        second_term_d.astype(bf16),
    )
    kv = sum_weights(kv_grads, cuts, 768, place, kv_sent, got, qo_sent, grads[:1], last_sent)
    kv_a, kv_d = kv[:64], kv[64:, :640]
    qo_a, qo_b = qo[:128], qo[128:]
    kv_other = mp_swap(held(kv_part[BLOCK:].astype(bf16), tuple(last_sent)), 4)
    kv_sum = kv_part[:BLOCK] + kv_other.astype(f32)
    kv_raw_delta = jnp.concatenate(
        [unrotate(kv_sum[:, :HD], own_cos, own_sin), kv_sum[:, HD:]], axis=1
    ).astype(bf16)

    out = pair_sum(out, mp_swap)
    prefix_output = (hidden_d + out[:PREF]).astype(bf16)[None]
    action_output = (hidden_a + out[PREF:, :DA])[:ACT].astype(bf16)[None]

    last_d = jnp.concatenate([kv_d, qo_b[:72]], axis=1).reshape(8, 9, wide)
    last_a = jnp.concatenate(
        [kv_a[:, :640], qo_a[:64], qo_a[64:], qo_b[72:], kv_a[:, 640:]], axis=1
    ).reshape(8, 8, -1)
    last = jnp.concatenate(
        [
            last_d[:, :8],
            last_a,
            jnp.pad(last_d[:, 8:].reshape(8, 8, wide // 8), ((0, 0), (0, 0), (0, 48))),
        ],
        axis=2,
    )
    last = scatter_direct(last, yz, yz_swap)
    ninth = last[:, last.shape[1] - 256 : last.shape[1] - 48].reshape(1, wide)
    grads_d = join(last[:, :wide], ninth)
    grads_a = last[:, wide : last.shape[1] - 256]

    def split_grads(grads, query, key, value, gain):
        key_grad = grads[:, :256]
        value_grad = grads[:, 256:512]
        second = grads[:, 512]
        query_grad = grads[:, 640:1664]
        first = (
            jnp.sum(query_grad * query.astype(f32), axis=1)
            + jnp.sum(key_grad * key.astype(f32), axis=1)
            + jnp.sum(value_grad * value.astype(f32), axis=1)
        ) / gain.astype(f32)
        return query_grad, key_grad, value_grad, first, second

    gd = split_grads(grads_d, prefix_query, prefix_key, prefix_value, prefix_first_gain)
    ga = split_grads(grads_a, action_query, action_key, action_value, action_first_gain)
    action_out_grad = grads_a[:, 1664:2688]
    prefix_out_grad = grads_a[:, 2688:]

    first_delta_d = dot_t(query_delta[:PREF], wq_d) + dot_t(kv_raw_delta[:PREF], wkv_d)
    first_delta_a = dot_t(query_delta[PREF:], wq_a) + dot_t(kv_raw_delta[PREF:], wkv_a)
    first_gain_d, first_gain_a = gain_rows(gains_d)[0], gain_rows(gains_a)[0]
    input_d = hidden_delta_d + normalize_back(x_d, rms_d, first_gain_d, first_delta_d)
    input_a = hidden_delta_a + normalize_back(x_a, rms_a, first_gain_a, first_delta_a)

    return (
        prefix_output,
        action_output,
        input_d.astype(bf16)[None],
        input_a[:ACT].astype(bf16)[None],
        gd[0],
        gd[1],
        gd[2],
        prefix_out_grad,
        gd[3],
        gd[4],
        ga[0],
        ga[1],
        ga[2],
        action_out_grad,
        ga[3],
        ga[4],
        finished[0].T,
        finished[1].T,
        finished[2],
        finished[3][None],
        finished[4][None],
        finished[5][None],
    )


def solution(mesh):
    rows = P("dp", "mp", None)
    both = P(("dp", "mp"), None)
    vector = P(("dp", "mp"))
    slots = P("mp", None, None)
    return jax.shard_map(
        on_device,
        mesh=mesh,
        in_specs=(rows,) * 4
        + (P("dp", None), P("dp", None), P())
        + (both,) * 4
        + (vector,) * 2
        + (both,) * 4
        + (vector,) * 2
        + (P(None, "mp"), P(None, "mp"), P("mp", None))
        + (slots,) * 3,
        out_specs=(rows,) * 4
        + (both,) * 4
        + (vector,) * 2
        + (both,) * 4
        + (vector,) * 2
        + (P(None, "mp"), P(None, "mp"), P("mp", None))
        + (slots,) * 3,
        check_vma=False,
    )
```

```python
import functools

import jax
import jax.numpy as jnp
import numpy as np
from jax import lax
from jax.experimental import pallas as pl
from jax.experimental.pallas import tpu as pltpu
from jax.sharding import PartitionSpec as P

ACT_LEN = 48
EPSILON = 1e-06
ROPE_BASE = 10000.0
HEADS = 4
HD = 256
PREF = 192
ACT = 12
ACT_PAD = 16
BLOCK = PREF + ACT_PAD
N_MP = 8
HALF_A = 96
HALF_B = BLOCK - HALF_A
HIDDEN_PAD = 896
VMEM_FEED = 50
bf16 = jnp.bfloat16
f32 = jnp.float32
ANY = pl.BlockSpec(memory_space=pl.ANY)
SMEM = pl.BlockSpec(memory_space=pltpu.SMEM)
VMEM = pl.BlockSpec(memory_space=pltpu.VMEM)
ARRIVALS = (
    ((0, 0), (0, 1)),
    ((1, 0), (1, 1)),
    ((3, 0), (3, 1)),
    ((4, 0), (4, 1)),
    ((5, 0), (7, 0)),
    ((2, 0), (5, 1)),
    ((2, 1), (7, 1)),
    ((6, 0),),
    ((6, 1),),
)
PARTS = tuple(part for parts in ARRIVALS for part in parts)
KEY_BLOCK = np.concatenate(
    [np.full(HALF_A, k) for k, _ in PARTS] + [np.full(ACT_PAD, k) for k, h in PARTS if h]
).astype(np.int32)
KEY_ROW = np.concatenate(
    [np.arange(HALF_A) + h * HALF_A for _, h in PARTS]
    + [np.arange(PREF, BLOCK) for _, h in PARTS if h]
).astype(np.int32)


ROW_PAIR, ACT_PAIR = 3 * PREF, 3 * ACT_PAD


def mp_swap(array, step):
    return lax.ppermute(array, "mp", [(i, i ^ step) for i in range(N_MP)])


def dp_swap(array, step):
    return lax.ppermute(array, "dp", [(i, i ^ step) for i in range(16)])


def yz_swap(array, step):
    return dp_swap(array, (step >> 2) * 8 + (step & 3) * 2)


def core_swap(array):
    return dp_swap(array, 1)


def where_parts(first, arrays, sizes):
    where = {}
    for i in range(arrays):
        at = 0
        for k, h in ARRIVALS[first + i]:
            where[k, h] = (i, at)
            at += sizes[h]
    return where


def fence_kernel(*refs):
    pass


def fence(array, *after):
    return pl.pallas_call(
        fence_kernel,
        in_specs=[pl.BlockSpec(memory_space=pl.ANY)] * (1 + len(after)),
        out_specs=pl.BlockSpec(memory_space=pl.ANY),
        out_shape=jax.ShapeDtypeStruct(array.shape, array.dtype),
        input_output_aliases={0: 0},
        cost_estimate=pl.CostEstimate(flops=0, bytes_accessed=0, transcendentals=0),
        name="fence",
    )(array, *after)


def join(*parts):
    return jnp.concatenate(parts, axis=0)


def add_low(*parts):
    total = parts[0].astype(f32)
    for part in parts[1:]:
        total = total + part.astype(f32)
    return total.astype(bf16)


def held(array, after):
    return fence(array, *after) if after else array


def sends_kernel(count, layout, *refs):
    for out, parts in zip(refs[len(refs) - len(layout) :], layout):
        at = 0
        for which, first, n in parts:
            out[at : at + n] = refs[which][first : first + n]
            at += n


def make_sends(arrays, layout, after=()):
    width = arrays[0].shape[1]
    low = lambda parts: jax.ShapeDtypeStruct((sum(n for _, _, n in parts), width), arrays[0].dtype)
    return pl.pallas_call(
        functools.partial(sends_kernel, len(arrays), layout),
        in_specs=[VMEM] * len(arrays) + [ANY] * len(after),
        out_specs=[VMEM] * len(layout),
        out_shape=[low(parts) for parts in layout],
        compiler_params=pltpu.CompilerParams(vmem_limit_bytes=16 * 1024 * 1024),
        cost_estimate=pl.CostEstimate(flops=0, bytes_accessed=0, transcendentals=0),
        name="sends",
    )(*arrays, *after)


def relay_gather(own, na, swap, during=None, hold=None):
    nb = own.shape[0] - na
    during = during or (lambda stage, arrived, sends: ())
    hold = hold or {}
    own = held(own, hold.get(1, ()))
    s1, s3, s4 = swap(own, 1), swap(own, 3), swap(own, 4)
    after = during(1, (own,), (own,)) + hold.get(2, ())
    layout = (
        ((0, 0, na), (1, 0, na)),
        ((1, 0, na), (2, na, nb)),
        ((0, na, nb), (2, na, nb)),
    )
    sends = make_sends((s1, s3, s4), layout, after)
    zz, v1, v3 = swap(sends[0], 4), swap(sends[1], 1), swap(sends[2], 3)
    after = during(2, (s1, s3, s4), tuple(sends)) + hold.get(3, ())
    sends = make_sends((zz, v1), (((0, na, na),), ((1, na, nb),)), after)
    z2a, z2b = swap(sends[0], 1), swap(sends[1], 3)
    during(3, (zz, v1, v3), tuple(sends))
    return own, s1, s3, s4, zz, v1, v3, z2a, z2b


def relay_scatter(pa, pb, swap, hold=None, sent=None):
    na, nb = pa[0].shape[0], pb[0].shape[0]
    hold = hold or {}
    sent = {} if sent is None else sent
    get = lambda stage: hold[stage]() if stage in hold else ()
    after = get(1)
    sent[1] = (held(pa[6], after), held(pb[6], after))
    r1, r3 = swap(sent[1][0], 1), swap(sent[1][1], 3)
    p7a = add_low(pa[7], r1)
    p5b = add_low(pb[5], r3)
    after = get(2)
    sends = (join(pa[5], p7a), join(pa[2], p5b), join(pb[2], pb[7]))
    sent[2] = tuple(held(x, after) for x in sends)
    zz, v1, v3 = swap(sent[2][0], 4), swap(sent[2][1], 1), swap(sent[2][2], 3)
    p1 = join(add_low(pa[1], zz[:na]), add_low(pb[1], v3[:nb]))
    p3 = join(add_low(pa[3], zz[na:], v1[:na]), pb[3])
    p4 = join(pa[4], add_low(pb[4], v1[na:], v3[nb:]))
    after = get(3)
    sent[3] = tuple(held(x, after) for x in (p1, p3, p4))
    s1, s3, s4 = swap(sent[3][0], 1), swap(sent[3][1], 3), swap(sent[3][2], 4)
    return pa[0], pb[0], s1, s3, s4


def total_of(pieces):
    pa, pb, s1, s3, s4 = pieces
    na = pa.shape[0]
    total_a = pa.astype(f32) + s1[:na].astype(f32) + s3[:na].astype(f32) + s4[:na].astype(f32)
    total_b = pb.astype(f32) + s1[na:].astype(f32) + s3[na:].astype(f32) + s4[na:].astype(f32)
    return total_a, total_b


def ring_scatter(pieces, swap, after, sent):
    near = [join(pieces[j], pieces[j ^ 4]) for j in range(4)]
    near[1:] = [held(x, after) for x in near[1:]]
    sent += near[1:]
    total = near[0].astype(f32)
    for j in (1, 3, 2):
        total = total + swap(near[j], j).astype(f32)
    return total


def pair_sum(total, swap, after=()):
    half = total.shape[0] // 2
    return total[:half] + swap(held(total[half:].astype(bf16), after), 4).astype(f32)


def gather_direct(array, index, swap):
    pair = index & 4
    high = (index >> 2) & 1
    two = jnp.zeros((2,) + array.shape, array.dtype)
    two = lax.dynamic_update_index_in_dim(two, array, high, 0)
    two = lax.dynamic_update_index_in_dim(two, swap(array, 4), 1 - high, 0)
    ring = index & 3
    out = jnp.zeros((2, 4) + array.shape, array.dtype)
    out = lax.dynamic_update_index_in_dim(out, two, ring, 1)
    for step in (1, 3, 2):
        out = lax.dynamic_update_index_in_dim(out, swap(two, step), ring ^ step, 1)
    return out.reshape((8,) + array.shape)


def scatter_direct(pieces, index, swap):
    high = (index >> 2) & 1
    ring = index & 3
    quads = pieces.reshape((2, 4) + pieces.shape[1:])
    total = lax.dynamic_index_in_dim(quads, ring, 1, keepdims=False).astype(f32)
    for step in (1, 3, 2):
        piece = lax.dynamic_index_in_dim(quads, ring ^ step, 1, keepdims=False)
        total = total + swap(piece, step).astype(f32)
    mine = lax.dynamic_index_in_dim(total, high, 0, keepdims=False)
    theirs = lax.dynamic_index_in_dim(total, 1 - high, 0, keepdims=False)
    return mine + swap(theirs.astype(bf16), 4).astype(f32)


def assemble_kernel(cuts, sizes, place_ref, *refs):
    arrays, outs = refs[:18], refs[18:]
    index, core = place_ref[0], place_ref[1]
    for (k, h), (i, at) in where_parts(0, 9, sizes).items():
        for out, (which, first, n, column, width) in zip(outs, cuts):
            if which == h:
                rows, columns = slice(at + first, at + first + n), slice(column, column + width)
                out[index ^ k, core] = arrays[i][rows, :, columns]
                out[index ^ k, 1 - core] = arrays[9 + i][rows, :, columns]


def assemble(mine, theirs, na, cuts, index, core):
    rows, columns = mine[0].shape
    eights = [x.reshape(x.shape[0] // 8, 8, columns) for x in (*mine, *theirs)]
    sizes = (na // 8, (rows - na) // 8)
    outs = pl.pallas_call(
        functools.partial(assemble_kernel, cuts, sizes),
        in_specs=[SMEM] + [VMEM] * 18,
        out_specs=[VMEM] * len(cuts),
        out_shape=[jax.ShapeDtypeStruct((8, 2, n, 8, width), bf16) for _, _, n, _, width in cuts],
        compiler_params=pltpu.CompilerParams(vmem_limit_bytes=40 * 1024 * 1024),
        name="assemble",
    )(jnp.stack([index, core]), *eights)
    return [x.reshape(-1, x.shape[-1]) for x in outs]


def gain_rows(block):
    pick = lax.broadcasted_iota(jnp.int32, (ACT_PAD, 128), 0)
    pick = (pick == lax.broadcasted_iota(jnp.int32, (ACT_PAD, 128), 1)).astype(bf16)
    turned = dot_t(pick, block)
    return turned[0:1], turned[1:2]


def keys_kernel(*refs):
    rows, (gain_d, gain_a, weight_d, weight_a, cosine, sine) = refs[:9], refs[9:15]
    normed_d, normed_a, keys, values = refs[-4:]
    gain_d, gain_a = gain_rows(gain_d[...])[0], gain_rows(gain_a[...])[0]
    width = weight_a.shape[0]
    prefix, action = [], []
    for i, parts in enumerate(ARRIVALS):
        at = 0
        for _, h in parts:
            prefix.append(rows[i][at : at + HALF_A])
            at += HALF_A
            if h:
                action.append(rows[i][at : at + ACT_PAD, :width])
                at += ACT_PAD
    x = join(*prefix).astype(f32)
    low_d = (x * inverse_rms(x) * gain_d).astype(bf16)
    x = join(*action).astype(f32)
    low_a = (x * inverse_rms(x) * gain_a).astype(bf16)
    normed_d[:PREF] = low_d[:PREF]
    normed_a[:ACT_PAD] = low_a[:ACT_PAD]
    normed_d[PREF:] = low_d[ROW_PAIR : ROW_PAIR + PREF]
    normed_a[ACT_PAD:] = low_a[ACT_PAIR : ACT_PAIR + ACT_PAD]
    raw = join(dot(low_d, weight_d[...]), dot(low_a, weight_a[...]))
    keys[...] = rotate(raw[:, :HD], cosine[...], sine[...]).astype(bf16)
    values[...] = raw[:, HD:].astype(bf16)


def keys_of(rows, gain_d, gain_a, weight_d, weight_a, cosine, sine, after):
    width_d, width_a = gain_d.shape[0], gain_a.shape[0]
    count = cosine.shape[0]
    shape = lambda *dims: jax.ShapeDtypeStruct(dims, bf16)
    given = [*rows, gain_d, gain_a, weight_d, weight_a, cosine, sine]
    return pl.pallas_call(
        keys_kernel,
        in_specs=[VMEM] * len(given) + [ANY] * len(after),
        out_specs=[VMEM] * 4,
        out_shape=[
            shape(2 * PREF, width_d),
            shape(2 * ACT_PAD, width_a),
            shape(count, HD),
            shape(count, HD),
        ],
        compiler_params=pltpu.CompilerParams(vmem_limit_bytes=48 * 1024 * 1024),
        cost_estimate=pl.CostEstimate(
            flops=4 * count * width_d * HD, bytes_accessed=8 * 1024 * 1024, transcendentals=count
        ),
        name="keys_of",
    )(*given, *after)


def gelu_parts(gate):
    c0 = 0.7978845608028654
    c1 = 0.044715
    square = gate * gate
    tanh = jnp.tanh(c0 * gate * (1.0 + c1 * square))
    half = 0.5 * (1.0 + tanh)
    slope = half + 0.5 * gate * (1.0 - tanh * tanh) * c0 * (1.0 + 3.0 * c1 * square)
    return gate * half, slope


def feed_block(rows, seed, gate_weight, up_weight, down_weight, valid):
    into, out_of = (dot_t, dot) if valid is None else (dot, dot_t)
    gate = into(rows, gate_weight)
    up = into(rows, up_weight)
    active, slope = gelu_parts(gate)
    product_delta = dot_t(seed, down_weight)
    if valid is not None:
        active = active * valid
        product_delta = product_delta * valid
    product = (active * up).astype(bf16)
    gate_delta = (product_delta * up * slope).astype(bf16)
    up_delta = (product_delta * active).astype(bf16)
    rows_delta = out_of(gate_delta, gate_weight) + out_of(up_delta, up_weight)
    return product, gate_delta, up_delta, rows_delta.astype(bf16)


def feed_kernel(layout, *refs):
    arrays = 1 + max(i for parts in layout for i, _ in parts)
    rows_refs, seed_refs, refs = refs[:arrays], refs[arrays : 2 * arrays], refs[2 * arrays :]
    gate_ref, up_ref, down_ref = refs[:3]
    action_gate_ref, action_up_ref, action_down_ref, valid_ref = refs[3:7]
    count = len(layout)
    outs = refs[-(2 * count + 8) :]
    products, deltas, kept_rows, kept_seeds = outs[:4]
    action_products, action_deltas, action_rows, action_seeds = outs[4:8]
    width = action_gate_ref.shape[0]
    rest = PREF - HALF_A

    def prefix_of(blocks):
        parts = []
        for (ia, a), (ib, b) in layout:
            parts += [blocks[ia][a : a + HALF_A], blocks[ib][b : b + rest]]
        return join(*parts)

    def action_of(blocks):
        parts = []
        for _, (ib, b) in layout:
            parts.append(blocks[ib][b + rest : b + HALF_B, :width])
        return join(*parts) if count > 1 else parts[0]

    rows, seed = prefix_of(rows_refs), prefix_of(seed_refs)
    product, gate_delta, up_delta, rows_delta = feed_block(
        rows, seed, gate_ref[...], up_ref[...], down_ref[...], None
    )
    hidden = product.shape[1]
    spare = jnp.zeros((count * PREF, HIDDEN_PAD - hidden), bf16)
    products[:, :hidden] = product
    products[:, hidden:] = spare
    deltas[:, :hidden] = gate_delta
    deltas[:, hidden:HIDDEN_PAD] = spare
    deltas[:, HIDDEN_PAD : HIDDEN_PAD + hidden] = up_delta
    deltas[:, HIDDEN_PAD + hidden :] = spare
    kept_rows[...] = rows
    kept_seeds[...] = seed
    rows, seed = action_of(rows_refs), action_of(seed_refs)
    product, gate_delta, up_delta, action_rows_delta = feed_block(
        rows,
        seed,
        action_gate_ref[...],
        action_up_ref[...],
        action_down_ref[...],
        valid_ref[...],
    )
    slots = gate_delta.shape[1]
    action_products[...] = product
    action_deltas[:, :slots] = gate_delta
    action_deltas[:, slots:] = up_delta
    action_rows[...] = rows
    action_seeds[...] = seed
    blank = jnp.zeros((ACT_PAD, rows_delta.shape[1] - width), bf16)
    for i in range(count):
        a, b, c = i * PREF, i * PREF + HALF_A, (i + 1) * PREF
        extra = slice(i * ACT_PAD, (i + 1) * ACT_PAD)
        ref_a, ref_b = outs[8 + 2 * i : 10 + 2 * i]
        ref_a[...] = rows_delta[a:b]
        ref_b[:rest] = rows_delta[b:c]
        ref_b[rest:, :width] = action_rows_delta[extra]
        ref_b[rest:, width:] = blank


def feed(arrays, seeds, weights, layout, base, kept, after):
    count = len(layout)
    width = arrays[0].shape[1]
    hidden = weights[0].shape[0]
    action_width, slots = weights[3].shape
    once = pl.Buffered(1)
    at = base // count

    def whole(array):
        return pl.BlockSpec(array.shape, lambda i: (0, 0), pipeline_mode=once)

    def part(size, columns):
        return (
            jax.ShapeDtypeStruct((N_MP * size, columns), bf16),
            pl.BlockSpec((count * size, columns), lambda i: (at, 0), pipeline_mode=once),
        )

    def own(size):
        return (
            jax.ShapeDtypeStruct((size, width), bf16),
            pl.BlockSpec((size, width), lambda i: (0, 0), pipeline_mode=once),
        )

    outs = [
        part(PREF, HIDDEN_PAD),
        part(PREF, 2 * HIDDEN_PAD),
        part(PREF, width),
        part(PREF, width),
        part(ACT_PAD, slots),
        part(ACT_PAD, 2 * slots),
        part(ACT_PAD, action_width),
        part(ACT_PAD, action_width),
    ] + [own(HALF_A), own(HALF_B)] * count
    reused = [] if kept is None else list(kept)
    given = [*arrays, *seeds]
    placed = len(given) + len(weights)
    results = pl.pallas_call(
        functools.partial(feed_kernel, layout),
        grid=(1,),
        in_specs=[whole(x) for x in given]
        + [VMEM] * len(weights)
        + [ANY] * (len(reused) + len(after)),
        out_shape=[shape for shape, _ in outs],
        out_specs=[spec for _, spec in outs],
        input_output_aliases={placed + i: i for i in range(len(reused))},
        compiler_params=pltpu.CompilerParams(
            dimension_semantics=("arbitrary",), vmem_limit_bytes=VMEM_FEED * 1024 * 1024
        ),
        cost_estimate=pl.CostEstimate(
            flops=10 * count * (PREF * width * hidden + ACT_PAD * action_width * slots),
            bytes_accessed=6 * (width * hidden + action_width * slots),
            transcendentals=count * PREF * hidden,
        ),
        name="feed",
    )(*given, *weights, *reused, *after)
    blocks = [results[8 + 2 * i : 10 + 2 * i] for i in range(count)]
    return blocks, results[:8]


def see(own_ref, key_ref):
    own, key = own_ref[...], key_ref[...]
    return (own[:, 0:1] == key[0:1]) | (own[:, 1:2] == key[1:2])


def attend_kernel(*refs):
    (normed_d, normed_a, x_d, x_a, wq_d, wq_a, wo_m, wo_e, wo_a) = refs[:9]
    (gain_d, gain_a, cosine, sine, own_codes, key_codes) = refs[9:15]
    keys, values = refs[15][...], refs[16][...]
    (queries, context, tops, totals, hidden_d, hidden_a, block) = refs[-7:]
    gain_d, gain_a = gain_rows(gain_d[...])[1], gain_rows(gain_a[...])[1]
    raw = join(dot(normed_d[:PREF], wq_d[...]), dot(normed_a[:ACT_PAD], wq_a[...]))
    visible = see(own_codes, key_codes)
    cos, sin = cosine[...], sine[...]
    heads = []
    for h in range(HEADS):
        rows = slice(h * BLOCK, (h + 1) * BLOCK)
        query = (rotate(raw[:, h * HD : (h + 1) * HD], cos, sin) * HD**-0.5).astype(bf16)
        queries[rows] = query
        scores = jnp.where(visible, dot_t(query, keys), -1e30)
        top = jnp.max(scores, axis=1, keepdims=True)
        shifted = jnp.exp(scores - top)
        total = jnp.sum(shifted, axis=1, keepdims=True)
        tops[rows] = top
        totals[rows] = total
        heads.append(dot((shifted / total).astype(bf16), values).astype(bf16))
    mixed = jnp.concatenate(heads, axis=1)
    context[...] = mixed
    main, width_d, width_a = wo_m.shape[1], x_d.shape[1], x_a.shape[1]
    low_d, low_a = mixed[:PREF], mixed[PREF:]
    state = x_d[...].astype(f32) + jnp.concatenate(
        [dot(low_d, wo_m[...]), dot(low_d, wo_e[...])], axis=1
    )
    hidden_d[...] = state
    second_d = (state * inverse_rms(state) * gain_d).astype(bf16)
    real = lax.broadcasted_iota(jnp.int32, (ACT_PAD, width_a), 0) < ACT
    state = jnp.where(real, x_a[...].astype(f32) + dot(low_a, wo_a[...]), 0.0)
    hidden_a[...] = state
    second_a = (state * inverse_rms(state) * gain_a).astype(bf16)
    block[:PREF] = second_d
    block[PREF:, :width_a] = second_a
    block[PREF:, width_a:] = jnp.zeros((ACT_PAD, width_d - width_a), bf16)


def attend(*given, after):
    x_d, x_a = given[2:4]
    width_d, width_a = x_d.shape[1], x_a.shape[1]
    shape = jax.ShapeDtypeStruct
    stacked = HEADS * BLOCK
    return pl.pallas_call(
        attend_kernel,
        in_specs=[VMEM] * len(given) + [ANY] * len(after),
        out_specs=[VMEM] * 7,
        out_shape=[
            shape((stacked, HD), bf16),
            shape((BLOCK, HEADS * HD), bf16),
            shape((stacked, 1), f32),
            shape((stacked, 1), f32),
            shape((PREF, width_d), f32),
            shape((ACT_PAD, width_a), f32),
            shape((BLOCK, width_d), bf16),
        ],
        compiler_params=pltpu.CompilerParams(vmem_limit_bytes=50 * 1024 * 1024),
        cost_estimate=pl.CostEstimate(
            flops=4 * BLOCK * HEADS * HD * (N_MP * BLOCK + width_d),
            bytes_accessed=4 * 1024 * 1024 * 5,
            transcendentals=stacked * N_MP * BLOCK,
        ),
        name="attend",
    )(*given, *after)


def attend_back_kernel(*refs):
    pieces = refs[:5]
    (hidden_d, hidden_a, cotangent_d, cotangent_a, share, gain_d, gain_a) = refs[5:12]
    (wo_m, wo_e, wo_a, queries, tops, totals, cosine, sine, own_codes, key_codes) = refs[12:22]
    keys, values = refs[22][...], refs[23][...]
    outs = refs[-(6 + len(PARTS)) :]
    (hidden_delta_d, hidden_delta_a, low, terms_d, terms_a, query_delta) = outs[:6]
    kv_deltas = outs[6:]
    gain_d, gain_a = gain_rows(gain_d[...])[1], gain_rows(gain_a[...])[1]
    delta = join(*total_of([piece[...] for piece in pieces]))
    width_d, width_a = hidden_d.shape[1], hidden_a.shape[1]
    lows = []
    for rows, state_ref, cotangent, gain, out, terms in (
        (slice(0, PREF), hidden_d, cotangent_d, gain_d, hidden_delta_d, terms_d),
        (slice(PREF, BLOCK), hidden_a, cotangent_a, gain_a, hidden_delta_a, terms_a),
    ):
        state = state_ref[...]
        change = delta[rows, : state.shape[1]]
        scale = inverse_rms(state)
        seed = cotangent[...].astype(f32) * share[rows]
        back = seed + normalize_back(state, scale, gain, change)
        out[...] = back
        terms[...] = (change * state * scale).astype(bf16)
        lows.append(back.astype(bf16))
    low_d, low_a = lows
    low[:PREF] = low_d
    low[PREF:, :width_a] = low_a
    low[PREF:, width_a:] = jnp.zeros((ACT_PAD, width_d - width_a), bf16)
    main = wo_m.shape[1]
    context_delta = join(
        dot_t(low_d[:, :main], wo_m[...]) + dot_t(low_d[:, main:], wo_e[...]),
        dot_t(low_a, wo_a[...]),
    ).astype(bf16)
    visible = see(own_codes, key_codes)
    cos, sin = cosine[...], sine[...]
    keys_delta, values_delta = None, None
    for h in range(HEADS):
        rows = slice(h * BLOCK, (h + 1) * BLOCK)
        query = queries[rows]
        change = context_delta[:, h * HD : (h + 1) * HD]
        scores = jnp.where(visible, dot_t(query, keys), -1e30)
        probs = jnp.exp(scores - tops[rows]) / totals[rows]
        probs_delta = dot_t(change, values)
        row_dot = jnp.sum(probs * probs_delta, axis=1, keepdims=True)
        score_delta = (probs * (probs_delta - row_dot)).astype(bf16)
        turned = unrotate(dot(score_delta, keys), cos, sin) * HD**-0.5
        query_delta[:, h * HD : (h + 1) * HD] = turned.astype(bf16)
        key_part = t_dot(score_delta, query)
        value_part = t_dot(probs.astype(bf16), change)
        keys_delta = key_part if h == 0 else keys_delta + key_part
        values_delta = value_part if h == 0 else values_delta + value_part
    at, extra = 0, len(PARTS) * HALF_A
    for (_, half), out in zip(PARTS, kv_deltas):
        for columns, change in ((slice(0, HD), keys_delta), (slice(HD, 2 * HD), values_delta)):
            out[:HALF_A, columns] = change[at : at + HALF_A].astype(bf16)
            if half:
                out[HALF_A:, columns] = change[extra : extra + ACT_PAD].astype(bf16)
        at += HALF_A
        extra += half * ACT_PAD


def attend_back(*given, after):
    hidden_d, hidden_a = given[5:7]
    width_d, width_a = hidden_d.shape[1], hidden_a.shape[1]
    shape = jax.ShapeDtypeStruct
    stacked = HEADS * BLOCK
    outs = pl.pallas_call(
        attend_back_kernel,
        in_specs=[VMEM] * len(given) + [ANY] * len(after),
        out_specs=[VMEM] * (6 + len(PARTS)),
        out_shape=[
            shape((PREF, width_d), f32),
            shape((ACT_PAD, width_a), f32),
            shape((BLOCK, width_d), bf16),
            shape((PREF, width_d), bf16),
            shape((ACT_PAD, width_a), bf16),
            shape((BLOCK, HEADS * HD), bf16),
        ]
        + [shape(((HALF_A, HALF_B)[half], 2 * HD), bf16) for _, half in PARTS],
        compiler_params=pltpu.CompilerParams(vmem_limit_bytes=50 * 1024 * 1024),
        cost_estimate=pl.CostEstimate(
            flops=2 * BLOCK * HEADS * HD, bytes_accessed=4 * BLOCK, transcendentals=stacked
        ),
        name="attend_back",
    )(*given, *after)
    kv_deltas = dict(zip(PARTS, outs[6:]))
    pa = {k: kv_deltas[k, 0] for k in range(8)}
    pb = {k: kv_deltas[k, 1] for k in range(8)}
    return outs[:6], pa, pb


def theirs_kernel(cuts, place_ref, *refs):
    out = refs[-1]
    core = place_ref[1]
    for ref, (row, n, source, column, width) in zip(refs, cuts):
        out[:, row : row + n, :, column : column + width] = ref[
            1 - core, :, :, :, source : source + width
        ]


def near_kernel(cuts, place_ref, *refs):
    got, outs = refs[len(cuts)], refs[-4:]
    mp, core = place_ref[0], place_ref[1]
    for step, out in zip((0, 1, 3, 2), outs):
        for pair in range(2):
            block = mp ^ step ^ (4 * pair)
            base = pair * got.shape[1]
            for ref, (row, n, source, column, width) in zip(refs, cuts):
                columns = slice(column, column + width)
                mine = ref[core, block, :, :, source : source + width].astype(f32)
                total = mine + got[block, row : row + n, :, columns].astype(f32)
                out[base + row : base + row + n, :, columns] = total.astype(bf16)


def sum_weights(grads, cuts, columns, place, sent, got, after, before_last, last_sent):
    views = [g.reshape(2, 8, -1, 8, g.shape[1]) for g in grads]
    eights = max(row + n for row, n, _, _, _ in cuts)
    params = pltpu.CompilerParams(vmem_limit_bytes=44 * 1024 * 1024)
    cost = pl.CostEstimate(flops=0, bytes_accessed=0, transcendentals=0)
    low = lambda *dims: jax.ShapeDtypeStruct(dims, bf16)
    theirs = pl.pallas_call(
        functools.partial(theirs_kernel, cuts),
        in_specs=[SMEM] + [VMEM] * len(views),
        out_specs=VMEM,
        out_shape=low(8, eights, 8, columns),
        compiler_params=params,
        cost_estimate=cost,
        name="theirs",
    )(place, *views)
    near = pl.pallas_call(
        functools.partial(near_kernel, cuts),
        in_specs=[SMEM] + [VMEM] * (len(views) + 1) + [ANY] * len(after),
        out_specs=[VMEM] * 4,
        out_shape=[low(2 * eights, 8, columns)] * 4,
        compiler_params=params,
        cost_estimate=cost,
        name="near",
    )(place, *views, core_swap(theirs), *after)
    near = [x.reshape(16 * eights, columns) for x in near]
    sent += near[1:]
    total = near[0].astype(f32)
    for step, x in zip((1, 3, 2), near[1:]):
        got.append(mp_swap(x, step))
        total = total + got[-1].astype(f32)
    half = 8 * eights
    last_sent.append(held(total[half:].astype(bf16), before_last))
    return (total[:half] + mp_swap(last_sent[-1], 4).astype(f32)).astype(bf16)


def pad_action(rows):
    return jnp.pad(rows, ((0, ACT_PAD - ACT), (0, 0)))


def widen(rows, width):
    return jnp.pad(rows, ((0, 0), (0, width - rows.shape[1])))


def block_of(prefix_rows, action_rows):
    return join(prefix_rows, widen(action_rows, prefix_rows.shape[1]))


def order_matrix(size, rows):
    d = jnp.arange(size, dtype=jnp.int32)
    r = d % rows
    mp = (d // rows) % 8
    dp = d // (8 * rows)
    place = (dp % 2) * (size // 2) + mp * (8 * rows) + (dp // 2) * rows + r
    return (place[:, None] == jnp.arange(size, dtype=jnp.int32)[None, :]).astype(bf16)


def dot(a, b):
    return jnp.dot(a, b, preferred_element_type=f32)


def dot_t(a, b):
    return lax.dot_general(a, b, (((1,), (1,)), ((), ())), preferred_element_type=f32)


def t_dot(a, b):
    return lax.dot_general(a, b, (((0,), (0,)), ((), ())), preferred_element_type=f32)


def inverse_rms(rows):
    return lax.rsqrt(jnp.mean(rows * rows, axis=-1, keepdims=True) + EPSILON)


def normalize_back(rows, scale, gain, delta):
    a = delta * gain
    return scale * (a - rows * (scale * scale) * jnp.mean(a * rows, axis=-1, keepdims=True))


def rotate(rows, cosine, sine):
    half = HD // 2
    first, second = rows[:, :half], rows[:, half:]
    return jnp.concatenate(
        [first * cosine - second * sine, second * cosine + first * sine], axis=1
    )


def unrotate(rows, cosine, sine):
    return rotate(rows, cosine, -sine)


def angle_tables(place):
    half = HD // 2
    frequency = ROPE_BASE ** (-jnp.arange(half, dtype=f32) / half)
    angles = place.astype(f32)[:, None] * frequency[None, :]
    return jnp.cos(angles), jnp.sin(angles)


def on_device(
    prefix_input,
    action_input,
    prefix_cotangent,
    action_cotangent,
    prefix_lengths,
    mixture,
    cut_points,
    prefix_query,
    prefix_key,
    prefix_value,
    prefix_out,
    prefix_first_gain,
    prefix_second_gain,
    action_query,
    action_key,
    action_value,
    action_out,
    action_first_gain,
    action_second_gain,
    prefix_gate,
    prefix_up,
    prefix_down,
    action_gate,
    action_up,
    action_down,
):
    mp = lax.axis_index("mp")
    dp = lax.axis_index("dp")
    core = dp & 1
    yz = (dp >> 3) * 4 + ((dp >> 1) & 3)
    D = prefix_input.shape[2]
    DA = action_input.shape[2]

    def column_block(first, second):
        return jnp.pad(jnp.stack([first, second], axis=1), ((0, 0), (0, 126)))

    pack_d = jnp.concatenate(
        [
            prefix_key,
            prefix_value,
            column_block(prefix_first_gain, prefix_second_gain),
            prefix_query,
        ],
        axis=1,
    )
    wide = pack_d.shape[1]
    pack = jnp.concatenate(
        [
            pack_d[:8],
            action_key,
            action_value,
            column_block(action_first_gain, action_second_gain),
            action_query,
            action_out,
            prefix_out,
            jnp.pad(pack_d[8:].reshape(8, wide // 8), ((0, 0), (0, 48))),
        ],
        axis=1,
    )
    lengths = prefix_lengths[0]
    first_length = lengths[0]

    def tables(source, row):
        is_action = row >= PREF
        prefix_row = source * PREF + row
        prefix_item = (prefix_row >= first_length).astype(jnp.int32)
        prefix_place = prefix_row - jnp.where(prefix_item == 1, first_length, 0)
        action_row = source * ACT + row - PREF
        action_item = (action_row >= ACT_LEN).astype(jnp.int32)
        action_place = jnp.where(action_item == 1, lengths[1], first_length) + action_row % ACT_LEN
        action_item = jnp.where(row - PREF < ACT, action_item, 2)
        item = jnp.where(is_action, action_item, prefix_item)
        place = jnp.where(is_action, action_place, prefix_place)
        return item, place, is_action

    own_item, own_place, own_is_action = tables(mp, jnp.arange(BLOCK, dtype=jnp.int32))
    key_item, key_place, key_is_action = tables(jnp.asarray(KEY_BLOCK) ^ mp, jnp.asarray(KEY_ROW))
    key_cos, key_sin = angle_tables(key_place)
    own_codes = jnp.stack([own_item, jnp.where(own_is_action, own_item, -2)], axis=1)
    key_codes = jnp.stack(
        [jnp.where(key_is_action, -1, key_item), jnp.where(key_is_action, key_item, -1)], axis=0
    )
    own_cos, own_sin = angle_tables(own_place)

    share = mixture[0].astype(f32) / 32.0
    row_share = jnp.where(own_item == 1, share[1], share[0])[:, None]
    cotangent_a = pad_action(action_cotangent[0])
    prefix_seed = prefix_cotangent[0].astype(f32) * row_share[:PREF]
    action_seed = cotangent_a.astype(f32) * row_share[PREF:]
    seed_block = block_of(prefix_seed.astype(bf16), action_seed.astype(bf16))

    near = gather_direct(pack, mp, mp_swap)
    last_row = near[:, :, pack.shape[1] - 256 : pack.shape[1] - 48].reshape(8, 1, wide)
    near_d = jnp.concatenate([near[:, :, :wide], last_row], axis=1).reshape(72, wide)
    near_a = near[:, :, wide : pack.shape[1] - 256].reshape(64, -1)
    edge = near_a[:, 2688 + 1024 :]
    kv_a = widen(jnp.concatenate([near_a[:, :640], edge], axis=1), 1024)
    pack_a = join(near_a[:, 640:1664], near_a[:, 1664:2688], kv_a)
    pack_b = join(near_d[:, 640:], near_a[:, 2688 : 2688 + 1024], widen(near_d[:, :640], 1024))
    arrived = {}

    def note(name):
        def during(stage, blocks, sends):
            arrived[name, stage] = blocks
            arrived[name, "sends", stage] = sends
            return ()

        return during

    own_action = pad_action(action_input[0])
    own_block = block_of(prefix_input[0], own_action)
    own_block = fence(own_block, near)
    x_rows = relay_gather(own_block, HALF_A, mp_swap)
    hold = {2: x_rows[1:4], 3: x_rows[4:7]}
    mine = relay_gather(join(pack_a, pack_b), pack_a.shape[0], yz_swap, note("weights"), hold)
    theirs = [core_swap(x) for x in mine]
    cuts = (
        (0, 0, 8, 0, 1024),
        (0, 8, 8, 0, 1024),
        (0, 16, 8, 0, 512),
        (0, 16, 8, 512, 128),
        (0, 16, 8, 640, 128),
        (1, 0, 9, 0, 1024),
        (1, 9, 8, 0, 1024),
        (1, 17, 9, 0, 512),
        (1, 17, 9, 512, 128),
    )
    wq_a, wo_a, wkv_a, gains_a, wo_e, wq_d, wo_m, wkv_d, gains_d = assemble(
        mine, theirs, pack_a.shape[0], cuts, yz, core
    )
    seeds = relay_gather(
        seed_block,
        HALF_A,
        mp_swap,
        note("seeds"),
        {1: arrived["weights", "sends", 3][:1]},
    )

    normed_d, normed_a, keys, values = keys_of(
        x_rows,
        gains_d,
        gains_a,
        wkv_d,
        wkv_a,
        key_cos,
        key_sin,
        arrived["seeds", "sends", 2],
    )
    x_d, x_a = prefix_input[0].astype(f32), own_action.astype(f32)
    rms_d, rms_a = inverse_rms(x_d), inverse_rms(x_a)
    queries, context, tops, totals, hidden_d, hidden_a, second_block = attend(
        normed_d,
        normed_a,
        prefix_input[0],
        own_action,
        wq_d,
        wq_a,
        wo_m,
        wo_e,
        wo_a,
        gains_d,
        gains_a,
        own_cos,
        own_sin,
        own_codes,
        key_codes,
        keys,
        values,
        after=arrived["seeds", "sends", 3],
    )

    slots = action_gate.shape[2]
    cut_pair = lax.dynamic_slice_in_dim(cut_points, mp, 2)
    valid = (jnp.arange(slots, dtype=jnp.int32) < cut_pair[1] - cut_pair[0]).astype(f32)[None, :]
    weights = (prefix_gate.T, prefix_up.T, prefix_down)
    weights += (action_gate[0], action_up[0], action_down[0], valid)
    kept = None
    results = {}

    def run(arrays, first, blocks, base, after):
        nonlocal kept
        where = where_parts(first, len(arrays), (HALF_A, HALF_B))
        layout = tuple((where[k, 0], where[k, 1]) for k in blocks)
        some = seeds[first : first + len(arrays)]
        done, kept = feed(arrays, some, weights, layout, base, kept, after)
        results.update(zip(blocks, done))
        return (done[0][0],)

    def feed_during(stage, arrays, sends):
        if stage == 3:
            return ()
        first, blocks, base = {1: (0, (0,), 3), 2: (1, (1, 3, 4), 0)}[stage]
        return run(arrays, first, blocks, base, sends)

    second_block = fence(second_block, seeds[8])
    arrays = relay_gather(second_block, HALF_A, mp_swap, feed_during)
    run(arrays[4:], 4, (2, 5, 7, 6), 4, ())
    product_d, deltas_d, rows_d, seeds_d, product_a, deltas_a, rows_a, seeds_a = kept

    grads = (
        t_dot(deltas_d, rows_d),
        t_dot(product_d, seeds_d),
        t_dot(rows_a, deltas_a),
        t_dot(product_a, seeds_a),
    )
    hidden = prefix_down.shape[0]
    grads = tuple(g.astype(bf16) for g in grads)
    pa = {k: v[0] for k, v in results.items()}
    pb = {k: v[1] for k, v in results.items()}
    delta_pieces = relay_scatter(pa, pb, mp_swap)
    grads = grads[:3] + (fence(grads[3], *delta_pieces[2:]),)
    grads = tuple(lax.psum(g, "dp") for g in grads)
    finished = (
        grads[0][:hidden].astype(f32),
        grads[0][HIDDEN_PAD : HIDDEN_PAD + hidden].astype(f32),
        grads[1][:hidden].astype(f32),
        grads[2][:, :slots].astype(f32),
        grads[2][:, slots:].astype(f32),
        grads[3].astype(f32),
    )

    partial_d = dot(product_d[:, :hidden], prefix_down).astype(bf16)
    partial_a = dot(product_a, action_down[0]).astype(bf16)
    out = []
    for k in range(8):
        i = (1, 3, 4, 0, 2, 5, 7, 6).index(k)
        mine = partial_a[i * ACT_PAD : (i + 1) * ACT_PAD]
        out.append(block_of(partial_d[i * PREF : (i + 1) * PREF], mine))
    out_sent = []
    out = ring_scatter(out, mp_swap, delta_pieces[2:], out_sent)
    (hidden_delta_d, hidden_delta_a, low, terms_d, terms_a, query_delta), pa, pb = attend_back(
        *delta_pieces,
        hidden_d,
        hidden_a,
        prefix_cotangent[0],
        cotangent_a,
        row_share,
        gains_d,
        gains_a,
        wo_m,
        wo_e,
        wo_a,
        queries,
        tops,
        totals,
        own_cos,
        own_sin,
        own_codes,
        key_codes,
        keys,
        values,
        after=tuple(out_sent),
    )
    low_d, low_a = low[:PREF], low[PREF:, :DA]

    kv_near = [join(pa[k], pb[k], pa[k ^ 4], pb[k ^ 4]) for k in range(4)]
    kv_part = kv_near[0].astype(f32)
    for k in (1, 3, 2):
        kv_part = kv_part + mp_swap(kv_near[k], k).astype(f32)
    pair = lambda table: join(
        own_cos if table is key_cos else own_sin,
        table[ROW_PAIR : ROW_PAIR + PREF],
        table[len(PARTS) * HALF_A + ACT_PAIR : len(PARTS) * HALF_A + ACT_PAIR + ACT_PAD],
    )
    kv_turned = jnp.concatenate(
        [unrotate(kv_part[:, :HD], pair(key_cos), pair(key_sin)), kv_part[:, HD:]], axis=1
    )
    kv_turned_low = kv_turned.astype(bf16)
    kv_rows_d = join(kv_turned_low[:PREF], kv_turned_low[BLOCK : BLOCK + PREF])
    kv_rows_a = join(kv_turned_low[PREF:BLOCK], kv_turned_low[BLOCK + PREF :])

    order_d, order_a = order_matrix(D, 9), order_matrix(DA, 8)
    turned_d = dot(normed_d, order_d).astype(bf16)
    turned_a = dot(normed_a, order_a).astype(bf16)
    turned_context = dot(context, order_a).astype(bf16)
    second_term_d = t_dot(dot(terms_d, order_d).astype(bf16), jnp.ones((PREF, 256), bf16))
    second_term_a = t_dot(dot(terms_a, order_a).astype(bf16), jnp.ones((ACT_PAD, 128), bf16))
    out_grad_d = t_dot(turned_context[:PREF], low_d).astype(bf16)
    out_grad_a = t_dot(turned_context[PREF:], low_a).astype(bf16)
    q_grad_d = t_dot(turned_d[:PREF], query_delta[:PREF]).astype(bf16)
    q_grad_a = t_dot(turned_a[:ACT_PAD], query_delta[PREF:]).astype(bf16)
    place = jnp.stack([mp, core])
    cuts = (
        (0, 8, 0, 0, 1024),
        (8, 8, 0, 0, 1024),
        (16, 9, 0, 0, 1024),
        (25, 8, 0, 0, 1024),
    )
    qo_sent, kv_sent, got, last_sent = [], [], [], []
    qo_grads = (q_grad_a, out_grad_a, q_grad_d, out_grad_d)
    qo = sum_weights(qo_grads, cuts, 1024, place, qo_sent, got, (), (), last_sent)
    kv_grad_d = t_dot(turned_d, kv_rows_d).astype(bf16)
    kv_grad_a = t_dot(turned_a, kv_rows_a).astype(bf16)
    cuts = (
        (0, 8, 0, 0, 512),
        (0, 8, 0, 512, 128),
        (0, 8, 1024, 640, 128),
        (8, 9, 0, 0, 512),
        (8, 9, 0, 512, 256),
    )
    kv_grads = (
        kv_grad_a,
        second_term_a.astype(bf16),
        out_grad_d,
        kv_grad_d,
        second_term_d.astype(bf16),
    )
    kv = sum_weights(kv_grads, cuts, 768, place, kv_sent, got, qo_sent, (), last_sent)
    kv_a, kv_d = kv[:64], kv[64:, :640]
    qo_a, qo_b = qo[:128], qo[128:]
    kv_other = mp_swap(held(kv_part[BLOCK:].astype(bf16), (*kv_sent, grads[0])), 4)
    kv_sum = kv_part[:BLOCK] + kv_other.astype(f32)
    kv_raw_delta = jnp.concatenate(
        [unrotate(kv_sum[:, :HD], own_cos, own_sin), kv_sum[:, HD:]], axis=1
    ).astype(bf16)

    out = pair_sum(out, mp_swap, (grads[0],))
    prefix_output = (hidden_d + out[:PREF]).astype(bf16)[None]
    action_output = (hidden_a + out[PREF:, :DA])[:ACT].astype(bf16)[None]

    last_d = jnp.concatenate([kv_d, qo_b[:72]], axis=1).reshape(8, 9, wide)
    last_a = jnp.concatenate(
        [kv_a[:, :640], qo_a[:64], qo_a[64:], qo_b[72:], kv_a[:, 640:]], axis=1
    ).reshape(8, 8, -1)
    last = jnp.concatenate(
        [
            last_d[:, :8],
            last_a,
            jnp.pad(last_d[:, 8:].reshape(8, 8, wide // 8), ((0, 0), (0, 0), (0, 48))),
        ],
        axis=2,
    )
    last = scatter_direct(fence(last, grads[0]), yz, yz_swap)
    ninth = last[:, last.shape[1] - 256 : last.shape[1] - 48].reshape(1, wide)
    grads_d = join(last[:, :wide], ninth)
    grads_a = last[:, wide : last.shape[1] - 256]

    def split_grads(grads, query, key, value, gain):
        key_grad = grads[:, :256]
        value_grad = grads[:, 256:512]
        second = grads[:, 512]
        query_grad = grads[:, 640:1664]
        first = (
            jnp.sum(query_grad * query.astype(f32), axis=1)
            + jnp.sum(key_grad * key.astype(f32), axis=1)
            + jnp.sum(value_grad * value.astype(f32), axis=1)
        ) / gain.astype(f32)
        return query_grad, key_grad, value_grad, first, second

    gd = split_grads(grads_d, prefix_query, prefix_key, prefix_value, prefix_first_gain)
    ga = split_grads(grads_a, action_query, action_key, action_value, action_first_gain)
    action_out_grad = grads_a[:, 1664:2688]
    prefix_out_grad = grads_a[:, 2688:]

    first_delta_d = dot_t(query_delta[:PREF], wq_d) + dot_t(kv_raw_delta[:PREF], wkv_d)
    first_delta_a = dot_t(query_delta[PREF:], wq_a) + dot_t(kv_raw_delta[PREF:], wkv_a)
    first_gain_d, first_gain_a = gain_rows(gains_d)[0], gain_rows(gains_a)[0]
    input_d = hidden_delta_d + normalize_back(x_d, rms_d, first_gain_d, first_delta_d)
    input_a = hidden_delta_a + normalize_back(x_a, rms_a, first_gain_a, first_delta_a)

    return (
        prefix_output,
        action_output,
        input_d.astype(bf16)[None],
        input_a[:ACT].astype(bf16)[None],
        gd[0],
        gd[1],
        gd[2],
        prefix_out_grad,
        gd[3],
        gd[4],
        ga[0],
        ga[1],
        ga[2],
        action_out_grad,
        ga[3],
        ga[4],
        finished[0].T,
        finished[1].T,
        finished[2],
        finished[3][None],
        finished[4][None],
        finished[5][None],
    )


def solution(mesh):
    rows = P("dp", "mp", None)
    both = P(("dp", "mp"), None)
    vector = P(("dp", "mp"))
    slots = P("mp", None, None)
    return jax.shard_map(
        on_device,
        mesh=mesh,
        in_specs=(rows,) * 4
        + (P("dp", None), P("dp", None), P())
        + (both,) * 4
        + (vector,) * 2
        + (both,) * 4
        + (vector,) * 2
        + (P(None, "mp"), P(None, "mp"), P("mp", None))
        + (slots,) * 3,
        out_specs=(rows,) * 4
        + (both,) * 4
        + (vector,) * 2
        + (both,) * 4
        + (vector,) * 2
        + (P(None, "mp"), P(None, "mp"), P("mp", None))
        + (slots,) * 3,
        check_vma=False,
    )
```
